32 devices in a mesh: fsdp: 4 (over x, core), ctx: 8 (over z, y).
Axes of the slice: x: 2, y: 2, z: 4, core: 2. Of those that a mesh axis runs over, the one named last changes fastest.
Arguments:
- layer_input: bfloat16 [8192, 1024], P(('fsdp', 'ctx')), may hold values from -6 to 6
- positions: int32 [8192], P(('fsdp', 'ctx')), may hold values from 0 to 3070, as said below
- value_expert_routes: int32 [8192, 4, 2], P(('fsdp', 'ctx')), may hold values from 0 to 4, all different within a row
- output_expert_routes: int32 [8192, 4, 2], P(('fsdp', 'ctx')), may hold values from 0 to 4, all different within a row
- first_layernorm_gain: bfloat16 [1024], P('ctx'), may hold values from 0.25 to 1.75
- first_layernorm_bias: bfloat16 [1024], P('ctx'), may hold values from -4 to 4
- query_weight: bfloat16 [1024, 448], P('ctx'), may hold values from -0.1875 to 0.1875
- key_weight: bfloat16 [1024, 448], P('ctx'), may hold values from -0.1875 to 0.1875
- relative_weight: bfloat16 [1024, 448], P('ctx'), may hold values from -0.25 to 0.25
- content_query_bias: bfloat16 [4, 112], replicated, may hold values from -4 to 4
- position_query_bias: bfloat16 [4, 112], replicated, may hold values from -4 to 4
- value_select_weight: bfloat16 [1024, 20], P('ctx'), may hold values from -0.125 to 0.125
- value_expert_weight: bfloat16 [1024, 2240], P('ctx'), may hold values from -0.1875 to 0.1875
- output_select_weight: bfloat16 [1024, 20], P('ctx'), may hold values from -0.125 to 0.125
- output_expert_weight: bfloat16 [2240, 1024], P('ctx'), as said below
- second_layernorm_gain: bfloat16 [1024], P('ctx'), may hold values from 0.25 to 1.75
- second_layernorm_bias: bfloat16 [1024], P('ctx'), may hold values from -4 to 4
- feedforward_in_weight1: bfloat16 [1024, 4096], P('ctx'), may hold values from -0.1875 to 0.1875
- feedforward_in_bias1: bfloat16 [4096], P('ctx'), may hold values from -4 to 4
- feedforward_out_weight2: bfloat16 [4096, 1024], P('ctx'), may hold values from -0.125 to 0.125
- feedforward_out_bias2: bfloat16 [1024], P('ctx'), may hold values from -4 to 4
- cotangent: bfloat16 [8192, 1024], P(('fsdp', 'ctx')), may hold values from -6 to 6
Outputs:
- output: bfloat16 [8192, 1024], P(('fsdp', 'ctx'))
- d_input: float32 [8192, 1024], P(('fsdp', 'ctx'))
- grad_ln1_gain: float32 [1024], P('ctx')
- grad_ln1_bias: float32 [1024], P('ctx')
- grad_w_query: float32 [1024, 448], P('ctx')
- grad_w_key: float32 [1024, 448], P('ctx')
- grad_w_rel: float32 [1024, 448], P('ctx')
- grad_u_bias: float32 [4, 112], replicated
- grad_v_bias: float32 [4, 112], replicated
- grad_w_vsel: float32 [1024, 20], P('ctx')
- grad_w_value: float32 [1024, 2240], P('ctx')
- grad_w_osel: float32 [1024, 20], P('ctx')
- grad_w_out: float32 [2240, 1024], P('ctx')
- grad_ln2_gain: float32 [1024], P('ctx')
- grad_ln2_bias: float32 [1024], P('ctx')
- grad_w_ffn1: float32 [1024, 4096], P('ctx')
- grad_b_ffn1: float32 [4096], P('ctx')
- grad_w_ffn2: float32 [4096, 1024], P('ctx')
- grad_b_ffn2: float32 [1024], P('ctx')
The draws below stay inside these ranges and needn't reach their ends.
Inputs may be any that keep to these rules, and one draw needn't show every extreme that they name: Within each sequence of 2048 tokens the positions start at 0 and rise by 1 or 2 from one token to the next, by 2 at exactly (2047) // 2 of the steps, so that every sequence ends at the largest value. `value_expert_routes`: in each token and head the 2 experts differ. `output_expert_routes`: in each token and head the 2 experts differ. `output_expert_weight`: entries of mean zero.
All inputs are finite; a program needn't handle non-finite values.
Results may differ from the reference program's by a relative error of at most 0.025.
Values may be sent and summed in bfloat16 or wider, within the bound.
A program may use at most 256 MiB of HBM per device.

```python
import math
import jax
import jax.numpy as jnp
from jax import lax

MODEL_DIM = 1024
HEAD_COUNT = 4
HEAD = 112
EXPERT_COUNT = 5
TOP = 2
FF = 4096
SEQ_LEN = 2048
SEQS = 4
TOKENS = 8192


def draw_positions(key, part):
    key = jax.random.fold_in(key, 11)
    step_count = SEQ_LEN - 1
    double_count = step_count // 2
    seq_keys = jax.random.split(key, SEQS)
    orders = jax.vmap(lambda one_key: jax.random.permutation(one_key, step_count))(seq_keys)
    steps = 1 + (orders < double_count).astype(jnp.int32)
    places = jnp.concatenate([jnp.zeros((SEQS, 1), jnp.int32), jnp.cumsum(steps, axis=1).astype(jnp.int32)], axis=1)
    return places.reshape(SEQS * SEQ_LEN)


def draw_output_expert_weight(key, part):
    key = jax.random.fold_in(key, 23)
    spread = jnp.sqrt(SEQ_LEN / 2048.0)
    return (jax.random.truncated_normal(key, -6.0, 6.0, (HEAD_COUNT * EXPERT_COUNT * HEAD, MODEL_DIM), jnp.float32) * spread).astype(jnp.bfloat16)


def block_scale(own_key, shape, pieces, low, top_value):
    level, own = 1.0, jax.random.fold_in(own_key, 6)
    for position, shards_of in pieces:
        steps = jnp.exp(jax.random.uniform(jax.random.fold_in(own, position), (shards_of,), jnp.float32, low / len(pieces), top_value / len(pieces)))
        level = level * jnp.repeat(steps, shape[position] // shards_of).reshape([-1 if axis == position else 1 for axis in range(len(shape))])
    return level


def different_ones(key, rows, number_of, top, lift):
    sequence = jax.random.permutation(jax.random.fold_in(key, 1), number_of)
    pull = sequence
    for power in range(3):
        pull = pull * pull // number_of
    pull = pull * lift // number_of
    chance = jax.random.randint(jax.random.fold_in(key, 2), (rows, number_of), 0, 4096) + pull
    holders = jax.random.permutation(jax.random.fold_in(key, 3), rows)[jnp.arange(number_of) % rows]
    chance = jnp.where(jnp.arange(rows)[:, None] == holders[None, :], 1 << 14, chance)
    score = chance * number_of + jnp.arange(number_of)
    return lax.top_k(score.astype(jnp.int32), top)[1].astype(jnp.int32)


def noise(stream_key, dims, deviation, bound, shards=(), held_as=jnp.bfloat16):
    drawn = jax.random.normal(stream_key, dims, jnp.float32) * deviation
    if len(shards) > 0:
        drawn = block_scale(stream_key, dims, shards, -0.22, 0.18) * drawn
    return jnp.clip(drawn, min=-bound, max=bound).astype(held_as)


def setup_inputs(seed: int = 0) -> dict:
    streams_of = jax.random.split(jax.random.key(seed), 23)
    return {
        "layer_input": noise(streams_of[0], (TOKENS, MODEL_DIM), 1.0, 6.0, ((0, 32),)),
        "positions": draw_positions(jax.random.fold_in(streams_of[22], 71), 0),
        "value_expert_routes": different_ones(streams_of[2], TOKENS * HEAD_COUNT, EXPERT_COUNT, TOP, 0).reshape((TOKENS, HEAD_COUNT, TOP)),
        "output_expert_routes": different_ones(streams_of[3], TOKENS * HEAD_COUNT, EXPERT_COUNT, TOP, 3276).reshape((TOKENS, HEAD_COUNT, TOP)),
        "first_layernorm_gain": jnp.clip(1.0 + 0.15 * jax.random.normal(streams_of[4], (MODEL_DIM,), jnp.float32), 0.25, 1.75).astype(jnp.bfloat16),
        "first_layernorm_bias": noise(streams_of[5], (MODEL_DIM,), 0.3, 4.0, ((0, 8),)),
        "query_weight": noise(streams_of[6], (MODEL_DIM, HEAD_COUNT * HEAD), MODEL_DIM ** -0.5, 0.1875, ((0, 8),)),
        "key_weight": noise(streams_of[7], (MODEL_DIM, HEAD_COUNT * HEAD), MODEL_DIM ** -0.5, 0.1875, ((0, 8),)),
        "relative_weight": noise(streams_of[8], (MODEL_DIM, HEAD_COUNT * HEAD), (HEAD_COUNT * HEAD) ** -0.5, 0.25, ((0, 8),)),
        "content_query_bias": noise(streams_of[9], (HEAD_COUNT, HEAD), 0.5, 4.0),
        "position_query_bias": noise(streams_of[10], (HEAD_COUNT, HEAD), 0.5, 4.0),
        "value_select_weight": noise(streams_of[11], (MODEL_DIM, HEAD_COUNT * EXPERT_COUNT), (2 * MODEL_DIM) ** -0.5, 0.125, ((0, 8),)),
        "value_expert_weight": noise(streams_of[12], (MODEL_DIM, HEAD_COUNT * EXPERT_COUNT * HEAD), MODEL_DIM ** -0.5, 0.1875, ((0, 8),)),
        "output_select_weight": noise(streams_of[13], (MODEL_DIM, HEAD_COUNT * EXPERT_COUNT), (2 * MODEL_DIM) ** -0.5, 0.125, ((0, 8),)),
        "output_expert_weight": draw_output_expert_weight(jax.random.fold_in(streams_of[22], 71), 0),
        "second_layernorm_gain": jnp.clip(1.0 + 0.15 * jax.random.normal(streams_of[15], (MODEL_DIM,), jnp.float32), 0.25, 1.75).astype(jnp.bfloat16),
        "second_layernorm_bias": noise(streams_of[16], (MODEL_DIM,), 0.3, 4.0, ((0, 8),)),
        "feedforward_in_weight1": noise(streams_of[17], (MODEL_DIM, FF), MODEL_DIM ** -0.5, 0.1875, ((0, 8),)),
        "feedforward_in_bias1": noise(streams_of[18], (FF,), 0.3, 4.0, ((0, 8),)),
        "feedforward_out_weight2": noise(streams_of[19], (FF, MODEL_DIM), (FF // 2) ** -0.5, 0.125, ((0, 8),)),
        "feedforward_out_bias2": noise(streams_of[20], (MODEL_DIM,), 0.3, 4.0, ((0, 8),)),
        "cotangent": noise(streams_of[21], (TOKENS, MODEL_DIM), 1.0, 6.0, ((0, 32),)),
    }


norm_eps = 1e-05
masked_score = -1e+30
highest = lax.Precision.HIGHEST

@jax.custom_vjp
def low(v):
    return lax.optimization_barrier(v.astype(jnp.bfloat16)).astype(jnp.float32)

@jax.custom_vjp
def low_back(v):
    return v

def low_keep(v):
    return (low(v), None)

def low_pass(kept, grad):
    return (grad,)

def back_keep(v):
    return (v, None)

def back_low(kept, grad):
    return (low(grad),)
low.defvjp(low_keep, low_pass)
low_back.defvjp(back_keep, back_low)

def layer_norm(values_in, gain, shift):
    center = lax.optimization_barrier(jnp.mean(values_in, axis=-1, keepdims=True))
    offsets = values_in - center
    spread = lax.optimization_barrier(jnp.mean(offsets * offsets, axis=-1, keepdims=True))
    return offsets * lax.rsqrt(spread + norm_eps) * gain + shift

def frequencies(model_width):
    return 1.0 / 10000.0 ** (jnp.arange(0, model_width, 2, dtype=jnp.float32) / model_width)

def routing_mask(routes, experts_total):
    labels = jnp.arange(experts_total, dtype=jnp.int32)
    return lax.optimization_barrier(jnp.sum((routes[..., None] == labels).astype(jnp.float32), axis=-2))

def matrix_product(spec, left, right):
    return jnp.einsum(spec, left, right, precision=highest)

def sequence_layer(parameters, seq_hidden, places, value_routing, oroutes):
    first_norm_gain, first_norm_shift, query_matrix, key_matrix, relative_matrix, content_bias_vector, position_bias_vector, value_select_matrix, value_matrix, output_select_matrix, output_matrix, second_norm_gain, second_norm_shift, feedforward_in_matrix, feedforward_in_bias, feedforward_out_matrix, feedforward_out_bias = parameters
    sequence_length, model_width = seq_hidden.shape
    heads_total, head_size = content_bias_vector.shape
    experts_total = value_select_matrix.shape[1] // heads_total
    half_width = model_width // 2
    score_scale = 1.0 / math.sqrt(head_size)
    normalized_reduced = low(layer_norm(seq_hidden, first_norm_gain, first_norm_shift))
    query = low_back(matrix_product('lh,hc->lc', normalized_reduced, query_matrix)).reshape(sequence_length, heads_total, head_size)
    q_content = low((query + content_bias_vector) * score_scale)
    q_position = low(query + position_bias_vector)
    rel_query = low_back(matrix_product('thc,dhc->thd', q_position, relative_matrix.reshape(model_width, heads_total, head_size)))
    angle_rows = places.astype(jnp.float32)[:, None] * frequencies(model_width)[None, :]
    query_sin = jnp.sin(angle_rows)[:, None, :]
    query_cos = jnp.cos(angle_rows)[:, None, :]
    part_sin = rel_query[..., :half_width]
    part_cos = rel_query[..., half_width:]
    g_position = low(jnp.concatenate([part_sin * query_sin + part_cos * query_cos, part_cos * query_sin - part_sin * query_cos], axis=-1) * score_scale)
    key_features = low(jnp.concatenate([jnp.cos(angle_rows), jnp.sin(angle_rows)], axis=-1))
    keys = low(low_back(matrix_product('lh,hc->lc', normalized_reduced, key_matrix))).reshape(sequence_length, heads_total, head_size)
    value_select_sigmoid = jax.nn.sigmoid(low_back(matrix_product('lh,hc->lc', normalized_reduced, value_select_matrix))).reshape(sequence_length, heads_total, experts_total)
    value_expert_gate = value_select_sigmoid * routing_mask(value_routing, experts_total)
    expert_vals = low_back(matrix_product('lh,hc->lc', normalized_reduced, value_matrix)).reshape(sequence_length, heads_total, experts_total, head_size)
    values = low(lax.optimization_barrier(jnp.sum(value_expert_gate[..., None] * expert_vals, axis=2)))
    block_rows = math.gcd(sequence_length, 512)
    key_index = jnp.arange(sequence_length, dtype=jnp.int32)

    def attend(start):
        content_blk = lax.dynamic_slice_in_dim(q_content, start, block_rows, 0)
        position_blk = lax.dynamic_slice_in_dim(g_position, start, block_rows, 0)
        scores = low_back(matrix_product('thc,khc->htk', content_blk, keys) + matrix_product('thd,kd->htk', position_blk, key_features))
        row_index = start + jnp.arange(block_rows, dtype=jnp.int32)
        allowed = key_index[None, :] <= row_index[:, None]
        scores = jnp.where(allowed[None], scores, masked_score)
        largest = lax.optimization_barrier(jnp.max(scores, axis=-1, keepdims=True))
        expos = jnp.exp(scores - largest)
        probs = expos / lax.optimization_barrier(jnp.sum(expos, axis=-1, keepdims=True))
        return matrix_product('htk,khc->thc', low(probs), values)
    starts = jnp.arange(0, sequence_length, block_rows, dtype=jnp.int32)
    attn_o = lax.map(jax.checkpoint(attend), starts).reshape(sequence_length, heads_total, head_size)
    attn_o = low_back(attn_o)
    osel_sig = jax.nn.sigmoid(low_back(matrix_product('lh,hc->lc', normalized_reduced, output_select_matrix))).reshape(sequence_length, heads_total, experts_total)
    out_gate = osel_sig * routing_mask(oroutes, experts_total)
    mixed = low(out_gate[..., None] * attn_o[:, :, None, :]).reshape(sequence_length, heads_total * experts_total * head_size)
    attn_out = low_back(matrix_product('tk,kd->td', mixed, output_matrix))
    middle = seq_hidden + attn_out
    normed_two_low = low(layer_norm(middle, second_norm_gain, second_norm_shift))
    pre_act = low_back(matrix_product('td,df->tf', normed_two_low, feedforward_in_matrix) + feedforward_in_bias)
    act = low(jax.nn.gelu(pre_act, approximate=True))
    return middle + low_back(matrix_product('tf,fd->td', act, feedforward_out_matrix) + feedforward_out_bias)

def reference(layer_input, positions, value_expert_routes, output_expert_routes, first_layernorm_gain, first_layernorm_bias, query_weight, key_weight, relative_weight, content_query_bias, position_query_bias, value_select_weight, value_expert_weight, output_select_weight, output_expert_weight, second_layernorm_gain, second_layernorm_bias, feedforward_in_weight1, feedforward_in_bias1, feedforward_out_weight2, feedforward_out_bias2, cotangent):
    parameters = tuple((weight_matrix.astype(jnp.float32) for weight_matrix in (first_layernorm_gain, first_layernorm_bias, query_weight, key_weight, relative_weight, content_query_bias, position_query_bias, value_select_weight, value_expert_weight, output_select_weight, output_expert_weight, second_layernorm_gain, second_layernorm_bias, feedforward_in_weight1, feedforward_in_bias1, feedforward_out_weight2, feedforward_out_bias2)))
    seq_hidden = layer_input.astype(jnp.float32).reshape(SEQS, SEQ_LEN, MODEL_DIM)
    seq_places = positions.reshape(SEQS, SEQ_LEN)
    seq_vroutes = value_expert_routes.reshape(SEQS, SEQ_LEN, HEAD_COUNT, TOP)
    seq_oroutes = output_expert_routes.reshape(SEQS, SEQ_LEN, HEAD_COUNT, TOP)

    def forward(weights, hidden_all):

        def per_sequence(bundle):
            return sequence_layer(weights, bundle[0], bundle[1], bundle[2], bundle[3])
        return lax.map(per_sequence, (hidden_all, seq_places, seq_vroutes, seq_oroutes))
    result, pullback = jax.vjp(forward, parameters, seq_hidden)
    grads, d_hidden = pullback(cotangent.astype(jnp.float32).reshape(SEQS, SEQ_LEN, MODEL_DIM))
    return (result.reshape(TOKENS, MODEL_DIM).astype(jnp.bfloat16), d_hidden.reshape(TOKENS, MODEL_DIM), grads[0], grads[1], grads[2], grads[3], grads[4], grads[5], grads[6], grads[7], grads[8], grads[9], grads[10], grads[11], grads[12], grads[13], grads[14], grads[15], grads[16])
```

```python
import functools
import math

import jax
import jax.numpy as jnp
import numpy as np
from jax import lax
from jax.experimental import pallas as pl
from jax.experimental.pallas import tpu as pltpu
from jax.sharding import PartitionSpec as P

MESH = pl.DeviceIdType.MESH
F32 = jnp.float32
BF16 = jnp.bfloat16
LN_EPS = 1e-05
MASKED = -1e30
LANES = 128
SPOT_A, SPOT_B = 63, 127
VMEM = pl.BlockSpec(memory_space=pltpu.VMEM)
ANY = pl.BlockSpec(memory_space=pl.ANY)
DMA = pltpu.SemaphoreType.DMA


def turn_coefficients():
    nodes = (np.cos(np.pi * (np.arange(400) + 0.5) / 400) + 1) / 8
    root = np.sqrt(nodes)
    powers = nodes[:, None] ** np.arange(7)[None, :]
    sine = np.linalg.lstsq(powers, np.sin(2 * np.pi * root) / root, rcond=None)[0]
    cosine = np.linalg.lstsq(powers, np.cos(2 * np.pi * root), rcond=None)[0]
    return [float(v) for v in sine], [float(v) for v in cosine]


SIN_TURN, COS_TURN = turn_coefficients()


def horner(coefs, v):
    total = coefs[-1]
    for coef in coefs[-2::-1]:
        total = total * v + coef
    return total


def turn_table(model_width):
    freq = 10000.0 ** (-np.arange(0, model_width, 2, dtype=np.float64) / model_width) / (2 * np.pi)
    mantissa, exponent = np.frexp(freq)
    coarse = np.ldexp(np.floor(mantissa * 256) / 256, exponent)
    table = np.zeros((8, model_width // 2), np.float32)
    table[0] = coarse
    table[1] = freq - coarse
    return table


def sin_cos(places, table_ref):
    coarse = places * table_ref[0:1, :]
    part = (coarse - jnp.round(coarse)) + places * table_ref[1:2, :]
    part = part - jnp.round(part)
    square = part * part
    return horner(SIN_TURN, square) * part, horner(COS_TURN, square)


def mm(left, right):
    return lax.dot_general(left, right, (((1,), (0,)), ((), ())), preferred_element_type=F32)


def mm_t(left, right):
    return lax.dot_general(left, right, (((1,), (1,)), ((), ())), preferred_element_type=F32)


def mm_left_t(left, right):
    return lax.dot_general(left, right, (((0,), (0,)), ((), ())), preferred_element_type=F32)


def copy_to(src, dst, send, recv, f, c):
    return pltpu.make_async_remote_copy(
        src_ref=src, dst_ref=dst, send_sem=send, recv_sem=recv, device_id=(f, c), device_id_type=MESH
    )


def greet(f, c, fsdp, n):
    barrier = pltpu.get_barrier_semaphore()

    def one(k, _):
        pl.semaphore_signal(barrier, inc=1, device_id=(f, lax.rem(c + k, n)), device_id_type=MESH)
        return 0

    lax.fori_loop(1, n, one, 0)
    for k in range(1, fsdp):
        pl.semaphore_signal(barrier, inc=1, device_id=(f ^ k, c), device_id_type=MESH)
    pl.semaphore_wait(barrier, n - 1 + fsdp - 1)


class LineGather:
    def __init__(self, f, c, n, own, at, recv, right, left, pair, lone=False):
        self.f, self.c, self.n, self.size = f, c, n, n // 2
        self.place, self.bit = c // 2, lax.rem(c, 2)
        self.own, self.at = own, at
        self.recv, self.right, self.left, self.pair = recv, right, left, pair
        self.lone = lone

    def valid(self, o):
        ok = jnp.logical_and(o >= 0, o < self.size)
        if self.lone:
            span = self.size // 4
            ok = jnp.logical_and(ok, jnp.logical_and(o >= self.f * span, o < (self.f + 1) * span))
        return ok

    def slot(self, block):
        return block - self.f * (self.n // 4) if self.lone else block

    def copy(self, src, block, sems, c):
        slot = self.slot(block)
        return copy_to(src, self.at(slot), sems.at[slot], self.recv.at[slot], self.f, c)

    def spread(self, src, block, go_right, go_left):
        @pl.when(go_right)
        def _():
            self.copy(src, block, self.right, self.c + 2).start()

        @pl.when(go_left)
        def _():
            self.copy(src, block, self.left, self.c - 2).start()

        self.copy(src, block, self.pair, self.c + 1 - 2 * self.bit).start()

    def begin(self, local):
        @pl.when(self.valid(self.place))
        def _():
            self.spread(self.own, self.c, self.place < self.size - 1, self.place > 0)
            local()

    def arrived(self, block):
        slot = self.slot(block)
        self.copy(self.at(slot), block, self.pair, self.c).wait_recv()

    def step(self, t):
        for sign in (-1, 1):
            o = self.place + sign * t
            block = 2 * o + self.bit

            @pl.when(self.valid(o))
            def _():
                self.arrived(block)
                self.spread(
                    self.at(self.slot(block)),
                    block,
                    jnp.logical_and(sign < 0, self.place < self.size - 1),
                    jnp.logical_and(sign > 0, self.place > 0),
                )

    def steps(self):
        lax.fori_loop(1, self.size, lambda t, u: (self.step(t), u)[1], 0)

    def finish(self):
        def one(o, _):
            @pl.when(self.valid(o))
            def _():
                self.arrived(2 * o + 1 - self.bit)
                block = 2 * o + self.bit
                source = self.at(self.slot(block))
                self.copy(source, block, self.pair, self.c).wait_send()

                @pl.when(jnp.logical_and(o <= self.place, self.place < self.size - 1))
                def _():
                    self.copy(source, block, self.right, self.c).wait_send()

                @pl.when(jnp.logical_and(o >= self.place, self.place > 0))
                def _():
                    self.copy(source, block, self.left, self.c).wait_send()

            return 0

        lax.fori_loop(0, self.size, one, 0)


class QuadGather:
    def __init__(self, f, c, out, send, recv):
        self.f, self.c, self.out, self.send, self.recv = f, c, out, send, recv

    def copy(self, slot, k, to, src=None):
        src = self.out.at[slot] if src is None else src
        return copy_to(src, self.out.at[slot], self.send.at[k], self.recv.at[slot], to, self.c)

    def begin(self, src=None):
        self.copy(self.f, 1, self.f ^ 2, src).start()
        self.copy(self.f, 0, self.f ^ 1, src).start()

    def got(self, slot):
        self.copy(slot, 0, self.f).wait_recv()

    def relay(self):
        self.got(self.f ^ 2)
        self.copy(self.f ^ 2, 2, self.f ^ 1).start()

    def sent(self):
        for k in range(3):
            self.copy(self.f, k, self.f).wait_send()


def spread_vector(rows, width):
    count = rows.shape[0]
    total = count * width
    lane = lax.broadcasted_iota(jnp.int32, (LANES, total), 0)
    column = lax.broadcasted_iota(jnp.int32, (LANES, total), 1)
    onehot = jnp.where(lane == lax.rem(column, width), 1.0, 0.0).astype(BF16)
    wide = mm(rows.astype(BF16), onehot)
    row = lax.broadcasted_iota(jnp.int32, (count, total), 0)
    column = lax.broadcasted_iota(jnp.int32, (count, total), 1)
    return jnp.sum(jnp.where(column // width == row, wide, 0.0), axis=0, keepdims=True)


def block_of(j, i, groups):
    return i * groups + jnp.where(lax.rem(i, 2) == 0, j, groups - 1 - j)


def holder_of(block, groups):
    row, within = block // groups, lax.rem(block, groups)
    return jnp.where(lax.rem(row, 2) == 0, within, groups - 1 - within), row


def key_places(kv):
    return kv[:, SPOT_A : SPOT_A + 1].astype(F32) * 128.0 + kv[:, SPOT_B : SPOT_B + 1].astype(F32)


def attend_kernel(
    n,
    x_ref, aux_ref, cot_ref, p1_ref, small_ref, wout_ref, bias_ref, table_ref,
    tok_ref, p1g_ref, smallg_ref, woutg_ref, cotg_ref, ev_ref, gates_ref, o_ref,
    qcat_ref, qpos_ref, kv_ref, lse_ref, of_ref,
    qs_ref, kvs_ref, qr_ref, os_ref, kcat_ref, m_ref, l_ref,
    sm_s, sm_r, p_r, p_a, p_b, p_c, w_r, w_a, w_b, w_c,
    t_s, t_r, c_s, c_r, q_s, q_r, kv_s, kv_r, o_s, o_r, loc,
):
    f, c = lax.axis_index("fsdp"), lax.axis_index("ctx")
    groups = n // 4
    seq, turn = c // groups, lax.rem(c, groups)
    tokens, width = x_ref.shape
    scale = 1.0 / math.sqrt(112)
    greet(f, c, 4, n)

    def small_send(k, _):
        to = lax.rem(c + k, n)
        copy_to(small_ref, smallg_ref.at[c], sm_s.at[to], sm_r.at[c], f, to).start()
        return 0

    lax.fori_loop(1, n, small_send, 0)
    smallg_ref[c] = small_ref[...]
    gather_p = LineGather(f, c, n, p1_ref, lambda k: p1g_ref.at[k], p_r, p_a, p_b, p_c)

    def own_p():
        p1g_ref[c] = p1_ref[...]

    gather_p.begin(own_p)
    wout_copy = pltpu.make_async_copy(wout_ref, woutg_ref.at[c - f * groups], loc.at[0])
    gather_w = LineGather(f, c, n, wout_ref, lambda k: woutg_ref.at[k], w_r, w_a, w_b, w_c, lone=True)
    cot_copy = pltpu.make_async_copy(cot_ref, cotg_ref.at[f], loc.at[1])
    cot_copy.start()

    hidden = x_ref[...].astype(F32)
    offsets = hidden - jnp.mean(hidden, axis=1, keepdims=True)
    spread = jnp.mean(offsets * offsets, axis=1, keepdims=True)
    xhat = offsets * lax.rsqrt(spread + LN_EPS)

    def small_wait(k, _):
        to = lax.rem(c + k, n)
        copy_to(small_ref, smallg_ref.at[to], sm_s.at[to], sm_r.at[to], f, to).wait()
        return 0

    lax.fori_loop(1, n, small_wait, 0)
    gain = spread_vector(smallg_ref[:, 0, :], width // n)
    shift = spread_vector(smallg_ref[:, 1, :], width // n)
    tok_ref[f, :, 0:width] = (xhat * gain + shift).astype(BF16)
    tok_ref[f, :, width:] = aux_ref[...]
    tok_gather = QuadGather(f, c, tok_ref, t_s, t_r)
    tok_gather.begin()
    gather_p.steps()
    tok_gather.relay()
    gather_w.begin(wout_copy.start)
    gather_p.finish()
    tok_gather.got(f ^ 1)
    tok_gather.got(f ^ 3)
    tok_gather.sent()
    cot_gather = QuadGather(f, c, cotg_ref, c_s, c_r)
    cot_gather.begin(cot_ref)

    lane = lax.broadcasted_iota(jnp.int32, (tokens, LANES), 1)
    source = lax.broadcasted_iota(jnp.int32, (LANES, LANES), 0)
    target = lax.broadcasted_iota(jnp.int32, (LANES, LANES), 1)
    wanted = f * 16 + lax.rem(target, 8) + jnp.where(target < 16, 8, 0)
    pick = jnp.where(
        jnp.logical_and(source == wanted, jnp.logical_and(target < 32, lax.rem(target, 8) < 5)), 1.0, 0.0
    ).astype(BF16)
    own_turn, own_slot = holder_of(c, groups)

    def project(t, _):
        s = lax.rem(seq + 1 + t, 4)
        normed = tok_ref[s, :, 0:width]
        aux = tok_ref[s, :, width:]
        weights = p1g_ref[...].reshape(width, p1g_ref.shape[2])
        qk = mm(normed, weights[:, 0:256])
        experts = mm(normed, weights[:, 256:896])
        ev_ref[s] = experts.astype(BF16)
        logits = jnp.zeros((tokens, LANES), F32)
        for e in range(5):
            for spot, first in ((SPOT_B, 0), (SPOT_A, 16)):
                column = experts[:, e * LANES + spot : e * LANES + spot + 1]
                logits = jnp.where(
                    jnp.logical_or(lane == first + e, lane == first + 8 + e), column, logits
                )
        sig = jax.nn.sigmoid(logits)
        gates = mm(aux, pick) * jnp.where(lax.rem(lane, 16) >= 8, sig * (1.0 - sig), sig)
        gates_ref[s] = gates
        values = jnp.zeros((tokens, LANES), F32)
        for e in range(5):
            values = values + gates[:, 16 + e : 17 + e] * experts[:, e * LANES : (e + 1) * LANES]
        spots = jnp.logical_or(lane == SPOT_A, lane == SPOT_B)
        values = jnp.where(spots, 0.0, values)
        keys = jnp.where(lane == SPOT_A, aux[:, 64:65].astype(F32), qk[:, 128:256])
        keys = jnp.where(lane == SPOT_B, aux[:, 65:66].astype(F32), keys)
        qs_ref[s] = qk[:, 0:128].astype(BF16)
        kvs_ref[s, :, 0:128] = keys.astype(BF16)
        kvs_ref[s, :, 128:256] = values.astype(BF16)
        to = s * groups + own_turn

        @pl.when(to != c)
        def _():
            copy_to(qs_ref.at[s], qr_ref.at[own_slot], q_s.at[s], q_r.at[own_slot], f, to).start()

        @pl.when(to == c)
        def _():
            qr_ref[own_slot] = qs_ref[s]

        def kv_send(k, _):
            to = s * groups + k

            @pl.when(to != c)
            def _():
                copy_to(kvs_ref.at[s], kv_ref.at[c], kv_s.at[to], kv_r.at[c], f, to).start()

            @pl.when(to == c)
            def _():
                kv_ref[c] = kvs_ref[s]

            return 0

        lax.fori_loop(0, groups, kv_send, 0)
        return 0

    lax.fori_loop(0, 4, project, 0)

    def kv_wait(block):
        @pl.when(block != c)
        def _():
            copy_to(kvs_ref.at[0], kv_ref.at[block], kv_s.at[block], kv_r.at[block], f, c).wait_recv()

    def prepare(i, _):
        block = block_of(turn, i, groups)

        @pl.when(block != c)
        def _():
            copy_to(qs_ref.at[0], qr_ref.at[i], q_s.at[0], q_r.at[i], f, c).wait_recv()

        kv_wait(block)
        query = qr_ref[i].astype(F32)
        q_position = (query + bias_ref[pl.ds(4 + f, 1), :]).astype(BF16)
        qpos_ref[i] = q_position
        qcat_ref[i, :, width:] = ((query + bias_ref[pl.ds(f, 1), :]) * scale).astype(BF16)
        rel = p1g_ref[:, :, 896:].reshape(width, LANES)
        rel_query = mm_t(q_position, rel)
        sine, cosine = sin_cos(key_places(kv_ref[block]), table_ref)
        first, second = rel_query[:, : width // 2], rel_query[:, width // 2 :]
        qcat_ref[i, :, 0 : width // 2] = ((first * sine + second * cosine) * scale).astype(BF16)
        qcat_ref[i, :, width // 2 : width] = ((second * sine - first * cosine) * scale).astype(BF16)
        m_ref[i] = jnp.full((tokens, 1), MASKED, F32)
        l_ref[i] = jnp.zeros((tokens, 1), F32)
        of_ref[i] = jnp.zeros((tokens, LANES), F32)
        return 0

    lax.fori_loop(0, 4, prepare, 0)
    row_in = lax.broadcasted_iota(jnp.int32, (tokens, tokens), 0)
    col_in = lax.broadcasted_iota(jnp.int32, (tokens, tokens), 1)

    def key_block(kb, _):
        own = [block_of(turn, i, groups) for i in range(4)]
        first = sum((b < kb).astype(jnp.int32) for b in own)
        ready = sum((b == kb).astype(jnp.int32) for b in own)

        @pl.when(ready == 0)
        def _():
            kv_wait(kb)

        sine, cosine = sin_cos(key_places(kv_ref[kb]), table_ref)
        kcat_ref[:, 0 : width // 2] = cosine.astype(BF16)
        kcat_ref[:, width // 2 : width] = sine.astype(BF16)
        kcat_ref[:, width:] = kv_ref[kb, :, 0:128]

        def query_block(i, _):
            gap = (block_of(turn, i, groups) - kb) * tokens
            scores = mm_t(qcat_ref[i], kcat_ref[...])
            scores = jnp.where(col_in <= row_in + gap, scores, MASKED)
            before = m_ref[i]
            best = jnp.maximum(before, jnp.max(scores, axis=1, keepdims=True))
            shrink = jnp.exp(before - best)
            probs = jnp.exp(scores - best)
            m_ref[i] = best
            l_ref[i] = l_ref[i] * shrink + jnp.sum(probs, axis=1, keepdims=True)
            of_ref[i] = of_ref[i] * shrink + mm(probs.astype(BF16), kv_ref[kb, :, 128:256])
            return 0

        lax.fori_loop(first, 4, query_block, 0)
        return 0

    lax.fori_loop(0, n, key_block, 0)

    def give(i, _):
        block = block_of(turn, i, groups)
        total = l_ref[i]
        result = of_ref[i] / total
        of_ref[i] = result
        lse_ref[i] = m_ref[i] + jnp.log(total)
        os_ref[i] = result.astype(BF16)

        @pl.when(block != c)
        def _():
            copy_to(os_ref.at[i], o_ref.at[seq], o_s.at[i], o_r.at[seq], f, block).start()

        @pl.when(block == c)
        def _():
            o_ref[seq] = os_ref[i]

        return 0

    lax.fori_loop(0, 4, give, 0)
    gather_w.steps()
    cot_gather.relay()
    cot_gather.got(f ^ 1)
    cot_gather.got(f ^ 3)
    cot_gather.sent()
    gather_w.finish()

    @pl.when(gather_w.valid(c // 2))
    def _():
        wout_copy.wait()

    cot_copy.wait()

    def drain(s, _):
        to = s * groups + own_turn

        @pl.when(to != c)
        def _():
            copy_to(qs_ref.at[s], qr_ref.at[own_slot], q_s.at[s], q_r.at[0], f, to).wait_send()
            copy_to(os_ref.at[0], o_ref.at[s], o_s.at[0], o_r.at[s], f, to).wait_recv()

        @pl.when(block_of(turn, s, groups) != c)
        def _():
            copy_to(os_ref.at[s], o_ref.at[s], o_s.at[s], o_r.at[0], f, to).wait_send()

        return 0

    lax.fori_loop(0, 4, drain, 0)

    def kv_drain(to, _):
        @pl.when(to != c)
        def _():
            copy_to(kvs_ref.at[0], kv_ref.at[0], kv_s.at[to], kv_r.at[0], f, c).wait_send()

        return 0

    lax.fori_loop(0, n, kv_drain, 0)


def sds(shape, dtype):
    return jax.ShapeDtypeStruct(shape, dtype)


def attend(n, x, aux, cot, p1, small, wout, bias, table):
    t, d = x.shape
    rows = p1.shape[0]
    out_rows = wout.shape[0]
    g = n // 4
    return pl.pallas_call(
        functools.partial(attend_kernel, n),
        out_shape=[
            sds((4, t, d + LANES), BF16), sds((n, rows, d), BF16), sds((n, 16, LANES), F32),
            sds((g, out_rows, d), BF16), sds((4, t, d), BF16), sds((4, t, 640), BF16),
            sds((4, t, LANES), F32), sds((4, t, LANES), BF16), sds((4, t, d + LANES), BF16),
            sds((4, t, LANES), BF16), sds((n, t, 256), BF16), sds((4, t, 1), F32), sds((4, t, LANES), F32),
        ],
        in_specs=[VMEM, VMEM, ANY, VMEM, VMEM, ANY, VMEM, VMEM],
        out_specs=[VMEM, VMEM, VMEM, ANY, ANY] + [VMEM] * 8,
        scratch_shapes=[
            pltpu.VMEM((4, t, LANES), BF16), pltpu.VMEM((4, t, 256), BF16), pltpu.VMEM((4, t, LANES), BF16),
            pltpu.VMEM((4, t, LANES), BF16), pltpu.VMEM((t, d + LANES), BF16),
            pltpu.VMEM((4, t, 1), F32), pltpu.VMEM((4, t, 1), F32),
            DMA((n,)), DMA((n,)), DMA((n,)), DMA((n,)), DMA((n,)), DMA((n,)),
            DMA((g,)), DMA((g,)), DMA((g,)), DMA((g,)),
            DMA((3,)), DMA((4,)), DMA((3,)), DMA((4,)), DMA((4,)), DMA((4,)),
            DMA((n,)), DMA((n,)), DMA((4,)), DMA((4,)), DMA((2,)),
        ],
        compiler_params=pltpu.CompilerParams(
            collective_id=0, has_side_effects=True, vmem_limit_bytes=56 << 20
        ),
        name="attend",
    )(x, aux, cot, p1, small, wout, bias, table)


class QuadSum:
    def __init__(self, f, c, core_out, core_in, x_out, x_in, keep, send, recv):
        self.f, self.c = f, c
        self.core_out, self.core_in, self.x_out, self.x_in = core_out, core_in, x_out, x_in
        self.keep, self.send, self.recv = keep, send, recv

    def core(self, k):
        return copy_to(
            self.core_out.at[k], self.core_in.at[k], self.send.at[k], self.recv.at[k], self.f ^ 1, self.c
        )

    def across(self):
        return copy_to(self.x_out, self.x_in, self.send.at[2], self.recv.at[2], self.f ^ 2, self.c)

    def put(self, k, value):
        if k in (1, 3):
            self.core_out[k // 2] = value.astype(BF16)
            self.core(k // 2).start()
        else:
            self.keep[k // 2] = value

    def cross(self):
        self.core(1).wait_recv()
        self.x_out[...] = (self.keep[1] + self.core_in[1].astype(F32)).astype(BF16)
        self.across().start()

    def total(self):
        self.core(0).wait_recv()
        self.across().wait_recv()
        return self.keep[0] + self.core_in[0].astype(F32) + self.x_in[...].astype(F32)

    def sent(self):
        self.core(0).wait_send()
        self.core(1).wait_send()
        self.across().wait_send()


def quad_sum_scratch(t, d):
    return [
        pltpu.VMEM((2, t, d), BF16), pltpu.VMEM((2, t, d), BF16), pltpu.VMEM((t, d), BF16),
        pltpu.VMEM((t, d), BF16), pltpu.VMEM((2, t, d), F32), DMA((3,)), DMA((3,)),
    ]


def layer_stats(v):
    offsets = v - jnp.mean(v, axis=1, keepdims=True)
    scale = lax.rsqrt(jnp.mean(offsets * offsets, axis=1, keepdims=True) + LN_EPS)
    return offsets * scale, scale


def layer_back(grad, gain, xhat, scale):
    inner = grad * gain
    return scale * (
        inner - jnp.mean(inner, axis=1, keepdims=True) - xhat * jnp.mean(inner * xhat, axis=1, keepdims=True)
    )


def gelu_pair(v):
    k = math.sqrt(2.0 / math.pi)
    square = v * v
    t = jnp.tanh(k * v * (1.0 + 0.044715 * square))
    half = 0.5 * (1.0 + t)
    return v * half, half + 0.5 * v * (1.0 - t * t) * (k * (1.0 + 3 * 0.044715 * square))


def bias_quarter(small_ref, f, n, quarter):
    span = n // 4
    shard = quarter // span
    piece = min(LANES, shard)
    lane = lax.broadcasted_iota(jnp.int32, (LANES, quarter), 0)
    column = lax.broadcasted_iota(jnp.int32, (LANES, quarter), 1)
    onehot = jnp.where(lane == lax.rem(column, piece), 1.0, 0.0).astype(BF16)
    row = lax.broadcasted_iota(jnp.int32, (span, quarter), 0)
    column = lax.broadcasted_iota(jnp.int32, (span, quarter), 1)
    total = jnp.zeros((1, quarter), F32)
    for k in range(shard // piece):
        rows = small_ref[pl.ds(f * span, span), 5 + k, :]
        wide = mm(rows.astype(BF16), onehot)
        keep = jnp.logical_and(column // shard == row, lax.rem(column, shard) // piece == k)
        total = total + jnp.sum(jnp.where(keep, wide, 0.0), axis=0, keepdims=True)
    return total


def feed_kernel(
    n,
    x_ref, cot_ref, gates_ref, o_ref, wout_ref, small_ref, w1_ref, w2_ref,
    out_ref, dmid_ref, gwout_ref, gw1_ref, gw2_ref, da_ref, gsel_ref, vec_ref,
    w1g, w2g, n2_ref, act_ref, slope_ref, dpre_ref, mixed_ref, dml_ref, mid_ref,
    a0, a1, a2, a3, a4, a5, a6, b0, b1, b2, b3, b4, b5, b6, e0, e1, e2, e3, e4, e5, e6,
    w1_r, w1_a, w1_b, w1_c, w2_r, w2_a, w2_b, w2_c, n_s, n_r, d_s, d_r, loc,
):
    f, c = lax.axis_index("fsdp"), lax.axis_index("ctx")
    tokens, width = x_ref.shape
    quarter = w1g.shape[1]
    greet(f, c, 4, n)
    rows1, rows2 = w1_ref.shape[0], w2_ref.shape[0]
    own1 = w1_ref.at[:, pl.ds(pl.multiple_of(f * quarter, LANES), quarter)]
    at1 = lambda k: w1g.at[pl.ds(pl.multiple_of(k * rows1, rows1), rows1), :]
    at2 = lambda k: w2g.at[pl.ds(pl.multiple_of(k * rows2, rows2), rows2), :]
    gather1 = LineGather(f, c, n, own1, at1, w1_r, w1_a, w1_b, w1_c)
    gather2 = LineGather(f, c, n, w2_ref, at2, w2_r, w2_a, w2_b, w2_c, lone=True)
    local1 = pltpu.make_async_copy(own1, at1(c), loc.at[0])
    local2 = pltpu.make_async_copy(w2_ref, at2(c - f * (n // 4)), loc.at[1])
    gather1.begin(local1.start)
    gather2.begin(local2.start)
    attn_sum = QuadSum(f, c, a0, a1, a2, a3, a4, a5, a6)
    back_sum = QuadSum(f, c, b0, b1, b2, b3, b4, b5, b6)
    out_sum = QuadSum(f, c, e0, e1, e2, e3, e4, e5, e6)

    for k in (3, 2, 1, 0):
        r = f ^ k
        for e in range(5):
            mixed_ref[r, :, e * LANES : (e + 1) * LANES] = (
                gates_ref[r, :, e : e + 1] * o_ref[r].astype(F32)
            ).astype(BF16)
        attn_sum.put(k, mm(mixed_ref[r], wout_ref[...]))
        if k == 2:
            attn_sum.cross()
    gather1.step(1)
    middle = x_ref[...].astype(F32) + attn_sum.total()
    mid_ref[...] = middle
    xhat, scale = layer_stats(middle)
    gain = spread_vector(small_ref[:, 2, :], width // n)
    shift = spread_vector(small_ref[:, 3, :], width // n)
    n2_ref[f] = (xhat * gain + shift).astype(BF16)
    n2_gather = QuadGather(f, c, n2_ref, n_s, n_r)
    n2_gather.begin()
    lax.fori_loop(2, n // 2, lambda t, u: (gather1.step(t), u)[1], 0)
    gather1.finish()
    local1.wait()
    gather2.step(1)
    first_bias = bias_quarter(small_ref, f, n, quarter)

    def enter(k):
        r = f ^ k
        act, slope = gelu_pair(mm(n2_ref[r], w1g[...]) + first_bias)
        act_ref[r] = act.astype(BF16)
        slope_ref[r] = slope

    enter(0)
    n2_gather.got(f ^ 1)
    enter(1)
    n2_gather.relay()
    enter(2)
    n2_gather.got(f ^ 3)
    enter(3)
    lax.fori_loop(2, n // 2, lambda t, u: (gather2.step(t), u)[1], 0)
    gather2.finish()

    @pl.when(gather2.valid(c // 2))
    def _():
        local2.wait()

    for k in (3, 2, 1, 0):
        r = f ^ k
        d_act = mm_t(cot_ref[r], w2g[...])
        dpre_ref[r] = (d_act * slope_ref[r]).astype(BF16)
        back_sum.put(k, mm_t(dpre_ref[r], w1g[...]))
        if k == 2:
            back_sum.cross()
    for k in (3, 2, 1, 0):
        out_sum.put(k, mm(act_ref[f ^ k], w2g[...]))
    tile = 256
    all_tokens = 4 * tokens

    def weight_tile(left_ref, right_ref, result_ref):
        def one(i, _):
            spot = pl.multiple_of(i * tile, tile)
            left = left_ref[:, :, pl.ds(spot, tile)].reshape(all_tokens, tile)
            right = right_ref[...].reshape(all_tokens, right_ref.shape[2])
            result_ref[pl.ds(spot, tile), :] = mm_left_t(left, right).astype(BF16)
            return 0

        lax.fori_loop(0, left_ref.shape[2] // tile, one, 0)

    weight_tile(act_ref, cot_ref, gw2_ref)
    weight_tile(n2_ref, dpre_ref, gw1_ref)
    d_norm = back_sum.total()
    xhat, scale = layer_stats(mid_ref[...])
    d_middle = cot_ref[f].astype(F32) + layer_back(d_norm, gain, xhat, scale)
    dmid_ref[...] = d_middle
    dml_ref[f] = d_middle.astype(BF16)
    dml_gather = QuadGather(f, c, dml_ref, d_s, d_r)
    dml_gather.begin()
    out_sum.cross()
    vec_ref[...] = jnp.zeros_like(vec_ref)
    vec_ref[0:1, :] = jnp.sum(d_norm * xhat, axis=0, keepdims=True)
    vec_ref[1:2, :] = jnp.sum(d_norm, axis=0, keepdims=True)
    vec_ref[2:3, :] = jnp.sum(cot_ref[f].astype(F32), axis=0, keepdims=True)
    total = jnp.zeros((1, quarter), F32)
    for r in range(4):
        total = total + jnp.sum(dpre_ref[r].astype(F32), axis=0, keepdims=True)
    vec_ref[3:4, :] = total
    lane = lax.broadcasted_iota(jnp.int32, (tokens, LANES), 1)

    def leave(k):
        r = f ^ k
        d_attn = jnp.zeros((tokens, LANES), F32)
        select = jnp.zeros((tokens, LANES), F32)
        result = o_ref[r].astype(F32)
        d_mixed = mm_t(dml_ref[r], wout_ref[...])
        for e in range(5):
            part = d_mixed[:, e * LANES : (e + 1) * LANES]
            d_attn = d_attn + gates_ref[r, :, e : e + 1] * part
            column = jnp.sum(result * part, axis=1, keepdims=True) * gates_ref[r, :, 8 + e : 9 + e]
            select = jnp.where(lane == e, column, select)
        da_ref[r] = d_attn.astype(BF16)
        gsel_ref[r] = select

    leave(0)
    dml_gather.got(f ^ 1)
    leave(1)
    dml_gather.relay()
    leave(2)
    dml_gather.got(f ^ 3)
    leave(3)

    def out_tile(i, _):
        spot = pl.multiple_of(i * LANES, LANES)
        left = mixed_ref[:, :, pl.ds(spot, LANES)].reshape(all_tokens, LANES)
        right = dml_ref[...].reshape(all_tokens, width)
        gwout_ref[pl.ds(spot, LANES), :] = mm_left_t(left, right).astype(BF16)
        return 0

    lax.fori_loop(0, 5, out_tile, 0)
    second_bias = spread_vector(small_ref[:, 4, :], width // n)
    out_ref[...] = (mid_ref[...] + out_sum.total() + second_bias).astype(BF16)
    for one in (attn_sum, back_sum, out_sum, n2_gather, dml_gather):
        one.sent()


def feed(n, x, cot, gates, o, wout, small, w1, w2):
    t, d = x.shape
    quarter = w1.shape[1] // 4
    g = n // 4
    return pl.pallas_call(
        functools.partial(feed_kernel, n),
        out_shape=[
            sds((t, d), BF16), sds((t, d), F32), sds((640, d), BF16), sds((d, quarter), BF16),
            sds((quarter, d), BF16), sds((4, t, LANES), BF16), sds((4, t, LANES), F32), sds((8, d), F32),
        ],
        in_specs=[VMEM] * 6 + [ANY, ANY],
        out_specs=[VMEM] * 8,
        scratch_shapes=[
            pltpu.VMEM((d, quarter), BF16), pltpu.VMEM((quarter, d), BF16), pltpu.VMEM((4, t, d), BF16),
            pltpu.VMEM((4, t, quarter), BF16), pltpu.VMEM((4, t, quarter), F32), pltpu.VMEM((4, t, quarter), BF16),
            pltpu.VMEM((4, t, 640), BF16), pltpu.VMEM((4, t, d), BF16), pltpu.VMEM((t, d), F32),
        ]
        + quad_sum_scratch(t, d) * 3
        + [DMA((n,))] * 4 + [DMA((g,))] * 4
        + [DMA((3,)), DMA((4,)), DMA((3,)), DMA((4,)), DMA((2,))],
        compiler_params=pltpu.CompilerParams(
            collective_id=1, has_side_effects=True, vmem_limit_bytes=60 << 20
        ),
        name="feed",
    )(x, cot, gates, o, wout, small, w1, w2)


class LineSum:
    def __init__(self, f, c, n, source, got, inbox, stage, pair_s, pair_r, line_s, line_r, subs, lone=False):
        self.f, self.c, self.n, self.size = f, c, n, n // 2
        self.place, self.bit = c // 2, lax.rem(c, 2)
        self.source = source
        self.got, self.inbox, self.stage = got, inbox, stage
        self.pair_s, self.pair_r, self.line_s, self.line_r = pair_s, pair_r, line_s, line_r
        self.subs, self.lone = subs, lone
        self.span = self.size // 4 if lone else self.size
        self.first = f * self.span if lone else 0

    def valid(self, o):
        return jnp.logical_and(o >= self.first, o < self.first + self.span)

    def index(self, o, sub):
        return (o - self.first) * self.subs + sub

    def term(self, o, sub, bit):
        return self.source(2 * (o - self.first) + bit, sub)

    def pair_copy(self, o, sub):
        i = self.index(o, sub)
        return copy_to(
            self.term(o, sub, 1 - self.bit), self.got.at[i], self.pair_s.at[i], self.pair_r.at[i],
            self.f, self.c + 1 - 2 * self.bit,
        )

    def line_copy(self, i, slot, c):
        return copy_to(self.stage.at[i], self.inbox.at[slot], self.line_s.at[i], self.line_r.at[slot], self.f, c)

    def each(self, work):
        def one(k, _):
            work(self.first + k // self.subs, lax.rem(k, self.subs))
            return 0

        lax.fori_loop(0, self.span * self.subs, one, 0)

    def begin(self):
        self.each(lambda o, sub: self.pair_copy(o, sub).start())

    def gathered(self, o, sub):
        self.pair_copy(o, sub).wait_recv()
        return self.term(o, sub, self.bit)[...].astype(F32) + self.got[self.index(o, sub)].astype(F32)

    def extra(self, sub):
        return self.span * self.subs + sub

    def move(self, o, sub, go_right):
        i = self.index(o, sub)
        total = self.gathered(o, sub)
        starts = self.place == 0 if go_right else self.place == self.size - 1

        @pl.when(starts)
        def _():
            self.stage[i] = total.astype(BF16)

        @pl.when(jnp.logical_not(starts))
        def _():
            self.line_copy(i, i, self.c).wait_recv()
            self.stage[i] = (total + self.inbox[i].astype(F32)).astype(BF16)

        if go_right:
            self.line_copy(i, i, self.c + 2).start()
        else:
            slot = jnp.where(o == self.place - 1, self.extra(sub), i)
            self.line_copy(i, slot, self.c - 2).start()

    def step(self, k):
        def one(sub, _):
            far, near = self.size - 1 - k, k

            @pl.when(jnp.logical_and(self.valid(far), far > self.place))
            def _():
                self.move(far, sub, True)

            @pl.when(jnp.logical_and(self.valid(near), near < self.place))
            def _():
                self.move(near, sub, False)

            return 0

        lax.fori_loop(0, self.subs, one, 0)

    def settle(self, sub):
        i = self.index(self.place, sub)
        self.stage[i] = self.gathered(self.place, sub).astype(BF16)
        own = self.gathered_again(self.place, sub)

        left = self.place > 0
        right = self.place < self.size - 1

        @pl.when(left)
        def _():
            self.line_copy(i, i, self.c).wait_recv()

        @pl.when(right)
        def _():
            self.line_copy(i, self.extra(sub), self.c).wait_recv()

        @pl.when(jnp.logical_and(left, right))
        def _():
            self.stage[i] = (
                own + self.inbox[i].astype(F32) + self.inbox[self.extra(sub)].astype(F32)
            ).astype(BF16)

        @pl.when(jnp.logical_and(left, jnp.logical_not(right)))
        def _():
            self.stage[i] = (own + self.inbox[i].astype(F32)).astype(BF16)

        @pl.when(jnp.logical_and(right, jnp.logical_not(left)))
        def _():
            self.stage[i] = (own + self.inbox[self.extra(sub)].astype(F32)).astype(BF16)

    def gathered_again(self, o, sub):
        return self.term(o, sub, self.bit)[...].astype(F32) + self.got[self.index(o, sub)].astype(F32)

    def finish(self):
        @pl.when(self.valid(self.place))
        def _():
            lax.fori_loop(0, self.subs, lambda sub, u: (self.settle(sub), u)[1], 0)

    def sent(self):
        def one(o, sub):
            self.pair_copy(o, sub).wait_send()

            @pl.when(o != self.place)
            def _():
                self.line_copy(self.index(o, sub), 0, self.c).wait_send()

        self.each(one)


class LoneShare:
    def __init__(self, total, out, send, recv):
        self.f, self.c = total.f, total.c
        self.owner = total.place // (total.size // 4)
        self.rel = total.f ^ self.owner
        start = jnp.where(self.rel == 0, (total.place - total.first) * total.subs, 0)
        self.held = total.stage.at[pl.ds(start, total.subs)]
        self.out, self.send, self.recv = out, send, recv
        self.local = pltpu.make_async_copy(self.held, out, recv)

    def copy(self, src, k, to):
        return copy_to(src, self.out, self.send.at[k], self.recv, to, self.c)

    def begin(self):
        @pl.when(self.rel == 0)
        def _():
            self.copy(self.held, 1, self.f ^ 2).start()
            self.copy(self.held, 0, self.f ^ 1).start()
            self.local.start()

    def relay(self):
        @pl.when(self.rel == 2)
        def _():
            self.copy(self.out, 0, self.f).wait_recv()
            self.copy(self.out, 0, self.f ^ 1).start()

    def finish(self):
        @pl.when(self.rel == 0)
        def _():
            self.local.wait()
            self.copy(self.held, 0, self.f).wait_send()
            self.copy(self.held, 1, self.f).wait_send()

        @pl.when(self.rel == 2)
        def _():
            self.copy(self.out, 0, self.f).wait_send()

        @pl.when(lax.rem(self.rel, 2) == 1)
        def _():
            self.copy(self.out, 0, self.f).wait_recv()


def back_kernel(
    n, far_kv,
    da_ref, gwout_ref, gw1_ref, gw2_ref, qcat_ref, qpos_ref, kv_ref, lse_ref, of_ref,
    tok_ref, p1_ref, ev_ref, gates_ref, gsel_ref, x_ref, small_ref, dmid_ref, vec_ref, table_ref,
    din_ref, gp_ref, g1_ref, g2_ref, go_ref, vq_ref, dkv_ref,
    do_ref, delta_ref, grad_ref, kcat_ref, acc_ref, ring_ref, drel_ref, dqs_ref, dq_ref, part_ref, dp_ref,
    gpart_ref, mine_ref, vin_ref,
    s0, s1, s2, s3, s4, s5, s6,
    p0, p1, p2, p3, p4, p5, p6, u0, u1, u2, u3, u4, u5, u6,
    v0, v1, v2, v3, v4, v5, v6, w0, w1, w2, w3, w4, w5, w6,
    da_s, da_r, kv_s, kv_r, dq_s, dq_r, gp_s, gp_r, g1_s, g1_r, g2_s, g2_r, go_s, go_r,
    vc_s, vc_r, vf_s, vf_r, loc,
):
    f, c = lax.axis_index("fsdp"), lax.axis_index("ctx")
    groups = n // 4
    seq, turn = c // groups, lax.rem(c, groups)
    tokens, width = x_ref.shape
    scale = 1.0 / math.sqrt(112)
    own_turn, own_slot = holder_of(c, groups)
    rows = width // n
    greet(f, c, 4, n)

    def send_da(s, _):
        to = s * groups + own_turn

        @pl.when(to != c)
        def _():
            copy_to(da_ref.at[s], do_ref.at[own_slot], da_s.at[s], da_r.at[own_slot], f, to).start()

        @pl.when(to == c)
        def _():
            do_ref[own_slot] = da_ref[s]

        return 0

    lax.fori_loop(0, 4, send_da, 0)
    sub_out, sub_two = p0.shape[0] // max(1, groups // 2), v0.shape[0] // max(1, groups // 2)

    def rows_at(ref, count):
        return lambda block, sub: ref.at[pl.ds(pl.multiple_of(block * count, count), count), :]

    def piece_at(ref, subs):
        count = ref.shape[1] // subs
        return lambda block, sub: ref.at[block, pl.ds(pl.multiple_of(sub * count, count), count), :]

    sum_out = LineSum(f, c, n, piece_at(gwout_ref, sub_out), p0, p1, p2, p3, p4, p5, p6, sub_out, lone=True)
    sum_one = LineSum(f, c, n, rows_at(gw1_ref, rows), u0, u1, u2, u3, u4, u5, u6, 1)
    sum_two = LineSum(f, c, n, piece_at(gw2_ref, sub_two), v0, v1, v2, v3, v4, v5, v6, sub_two, lone=True)
    sum_in = LineSum(f, c, n, rows_at(gpart_ref, rows), w0, w1, w2, w3, w4, w5, w6, 1)
    big = (sum_two, sum_one, sum_out)
    for one in big:
        one.begin()

    def prepare(i, _):
        @pl.when(block_of(turn, i, groups) != c)
        def _():
            copy_to(da_ref.at[0], do_ref.at[i], da_s.at[0], da_r.at[i], f, c).wait_recv()

        delta_ref[i] = jnp.sum(do_ref[i].astype(F32) * of_ref[i], axis=1, keepdims=True)
        grad_ref[i] = jnp.zeros((tokens, width + LANES), F32)
        return 0

    lax.fori_loop(0, 4, prepare, 0)
    row_in = lax.broadcasted_iota(jnp.int32, (tokens, tokens), 0)
    col_in = lax.broadcasted_iota(jnp.int32, (tokens, tokens), 1)
    lane = lax.broadcasted_iota(jnp.int32, (tokens, LANES), 1)
    spots = jnp.logical_or(lane == SPOT_A, lane == SPOT_B)
    last_own = block_of(turn, 3, groups)
    mine_ref[...] = vec_ref[...]

    def close_query(i, sine, cosine):
        first = grad_ref[i, :, 0 : width // 2]
        second = grad_ref[i, :, width // 2 : width]
        drel_ref[i, :, 0 : width // 2] = ((first * sine - second * cosine) * scale).astype(BF16)
        drel_ref[i, :, width // 2 : width] = ((first * cosine + second * sine) * scale).astype(BF16)
        d_place = mm(drel_ref[i], p1_ref[:, :, 896:].reshape(width, LANES))
        d_content = jnp.where(spots, 0.0, grad_ref[i, :, width:] * scale)
        dqs_ref[i] = (d_content + d_place).astype(BF16)
        mine_ref[6:7, 0:LANES] += jnp.sum(d_content, axis=0, keepdims=True)
        mine_ref[7:8, 0:LANES] += jnp.sum(d_place, axis=0, keepdims=True)
        block = block_of(turn, i, groups)

        @pl.when(block != c)
        def _():
            copy_to(dqs_ref.at[i], dq_ref.at[seq], dq_s.at[i], dq_r.at[seq], f, block).start()

        @pl.when(block == c)
        def _():
            dq_ref[seq] = dqs_ref[i]

    def ring_copy(slot, to):
        return copy_to(ring_ref.at[slot], dkv_ref.at[c], kv_s.at[slot], kv_r.at[c], f, to)

    def ring_local(slot):
        return pltpu.make_async_copy(ring_ref.at[slot], dkv_ref.at[c], kv_s.at[slot])

    def ring_free(kb):
        slot = lax.rem(kb, 4)

        @pl.when(jnp.logical_and(kb != c, kb <= last_own))
        def _():
            ring_copy(slot, c).wait_send()

        @pl.when(jnp.logical_and(kb == c, kb <= last_own))
        def _():
            ring_local(slot).wait()

    def key_block(kb, _):
        own = [block_of(turn, i, groups) for i in range(4)]
        first = sum((b < kb).astype(jnp.int32) for b in own)
        ready = sum((b == kb).astype(jnp.int32) for b in own)
        sine, cosine = sin_cos(key_places(kv_ref[kb]), table_ref)
        kcat_ref[:, 0 : width // 2] = cosine.astype(BF16)
        kcat_ref[:, width // 2 : width] = sine.astype(BF16)
        kcat_ref[:, width:] = kv_ref[kb, :, 0:128]
        acc_ref[...] = jnp.zeros_like(acc_ref)

        def query_block(i, _):
            gap = (block_of(turn, i, groups) - kb) * tokens
            scores = mm_t(qcat_ref[i], kcat_ref[...])
            probs = jnp.where(col_in <= row_in + gap, jnp.exp(scores - lse_ref[i]), 0.0)
            d_probs = mm_t(do_ref[i], kv_ref[kb, :, 128:256])
            d_scores = (probs * (d_probs - delta_ref[i])).astype(BF16)
            acc_ref[:, 0:128] += mm_left_t(d_scores, qcat_ref[i, :, width:])
            acc_ref[:, 128:256] += mm_left_t(probs.astype(BF16), do_ref[i])
            grad_ref[i] += mm(d_scores, kcat_ref[...])
            return 0

        lax.fori_loop(first, 4, query_block, 0)

        @pl.when(ready == 1)
        def _():
            close_query(first, sine, cosine)

        @pl.when(kb >= 4)
        def _():
            ring_free(kb - 4)

        @pl.when(kb <= last_own)
        def _():
            slot = lax.rem(kb, 4)
            ring_ref[slot] = acc_ref[...].astype(BF16)

            @pl.when(kb != c)
            def _():
                ring_copy(slot, kb).start()

            @pl.when(kb == c)
            def _():
                ring_local(slot).start()

        @pl.when(kb >= n // 2)
        def _():
            def progress(k, _):
                index = (kb - n // 2) * 3 + k
                for which, one in enumerate(big):
                    @pl.when(index // (n // 2) == which)
                    def _():
                        one.step(lax.rem(index, n // 2))

                return 0

            lax.fori_loop(0, 3, progress, 0)

        return 0

    lax.fori_loop(0, n, key_block, 0)
    for one in big:
        one.finish()
    share_two = LoneShare(sum_two, g2_ref, g2_s, g2_r)
    share_out = LoneShare(sum_out, go_ref, go_s, go_r)
    gather_one = QuadGather(f, c, g1_ref, g1_s, g1_r)
    local_one = pltpu.make_async_copy(u2.at[c // 2], g1_ref.at[f], loc.at[0])
    local_one.start()
    share_two.begin()
    gather_one.begin(u2.at[c // 2])
    share_out.begin()

    all_tokens = 4 * tokens
    d_rel = drel_ref[...].reshape(all_tokens, width)
    gpart_ref[:, 896:] = mm_left_t(d_rel, qpos_ref[...].reshape(all_tokens, LANES)).astype(BF16)

    def collect(s, _):
        to = s * groups + own_turn

        @pl.when(to != c)
        def _():
            copy_to(dqs_ref.at[0], dq_ref.at[s], dq_s.at[0], dq_r.at[s], f, c).wait_recv()

        acc_ref[...] = jnp.zeros_like(acc_ref)

        def add(k, _):
            at = s * groups + k

            @pl.when(block_of(k, 3, groups) >= c)
            def _():
                @pl.when(at != c)
                def _():
                    copy_to(ring_ref.at[0], dkv_ref.at[at], kv_s.at[0], kv_r.at[at], f, c).wait_recv()

                if far_kv:
                    bring = pltpu.make_async_copy(dkv_ref.at[at], part_ref, loc.at[1])
                    bring.start()
                    bring.wait()
                    acc_ref[...] += part_ref[...].astype(F32)
                else:
                    acc_ref[...] += dkv_ref[at].astype(F32)

            return 0

        lax.fori_loop(0, groups, add, 0)
        dp_ref[s, :, 0:128] = dq_ref[s]
        dp_ref[s, :, 128:256] = acc_ref[:, 0:128].astype(BF16)
        d_values = acc_ref[:, 128:256]
        for e in range(5):
            values = ev_ref[s, :, e * LANES : (e + 1) * LANES].astype(F32)
            column = jnp.sum(values * d_values, axis=1, keepdims=True) * gates_ref[s, :, 24 + e : 25 + e]
            part = gates_ref[s, :, 16 + e : 17 + e] * d_values
            part = jnp.where(lane == SPOT_A, column, part)
            part = jnp.where(lane == SPOT_B, gsel_ref[s, :, e : e + 1], part)
            dp_ref[s, :, 256 + e * LANES : 384 + e * LANES] = part.astype(BF16)
        return 0

    def ring_drain(k, _):
        ring_free(n - 4 + k)
        return 0

    lax.fori_loop(0, 4, ring_drain, 0)
    lax.fori_loop(0, 4, collect, 0)
    tile = 256

    def weight_tile(i, _):
        spot = pl.multiple_of(i * tile, tile)
        left = tok_ref[:, :, pl.ds(spot, tile)].reshape(all_tokens, tile)
        right = dp_ref[...].reshape(all_tokens, 896)
        gpart_ref[pl.ds(spot, tile), 0:896] = mm_left_t(left, right).astype(BF16)
        return 0

    lax.fori_loop(0, width // tile, weight_tile, 0)
    sum_in.begin()
    share_two.relay()
    gather_one.relay()
    share_out.relay()
    in_sum = QuadSum(f, c, s0, s1, s2, s3, s4, s5, s6)
    for k in (3, 2, 1, 0):
        weights = p1_ref[:, :, 0:896].reshape(width, 896)
        in_sum.put(k, mm_t(dp_ref[f ^ k], weights))
        if k == 2:
            in_sum.cross()
    lax.fori_loop(0, n // 2, lambda k, u: (sum_in.step(k), u)[1], 0)
    d_norm = in_sum.total()
    xhat, spread = layer_stats(x_ref[...].astype(F32))
    gain = spread_vector(small_ref[:, 0, :], width // n)
    din_ref[...] = dmid_ref[...] + layer_back(d_norm, gain, xhat, spread)
    mine_ref[4:5, :] = jnp.sum(d_norm * xhat, axis=0, keepdims=True)
    mine_ref[5:6, :] = jnp.sum(d_norm, axis=0, keepdims=True)

    def vec_send(k, _):
        to = lax.rem(c + k, n)
        copy_to(mine_ref, vin_ref.at[c], vc_s.at[to], vc_r.at[c], f, to).start()
        return 0

    lax.fori_loop(1, n, vec_send, 0)
    vin_ref[c] = mine_ref[...]
    sum_in.finish()
    gather_in = QuadGather(f, c, gp_ref, gp_s, gp_r)
    local_in = pltpu.make_async_copy(w2.at[c // 2], gp_ref.at[f], loc.at[1])
    local_in.start()
    gather_in.begin(w2.at[c // 2])

    def vec_wait(k, _):
        to = lax.rem(c + k, n)
        copy_to(mine_ref, vin_ref.at[to], vc_s.at[to], vc_r.at[to], f, to).wait()
        return 0

    lax.fori_loop(1, n, vec_wait, 0)
    vq_ref[f] = jnp.sum(vin_ref[...], axis=0)
    for k in range(1, 4):
        copy_to(vq_ref.at[f], vq_ref.at[f], vf_s.at[k], vf_r.at[f], f ^ k, c).start()
    gather_in.relay()
    for k in range(1, 4):
        copy_to(vq_ref.at[f ^ k], vq_ref.at[f ^ k], vf_s.at[k], vf_r.at[f ^ k], f, c).wait_recv()
        copy_to(vq_ref.at[f], vq_ref.at[f], vf_s.at[k], vf_r.at[f], f, c).wait_send()
    for one in (gather_one, gather_in):
        one.got(f ^ 1)
        one.got(f ^ 3)
        one.sent()
    local_one.wait()
    local_in.wait()
    share_two.finish()
    share_out.finish()
    for one in big + (sum_in,):
        one.sent()
    in_sum.sent()

    def drain(i, _):
        @pl.when(i * groups + own_turn != c)
        def _():
            copy_to(da_ref.at[i], do_ref.at[0], da_s.at[i], da_r.at[0], f, c).wait_send()

        @pl.when(block_of(turn, i, groups) != c)
        def _():
            copy_to(dqs_ref.at[i], dq_ref.at[0], dq_s.at[i], dq_r.at[0], f, c).wait_send()

        return 0

    lax.fori_loop(0, 4, drain, 0)


def cuts(count):
    parts = max(1, count // 128)
    return parts if count % (16 * parts) == 0 else 1


def line_sum_scratch(blocks, subs, rows, cols):
    return [
        pltpu.VMEM((blocks * subs, rows // subs, cols), BF16), pltpu.VMEM(((blocks + 1) * subs, rows // subs, cols), BF16),
        pltpu.VMEM((blocks * subs, rows // subs, cols), BF16),
        DMA((blocks * subs,)), DMA((blocks * subs,)), DMA((blocks * subs,)), DMA(((blocks + 1) * subs,)),
    ]


def back(n, da, gwout, gw1, gw2, qcat, qpos, kv, lse, of, tok, p1, ev, gates, gsel, x, small, dmid, vec, table):
    t, d = x.shape
    g = n // 4
    quarter = gw1.shape[1]
    rows, out_rows, two_rows = d // n, gwout.shape[1], gw2.shape[1]
    sub_out, sub_two = cuts(out_rows), cuts(two_rows)
    lone = n // 8
    far_kv = g > 4
    return pl.pallas_call(
        functools.partial(back_kernel, n, far_kv),
        out_shape=[
            sds((t, d), F32), sds((4, rows, d), BF16), sds((4, rows, quarter), BF16),
            sds((sub_two, two_rows // sub_two, d), BF16), sds((sub_out, out_rows // sub_out, d), BF16),
            sds((4, 8, d), F32), sds((n, t, 256), BF16),
        ],
        in_specs=[VMEM] * 19,
        out_specs=[VMEM, ANY, ANY, ANY, ANY, VMEM, ANY if far_kv else VMEM],
        scratch_shapes=[
            pltpu.VMEM((4, t, LANES), BF16), pltpu.VMEM((4, t, 1), F32), pltpu.VMEM((4, t, d + LANES), F32),
            pltpu.VMEM((t, d + LANES), BF16), pltpu.VMEM((t, 256), F32), pltpu.VMEM((4, t, 256), BF16),
            pltpu.VMEM((4, t, d), BF16), pltpu.VMEM((4, t, LANES), BF16), pltpu.VMEM((4, t, LANES), BF16),
            pltpu.VMEM((t, 256), BF16), pltpu.VMEM((4, t, 896), BF16), pltpu.VMEM((d, d), BF16),
            pltpu.VMEM((8, d), F32), pltpu.VMEM((n, 8, d), F32),
        ]
        + quad_sum_scratch(t, d)
        + line_sum_scratch(lone, sub_out, out_rows, d)
        + line_sum_scratch(n // 2, 1, rows, quarter)
        + line_sum_scratch(lone, sub_two, two_rows, d)
        + line_sum_scratch(n // 2, 1, rows, d)
        + [
            DMA((4,)), DMA((4,)), DMA((4,)), DMA((n,)), DMA((4,)), DMA((4,)), DMA((3,)), DMA((4,)),
            DMA((3,)), DMA((4,)), DMA((2,)), DMA, DMA((2,)), DMA, DMA((n,)), DMA((n,)), DMA((4,)), DMA((4,)), DMA((2,)),
        ],
        compiler_params=pltpu.CompilerParams(
            collective_id=2, has_side_effects=True, vmem_limit_bytes=63 << 20
        ),
        name="back",
    )(da, gwout, gw1, gw2, qcat, qpos, kv, lse, of, tok, p1, ev, gates, gsel, x, small, dmid, vec, table)


def pad_channels(v, group):
    lead = v.shape[:-1]
    v = v.reshape(lead + (112 // group, group))
    v = jnp.pad(v, [(0, 0)] * len(lead) + [(0, 0), (0, group // 7)])
    return v.reshape(lead + (LANES,))


def head_pick(w, f, heads=4):
    w = w.reshape(w.shape[0], heads, -1)
    return lax.dynamic_index_in_dim(w, f, 1, keepdims=False)


def route_lanes(routes):
    hot = routes[..., None] == jnp.arange(8, dtype=jnp.int32)
    return jnp.sum(hot.astype(F32), axis=-2)


def pack_inputs(
    n, f, positions, value_routes, output_routes, ln1_gain, ln1_bias, wq, wk, wrel, u_bias, v_bias,
    wvsel, wv, wosel, wout, ln2_gain, ln2_bias, b1, b2,
):
    t = positions.shape[0]
    rows = wq.shape[0]
    group = math.gcd(112, wout.shape[0])
    masks = jnp.concatenate([route_lanes(value_routes), route_lanes(output_routes)], axis=-1).reshape(t, 64)
    place = jnp.stack([positions // 128, positions % 128], axis=-1).astype(F32)
    aux = jnp.concatenate([masks, place, jnp.zeros((t, 62), F32)], axis=-1).astype(BF16)
    lane = jnp.arange(LANES)
    experts = pad_channels(head_pick(wv, f).reshape(rows, 5, 112), group)
    experts = jnp.where(lane == SPOT_A, head_pick(wvsel, f)[..., None], experts)
    experts = jnp.where(lane == SPOT_B, head_pick(wosel, f)[..., None], experts)
    p1 = jnp.concatenate(
        [
            pad_channels(head_pick(wq, f), group), pad_channels(head_pick(wk, f), group),
            experts.reshape(rows, 640), pad_channels(head_pick(wrel, f), group),
        ],
        axis=-1,
    )
    piece = min(LANES, b1.shape[0])
    vectors = [ln1_gain, ln1_bias, ln2_gain, ln2_bias, b2]
    vectors = [jnp.pad(v, (0, LANES - v.shape[0])) for v in vectors]
    extra = jnp.pad(b1.reshape(-1, piece), ((0, 0), (0, LANES - piece)))
    small = jnp.concatenate([jnp.stack(vectors), extra]).astype(F32)
    small = jnp.pad(small, ((0, 16 - small.shape[0]), (0, 0)))
    pieces = wout.reshape(-1, group, wout.shape[1])
    pieces = jnp.pad(pieces, ((0, 0), (0, group // 7), (0, 0))).reshape(-1, wout.shape[1])
    pieces = jnp.pad(pieces, ((0, -pieces.shape[0] % 16), (0, 0)))
    bias = jnp.concatenate([pad_channels(u_bias, group), pad_channels(v_bias, group)]).astype(F32)
    return aux, p1, small, pieces, bias


def drop_pads(v, group):
    lead = v.shape[:-1]
    wide = group * 8 // 7
    return v.reshape(lead + (LANES // wide, wide))[..., :group].reshape(lead + (112,))


def on_device(n, *args):
    (
        x, positions, value_routes, output_routes, ln1_gain, ln1_bias, wq, wk, wrel, u_bias, v_bias,
        wvsel, wv, wosel, wout, ln2_gain, ln2_bias, w1, b1, w2, b2, cot,
    ) = args
    f, c = lax.axis_index("fsdp"), lax.axis_index("ctx")
    d = x.shape[1]
    g = n // 4
    group = math.gcd(112, wout.shape[0])
    aux, p1, small, pieces, bias = pack_inputs(
        n, f, positions, value_routes, output_routes, ln1_gain, ln1_bias, wq, wk, wrel, u_bias, v_bias,
        wvsel, wv, wosel, wout, ln2_gain, ln2_bias, b1, b2,
    )
    table = jnp.asarray(turn_table(d))
    tok, p1g, smallg, woutg, cotg, ev, gates, o, qcat, qpos, kv, lse, of = attend(
        n, x, aux, cot, p1, small, pieces, bias, table
    )
    block = 640 // g
    out, dmid, gwout, gw1, gw2, da, gsel, vec = feed(
        n, x, cotg, gates, o, woutg[:, :block].reshape(640, d), smallg, w1, w2
    )
    gwout = gwout.reshape(g, block, d)
    gwout = jnp.pad(gwout, ((0, 0), (0, pieces.shape[0] - block), (0, 0)))
    d_in, gp, g1, g2, go, vq, _ = back(
        n, da, gwout, gw1, gw2.reshape(g, -1, d), qcat, qpos, kv, lse, of, tok, p1g, ev, gates, gsel,
        x, smallg, dmid, vec, table,
    )
    gp = jnp.transpose(gp, (1, 0, 2))
    rows = gp.shape[0]
    g_query = drop_pads(gp[..., 0:128], group).reshape(rows, 448).astype(F32)
    g_key = drop_pads(gp[..., 128:256], group).reshape(rows, 448).astype(F32)
    g_rel = drop_pads(gp[..., 896:], group).reshape(rows, 448).astype(F32)
    experts = gp[..., 256:896].reshape(rows, 4, 5, LANES)
    g_value = drop_pads(experts, group).reshape(rows, 2240).astype(F32)
    g_vsel = experts[..., SPOT_A].reshape(rows, 20).astype(F32)
    g_osel = experts[..., SPOT_B].reshape(rows, 20).astype(F32)
    g_one = jnp.transpose(g1, (1, 0, 2)).reshape(rows, -1).astype(F32)
    g_two = g2.reshape(-1, d).astype(F32)
    g_out = go.reshape(-1, d)[:block].reshape(-1, group * 8 // 7, d)[:, :group].reshape(-1, d).astype(F32)
    sums = jnp.sum(vq, axis=0)
    own = lax.dynamic_slice_in_dim(sums, c * rows, rows, 1)
    b1_rows = b1.shape[0]
    g_b1 = lax.dynamic_slice_in_dim(vq[:, 3, :].reshape(-1), c * b1_rows, b1_rows, 0)
    g_u = drop_pads(vq[:, 6, 0:LANES], group)
    g_v = drop_pads(vq[:, 7, 0:LANES], group)
    return (
        out, d_in, own[4], own[5], g_query, g_key, g_rel, g_u, g_v, g_vsel, g_value, g_osel, g_out,
        own[0], own[1], g_one, g_b1, g_two, own[2],
    )


def solution(mesh):
    both = ("fsdp", "ctx")
    row, vector, matrix = P(both, None), P("ctx"), P("ctx", None)
    in_specs = (
        row, P(both), P(both, None, None), P(both, None, None), vector, vector, matrix, matrix, matrix,
        P(), P(), matrix, matrix, matrix, matrix, vector, vector, matrix, vector, matrix, vector, row,
    )
    out_specs = (
        row, row, vector, vector, matrix, matrix, matrix, P(), P(), matrix, matrix, matrix, matrix,
        vector, vector, matrix, vector, matrix, vector,
    )
    return jax.shard_map(
        functools.partial(on_device, mesh.shape["ctx"]),
        mesh=mesh, in_specs=in_specs, out_specs=out_specs, check_vma=False,
    )
```

```python
import functools
import math

import jax
import jax.numpy as jnp
import numpy as np
from jax import lax
from jax.experimental import pallas as pl
from jax.experimental.pallas import tpu as pltpu
from jax.sharding import PartitionSpec as P

MESH = pl.DeviceIdType.MESH
F32 = jnp.float32
BF16 = jnp.bfloat16
LN_EPS = 1e-05
MASKED = -1e30
LANES = 128
SPOT_A, SPOT_B = 63, 127
VMEM = pl.BlockSpec(memory_space=pltpu.VMEM)
ANY = pl.BlockSpec(memory_space=pl.ANY)
DMA = pltpu.SemaphoreType.DMA


def turn_coefficients():
    nodes = (np.cos(np.pi * (np.arange(400) + 0.5) / 400) + 1) / 8
    root = np.sqrt(nodes)
    powers = nodes[:, None] ** np.arange(7)[None, :]
    sine = np.linalg.lstsq(powers, np.sin(2 * np.pi * root) / root, rcond=None)[0]
    cosine = np.linalg.lstsq(powers, np.cos(2 * np.pi * root), rcond=None)[0]
    return [float(v) for v in sine], [float(v) for v in cosine]


SIN_TURN, COS_TURN = turn_coefficients()


def horner(coefs, v):
    total = coefs[-1]
    for coef in coefs[-2::-1]:
        total = total * v + coef
    return total


def turn_table(model_width):
    freq = 10000.0 ** (-np.arange(0, model_width, 2, dtype=np.float64) / model_width) / (2 * np.pi)
    mantissa, exponent = np.frexp(freq)
    coarse = np.ldexp(np.floor(mantissa * 256) / 256, exponent)
    table = np.zeros((8, model_width // 2), np.float32)
    table[0] = coarse
    table[1] = freq - coarse
    return table


def sin_cos(places, table_ref):
    coarse = places * table_ref[0:1, :]
    part = (coarse - jnp.round(coarse)) + places * table_ref[1:2, :]
    part = part - jnp.round(part)
    square = part * part
    return horner(SIN_TURN, square) * part, horner(COS_TURN, square)


def mm(left, right):
    return lax.dot_general(left, right, (((1,), (0,)), ((), ())), preferred_element_type=F32)


def mm_t(left, right):
    return lax.dot_general(left, right, (((1,), (1,)), ((), ())), preferred_element_type=F32)


def mm_left_t(left, right):
    return lax.dot_general(left, right, (((0,), (0,)), ((), ())), preferred_element_type=F32)


def copy_to(src, dst, send, recv, f, c):
    return pltpu.make_async_remote_copy(
        src_ref=src, dst_ref=dst, send_sem=send, recv_sem=recv, device_id=(f, c), device_id_type=MESH
    )


def greet(f, c, fsdp, n):
    barrier = pltpu.get_barrier_semaphore()

    def one(k, _):
        pl.semaphore_signal(barrier, inc=1, device_id=(f, lax.rem(c + k, n)), device_id_type=MESH)
        return 0

    lax.fori_loop(1, n, one, 0)
    for k in range(1, fsdp):
        pl.semaphore_signal(barrier, inc=1, device_id=(f ^ k, c), device_id_type=MESH)
    pl.semaphore_wait(barrier, n - 1 + fsdp - 1)


class LineGather:
    def __init__(self, f, c, n, own, at, recv, right, left, pair, subs=1, lone=False):
        self.f, self.c, self.n, self.size = f, c, n, n // 2
        self.place, self.bit = c // 2, lax.rem(c, 2)
        self.own, self.at = own, at
        self.recv, self.right, self.left, self.pair = recv, right, left, pair
        self.subs, self.lone = subs, lone

    def valid(self, o):
        ok = jnp.logical_and(o >= 0, o < self.size)
        if self.lone:
            span = self.size // 4
            ok = jnp.logical_and(ok, jnp.logical_and(o >= self.f * span, o < (self.f + 1) * span))
        return ok

    def slot(self, block):
        return block - self.f * (self.n // 4) if self.lone else block

    def copy(self, src, block, sub, sems, c):
        slot = self.slot(block)
        i = slot * self.subs + sub
        return copy_to(src, self.at(slot, sub), sems.at[i], self.recv.at[i], self.f, c)

    def held(self, block, sub):
        return self.at(self.slot(block), sub)

    def each(self, work):
        if self.subs == 1:
            work(0)
        else:
            lax.fori_loop(0, self.subs, lambda sub, u: (work(sub), u)[1], 0)

    def spread(self, src, block, sub, go_right, go_left):
        @pl.when(go_right)
        def _():
            self.copy(src, block, sub, self.right, self.c + 2).start()

        @pl.when(go_left)
        def _():
            self.copy(src, block, sub, self.left, self.c - 2).start()

        self.copy(src, block, sub, self.pair, self.c + 1 - 2 * self.bit).start()

    def begin(self, local):
        @pl.when(self.valid(self.place))
        def _():
            self.each(
                lambda sub: self.spread(
                    self.own(sub), self.c, sub, self.place < self.size - 1, self.place > 0
                )
            )
            local()

    def arrived(self, block, sub):
        self.copy(self.held(block, sub), block, sub, self.pair, self.c).wait_recv()

    def step(self, t):
        for sign in (-1, 1):
            o = self.place + sign * t
            block = 2 * o + self.bit

            @pl.when(self.valid(o))
            def _():
                def one(sub):
                    self.arrived(block, sub)
                    self.spread(
                        self.held(block, sub), block, sub,
                        jnp.logical_and(sign < 0, self.place < self.size - 1),
                        jnp.logical_and(sign > 0, self.place > 0),
                    )

                self.each(one)

    def steps(self, first=1):
        lax.fori_loop(first, self.size, lambda t, u: (self.step(t), u)[1], 0)

    def finish(self):
        def one(o, _):
            block = 2 * o + self.bit

            def piece(sub):
                self.arrived(2 * o + 1 - self.bit, sub)
                source = self.held(block, sub)
                self.copy(source, block, sub, self.pair, self.c).wait_send()

                @pl.when(jnp.logical_and(o <= self.place, self.place < self.size - 1))
                def _():
                    self.copy(source, block, sub, self.right, self.c).wait_send()

                @pl.when(jnp.logical_and(o >= self.place, self.place > 0))
                def _():
                    self.copy(source, block, sub, self.left, self.c).wait_send()

            @pl.when(self.valid(o))
            def _():
                self.each(piece)

            return 0

        lax.fori_loop(0, self.size, one, 0)


class QuadGather:
    def __init__(self, f, c, out, send, recv):
        self.f, self.c, self.out, self.send, self.recv = f, c, out, send, recv

    def copy(self, slot, k, to, src=None):
        src = self.out.at[slot] if src is None else src
        return copy_to(src, self.out.at[slot], self.send.at[k], self.recv.at[slot], to, self.c)

    def begin(self, src=None):
        self.copy(self.f, 1, self.f ^ 2, src).start()
        self.copy(self.f, 0, self.f ^ 1, src).start()

    def got(self, slot):
        self.copy(slot, 0, self.f).wait_recv()

    def relay(self):
        self.got(self.f ^ 2)
        self.copy(self.f ^ 2, 2, self.f ^ 1).start()

    def sent(self):
        for k in range(3):
            self.copy(self.f, k, self.f).wait_send()


def spread_vector(rows, width):
    count = rows.shape[0]
    total = count * width
    lane = lax.broadcasted_iota(jnp.int32, (LANES, total), 0)
    column = lax.broadcasted_iota(jnp.int32, (LANES, total), 1)
    onehot = jnp.where(lane == lax.rem(column, width), 1.0, 0.0).astype(BF16)
    wide = mm(rows.astype(BF16), onehot)
    row = lax.broadcasted_iota(jnp.int32, (count, total), 0)
    column = lax.broadcasted_iota(jnp.int32, (count, total), 1)
    return jnp.sum(jnp.where(column // width == row, wide, 0.0), axis=0, keepdims=True)


def block_of(j, i, groups):
    return i * groups + jnp.where(lax.rem(i, 2) == 0, j, groups - 1 - j)


def holder_of(block, groups):
    row, within = block // groups, lax.rem(block, groups)
    return jnp.where(lax.rem(row, 2) == 0, within, groups - 1 - within), row


def key_places(kv):
    return kv[:, SPOT_A : SPOT_A + 1].astype(F32) * 128.0 + kv[:, SPOT_B : SPOT_B + 1].astype(F32)


def attend_kernel(
    n,
    x_ref, aux_ref, cot_ref, p1_ref, small_ref, wout_ref, w1_ref, bias_ref, table_ref,
    tok_ref, p1g_ref, smallg_ref, woutg_ref, w1g_ref, cotg_ref, ev_ref, gates_ref, o_ref,
    qcat_ref, qpos_ref, kv_ref, lse_ref, of_ref,
    qs_ref, kvs_ref, qr_ref, os_ref, kcat_ref, m_ref, l_ref,
    sm_s, sm_r, p_r, p_a, p_b, p_c, w_r, w_a, w_b, w_c, h_r, h_a, h_b, h_c,
    t_s, t_r, c_s, c_r, q_s, q_r, kv_s, kv_r, kv_p, o_s, o_r, loc,
):
    f, c = lax.axis_index("fsdp"), lax.axis_index("ctx")
    groups = n // 4
    seq, turn = c // groups, lax.rem(c, groups)
    tokens, width = x_ref.shape
    scale = 1.0 / math.sqrt(112)
    greet(f, c, 4, n)

    def small_send(k, _):
        to = lax.rem(c + k, n)
        copy_to(small_ref, smallg_ref.at[c], sm_s.at[to], sm_r.at[c], f, to).start()
        return 0

    lax.fori_loop(1, n, small_send, 0)
    smallg_ref[c] = small_ref[...]
    gather_p = LineGather(f, c, n, lambda sub: p1_ref, lambda k, sub: p1g_ref.at[k], p_r, p_a, p_b, p_c)

    def own_p():
        p1g_ref[c] = p1_ref[...]

    gather_p.begin(own_p)
    wout_copy = pltpu.make_async_copy(wout_ref, woutg_ref.at[c - f * groups], loc.at[0])
    subs = w_r.shape[0] // groups
    piece = wout_ref.shape[0] // subs
    gather_w = LineGather(
        f, c, n,
        lambda sub: wout_ref.at[pl.ds(pl.multiple_of(sub * piece, piece), piece), :],
        lambda k, sub: woutg_ref.at[k, pl.ds(pl.multiple_of(sub * piece, piece), piece), :],
        w_r, w_a, w_b, w_c, subs=subs, lone=True,
    )
    w1_copy = pltpu.make_async_copy(w1_ref, w1g_ref.at[c], loc.at[2])
    gather_h = LineGather(f, c, n, lambda sub: w1_ref, lambda k, sub: w1g_ref.at[k], h_r, h_a, h_b, h_c)
    cot_copy = pltpu.make_async_copy(cot_ref, cotg_ref.at[f], loc.at[1])
    cot_copy.start()

    hidden = x_ref[...].astype(F32)
    offsets = hidden - jnp.mean(hidden, axis=1, keepdims=True)
    spread = jnp.mean(offsets * offsets, axis=1, keepdims=True)
    xhat = offsets * lax.rsqrt(spread + LN_EPS)

    def small_wait(k, _):
        to = lax.rem(c + k, n)
        copy_to(small_ref, smallg_ref.at[to], sm_s.at[to], sm_r.at[to], f, to).wait()
        return 0

    lax.fori_loop(1, n, small_wait, 0)
    gain = spread_vector(smallg_ref[:, 0, :], width // n)
    shift = spread_vector(smallg_ref[:, 1, :], width // n)
    tok_ref[f, :, 0:width] = (xhat * gain + shift).astype(BF16)
    tok_ref[f, :, width:] = aux_ref[...]
    tok_gather = QuadGather(f, c, tok_ref, t_s, t_r)
    tok_gather.begin()
    gather_p.steps()
    tok_gather.relay()
    gather_p.finish()
    tok_gather.got(f ^ 1)
    tok_gather.got(f ^ 3)
    tok_gather.sent()
    cot_gather = QuadGather(f, c, cotg_ref, c_s, c_r)
    cot_gather.begin(cot_ref)

    lane = lax.broadcasted_iota(jnp.int32, (tokens, LANES), 1)
    source = lax.broadcasted_iota(jnp.int32, (LANES, LANES), 0)
    target = lax.broadcasted_iota(jnp.int32, (LANES, LANES), 1)
    wanted = f * 16 + lax.rem(target, 8) + jnp.where(target < 16, 8, 0)
    pick = jnp.where(
        jnp.logical_and(source == wanted, jnp.logical_and(target < 32, lax.rem(target, 8) < 5)), 1.0, 0.0
    ).astype(BF16)
    own_turn, own_slot = holder_of(c, groups)
    bit = lax.rem(c, 2)
    spots = jnp.logical_or(lane == SPOT_A, lane == SPOT_B)

    def project(t, _):
        s = lax.rem(seq + 1 + t, 4)
        normed = tok_ref[s, :, 0:width]
        aux = tok_ref[s, :, width:]
        weights = p1g_ref[...].reshape(width, p1g_ref.shape[2])
        qk = mm(normed, weights[:, 0:256])
        experts = mm(normed, weights[:, 256:896])
        ev_ref[s] = experts.astype(BF16)
        logits = jnp.zeros((tokens, LANES), F32)
        for e in range(5):
            for spot, first in ((SPOT_B, 0), (SPOT_A, 16)):
                column = experts[:, e * LANES + spot : e * LANES + spot + 1]
                logits = jnp.where(
                    jnp.logical_or(lane == first + e, lane == first + 8 + e), column, logits
                )
        sig = jax.nn.sigmoid(logits)
        gates = mm(aux, pick) * jnp.where(lax.rem(lane, 16) >= 8, sig * (1.0 - sig), sig)
        gates_ref[s] = gates
        values = jnp.zeros((tokens, LANES), F32)
        for e in range(5):
            values = values + gates[:, 16 + e : 17 + e] * experts[:, e * LANES : (e + 1) * LANES]
        values = jnp.where(spots, 0.0, values)
        high, rest = aux[:, 64:65].astype(F32), aux[:, 65:66].astype(F32)

        def with_place(v):
            return jnp.where(lane == SPOT_A, high, jnp.where(lane == SPOT_B, rest, v)).astype(BF16)

        qs_ref[s] = with_place(qk[:, 0:128])
        kvs_ref[s, :, 0:128] = with_place(qk[:, 128:256])
        kvs_ref[s, :, 128:256] = values.astype(BF16)
        to = s * groups + own_turn

        @pl.when(to != c)
        def _():
            copy_to(qs_ref.at[s], qr_ref.at[own_slot], q_s.at[s], q_r.at[own_slot], f, to).start()

        @pl.when(to == c)
        def _():
            qr_ref[own_slot] = qs_ref[s]

        def kv_send(k, _):
            to = s * groups + 2 * k + bit

            @pl.when(to != c)
            def _():
                copy_to(kvs_ref.at[s], kv_ref.at[c], kv_s.at[to], kv_r.at[c], f, to).start()

            @pl.when(to == c)
            def _():
                kv_ref[c] = kvs_ref[s]

            return 0

        lax.fori_loop(0, groups // 2, kv_send, 0)
        return 0

    lax.fori_loop(0, 4, project, 0)
    gather_w.begin(wout_copy.start)
    gather_h.begin(w1_copy.start)

    def kv_wait(block):
        copy_to(kvs_ref.at[0], kv_ref.at[block], kv_s.at[0], kv_r.at[block], f, c).wait_recv()

    def kv_pass(block):
        return copy_to(kv_ref.at[block], kv_ref.at[block], kv_p.at[block // 2], kv_r.at[block], f, c + 1 - 2 * bit)

    def hand_on(m):
        block = 2 * m + bit

        @pl.when(block != c)
        def _():
            kv_wait(block)

        kv_pass(block).start()

    def prepare(i, _):
        block = block_of(turn, i, groups)

        @pl.when(block != c)
        def _():
            copy_to(qs_ref.at[0], qr_ref.at[i], q_s.at[0], q_r.at[i], f, c).wait_recv()

        places = key_places(qr_ref[i])
        query = jnp.where(spots, 0.0, qr_ref[i].astype(F32))
        q_position = (query + bias_ref[pl.ds(4 + f, 1), :]).astype(BF16)
        qpos_ref[i] = q_position
        qcat_ref[i, :, width:] = ((query + bias_ref[pl.ds(f, 1), :]) * scale).astype(BF16)
        rel = p1g_ref[:, :, 896:].reshape(width, LANES)
        rel_query = mm_t(q_position, rel)
        sine, cosine = sin_cos(places, table_ref)
        first, second = rel_query[:, : width // 2], rel_query[:, width // 2 :]
        qcat_ref[i, :, 0 : width // 2] = ((first * sine + second * cosine) * scale).astype(BF16)
        qcat_ref[i, :, width // 2 : width] = ((second * sine - first * cosine) * scale).astype(BF16)
        m_ref[i] = jnp.full((tokens, 1), MASKED, F32)
        l_ref[i] = jnp.zeros((tokens, 1), F32)
        of_ref[i] = jnp.zeros((tokens, LANES), F32)
        return 0

    lax.fori_loop(0, 4, prepare, 0)
    hand_on(0)
    row_in = lax.broadcasted_iota(jnp.int32, (tokens, tokens), 0)
    col_in = lax.broadcasted_iota(jnp.int32, (tokens, tokens), 1)

    def give(i):
        total = l_ref[i]
        result = of_ref[i] / total
        of_ref[i] = result
        lse_ref[i] = m_ref[i] + jnp.log(total)
        os_ref[i] = result.astype(BF16)
        block = block_of(turn, i, groups)

        @pl.when(block != c)
        def _():
            copy_to(os_ref.at[i], o_ref.at[seq], o_s.at[i], o_r.at[seq], f, block).start()

        @pl.when(block == c)
        def _():
            o_ref[seq] = os_ref[i]

    def key_block(kb, _):
        own = [block_of(turn, i, groups) for i in range(4)]
        first = sum((b < kb).astype(jnp.int32) for b in own)
        ready = sum((b == kb).astype(jnp.int32) for b in own)

        @pl.when(lax.rem(kb, 2) != bit)
        def _():
            kv_wait(kb)

        @pl.when(jnp.logical_and(lax.rem(kb, 2) == 0, kb < n - 2))
        def _():
            hand_on(kb // 2 + 1)

        sine, cosine = sin_cos(key_places(kv_ref[kb]), table_ref)
        kcat_ref[:, 0 : width // 2] = cosine.astype(BF16)
        kcat_ref[:, width // 2 : width] = sine.astype(BF16)
        kcat_ref[:, width:] = kv_ref[kb, :, 0:128]

        def query_block(i, _):
            gap = (block_of(turn, i, groups) - kb) * tokens
            scores = mm_t(qcat_ref[i], kcat_ref[...])
            scores = jnp.where(col_in <= row_in + gap, scores, MASKED)
            before = m_ref[i]
            best = jnp.maximum(before, jnp.max(scores, axis=1, keepdims=True))
            shrink = jnp.exp(before - best)
            probs = jnp.exp(scores - best)
            m_ref[i] = best
            l_ref[i] = l_ref[i] * shrink + jnp.sum(probs, axis=1, keepdims=True)
            of_ref[i] = of_ref[i] * shrink + mm(probs.astype(BF16), kv_ref[kb, :, 128:256])
            return 0

        lax.fori_loop(first, 4, query_block, 0)

        @pl.when(ready == 1)
        def _():
            give(first)

        @pl.when(kb == n // 2 - 1)
        def _():
            cot_gather.relay()

        @pl.when(jnp.logical_and(kb >= n // 2, kb < n - 1))
        def _():
            gather_w.step(kb - n // 2 + 1)
            gather_h.step(kb - n // 2 + 1)

        return 0

    lax.fori_loop(0, n, key_block, 0)
    cot_gather.got(f ^ 1)
    cot_gather.got(f ^ 3)
    cot_gather.sent()
    gather_w.finish()
    gather_h.finish()
    w1_copy.wait()

    @pl.when(gather_w.valid(c // 2))
    def _():
        wout_copy.wait()

    cot_copy.wait()

    def drain(s, _):
        to = s * groups + own_turn

        @pl.when(to != c)
        def _():
            copy_to(qs_ref.at[s], qr_ref.at[own_slot], q_s.at[s], q_r.at[0], f, to).wait_send()
            copy_to(os_ref.at[0], o_ref.at[s], o_s.at[0], o_r.at[s], f, to).wait_recv()

        @pl.when(block_of(turn, s, groups) != c)
        def _():
            copy_to(os_ref.at[s], o_ref.at[s], o_s.at[s], o_r.at[0], f, to).wait_send()

        return 0

    lax.fori_loop(0, 4, drain, 0)

    def kv_drain(k, _):
        to = 2 * k + bit

        @pl.when(to != c)
        def _():
            copy_to(kvs_ref.at[0], kv_ref.at[0], kv_s.at[to], kv_r.at[0], f, c).wait_send()

        kv_pass(to).wait_send()
        return 0

    lax.fori_loop(0, n // 2, kv_drain, 0)


def sds(shape, dtype):
    return jax.ShapeDtypeStruct(shape, dtype)


def attend(n, x, aux, cot, p1, small, wout, w1, bias, table):
    t, d = x.shape
    rows = p1.shape[0]
    out_rows = wout.shape[0]
    g = n // 4
    subs = cuts(out_rows)
    return pl.pallas_call(
        functools.partial(attend_kernel, n),
        out_shape=[
            sds((4, t, d + LANES), BF16), sds((n, rows, d), BF16), sds((n, 16, LANES), F32),
            sds((g, out_rows, d), BF16), sds((n,) + w1.shape, BF16), sds((4, t, d), BF16), sds((4, t, 640), BF16),
            sds((4, t, LANES), F32), sds((4, t, LANES), BF16), sds((4, t, d + LANES), BF16),
            sds((4, t, LANES), BF16), sds((n, t, 256), BF16), sds((4, t, 1), F32), sds((4, t, LANES), F32),
        ],
        in_specs=[VMEM, VMEM, ANY, VMEM, VMEM, ANY, ANY, VMEM, VMEM],
        out_specs=[VMEM, VMEM, VMEM, ANY, ANY, ANY] + [VMEM] * 8,
        scratch_shapes=[
            pltpu.VMEM((4, t, LANES), BF16), pltpu.VMEM((4, t, 256), BF16), pltpu.VMEM((4, t, LANES), BF16),
            pltpu.VMEM((4, t, LANES), BF16), pltpu.VMEM((t, d + LANES), BF16),
            pltpu.VMEM((4, t, 1), F32), pltpu.VMEM((4, t, 1), F32),
            DMA((n,)), DMA((n,)), DMA((n,)), DMA((n,)), DMA((n,)), DMA((n,)),
            DMA((g * subs,)), DMA((g * subs,)), DMA((g * subs,)), DMA((g * subs,)),
            DMA((n,)), DMA((n,)), DMA((n,)), DMA((n,)),
            DMA((3,)), DMA((4,)), DMA((3,)), DMA((4,)), DMA((4,)), DMA((4,)),
            DMA((n,)), DMA((n,)), DMA((n // 2,)), DMA((4,)), DMA((4,)), DMA((3,)),
        ],
        compiler_params=pltpu.CompilerParams(
            collective_id=0, has_side_effects=True, vmem_limit_bytes=56 << 20
        ),
        name="attend",
    )(x, aux, cot, p1, small, wout, w1, bias, table)


class QuadSum:
    def __init__(self, f, c, core_out, core_in, x_out, x_in, keep, send, recv):
        self.f, self.c = f, c
        self.core_out, self.core_in, self.x_out, self.x_in = core_out, core_in, x_out, x_in
        self.keep, self.send, self.recv = keep, send, recv

    def core(self, k):
        return copy_to(
            self.core_out.at[k], self.core_in.at[k], self.send.at[k], self.recv.at[k], self.f ^ 1, self.c
        )

    def across(self):
        return copy_to(self.x_out, self.x_in, self.send.at[2], self.recv.at[2], self.f ^ 2, self.c)

    def put(self, k, value):
        if k in (1, 3):
            self.core_out[k // 2] = value.astype(BF16)
            self.core(k // 2).start()
        else:
            self.keep[k // 2] = value

    def cross(self):
        self.core(1).wait_recv()
        self.x_out[...] = (self.keep[1] + self.core_in[1].astype(F32)).astype(BF16)
        self.across().start()

    def total(self):
        self.core(0).wait_recv()
        self.across().wait_recv()
        return self.keep[0] + self.core_in[0].astype(F32) + self.x_in[...].astype(F32)

    def sent(self):
        self.core(0).wait_send()
        self.core(1).wait_send()
        self.across().wait_send()


def quad_sum_scratch(t, d):
    return [
        pltpu.VMEM((2, t, d), BF16), pltpu.VMEM((2, t, d), BF16), pltpu.VMEM((t, d), BF16),
        pltpu.VMEM((t, d), BF16), pltpu.VMEM((2, t, d), F32), DMA((3,)), DMA((3,)),
    ]


def layer_stats(v):
    offsets = v - jnp.mean(v, axis=1, keepdims=True)
    scale = lax.rsqrt(jnp.mean(offsets * offsets, axis=1, keepdims=True) + LN_EPS)
    return offsets * scale, scale


def layer_back(grad, gain, xhat, scale):
    inner = grad * gain
    return scale * (
        inner - jnp.mean(inner, axis=1, keepdims=True) - xhat * jnp.mean(inner * xhat, axis=1, keepdims=True)
    )


def gelu_pair(v):
    k = math.sqrt(2.0 / math.pi)
    square = v * v
    t = jnp.tanh(k * v * (1.0 + 0.044715 * square))
    half = 0.5 * (1.0 + t)
    return v * half, half + 0.5 * v * (1.0 - t * t) * (k * (1.0 + 3 * 0.044715 * square))


class PairSum:
    def __init__(self, f, c, n, source, got, out, send, recv):
        self.f, self.c, self.size = f, c, n // 2
        self.bit = lax.rem(c, 2)
        self.source, self.got, self.out, self.send, self.recv = source, got, out, send, recv

    def copy(self, o):
        return copy_to(
            self.source(2 * o + 1 - self.bit), self.got.at[o], self.send.at[o], self.recv.at[o],
            self.f, self.c + 1 - 2 * self.bit,
        )

    def begin(self):
        lax.fori_loop(0, self.size, lambda o, u: (self.copy(o).start(), u)[1], 0)

    def finish(self):
        def one(o, _):
            self.copy(o).wait_recv()
            term = self.source(2 * o + self.bit)[...].astype(F32)
            self.out[o] = (term + self.got[o].astype(F32)).astype(BF16)
            self.copy(o).wait_send()
            return 0

        lax.fori_loop(0, self.size, one, 0)


class LineSum:
    def __init__(self, f, c, n, source, inbox, stage, line_s, line_r, pair=None, subs=1, lone=False):
        self.f, self.c, self.n, self.size = f, c, n, n // 2
        self.place, self.bit = c // 2, lax.rem(c, 2)
        self.source = source
        self.inbox, self.stage, self.line_s, self.line_r = inbox, stage, line_s, line_r
        self.pair = pair
        self.subs = subs
        self.span = self.size // 4 if lone else self.size
        self.first = f * self.span if lone else 0

    def valid(self, o):
        return jnp.logical_and(o >= self.first, o < self.first + self.span)

    def index(self, o, sub):
        return (o - self.first) * self.subs + sub

    def pair_copy(self, o, sub):
        i = self.index(o, sub)
        got, send, recv = self.pair
        return copy_to(
            self.source(2 * (o - self.first) + 1 - self.bit, sub), got.at[i], send.at[i], recv.at[i],
            self.f, self.c + 1 - 2 * self.bit,
        )

    def line_copy(self, i, slot, c):
        return copy_to(self.stage.at[i], self.inbox.at[slot], self.line_s.at[i], self.line_r.at[slot], self.f, c)

    def each(self, work):
        def one(k, _):
            work(self.first + k // self.subs, lax.rem(k, self.subs))
            return 0

        lax.fori_loop(0, self.span * self.subs, one, 0)

    def begin(self):
        self.each(lambda o, sub: self.pair_copy(o, sub).start())

    def begin_block(self, block):
        @pl.when(lax.rem(block, 2) != self.bit)
        def _():
            self.pair_copy(block // 2, 0).start()

    def term(self, o, sub):
        if self.pair is None:
            return self.source(o - self.first, sub)[...].astype(F32)
        self.pair_copy(o, sub).wait_recv()
        own = self.source(2 * (o - self.first) + self.bit, sub)[...].astype(F32)
        return own + self.pair[0][self.index(o, sub)].astype(F32)

    def extra(self, sub):
        return self.span * self.subs + sub

    def move(self, o, sub, go_right):
        i = self.index(o, sub)
        total = self.term(o, sub)
        starts = self.place == 0 if go_right else self.place == self.size - 1

        @pl.when(starts)
        def _():
            self.stage[i] = total.astype(BF16)

        @pl.when(jnp.logical_not(starts))
        def _():
            self.line_copy(i, i, self.c).wait_recv()
            self.stage[i] = (total + self.inbox[i].astype(F32)).astype(BF16)

        if go_right:
            self.line_copy(i, i, self.c + 2).start()
        else:
            slot = jnp.where(o == self.place - 1, self.extra(sub), i)
            self.line_copy(i, slot, self.c - 2).start()

    def turn(self, time):
        far = self.size - 1 - (time - self.place)
        near = time - (self.size - 1 - self.place)

        def one(sub, _):
            @pl.when(jnp.logical_and(jnp.logical_and(far < self.size, self.valid(far)), far > self.place))
            def _():
                self.move(far, sub, True)

            @pl.when(jnp.logical_and(jnp.logical_and(near >= 0, self.valid(near)), near < self.place))
            def _():
                self.move(near, sub, False)

            return 0

        lax.fori_loop(0, self.subs, one, 0)

    def settle(self, sub):
        i = self.index(self.place, sub)
        own = self.term(self.place, sub)
        left = self.place > 0
        right = self.place < self.size - 1

        @pl.when(left)
        def _():
            self.line_copy(i, i, self.c).wait_recv()

        @pl.when(right)
        def _():
            self.line_copy(i, self.extra(sub), self.c).wait_recv()

        @pl.when(jnp.logical_and(left, right))
        def _():
            self.stage[i] = (
                own + self.inbox[i].astype(F32) + self.inbox[self.extra(sub)].astype(F32)
            ).astype(BF16)

        @pl.when(jnp.logical_and(left, jnp.logical_not(right)))
        def _():
            self.stage[i] = (own + self.inbox[i].astype(F32)).astype(BF16)

        @pl.when(jnp.logical_and(right, jnp.logical_not(left)))
        def _():
            self.stage[i] = (own + self.inbox[self.extra(sub)].astype(F32)).astype(BF16)

    def finish(self):
        @pl.when(self.valid(self.place))
        def _():
            lax.fori_loop(0, self.subs, lambda sub, u: (self.settle(sub), u)[1], 0)

    def sent(self):
        def one(o, sub):
            if self.pair is not None:
                self.pair_copy(o, sub).wait_send()

            @pl.when(o != self.place)
            def _():
                self.line_copy(self.index(o, sub), 0, self.c).wait_send()

        self.each(one)


def feed_kernel(
    n,
    x_ref, cot_ref, gates_ref, o_ref, wout_ref, small_ref, w1g, w2_ref,
    out_ref, dmid_ref, gwout_ref, s1_ref, s2_ref, da_ref, gsel_ref, vec_ref,
    w2g, n2_ref, act_ref, slope_ref, dpre_ref, mixed_ref, dml_ref, mid_ref, gw1_ref, gw2_ref, got1, in2, stage2,
    a0, a1, a2, a3, a4, a5, a6, b0, b1, b2, b3, b4, b5, b6, e0, e1, e2, e3, e4, e5, e6,
    w2_r, w2_a, w2_b, w2_c, h1_s, h1_r, h2_s, h2_r, n_s, n_r, d_s, d_r, loc,
):
    f, c = lax.axis_index("fsdp"), lax.axis_index("ctx")
    tokens, width = x_ref.shape
    quarter = w1g.shape[1]
    greet(f, c, 4, n)
    rows1, rows2 = width // n, quarter // n

    def rows_of(ref, count):
        return lambda k: ref.at[pl.ds(pl.multiple_of(k * count, count), count), :]

    own2 = w2_ref.at[pl.ds(pl.multiple_of(f * rows2, rows2), rows2), :]
    at2 = rows_of(w2g, rows2)
    gather2 = LineGather(f, c, n, lambda sub: own2, lambda k, sub: at2(k), w2_r, w2_a, w2_b, w2_c)
    local2 = pltpu.make_async_copy(own2, at2(c), loc.at[0])
    gather2.begin(local2.start)
    pair1 = PairSum(f, c, n, rows_of(gw1_ref, rows1), got1, s1_ref, h1_s, h1_r)
    line2 = LineSum(f, c, n, lambda o, sub: rows_of(gw2_ref, rows2)(2 * o + sub), in2, stage2, h2_s, h2_r, subs=2)
    attn_sum = QuadSum(f, c, a0, a1, a2, a3, a4, a5, a6)
    back_sum = QuadSum(f, c, b0, b1, b2, b3, b4, b5, b6)
    out_sum = QuadSum(f, c, e0, e1, e2, e3, e4, e5, e6)

    for k in (3, 2, 1, 0):
        r = f ^ k
        for e in range(5):
            mixed_ref[r, :, e * LANES : (e + 1) * LANES] = (
                gates_ref[r, :, e : e + 1] * o_ref[r].astype(F32)
            ).astype(BF16)
        attn_sum.put(k, mm(mixed_ref[r], wout_ref[...]))
        if k == 2:
            attn_sum.cross()
    gather2.step(1)
    middle = x_ref[...].astype(F32) + attn_sum.total()
    mid_ref[...] = middle
    xhat, scale = layer_stats(middle)
    gain = spread_vector(small_ref[:, 2, :], width // n)
    shift = spread_vector(small_ref[:, 3, :], width // n)
    n2_ref[f] = (xhat * gain + shift).astype(BF16)
    n2_gather = QuadGather(f, c, n2_ref, n_s, n_r)
    n2_gather.begin()
    first_bias = spread_vector(small_ref[:, pl.ds(5 + f, 1), :].reshape(n, LANES), rows2)

    def enter(k):
        r = f ^ k
        act, slope = gelu_pair(mm(n2_ref[r], w1g[...]) + first_bias)
        act_ref[r] = act.astype(BF16)
        slope_ref[r] = slope

    gather2.step(2)
    enter(0)
    n2_gather.got(f ^ 1)
    gather2.steps(3)
    enter(1)
    n2_gather.relay()
    enter(2)
    n2_gather.got(f ^ 3)
    enter(3)
    gather2.finish()
    local2.wait()

    for k in (3, 2, 1, 0):
        r = f ^ k
        d_act = mm_t(cot_ref[r], w2g[...])
        dpre_ref[r] = (d_act * slope_ref[r]).astype(BF16)
        back_sum.put(k, mm_t(dpre_ref[r], w1g[...]))
        if k == 2:
            back_sum.cross()
    for k in (3, 2, 1, 0):
        out_sum.put(k, mm(act_ref[f ^ k], w2g[...]))
    tile = 256
    all_tokens = 4 * tokens

    def weight_tile(left_ref, right_ref, result_ref):
        def one(i, _):
            spot = pl.multiple_of(i * tile, tile)
            left = left_ref[:, :, pl.ds(spot, tile)].reshape(all_tokens, tile)
            right = right_ref[...].reshape(all_tokens, right_ref.shape[2])
            result_ref[pl.ds(spot, tile), :] = mm_left_t(left, right).astype(BF16)
            return 0

        lax.fori_loop(0, left_ref.shape[2] // tile, one, 0)

    weight_tile(act_ref, cot_ref, gw2_ref)
    line2.turn(0)
    weight_tile(n2_ref, dpre_ref, gw1_ref)
    pair1.begin()
    d_norm = back_sum.total()
    xhat, scale = layer_stats(mid_ref[...])
    d_middle = cot_ref[f].astype(F32) + layer_back(d_norm, gain, xhat, scale)
    dmid_ref[...] = d_middle
    dml_ref[f] = d_middle.astype(BF16)
    dml_gather = QuadGather(f, c, dml_ref, d_s, d_r)
    dml_gather.begin()
    out_sum.cross()
    vec_ref[...] = jnp.zeros_like(vec_ref)
    vec_ref[0:1, :] = jnp.sum(d_norm * xhat, axis=0, keepdims=True)
    vec_ref[1:2, :] = jnp.sum(d_norm, axis=0, keepdims=True)
    vec_ref[2:3, :] = jnp.sum(cot_ref[f].astype(F32), axis=0, keepdims=True)
    total = jnp.zeros((1, quarter), F32)
    for r in range(4):
        total = total + jnp.sum(dpre_ref[r].astype(F32), axis=0, keepdims=True)
    vec_ref[3:4, :] = total
    lane = lax.broadcasted_iota(jnp.int32, (tokens, LANES), 1)

    def leave(k):
        r = f ^ k
        d_attn = jnp.zeros((tokens, LANES), F32)
        select = jnp.zeros((tokens, LANES), F32)
        result = o_ref[r].astype(F32)
        d_mixed = mm_t(dml_ref[r], wout_ref[...])
        for e in range(5):
            part = d_mixed[:, e * LANES : (e + 1) * LANES]
            d_attn = d_attn + gates_ref[r, :, e : e + 1] * part
            column = jnp.sum(result * part, axis=1, keepdims=True) * gates_ref[r, :, 8 + e : 9 + e]
            select = jnp.where(lane == e, column, select)
        da_ref[r] = d_attn.astype(BF16)
        gsel_ref[r] = select

    line2.turn(1)
    leave(0)
    dml_gather.got(f ^ 1)
    leave(1)
    dml_gather.relay()
    line2.turn(2)
    leave(2)
    dml_gather.got(f ^ 3)
    leave(3)

    def out_tile(i, _):
        spot = pl.multiple_of(i * LANES, LANES)
        left = mixed_ref[:, :, pl.ds(spot, LANES)].reshape(all_tokens, LANES)
        right = dml_ref[...].reshape(all_tokens, width)
        gwout_ref[pl.ds(spot, LANES), :] = mm_left_t(left, right).astype(BF16)
        return 0

    lax.fori_loop(0, 5, out_tile, 0)
    second_bias = spread_vector(small_ref[:, 4, :], width // n)
    out_ref[...] = (mid_ref[...] + out_sum.total() + second_bias).astype(BF16)
    lax.fori_loop(3, n // 2 - 1, lambda k, u: (line2.turn(k), u)[1], 0)
    line2.finish()
    own = 2 * (c // 2) + lax.rem(c, 2)
    s2_ref[0] = stage2[own]
    s2_ref[1] = stage2[own + 1 - 2 * lax.rem(c, 2)]
    line2.sent()
    pair1.finish()
    for one in (attn_sum, back_sum, out_sum, n2_gather, dml_gather):
        one.sent()


def feed(n, x, cot, gates, o, wout, small, w1, w2):
    t, d = x.shape
    quarter = w1.shape[1]
    line = n // 2
    return pl.pallas_call(
        functools.partial(feed_kernel, n),
        out_shape=[
            sds((t, d), BF16), sds((t, d), F32), sds((640, d), BF16), sds((line, d // n, quarter), BF16),
            sds((2, quarter // n, d), BF16), sds((4, t, LANES), BF16), sds((4, t, LANES), F32), sds((8, d), F32),
        ],
        in_specs=[VMEM] * 7 + [ANY],
        out_specs=[VMEM] * 8,
        scratch_shapes=[
            pltpu.VMEM((quarter, d), BF16), pltpu.VMEM((4, t, d), BF16),
            pltpu.VMEM((4, t, quarter), BF16), pltpu.VMEM((4, t, quarter), F32), pltpu.VMEM((4, t, quarter), BF16),
            pltpu.VMEM((4, t, 640), BF16), pltpu.VMEM((4, t, d), BF16), pltpu.VMEM((t, d), F32),
            pltpu.VMEM((d, quarter), BF16), pltpu.VMEM((quarter, d), BF16),
            pltpu.VMEM((line, d // n, quarter), BF16),
        ]
        + line_scratch(line, 2, 2 * quarter // n, d)
        + quad_sum_scratch(t, d) * 3
        + [DMA((n,))] * 4 + [DMA((line,))] * 2 + line_sems(line, 2)
        + [DMA((3,)), DMA((4,)), DMA((3,)), DMA((4,)), DMA((1,))],
        compiler_params=pltpu.CompilerParams(
            collective_id=1, has_side_effects=True, vmem_limit_bytes=62 << 20
        ),
        name="feed",
    )(x, cot, gates, o, wout, small, w1, w2)


class LoneShare:
    def __init__(self, total, out, send, recv):
        self.f, self.c = total.f, total.c
        self.owner = total.place // (total.size // 4)
        self.rel = total.f ^ self.owner
        start = jnp.where(self.rel == 0, (total.place - total.first) * total.subs, 0)
        self.held = total.stage.at[pl.ds(start, total.subs)]
        self.out, self.send, self.recv = out, send, recv
        self.local = pltpu.make_async_copy(self.held, out, recv)

    def copy(self, src, k, to):
        return copy_to(src, self.out, self.send.at[k], self.recv, to, self.c)

    def begin(self):
        @pl.when(self.rel == 0)
        def _():
            self.copy(self.held, 1, self.f ^ 2).start()
            self.copy(self.held, 0, self.f ^ 1).start()
            self.local.start()

    def relay(self):
        @pl.when(self.rel == 2)
        def _():
            self.copy(self.out, 0, self.f).wait_recv()
            self.copy(self.out, 0, self.f ^ 1).start()

    def finish(self):
        @pl.when(self.rel == 0)
        def _():
            self.local.wait()
            self.copy(self.held, 0, self.f).wait_send()
            self.copy(self.held, 1, self.f).wait_send()

        @pl.when(self.rel == 2)
        def _():
            self.copy(self.out, 0, self.f).wait_send()

        @pl.when(lax.rem(self.rel, 2) == 1)
        def _():
            self.copy(self.out, 0, self.f).wait_recv()


def back_kernel(
    n, far_kv,
    da_ref, gwout_ref, s1_ref, s2_ref, qcat_ref, qpos_ref, kv_ref, lse_ref, of_ref,
    tok_ref, p1_ref, ev_ref, gates_ref, gsel_ref, x_ref, small_ref, dmid_ref, vec_ref, table_ref,
    din_ref, gp_ref, gq_ref, g1_ref, g2_ref, go_ref, vq_ref, dkv_ref,
    do_ref, delta_ref, grad_ref, kcat_ref, acc_ref, ring_ref, pin_ref, drel_ref, dqs_ref, dq_ref, part_ref, dp_ref,
    gpa_ref, gpb_ref, mine_ref, vin_ref,
    s0, s1, s2, s3, s4, s5, s6,
    p0, p1, p2, p3, p4, p5, p6, u1, u2, u5, u6,
    fin2, got2, two_s, two_r, w0, w1, w2, w3, w4, w5, w6, y1, y2, y5, y6, goty, swap_s, swap_r,
    da_s, da_r, kv_s, kv_r, pin_r, dq_s, dq_r, gp_s, gp_r, gq_s, gq_r, g1_s, g1_r, g2_s, g2_r, go_s, go_r,
    vc_s, vc_r, vf_s, vf_r, loc,
):
    f, c = lax.axis_index("fsdp"), lax.axis_index("ctx")
    groups = n // 4
    seq, turn = c // groups, lax.rem(c, groups)
    tokens, width = x_ref.shape
    scale = 1.0 / math.sqrt(112)
    own_turn, own_slot = holder_of(c, groups)
    rows = width // n
    greet(f, c, 4, n)

    def send_da(s, _):
        to = s * groups + own_turn

        @pl.when(to != c)
        def _():
            copy_to(da_ref.at[s], do_ref.at[own_slot], da_s.at[s], da_r.at[own_slot], f, to).start()

        @pl.when(to == c)
        def _():
            do_ref[own_slot] = da_ref[s]

        return 0

    lax.fori_loop(0, 4, send_da, 0)
    sub_out = p0.shape[0] // max(1, groups // 2)
    cut = gwout_ref.shape[1] // sub_out
    sum_out = LineSum(
        f, c, n, lambda k, sub: gwout_ref.at[k, pl.ds(pl.multiple_of(sub * cut, cut), cut), :],
        p1, p2, p5, p6, pair=(p0, p3, p4), subs=sub_out, lone=True,
    )
    sum_one = LineSum(f, c, n, lambda o, sub: s1_ref.at[o], u1, u2, u5, u6)
    half = gpa_ref.shape[1]
    pair_to = c + 1 - 2 * lax.rem(c, 2)

    def block_rows(ref, k):
        return ref.at[pl.ds(pl.multiple_of(k * rows, rows), rows), :]

    sum_in = LineSum(
        f, c, n, lambda k, sub: block_rows(gpa_ref, k), w1, w2, w5, w6, pair=(w0, w3, w4)
    )
    sum_late = LineSum(f, c, n, lambda o, sub: block_rows(gpb_ref, 2 * o + sub), y1, y2, y5, y6, subs=2)
    swap_two = copy_to(s2_ref.at[1], got2, two_s, two_r, f, pair_to)
    swap_late = copy_to(y2.at[pair_to], goty, swap_s, swap_r, f, pair_to)

    def prepare(i, _):
        @pl.when(block_of(turn, i, groups) != c)
        def _():
            copy_to(da_ref.at[0], do_ref.at[i], da_s.at[0], da_r.at[i], f, c).wait_recv()

        delta_ref[i] = jnp.sum(do_ref[i].astype(F32) * of_ref[i], axis=1, keepdims=True)
        grad_ref[i] = jnp.zeros((tokens, width + LANES), F32)
        return 0

    lax.fori_loop(0, 4, prepare, 0)
    sum_out.begin()
    swap_two.start()
    row_in = lax.broadcasted_iota(jnp.int32, (tokens, tokens), 0)
    col_in = lax.broadcasted_iota(jnp.int32, (tokens, tokens), 1)
    lane = lax.broadcasted_iota(jnp.int32, (tokens, LANES), 1)
    spots = jnp.logical_or(lane == SPOT_A, lane == SPOT_B)
    last_own = block_of(turn, 3, groups)
    mine_ref[...] = vec_ref[...]

    def close_query(i, sine, cosine):
        first = grad_ref[i, :, 0 : width // 2]
        second = grad_ref[i, :, width // 2 : width]
        drel_ref[i, :, 0 : width // 2] = ((first * sine - second * cosine) * scale).astype(BF16)
        drel_ref[i, :, width // 2 : width] = ((first * cosine + second * sine) * scale).astype(BF16)
        d_place = mm(drel_ref[i], p1_ref[:, :, 896:].reshape(width, LANES))
        d_content = jnp.where(spots, 0.0, grad_ref[i, :, width:] * scale)
        dqs_ref[i] = (d_content + d_place).astype(BF16)
        mine_ref[6:7, 0:LANES] += jnp.sum(d_content, axis=0, keepdims=True)
        mine_ref[7:8, 0:LANES] += jnp.sum(d_place, axis=0, keepdims=True)
        block = block_of(turn, i, groups)

        @pl.when(block != c)
        def _():
            copy_to(dqs_ref.at[i], dq_ref.at[seq], dq_s.at[i], dq_r.at[seq], f, block).start()

        @pl.when(block == c)
        def _():
            dq_ref[seq] = dqs_ref[i]

    bit = lax.rem(c, 2)
    pair_last = block_of(turn + 1 - 2 * bit, 3, groups)

    def ring_pair(kb):
        slot = lax.rem(kb, 4)
        return copy_to(ring_ref.at[slot], pin_ref.at[kb // 2], kv_s.at[slot], pin_r.at[kb // 2], f, pair_to)

    def ring_copy(kb):
        slot = lax.rem(kb, 4)
        return copy_to(ring_ref.at[slot], dkv_ref.at[c // 2], kv_s.at[slot], kv_r.at[c // 2], f, kb)

    def ring_local(kb):
        slot = lax.rem(kb, 4)
        return pltpu.make_async_copy(ring_ref.at[slot], dkv_ref.at[c // 2], kv_s.at[slot])

    def sums(kb):
        return jnp.logical_and(lax.rem(kb, 2) == bit, kb <= jnp.maximum(last_own, pair_last))

    def gives(kb):
        return jnp.logical_and(lax.rem(kb, 2) != bit, kb <= last_own)

    def ring_free(kb):
        @pl.when(gives(kb))
        def _():
            ring_pair(kb).wait_send()

        @pl.when(jnp.logical_and(sums(kb), kb != c))
        def _():
            ring_copy(kb).wait_send()

        @pl.when(jnp.logical_and(sums(kb), kb == c))
        def _():
            ring_local(kb).wait()

    def pass_on(kb):
        @pl.when(sums(kb))
        def _():
            total = acc_ref[lax.rem(kb, 2)]
            slot = lax.rem(kb, 4)

            @pl.when(kb <= pair_last)
            def _():
                ring_pair(kb).wait_recv()
                ring_ref[slot] = (total + pin_ref[kb // 2].astype(F32)).astype(BF16)

            @pl.when(kb > pair_last)
            def _():
                ring_ref[slot] = total.astype(BF16)

            @pl.when(kb != c)
            def _():
                ring_copy(kb).start()

            @pl.when(kb == c)
            def _():
                ring_local(kb).start()

    def key_block(kb, _):
        own = [block_of(turn, i, groups) for i in range(4)]
        first = sum((b < kb).astype(jnp.int32) for b in own)
        ready = sum((b == kb).astype(jnp.int32) for b in own)
        sine, cosine = sin_cos(key_places(kv_ref[kb]), table_ref)
        kcat_ref[:, 0 : width // 2] = cosine.astype(BF16)
        kcat_ref[:, width // 2 : width] = sine.astype(BF16)
        kcat_ref[:, width:] = kv_ref[kb, :, 0:128]
        now = lax.rem(kb, 2)
        acc_ref[now] = jnp.zeros((tokens, 256), F32)

        def query_block(i, _):
            gap = (block_of(turn, i, groups) - kb) * tokens
            scores = mm_t(qcat_ref[i], kcat_ref[...])
            probs = jnp.where(col_in <= row_in + gap, jnp.exp(scores - lse_ref[i]), 0.0)
            d_probs = mm_t(do_ref[i], kv_ref[kb, :, 128:256])
            d_scores = (probs * (d_probs - delta_ref[i])).astype(BF16)
            acc_ref[now, :, 0:128] += mm_left_t(d_scores, qcat_ref[i, :, width:])
            acc_ref[now, :, 128:256] += mm_left_t(probs.astype(BF16), do_ref[i])
            grad_ref[i] += mm(d_scores, kcat_ref[...])
            return 0

        lax.fori_loop(first, 4, query_block, 0)

        @pl.when(ready == 1)
        def _():
            close_query(first, sine, cosine)

        @pl.when(kb >= 4)
        def _():
            ring_free(kb - 4)

        @pl.when(gives(kb))
        def _():
            ring_ref[lax.rem(kb, 4)] = acc_ref[now].astype(BF16)
            ring_pair(kb).start()

        @pl.when(kb >= 1)
        def _():
            pass_on(kb - 1)

        @pl.when(jnp.logical_and(now == 1, kb < n - 1))
        def _():
            sum_one.turn(kb // 2)

        @pl.when(jnp.logical_and(now == 0, kb >= 4))
        def _():
            sum_out.turn(kb // 2 - 2)

        return 0

    lax.fori_loop(0, n, key_block, 0)
    pass_on(n - 1)
    sum_out.turn(n // 2 - 2)
    swap_two.wait()
    fin2[...] = (s2_ref[0].astype(F32) + got2[...].astype(F32)).astype(BF16)
    sum_one.finish()
    sum_out.finish()
    share_out = LoneShare(sum_out, go_ref, go_s, go_r)
    gathers = []
    def hand_out(held, out, send, recv):
        local = pltpu.make_async_copy(held, out.at[f], loc.at[len(gathers)])
        local.start()
        gather = QuadGather(f, c, out, send, recv)
        gather.begin(held)
        gathers.append((gather, local))

    hand_out(fin2, g2_ref, g2_s, g2_r)
    hand_out(u2.at[c // 2], g1_ref, g1_s, g1_r)
    share_out.begin()

    all_tokens = 4 * tokens
    d_rel = drel_ref[...].reshape(all_tokens, width)
    gpb_ref[:, 896 - half :] = mm_left_t(d_rel, qpos_ref[...].reshape(all_tokens, LANES)).astype(BF16)

    def collect(s, _):
        to = s * groups + own_turn

        @pl.when(to != c)
        def _():
            copy_to(dqs_ref.at[0], dq_ref.at[s], dq_s.at[0], dq_r.at[s], f, c).wait_recv()

        acc_ref[0] = jnp.zeros((tokens, 256), F32)

        def add(k, _):
            giver = 2 * k + bit
            at = (s * groups + giver) // 2
            last = jnp.maximum(block_of(giver, 3, groups), block_of(giver + 1 - 2 * bit, 3, groups))

            @pl.when(last >= c)
            def _():
                @pl.when(s * groups + giver != c)
                def _():
                    copy_to(ring_ref.at[0], dkv_ref.at[at], kv_s.at[0], kv_r.at[at], f, c).wait_recv()

                if far_kv:
                    bring = pltpu.make_async_copy(dkv_ref.at[at], part_ref, loc.at[4])
                    bring.start()
                    bring.wait()
                    acc_ref[0] += part_ref[...].astype(F32)
                else:
                    acc_ref[0] += dkv_ref[at].astype(F32)

            return 0

        lax.fori_loop(0, groups // 2, add, 0)
        dp_ref[s, :, 0:128] = dq_ref[s]
        dp_ref[s, :, 128:256] = acc_ref[0, :, 0:128].astype(BF16)
        d_values = acc_ref[0, :, 128:256]
        for e in range(5):
            values = ev_ref[s, :, e * LANES : (e + 1) * LANES].astype(F32)
            column = jnp.sum(values * d_values, axis=1, keepdims=True) * gates_ref[s, :, 24 + e : 25 + e]
            part = gates_ref[s, :, 16 + e : 17 + e] * d_values
            part = jnp.where(lane == SPOT_A, column, part)
            part = jnp.where(lane == SPOT_B, gsel_ref[s, :, e : e + 1], part)
            dp_ref[s, :, 256 + e * LANES : 384 + e * LANES] = part.astype(BF16)
        return 0

    def ring_drain(k, _):
        ring_free(n - 4 + k)
        return 0

    lax.fori_loop(0, 4, ring_drain, 0)
    lax.fori_loop(0, 4, collect, 0)
    tile = 256

    def weight_tile(i, _):
        spot = pl.multiple_of(i * tile, tile)
        left = tok_ref[:, :, pl.ds(spot, tile)].reshape(all_tokens, tile)
        right = dp_ref[...].reshape(all_tokens, 896)
        result = mm_left_t(left, right).astype(BF16)
        gpa_ref[pl.ds(spot, tile), :] = result[:, 0:half]
        gpb_ref[pl.ds(spot, tile), 0 : 896 - half] = result[:, half:]
        return 0

    lax.fori_loop(0, width // tile, weight_tile, 0)
    sum_in.begin()
    sum_late.turn(0)
    for gather, _ in gathers:
        gather.relay()
    share_out.relay()
    in_sum = QuadSum(f, c, s0, s1, s2, s3, s4, s5, s6)
    for k in (3, 2, 1, 0):
        weights = p1_ref[:, :, 0:896].reshape(width, 896)
        in_sum.put(k, mm_t(dp_ref[f ^ k], weights))
        if k == 2:
            in_sum.cross()
    lax.fori_loop(1, n // 2 - 1, lambda k, u: (sum_late.turn(k), u)[1], 0)
    sum_in.turn(0)
    sum_late.finish()
    swap_late.start()
    lax.fori_loop(1, n // 2 - 1, lambda k, u: (sum_in.turn(k), u)[1], 0)
    d_norm = in_sum.total()
    xhat, spread = layer_stats(x_ref[...].astype(F32))
    gain = spread_vector(small_ref[:, 0, :], width // n)
    din_ref[...] = dmid_ref[...] + layer_back(d_norm, gain, xhat, spread)
    mine_ref[4:5, :] = jnp.sum(d_norm * xhat, axis=0, keepdims=True)
    mine_ref[5:6, :] = jnp.sum(d_norm, axis=0, keepdims=True)

    def vec_send(k, _):
        to = lax.rem(c + k, n)
        copy_to(mine_ref, vin_ref.at[c], vc_s.at[to], vc_r.at[c], f, to).start()
        return 0

    lax.fori_loop(1, n, vec_send, 0)
    vin_ref[c] = mine_ref[...]
    swap_late.wait()
    y2[c] = (y2[c].astype(F32) + goty[...].astype(F32)).astype(BF16)
    hand_out(y2.at[c], gq_ref, gq_s, gq_r)
    sum_in.finish()
    hand_out(w2.at[c // 2], gp_ref, gp_s, gp_r)

    def vec_wait(k, _):
        to = lax.rem(c + k, n)
        copy_to(mine_ref, vin_ref.at[to], vc_s.at[to], vc_r.at[to], f, to).wait()
        return 0

    lax.fori_loop(1, n, vec_wait, 0)
    vq_ref[f] = jnp.sum(vin_ref[...], axis=0)
    for k in range(1, 4):
        copy_to(vq_ref.at[f], vq_ref.at[f], vf_s.at[k], vf_r.at[f], f ^ k, c).start()
    for gather, _ in gathers[2:]:
        gather.relay()
    for k in range(1, 4):
        copy_to(vq_ref.at[f ^ k], vq_ref.at[f ^ k], vf_s.at[k], vf_r.at[f ^ k], f, c).wait_recv()
        copy_to(vq_ref.at[f], vq_ref.at[f], vf_s.at[k], vf_r.at[f], f, c).wait_send()
    for one, local in gathers:
        one.got(f ^ 1)
        one.got(f ^ 3)
        one.sent()
        local.wait()
    share_out.finish()
    for one in (sum_one, sum_out, sum_in, sum_late):
        one.sent()
    in_sum.sent()

    def drain(i, _):
        @pl.when(i * groups + own_turn != c)
        def _():
            copy_to(da_ref.at[i], do_ref.at[0], da_s.at[i], da_r.at[0], f, c).wait_send()

        @pl.when(block_of(turn, i, groups) != c)
        def _():
            copy_to(dqs_ref.at[i], dq_ref.at[0], dq_s.at[i], dq_r.at[0], f, c).wait_send()

        return 0

    lax.fori_loop(0, 4, drain, 0)


def cuts(count):
    parts = max(1, count // 64)
    return parts if count % (16 * parts) == 0 else 1


def pair_scratch(blocks, subs, rows, cols):
    return [pltpu.VMEM((blocks * subs, rows // subs, cols), BF16)]


def line_scratch(blocks, subs, rows, cols):
    return [
        pltpu.VMEM(((blocks + 1) * subs, rows // subs, cols), BF16),
        pltpu.VMEM((blocks * subs, rows // subs, cols), BF16),
    ]


def line_sems(blocks, subs):
    return [DMA((blocks * subs,)), DMA(((blocks + 1) * subs,))]


def back(n, da, gwout, s1, s2, qcat, qpos, kv, lse, of, tok, p1, ev, gates, gsel, x, small, dmid, vec, table):
    t, d = x.shape
    g = n // 4
    quarter = s1.shape[2]
    rows, out_rows, two_rows = d // n, gwout.shape[1], s2.shape[1]
    half = d // 2
    sub_out = cuts(out_rows)
    lone, line = n // 8, n // 2
    far_kv = g > 4
    return pl.pallas_call(
        functools.partial(back_kernel, n, far_kv),
        out_shape=[
            sds((t, d), F32), sds((4, rows, half), BF16), sds((4, rows, half), BF16), sds((4, rows, quarter), BF16),
            sds((4, two_rows, d), BF16), sds((sub_out, out_rows // sub_out, d), BF16),
            sds((4, 8, d), F32), sds((line, t, 256), BF16),
        ],
        in_specs=[VMEM] * 19,
        out_specs=[VMEM, ANY, ANY, ANY, ANY, ANY, VMEM, ANY if far_kv else VMEM],
        scratch_shapes=[
            pltpu.VMEM((4, t, LANES), BF16), pltpu.VMEM((4, t, 1), F32), pltpu.VMEM((4, t, d + LANES), F32),
            pltpu.VMEM((t, d + LANES), BF16), pltpu.VMEM((2, t, 256), F32), pltpu.VMEM((4, t, 256), BF16),
            pltpu.VMEM((line, t, 256), BF16),
            pltpu.VMEM((4, t, d), BF16), pltpu.VMEM((4, t, LANES), BF16), pltpu.VMEM((4, t, LANES), BF16),
            pltpu.VMEM((t, 256), BF16), pltpu.VMEM((4, t, 896), BF16), pltpu.VMEM((d, half), BF16), pltpu.VMEM((d, half), BF16),
            pltpu.VMEM((8, d), F32), pltpu.VMEM((n, 8, d), F32),
        ]
        + quad_sum_scratch(t, d)
        + pair_scratch(lone, sub_out, out_rows, d) + line_scratch(lone, sub_out, out_rows, d)
        + [DMA((lone * sub_out,))] * 2 + line_sems(lone, sub_out)
        + line_scratch(line, 1, rows, quarter) + line_sems(line, 1)
        + [pltpu.VMEM((two_rows, d), BF16), pltpu.VMEM((two_rows, d), BF16), DMA, DMA]
        + pair_scratch(line, 1, rows, half) + line_scratch(line, 1, rows, half)
        + [DMA((line,))] * 2 + line_sems(line, 1)
        + line_scratch(line, 2, 2 * rows, half) + line_sems(line, 2)
        + [pltpu.VMEM((rows, half), BF16), DMA, DMA]
        + [
            DMA((4,)), DMA((4,)), DMA((4,)), DMA((line,)), DMA((line,)), DMA((4,)), DMA((4,)), DMA((3,)), DMA((4,)),
            DMA((3,)), DMA((4,)), DMA((3,)), DMA((4,)), DMA((3,)), DMA((4,)), DMA((2,)), DMA, DMA((n,)), DMA((n,)), DMA((4,)), DMA((4,)), DMA((5,)),
        ],
        compiler_params=pltpu.CompilerParams(
            collective_id=2, has_side_effects=True, vmem_limit_bytes=63 << 20
        ),
        name="back",
    )(da, gwout, s1, s2, qcat, qpos, kv, lse, of, tok, p1, ev, gates, gsel, x, small, dmid, vec, table)


def pad_channels(v, group):
    lead = v.shape[:-1]
    v = v.reshape(lead + (112 // group, group))
    v = jnp.pad(v, [(0, 0)] * len(lead) + [(0, 0), (0, group // 7)])
    return v.reshape(lead + (LANES,))


def head_pick(w, f, heads=4):
    w = w.reshape(w.shape[0], heads, -1)
    return lax.dynamic_index_in_dim(w, f, 1, keepdims=False)


def route_lanes(routes):
    hot = routes[..., None] == jnp.arange(8, dtype=jnp.int32)
    return jnp.sum(hot.astype(F32), axis=-2)


def pack_inputs(
    n, f, positions, value_routes, output_routes, ln1_gain, ln1_bias, wq, wk, wrel, u_bias, v_bias,
    wvsel, wv, wosel, wout, ln2_gain, ln2_bias, b1, b2,
):
    t = positions.shape[0]
    rows = wq.shape[0]
    group = math.gcd(112, wout.shape[0])
    masks = jnp.concatenate([route_lanes(value_routes), route_lanes(output_routes)], axis=-1).reshape(t, 64)
    place = jnp.stack([positions // 128, positions % 128], axis=-1).astype(F32)
    aux = jnp.concatenate([masks, place, jnp.zeros((t, 62), F32)], axis=-1).astype(BF16)
    lane = jnp.arange(LANES)
    experts = pad_channels(head_pick(wv, f).reshape(rows, 5, 112), group)
    experts = jnp.where(lane == SPOT_A, head_pick(wvsel, f)[..., None], experts)
    experts = jnp.where(lane == SPOT_B, head_pick(wosel, f)[..., None], experts)
    p1 = jnp.concatenate(
        [
            pad_channels(head_pick(wq, f), group), pad_channels(head_pick(wk, f), group),
            experts.reshape(rows, 640), pad_channels(head_pick(wrel, f), group),
        ],
        axis=-1,
    )
    piece = b1.shape[0] // 4
    vectors = [ln1_gain, ln1_bias, ln2_gain, ln2_bias, b2]
    vectors = [jnp.pad(v, (0, LANES - v.shape[0])) for v in vectors]
    extra = jnp.pad(b1.reshape(-1, piece), ((0, 0), (0, LANES - piece)))
    small = jnp.concatenate([jnp.stack(vectors), extra]).astype(F32)
    small = jnp.pad(small, ((0, 16 - small.shape[0]), (0, 0)))
    pieces = wout.reshape(-1, group, wout.shape[1])
    pieces = jnp.pad(pieces, ((0, 0), (0, group // 7), (0, 0))).reshape(-1, wout.shape[1])
    pieces = jnp.pad(pieces, ((0, -pieces.shape[0] % 16), (0, 0)))
    bias = jnp.concatenate([pad_channels(u_bias, group), pad_channels(v_bias, group)]).astype(F32)
    return aux, p1, small, pieces, bias


def drop_pads(v, group):
    lead = v.shape[:-1]
    wide = group * 8 // 7
    return v.reshape(lead + (LANES // wide, wide))[..., :group].reshape(lead + (112,))


def on_device(n, *args):
    (
        x, positions, value_routes, output_routes, ln1_gain, ln1_bias, wq, wk, wrel, u_bias, v_bias,
        wvsel, wv, wosel, wout, ln2_gain, ln2_bias, w1, b1, w2, b2, cot,
    ) = args
    f, c = lax.axis_index("fsdp"), lax.axis_index("ctx")
    d = x.shape[1]
    g = n // 4
    group = math.gcd(112, wout.shape[0])
    aux, p1, small, pieces, bias = pack_inputs(
        n, f, positions, value_routes, output_routes, ln1_gain, ln1_bias, wq, wk, wrel, u_bias, v_bias,
        wvsel, wv, wosel, wout, ln2_gain, ln2_bias, b1, b2,
    )
    table = jnp.asarray(turn_table(d))
    rows, hidden = w1.shape
    part = hidden // n // 4
    w1_own = lax.dynamic_index_in_dim(w1.reshape(rows, n, 4, part), f, 2, keepdims=False).reshape(rows, n * part)
    tok, p1g, smallg, woutg, w1g, cotg, ev, gates, o, qcat, qpos, kv, lse, of = attend(
        n, x, aux, cot, p1, small, pieces, w1_own, bias, table
    )
    block = 640 // g
    out, dmid, gwout, s1, s2, da, gsel, vec = feed(
        n, x, cotg, gates, o, woutg[:, :block].reshape(640, d), smallg, w1g.reshape(d, n * part), w2
    )
    gwout = gwout.reshape(g, block, d)
    gwout = jnp.pad(gwout, ((0, 0), (0, pieces.shape[0] - block), (0, 0)))
    d_in, gp, gq, g1, g2, go, vq, _ = back(
        n, da, gwout, s1, s2, qcat, qpos, kv, lse, of, tok, p1g, ev, gates, gsel, x, smallg, dmid, vec, table
    )
    gp = jnp.transpose(jnp.concatenate([gp, gq], axis=-1), (1, 0, 2))
    g_query = drop_pads(gp[..., 0:128], group).reshape(rows, 448).astype(F32)
    g_key = drop_pads(gp[..., 128:256], group).reshape(rows, 448).astype(F32)
    g_rel = drop_pads(gp[..., 896:], group).reshape(rows, 448).astype(F32)
    experts = gp[..., 256:896].reshape(rows, 4, 5, LANES)
    g_value = drop_pads(experts, group).reshape(rows, 2240).astype(F32)
    g_vsel = experts[..., SPOT_A].reshape(rows, 20).astype(F32)
    g_osel = experts[..., SPOT_B].reshape(rows, 20).astype(F32)
    g_one = jnp.transpose(g1.reshape(4, rows, n, part), (1, 2, 0, 3)).reshape(rows, hidden).astype(F32)
    g_two = g2.reshape(-1, d).astype(F32)
    g_out = go.reshape(-1, d)[:block].reshape(-1, group * 8 // 7, d)[:, :group].reshape(-1, d).astype(F32)
    sums = jnp.sum(vq, axis=0)
    own = lax.dynamic_slice_in_dim(sums, c * rows, rows, 1)
    g_b1 = lax.dynamic_slice_in_dim(vq[:, 3, :], c * part, part, 1).reshape(-1)
    g_u = drop_pads(vq[:, 6, 0:LANES], group)
    g_v = drop_pads(vq[:, 7, 0:LANES], group)
    return (
        out, d_in, own[4], own[5], g_query, g_key, g_rel, g_u, g_v, g_vsel, g_value, g_osel, g_out,
        own[0], own[1], g_one, g_b1, g_two, own[2],
    )


def solution(mesh):
    both = ("fsdp", "ctx")
    row, vector, matrix = P(both, None), P("ctx"), P("ctx", None)
    in_specs = (
        row, P(both), P(both, None, None), P(both, None, None), vector, vector, matrix, matrix, matrix,
        P(), P(), matrix, matrix, matrix, matrix, vector, vector, matrix, vector, matrix, vector, row,
    )
    out_specs = (
        row, row, vector, vector, matrix, matrix, matrix, P(), P(), matrix, matrix, matrix, matrix,
        vector, vector, matrix, vector, matrix, vector,
    )
    return jax.shard_map(
        functools.partial(on_device, mesh.shape["ctx"]),
        mesh=mesh, in_specs=in_specs, out_specs=out_specs, check_vma=False,
    )
```

```python
import functools
import math

import jax
import jax.numpy as jnp
import numpy as np
from jax import lax
from jax.experimental import pallas as pl
from jax.experimental.pallas import tpu as pltpu
from jax.sharding import PartitionSpec as P

MESH = pl.DeviceIdType.MESH
F32 = jnp.float32
BF16 = jnp.bfloat16
LN_EPS = 1e-05
MASKED = -1e30
LANES = 128
SPOT_A, SPOT_B = 63, 127
VMEM = pl.BlockSpec(memory_space=pltpu.VMEM)
ANY = pl.BlockSpec(memory_space=pl.ANY)
DMA = pltpu.SemaphoreType.DMA


def turn_coefficients():
    nodes = (np.cos(np.pi * (np.arange(400) + 0.5) / 400) + 1) / 8
    root = np.sqrt(nodes)
    powers = nodes[:, None] ** np.arange(7)[None, :]
    sine = np.linalg.lstsq(powers, np.sin(2 * np.pi * root) / root, rcond=None)[0]
    cosine = np.linalg.lstsq(powers, np.cos(2 * np.pi * root), rcond=None)[0]
    return [float(v) for v in sine], [float(v) for v in cosine]


SIN_TURN, COS_TURN = turn_coefficients()


def horner(coefs, v):
    total = coefs[-1]
    for coef in coefs[-2::-1]:
        total = total * v + coef
    return total


def turn_table(model_width):
    freq = 10000.0 ** (-np.arange(0, model_width, 2, dtype=np.float64) / model_width) / (2 * np.pi)
    mantissa, exponent = np.frexp(freq)
    coarse = np.ldexp(np.floor(mantissa * 256) / 256, exponent)
    table = np.zeros((8, model_width // 2), np.float32)
    table[0] = coarse
    table[1] = freq - coarse
    return table


def sin_cos(places, table_ref):
    coarse = places * table_ref[0:1, :]
    part = (coarse - jnp.round(coarse)) + places * table_ref[1:2, :]
    part = part - jnp.round(part)
    square = part * part
    return horner(SIN_TURN, square) * part, horner(COS_TURN, square)


def mm(left, right):
    return lax.dot_general(left, right, (((1,), (0,)), ((), ())), preferred_element_type=F32)


def mm_t(left, right):
    return lax.dot_general(left, right, (((1,), (1,)), ((), ())), preferred_element_type=F32)


def mm_left_t(left, right):
    return lax.dot_general(left, right, (((0,), (0,)), ((), ())), preferred_element_type=F32)


def copy_to(src, dst, send, recv, f, c):
    return pltpu.make_async_remote_copy(
        src_ref=src, dst_ref=dst, send_sem=send, recv_sem=recv, device_id=(f, c), device_id_type=MESH
    )


def greet(f, c, fsdp, n):
    barrier = pltpu.get_barrier_semaphore()

    def one(k, _):
        pl.semaphore_signal(barrier, inc=1, device_id=(f, lax.rem(c + k, n)), device_id_type=MESH)
        return 0

    lax.fori_loop(1, n, one, 0)
    for k in range(1, fsdp):
        pl.semaphore_signal(barrier, inc=1, device_id=(f ^ k, c), device_id_type=MESH)
    pl.semaphore_wait(barrier, n - 1 + fsdp - 1)


class LineGather:
    def __init__(self, f, c, n, own, at, recv, right, left, pair, subs=1, lone=False):
        self.f, self.c, self.n, self.size = f, c, n, n // 2
        self.place, self.bit = c // 2, lax.rem(c, 2)
        self.own, self.at = own, at
        self.recv, self.right, self.left, self.pair = recv, right, left, pair
        self.subs, self.lone = subs, lone

    def valid(self, o):
        ok = jnp.logical_and(o >= 0, o < self.size)
        if self.lone:
            span = self.size // 4
            ok = jnp.logical_and(ok, jnp.logical_and(o >= self.f * span, o < (self.f + 1) * span))
        return ok

    def slot(self, block):
        return block - self.f * (self.n // 4) if self.lone else block

    def copy(self, src, block, sub, sems, c):
        slot = self.slot(block)
        i = slot * self.subs + sub
        return copy_to(src, self.at(slot, sub), sems.at[i], self.recv.at[i], self.f, c)

    def held(self, block, sub):
        return self.at(self.slot(block), sub)

    def each(self, work):
        if self.subs == 1:
            work(0)
        else:
            lax.fori_loop(0, self.subs, lambda sub, u: (work(sub), u)[1], 0)

    def spread(self, src, block, sub, go_right, go_left):
        @pl.when(go_right)
        def _():
            self.copy(src, block, sub, self.right, self.c + 2).start()

        @pl.when(go_left)
        def _():
            self.copy(src, block, sub, self.left, self.c - 2).start()

        self.copy(src, block, sub, self.pair, self.c + 1 - 2 * self.bit).start()

    def begin(self, local):
        @pl.when(self.valid(self.place))
        def _():
            self.each(
                lambda sub: self.spread(
                    self.own(sub), self.c, sub, self.place < self.size - 1, self.place > 0
                )
            )
            local()

    def arrived(self, block, sub):
        self.copy(self.held(block, sub), block, sub, self.pair, self.c).wait_recv()

    def step(self, t):
        for sign in (-1, 1):
            o = self.place + sign * t
            block = 2 * o + self.bit

            @pl.when(self.valid(o))
            def _():
                def one(sub):
                    self.arrived(block, sub)
                    self.spread(
                        self.held(block, sub), block, sub,
                        jnp.logical_and(sign < 0, self.place < self.size - 1),
                        jnp.logical_and(sign > 0, self.place > 0),
                    )

                self.each(one)

    def steps(self, first=1):
        lax.fori_loop(first, self.size, lambda t, u: (self.step(t), u)[1], 0)

    def finish(self):
        def one(o, _):
            block = 2 * o + self.bit

            def piece(sub):
                self.arrived(2 * o + 1 - self.bit, sub)
                source = self.held(block, sub)
                self.copy(source, block, sub, self.pair, self.c).wait_send()

                @pl.when(jnp.logical_and(o <= self.place, self.place < self.size - 1))
                def _():
                    self.copy(source, block, sub, self.right, self.c).wait_send()

                @pl.when(jnp.logical_and(o >= self.place, self.place > 0))
                def _():
                    self.copy(source, block, sub, self.left, self.c).wait_send()

            @pl.when(self.valid(o))
            def _():
                self.each(piece)

            return 0

        lax.fori_loop(0, self.size, one, 0)


class QuadGather:
    def __init__(self, f, c, out, send, recv):
        self.f, self.c, self.out, self.send, self.recv = f, c, out, send, recv

    def copy(self, slot, k, to, src=None):
        src = self.out.at[slot] if src is None else src
        return copy_to(src, self.out.at[slot], self.send.at[k], self.recv.at[slot], to, self.c)

    def begin(self, src=None):
        self.copy(self.f, 1, self.f ^ 2, src).start()
        self.copy(self.f, 0, self.f ^ 1, src).start()

    def got(self, slot):
        self.copy(slot, 0, self.f).wait_recv()

    def relay(self):
        self.got(self.f ^ 2)
        self.copy(self.f ^ 2, 2, self.f ^ 1).start()

    def sent(self):
        for k in range(3):
            self.copy(self.f, k, self.f).wait_send()


def spread_vector(rows, width):
    count = rows.shape[0]
    total = count * width
    lane = lax.broadcasted_iota(jnp.int32, (LANES, total), 0)
    column = lax.broadcasted_iota(jnp.int32, (LANES, total), 1)
    onehot = jnp.where(lane == lax.rem(column, width), 1.0, 0.0).astype(BF16)
    wide = mm(rows.astype(BF16), onehot)
    row = lax.broadcasted_iota(jnp.int32, (count, total), 0)
    column = lax.broadcasted_iota(jnp.int32, (count, total), 1)
    return jnp.sum(jnp.where(column // width == row, wide, 0.0), axis=0, keepdims=True)


def block_of(j, i, groups):
    return i * groups + jnp.where(lax.rem(i, 2) == 0, j, groups - 1 - j)


def holder_of(block, groups):
    row, within = block // groups, lax.rem(block, groups)
    return jnp.where(lax.rem(row, 2) == 0, within, groups - 1 - within), row


def key_places(kv):
    return kv[:, SPOT_A : SPOT_A + 1].astype(F32) * 128.0 + kv[:, SPOT_B : SPOT_B + 1].astype(F32)


def attend_kernel(
    n,
    x_ref, aux_ref, cot_ref, p1_ref, small_ref, wout_ref, w2_ref, bias_ref, table_ref,
    tok_ref, p1g_ref, smallg_ref, woutg_ref, w2e_ref, cotg_ref, ev_ref, gates_ref, o_ref,
    qcat_ref, qpos_ref, kv_ref, lse_ref, of_ref,
    qs_ref, kvs_ref, qr_ref, os_ref, kcat_ref, vt_ref, m_ref, l_ref,
    sm_s, sm_r, p_r, p_a, p_b, p_c, w_r, w_a, w_b, w_c, h_r, h_a, h_b, h_c,
    t_s, t_r, c_s, c_r, q_s, q_r, kv_s, kv_r, kv_p, o_s, o_r, loc,
):
    f, c = lax.axis_index("fsdp"), lax.axis_index("ctx")
    groups = n // 4
    seq, turn = c // groups, lax.rem(c, groups)
    tokens, width = x_ref.shape
    scale = 1.0 / math.sqrt(112)
    greet(f, c, 4, n)

    def small_send(k, _):
        to = lax.rem(c + k, n)
        copy_to(small_ref, smallg_ref.at[c], sm_s.at[to], sm_r.at[c], f, to).start()
        return 0

    lax.fori_loop(1, n, small_send, 0)
    smallg_ref[c] = small_ref[...]
    gather_p = LineGather(f, c, n, lambda sub: p1_ref, lambda k, sub: p1g_ref.at[k], p_r, p_a, p_b, p_c)

    def own_p():
        p1g_ref[c] = p1_ref[...]

    gather_p.begin(own_p)
    wout_copy = pltpu.make_async_copy(wout_ref, woutg_ref.at[c - f * groups], loc.at[0])
    subs = w_r.shape[0] // groups
    piece = wout_ref.shape[0] // subs
    gather_w = LineGather(
        f, c, n,
        lambda sub: wout_ref.at[pl.ds(pl.multiple_of(sub * piece, piece), piece), :],
        lambda k, sub: woutg_ref.at[k, pl.ds(pl.multiple_of(sub * piece, piece), piece), :],
        w_r, w_a, w_b, w_c, subs=subs, lone=True,
    )
    early = w2e_ref.shape[1]
    own2 = w2_ref.at[pl.ds(pl.multiple_of(f * (w2_ref.shape[0] // 4), 16), early), :]
    w2_copy = pltpu.make_async_copy(own2, w2e_ref.at[c], loc.at[2])
    gather_h = LineGather(f, c, n, lambda sub: own2, lambda k, sub: w2e_ref.at[k], h_r, h_a, h_b, h_c)
    cot_copy = pltpu.make_async_copy(cot_ref, cotg_ref.at[f], loc.at[1])
    cot_copy.start()

    hidden = x_ref[...].astype(F32)
    offsets = hidden - jnp.mean(hidden, axis=1, keepdims=True)
    spread = jnp.mean(offsets * offsets, axis=1, keepdims=True)
    xhat = offsets * lax.rsqrt(spread + LN_EPS)

    def small_wait(k, _):
        to = lax.rem(c + k, n)
        copy_to(small_ref, smallg_ref.at[to], sm_s.at[to], sm_r.at[to], f, to).wait()
        return 0

    lax.fori_loop(1, n, small_wait, 0)
    gain = spread_vector(smallg_ref[:, 0, :], width // n)
    shift = spread_vector(smallg_ref[:, 1, :], width // n)
    tok_ref[f, :, 0:width] = (xhat * gain + shift).astype(BF16)
    tok_ref[f, :, width:] = aux_ref[...]
    tok_gather = QuadGather(f, c, tok_ref, t_s, t_r)
    tok_gather.begin()
    gather_p.steps()
    tok_gather.relay()
    gather_p.finish()
    tok_gather.got(f ^ 1)
    tok_gather.got(f ^ 3)
    tok_gather.sent()
    cot_gather = QuadGather(f, c, cotg_ref, c_s, c_r)
    cot_gather.begin(cot_ref)

    lane = lax.broadcasted_iota(jnp.int32, (tokens, LANES), 1)
    source = lax.broadcasted_iota(jnp.int32, (LANES, LANES), 0)
    target = lax.broadcasted_iota(jnp.int32, (LANES, LANES), 1)
    wanted = f * 16 + lax.rem(target, 8) + jnp.where(target < 16, 8, 0)
    pick = jnp.where(
        jnp.logical_and(source == wanted, jnp.logical_and(target < 32, lax.rem(target, 8) < 5)), 1.0, 0.0
    ).astype(BF16)
    own_turn, own_slot = holder_of(c, groups)
    bit = lax.rem(c, 2)
    spots = jnp.logical_or(lane == SPOT_A, lane == SPOT_B)

    def project(t, _):
        s = lax.rem(seq + 1 + t, 4)
        normed = tok_ref[s, :, 0:width]
        aux = tok_ref[s, :, width:]
        weights = p1g_ref[...].reshape(width, p1g_ref.shape[2])
        qk = mm(normed, weights[:, 0:256])
        experts = mm(normed, weights[:, 256:896])
        ev_ref[s] = experts.astype(BF16)
        logits = jnp.zeros((tokens, LANES), F32)
        for e in range(5):
            for spot, first in ((SPOT_B, 0), (SPOT_A, 16)):
                column = experts[:, e * LANES + spot : e * LANES + spot + 1]
                logits = jnp.where(
                    jnp.logical_or(lane == first + e, lane == first + 8 + e), column, logits
                )
        sig = jax.nn.sigmoid(logits)
        gates = mm(aux, pick) * jnp.where(lax.rem(lane, 16) >= 8, sig * (1.0 - sig), sig)
        gates_ref[s] = gates
        values = jnp.zeros((tokens, LANES), F32)
        for e in range(5):
            values = values + gates[:, 16 + e : 17 + e] * experts[:, e * LANES : (e + 1) * LANES]
        values = jnp.where(spots, 0.0, values)
        high, rest = aux[:, 64:65].astype(F32), aux[:, 65:66].astype(F32)

        def with_place(v):
            return jnp.where(lane == SPOT_A, high, jnp.where(lane == SPOT_B, rest, v)).astype(BF16)

        qs_ref[s] = with_place(qk[:, 0:128])
        kvs_ref[s, :, 0:128] = with_place(qk[:, 128:256])
        kvs_ref[s, :, 128:256] = values.astype(BF16)
        to = s * groups + own_turn

        @pl.when(to != c)
        def _():
            copy_to(qs_ref.at[s], qr_ref.at[own_slot], q_s.at[s], q_r.at[own_slot], f, to).start()

        @pl.when(to == c)
        def _():
            qr_ref[own_slot] = qs_ref[s]

        def kv_send(k, _):
            to = s * groups + 2 * k + bit

            @pl.when(to != c)
            def _():
                copy_to(kvs_ref.at[s], kv_ref.at[c], kv_s.at[to], kv_r.at[c], f, to).start()

            @pl.when(to == c)
            def _():
                kv_ref[c] = kvs_ref[s]

            return 0

        lax.fori_loop(0, groups // 2, kv_send, 0)
        return 0

    gather_h.begin(w2_copy.start)
    lax.fori_loop(0, 4, project, 0)
    gather_w.begin(wout_copy.start)

    def kv_wait(block):
        copy_to(kvs_ref.at[0], kv_ref.at[block], kv_s.at[0], kv_r.at[block], f, c).wait_recv()

    def kv_pass(block):
        return copy_to(kv_ref.at[block], kv_ref.at[block], kv_p.at[block // 2], kv_r.at[block], f, c + 1 - 2 * bit)

    def hand_on(m):
        block = 2 * m + bit

        @pl.when(block != c)
        def _():
            kv_wait(block)

        kv_pass(block).start()

    def prepare(i, _):
        block = block_of(turn, i, groups)

        @pl.when(block != c)
        def _():
            copy_to(qs_ref.at[0], qr_ref.at[i], q_s.at[0], q_r.at[i], f, c).wait_recv()

        places = key_places(qr_ref[i])
        query = jnp.where(spots, 0.0, qr_ref[i].astype(F32))
        q_position = (query + bias_ref[pl.ds(4 + f, 1), :]).astype(BF16)
        qpos_ref[i] = q_position
        qcat_ref[i, :, width:] = ((query + bias_ref[pl.ds(f, 1), :]) * scale).astype(BF16)
        rel = p1g_ref[:, :, 896:].reshape(width, LANES)
        rel_query = mm_t(q_position, rel)
        sine, cosine = sin_cos(places, table_ref)
        first, second = rel_query[:, : width // 2], rel_query[:, width // 2 :]
        qcat_ref[i, :, 0 : width // 2] = ((first * sine + second * cosine) * scale).astype(BF16)
        qcat_ref[i, :, width // 2 : width] = ((second * sine - first * cosine) * scale).astype(BF16)
        m_ref[i] = jnp.full((1, tokens), MASKED, F32)
        l_ref[i] = jnp.zeros((1, tokens), F32)
        of_ref[i] = jnp.zeros((LANES, tokens), F32)
        return 0

    lax.fori_loop(0, 4, prepare, 0)
    hand_on(0)
    row_in = lax.broadcasted_iota(jnp.int32, (tokens, tokens), 0)
    col_in = lax.broadcasted_iota(jnp.int32, (tokens, tokens), 1)

    def give(i):
        total = l_ref[i]
        result = of_ref[i] / total
        of_ref[i] = result
        lse_ref[i] = m_ref[i] + jnp.log(total)
        os_ref[i] = result.T.astype(BF16)
        block = block_of(turn, i, groups)

        @pl.when(block != c)
        def _():
            copy_to(os_ref.at[i], o_ref.at[seq], o_s.at[i], o_r.at[seq], f, block).start()

        @pl.when(block == c)
        def _():
            o_ref[seq] = os_ref[i]

    def key_block(kb, _):
        own = [block_of(turn, i, groups) for i in range(4)]
        first = sum((b < kb).astype(jnp.int32) for b in own)
        ready = sum((b == kb).astype(jnp.int32) for b in own)

        @pl.when(lax.rem(kb, 2) != bit)
        def _():
            kv_wait(kb)

        @pl.when(jnp.logical_and(lax.rem(kb, 2) == 0, kb < n - 2))
        def _():
            hand_on(kb // 2 + 1)

        sine, cosine = sin_cos(key_places(kv_ref[kb]), table_ref)
        kcat_ref[:, 0 : width // 2] = cosine.astype(BF16)
        kcat_ref[:, width // 2 : width] = sine.astype(BF16)
        kcat_ref[:, width:] = kv_ref[kb, :, 0:128]
        vt_ref[...] = kv_ref[kb, :, 128:256].astype(F32).T.astype(BF16)

        def query_block(i, _):
            gap = (block_of(turn, i, groups) - kb) * tokens
            scores = mm_t(kcat_ref[...], qcat_ref[i])
            scores = jnp.where(row_in <= col_in + gap, scores, MASKED)
            before = m_ref[i]
            best = jnp.maximum(before, jnp.max(scores, axis=0, keepdims=True))
            shrink = jnp.exp(before - best)
            probs = jnp.exp(scores - best)
            m_ref[i] = best
            l_ref[i] = l_ref[i] * shrink + jnp.sum(probs, axis=0, keepdims=True)
            of_ref[i] = of_ref[i] * shrink + mm(vt_ref[...], probs.astype(BF16))
            return 0

        lax.fori_loop(first, 4, query_block, 0)

        @pl.when(ready == 1)
        def _():
            give(first)

        @pl.when(kb == n // 2 - 1)
        def _():
            cot_gather.relay()

        @pl.when(jnp.logical_and(kb > 0, kb < n // 2))
        def _():
            gather_w.step(kb)

        @pl.when(kb < n // 2 - 1)
        def _():
            gather_h.step(kb + 1)

        return 0

    lax.fori_loop(0, n, key_block, 0)
    cot_gather.got(f ^ 1)
    cot_gather.got(f ^ 3)
    cot_gather.sent()
    gather_w.finish()
    gather_h.finish()
    w2_copy.wait()

    @pl.when(gather_w.valid(c // 2))
    def _():
        wout_copy.wait()

    cot_copy.wait()

    def drain(s, _):
        to = s * groups + own_turn

        @pl.when(to != c)
        def _():
            copy_to(qs_ref.at[s], qr_ref.at[own_slot], q_s.at[s], q_r.at[0], f, to).wait_send()
            copy_to(os_ref.at[0], o_ref.at[s], o_s.at[0], o_r.at[s], f, to).wait_recv()

        @pl.when(block_of(turn, s, groups) != c)
        def _():
            copy_to(os_ref.at[s], o_ref.at[s], o_s.at[s], o_r.at[0], f, to).wait_send()

        return 0

    lax.fori_loop(0, 4, drain, 0)

    def kv_drain(k, _):
        to = 2 * k + bit

        @pl.when(to != c)
        def _():
            copy_to(kvs_ref.at[0], kv_ref.at[0], kv_s.at[to], kv_r.at[0], f, c).wait_send()

        kv_pass(to).wait_send()
        return 0

    lax.fori_loop(0, n // 2, kv_drain, 0)


def sds(shape, dtype):
    return jax.ShapeDtypeStruct(shape, dtype)


def attend(n, x, aux, cot, p1, small, wout, w2, bias, table):
    t, d = x.shape
    rows = p1.shape[0]
    out_rows = wout.shape[0]
    g = n // 4
    subs = cuts(out_rows)
    return pl.pallas_call(
        functools.partial(attend_kernel, n),
        out_shape=[
            sds((4, t, d + LANES), BF16), sds((n, rows, d), BF16), sds((n, 16, LANES), F32),
            sds((g, out_rows, d), BF16), sds((n, early_rows(w2.shape[0] // 4), d), BF16), sds((4, t, d), BF16), sds((4, t, 640), BF16),
            sds((4, t, LANES), F32), sds((4, t, LANES), BF16), sds((4, t, d + LANES), BF16),
            sds((4, t, LANES), BF16), sds((n, t, 256), BF16), sds((4, 1, t), F32), sds((4, LANES, t), F32),
        ],
        in_specs=[VMEM, VMEM, ANY, VMEM, VMEM, ANY, ANY, VMEM, VMEM],
        out_specs=[VMEM, VMEM, VMEM, ANY, ANY, ANY] + [VMEM] * 8,
        scratch_shapes=[
            pltpu.VMEM((4, t, LANES), BF16), pltpu.VMEM((4, t, 256), BF16), pltpu.VMEM((4, t, LANES), BF16),
            pltpu.VMEM((4, t, LANES), BF16), pltpu.VMEM((t, d + LANES), BF16),
            pltpu.VMEM((LANES, t), BF16), pltpu.VMEM((4, 1, t), F32), pltpu.VMEM((4, 1, t), F32),
            DMA((n,)), DMA((n,)), DMA((n,)), DMA((n,)), DMA((n,)), DMA((n,)),
            DMA((g * subs,)), DMA((g * subs,)), DMA((g * subs,)), DMA((g * subs,)),
            DMA((n,)), DMA((n,)), DMA((n,)), DMA((n,)),
            DMA((3,)), DMA((4,)), DMA((3,)), DMA((4,)), DMA((4,)), DMA((4,)),
            DMA((n,)), DMA((n,)), DMA((n // 2,)), DMA((4,)), DMA((4,)), DMA((3,)),
        ],
        compiler_params=pltpu.CompilerParams(
            collective_id=0, has_side_effects=True, vmem_limit_bytes=56 << 20
        ),
        name="attend",
    )(x, aux, cot, p1, small, wout, w2, bias, table)


class QuadSum:
    def __init__(self, f, c, core_out, core_in, x_out, x_in, keep, send, recv):
        self.f, self.c = f, c
        self.core_out, self.core_in, self.x_out, self.x_in = core_out, core_in, x_out, x_in
        self.keep, self.send, self.recv = keep, send, recv

    def core(self, k):
        return copy_to(
            self.core_out.at[k], self.core_in.at[k], self.send.at[k], self.recv.at[k], self.f ^ 1, self.c
        )

    def across(self):
        return copy_to(self.x_out, self.x_in, self.send.at[2], self.recv.at[2], self.f ^ 2, self.c)

    def put(self, k, value):
        if k in (1, 3):
            self.core_out[k // 2] = value.astype(BF16)
            self.core(k // 2).start()
        else:
            self.keep[k // 2] = value

    def cross(self):
        self.core(1).wait_recv()
        self.x_out[...] = (self.keep[1] + self.core_in[1].astype(F32)).astype(BF16)
        self.across().start()

    def total(self):
        self.core(0).wait_recv()
        self.across().wait_recv()
        return self.keep[0] + self.core_in[0].astype(F32) + self.x_in[...].astype(F32)

    def sent(self):
        self.core(0).wait_send()
        self.core(1).wait_send()
        self.across().wait_send()


def quad_sum_scratch(t, d):
    return [
        pltpu.VMEM((2, t, d), BF16), pltpu.VMEM((2, t, d), BF16), pltpu.VMEM((t, d), BF16),
        pltpu.VMEM((t, d), BF16), pltpu.VMEM((2, t, d), F32), DMA((3,)), DMA((3,)),
    ]


def layer_stats(v):
    offsets = v - jnp.mean(v, axis=1, keepdims=True)
    scale = lax.rsqrt(jnp.mean(offsets * offsets, axis=1, keepdims=True) + LN_EPS)
    return offsets * scale, scale


def layer_back(grad, gain, xhat, scale):
    inner = grad * gain
    return scale * (
        inner - jnp.mean(inner, axis=1, keepdims=True) - xhat * jnp.mean(inner * xhat, axis=1, keepdims=True)
    )


def gelu_pair(v):
    k = math.sqrt(2.0 / math.pi)
    square = v * v
    t = jnp.tanh(k * v * (1.0 + 0.044715 * square))
    half = 0.5 * (1.0 + t)
    return v * half, half + 0.5 * v * (1.0 - t * t) * (k * (1.0 + 3 * 0.044715 * square))


class PairSum:
    def __init__(self, f, c, n, source, got, out, send, recv):
        self.f, self.c, self.size = f, c, n // 2
        self.bit = lax.rem(c, 2)
        self.source, self.got, self.out, self.send, self.recv = source, got, out, send, recv

    def copy(self, o):
        return copy_to(
            self.source(2 * o + 1 - self.bit), self.got.at[o], self.send.at[o], self.recv.at[o],
            self.f, self.c + 1 - 2 * self.bit,
        )

    def begin(self):
        lax.fori_loop(0, self.size, lambda o, u: (self.copy(o).start(), u)[1], 0)

    def finish(self):
        def one(o, _):
            self.copy(o).wait_recv()
            term = self.source(2 * o + self.bit)[...].astype(F32)
            self.out[o] = (term + self.got[o].astype(F32)).astype(BF16)
            self.copy(o).wait_send()
            return 0

        lax.fori_loop(0, self.size, one, 0)


class LineSum:
    def __init__(self, f, c, n, source, inbox, stage, line_s, line_r, pair=None, subs=1, lone=False):
        self.f, self.c, self.n, self.size = f, c, n, n // 2
        self.place, self.bit = c // 2, lax.rem(c, 2)
        self.source = source
        self.inbox, self.stage, self.line_s, self.line_r = inbox, stage, line_s, line_r
        self.pair = pair
        self.subs = subs
        self.span = self.size // 4 if lone else self.size
        self.first = f * self.span if lone else 0

    def valid(self, o):
        return jnp.logical_and(o >= self.first, o < self.first + self.span)

    def index(self, o, sub):
        return (o - self.first) * self.subs + sub

    def pair_copy(self, o, sub):
        i = self.index(o, sub)
        got, send, recv = self.pair
        return copy_to(
            self.source(2 * (o - self.first) + 1 - self.bit, sub), got.at[i], send.at[i], recv.at[i],
            self.f, self.c + 1 - 2 * self.bit,
        )

    def line_copy(self, i, slot, c):
        return copy_to(self.stage.at[i], self.inbox.at[slot], self.line_s.at[i], self.line_r.at[slot], self.f, c)

    def each(self, work):
        def one(k, _):
            work(self.first + k // self.subs, lax.rem(k, self.subs))
            return 0

        lax.fori_loop(0, self.span * self.subs, one, 0)

    def begin(self):
        self.each(lambda o, sub: self.pair_copy(o, sub).start())

    def begin_block(self, block):
        @pl.when(lax.rem(block, 2) != self.bit)
        def _():
            self.pair_copy(block // 2, 0).start()

    def term(self, o, sub):
        if self.pair is None:
            return self.source(o - self.first, sub)[...].astype(F32)
        self.pair_copy(o, sub).wait_recv()
        own = self.source(2 * (o - self.first) + self.bit, sub)[...].astype(F32)
        return own + self.pair[0][self.index(o, sub)].astype(F32)

    def extra(self, sub):
        return self.span * self.subs + sub

    def move(self, o, sub, go_right):
        i = self.index(o, sub)
        total = self.term(o, sub)
        starts = self.place == 0 if go_right else self.place == self.size - 1

        @pl.when(starts)
        def _():
            self.stage[i] = total.astype(BF16)

        @pl.when(jnp.logical_not(starts))
        def _():
            self.line_copy(i, i, self.c).wait_recv()
            self.stage[i] = (total + self.inbox[i].astype(F32)).astype(BF16)

        if go_right:
            self.line_copy(i, i, self.c + 2).start()
        else:
            slot = jnp.where(o == self.place - 1, self.extra(sub), i)
            self.line_copy(i, slot, self.c - 2).start()

    def turn(self, time):
        far = self.size - 1 - (time - self.place)
        near = time - (self.size - 1 - self.place)

        def one(sub, _):
            @pl.when(jnp.logical_and(jnp.logical_and(far < self.size, self.valid(far)), far > self.place))
            def _():
                self.move(far, sub, True)

            @pl.when(jnp.logical_and(jnp.logical_and(near >= 0, self.valid(near)), near < self.place))
            def _():
                self.move(near, sub, False)

            return 0

        lax.fori_loop(0, self.subs, one, 0)

    def settle(self, sub):
        i = self.index(self.place, sub)
        own = self.term(self.place, sub)
        left = self.place > 0
        right = self.place < self.size - 1

        @pl.when(left)
        def _():
            self.line_copy(i, i, self.c).wait_recv()

        @pl.when(right)
        def _():
            self.line_copy(i, self.extra(sub), self.c).wait_recv()

        @pl.when(jnp.logical_and(left, right))
        def _():
            self.stage[i] = (
                own + self.inbox[i].astype(F32) + self.inbox[self.extra(sub)].astype(F32)
            ).astype(BF16)

        @pl.when(jnp.logical_and(left, jnp.logical_not(right)))
        def _():
            self.stage[i] = (own + self.inbox[i].astype(F32)).astype(BF16)

        @pl.when(jnp.logical_and(right, jnp.logical_not(left)))
        def _():
            self.stage[i] = (own + self.inbox[self.extra(sub)].astype(F32)).astype(BF16)

    def finish(self):
        @pl.when(self.valid(self.place))
        def _():
            lax.fori_loop(0, self.subs, lambda sub, u: (self.settle(sub), u)[1], 0)

    def sent(self):
        def one(o, sub):
            if self.pair is not None:
                self.pair_copy(o, sub).wait_send()

            @pl.when(o != self.place)
            def _():
                self.line_copy(self.index(o, sub), 0, self.c).wait_send()

        self.each(one)


def feed_kernel(
    n,
    x_ref, cot_ref, gates_ref, o_ref, wout_ref, small_ref, w1_ref, w2_ref, w2e_ref,
    out_ref, dmid_ref, gwout_ref, s1_ref, s2_ref, do_ref, gsel_ref, vec_ref,
    w1g, w2g, n2_ref, act_ref, slope_ref, dpre_ref, mixed_ref, dml_ref, mid_ref, gw1_ref, gw2_ref, got1, in2, stage2,
    a0, a1, a2, a3, a4, a5, a6, b0, b1, b2, b3, b4, b5, b6, e0, e1, e2, e3, e4, e5, e6,
    w1_r, w1_a, w1_b, w1_c, w2_r, w2_a, w2_b, w2_c, h1_s, h1_r, h2_s, h2_r, n_s, n_r, d_s, d_r, loc, da_ref, da_s, da_r,
):
    f, c = lax.axis_index("fsdp"), lax.axis_index("ctx")
    tokens, width = x_ref.shape
    quarter = w1g.shape[1]
    groups = n // 4
    own_turn, own_slot = holder_of(c, groups)
    greet(f, c, 4, n)
    rows1, rows2 = width // n, quarter // n

    def rows_of(ref, count):
        return lambda k: ref.at[pl.ds(pl.multiple_of(k * count, count), count), :]

    early = w2e_ref.shape[1]
    at1 = rows_of(w1g, rows1)
    gather1 = LineGather(f, c, n, lambda sub: w1_ref, lambda k, sub: at1(k), w1_r, w1_a, w1_b, w1_c)
    local1 = pltpu.make_async_copy(w1_ref, at1(c), loc.at[0])
    bring2 = pltpu.make_async_copy(w2e_ref, w2g.at[:, 0:early, :], loc.at[1])
    gather1.begin(local1.start)
    bring2.start()
    gather2 = None
    if early < rows2:
        own2 = w2_ref.at[pl.ds(pl.multiple_of(f * rows2 + early, 16), rows2 - early), :]
        at2 = lambda k: w2g.at[k, early:rows2, :]
        gather2 = LineGather(f, c, n, lambda sub: own2, lambda k, sub: at2(k), w2_r, w2_a, w2_b, w2_c)
        local2 = pltpu.make_async_copy(own2, at2(c), loc.at[2])
    pair1 = PairSum(f, c, n, rows_of(gw1_ref, rows1), got1, s1_ref, h1_s, h1_r)
    line2 = LineSum(f, c, n, lambda o, sub: rows_of(gw2_ref, rows2)(2 * o + sub), in2, stage2, h2_s, h2_r, subs=2)
    attn_sum = QuadSum(f, c, a0, a1, a2, a3, a4, a5, a6)
    back_sum = QuadSum(f, c, b0, b1, b2, b3, b4, b5, b6)
    out_sum = QuadSum(f, c, e0, e1, e2, e3, e4, e5, e6)

    for k in (3, 2, 1, 0):
        r = f ^ k
        for e in range(5):
            mixed_ref[r, :, e * LANES : (e + 1) * LANES] = (
                gates_ref[r, :, e : e + 1] * o_ref[r].astype(F32)
            ).astype(BF16)
        attn_sum.put(k, mm(mixed_ref[r], wout_ref[...]))
        if k == 2:
            attn_sum.cross()
    gather1.step(1)
    middle = x_ref[...].astype(F32) + attn_sum.total()
    mid_ref[...] = middle
    xhat, scale = layer_stats(middle)
    gain = spread_vector(small_ref[:, 2, :], width // n)
    shift = spread_vector(small_ref[:, 3, :], width // n)
    n2_ref[f] = (xhat * gain + shift).astype(BF16)
    n2_gather = QuadGather(f, c, n2_ref, n_s, n_r)
    n2_gather.begin()
    gather1.steps(2)
    if gather2 is not None:
        gather2.begin(local2.start)
    gather1.finish()
    local1.wait()
    first_bias = spread_vector(small_ref[:, pl.ds(5 + f, 1), :].reshape(n, LANES), rows2)

    def enter(k):
        r = f ^ k
        act, slope = gelu_pair(mm(n2_ref[r], w1g[...]) + first_bias)
        act_ref[r] = act.astype(BF16)
        slope_ref[r] = slope

    enter(0)
    n2_gather.got(f ^ 1)
    if gather2 is not None:
        gather2.step(1)
    enter(1)
    n2_gather.relay()
    if gather2 is not None:
        gather2.step(2)
    enter(2)
    if gather2 is not None:
        gather2.steps(3)
    n2_gather.got(f ^ 3)
    enter(3)
    if gather2 is not None:
        gather2.finish()
        local2.wait()
    bring2.wait()
    second = w2g[...].reshape(quarter, width)

    for k in (3, 2, 1, 0):
        r = f ^ k
        d_act = mm_t(cot_ref[r], second)
        dpre_ref[r] = (d_act * slope_ref[r]).astype(BF16)
        back_sum.put(k, mm_t(dpre_ref[r], w1g[...]))
        if k == 2:
            back_sum.cross()
    for k in (3, 2, 1, 0):
        out_sum.put(k, mm(act_ref[f ^ k], second))
    tile = 256
    all_tokens = 4 * tokens

    def weight_tile(left_ref, right_ref, result_ref):
        def one(i, _):
            spot = pl.multiple_of(i * tile, tile)
            left = left_ref[:, :, pl.ds(spot, tile)].reshape(all_tokens, tile)
            right = right_ref[...].reshape(all_tokens, right_ref.shape[2])
            result_ref[pl.ds(spot, tile), :] = mm_left_t(left, right).astype(BF16)
            return 0

        lax.fori_loop(0, left_ref.shape[2] // tile, one, 0)

    weight_tile(act_ref, cot_ref, gw2_ref)
    line2.turn(0)
    weight_tile(n2_ref, dpre_ref, gw1_ref)
    pair1.begin()
    d_norm = back_sum.total()
    xhat, scale = layer_stats(mid_ref[...])
    d_middle = cot_ref[f].astype(F32) + layer_back(d_norm, gain, xhat, scale)
    dmid_ref[...] = d_middle
    dml_ref[f] = d_middle.astype(BF16)
    dml_gather = QuadGather(f, c, dml_ref, d_s, d_r)
    dml_gather.begin()
    out_sum.cross()
    vec_ref[...] = jnp.zeros_like(vec_ref)
    vec_ref[0:1, :] = jnp.sum(d_norm * xhat, axis=0, keepdims=True)
    vec_ref[1:2, :] = jnp.sum(d_norm, axis=0, keepdims=True)
    vec_ref[2:3, :] = jnp.sum(cot_ref[f].astype(F32), axis=0, keepdims=True)
    total = jnp.zeros((1, quarter), F32)
    for r in range(4):
        total = total + jnp.sum(dpre_ref[r].astype(F32), axis=0, keepdims=True)
    vec_ref[3:4, :] = total
    lane = lax.broadcasted_iota(jnp.int32, (tokens, LANES), 1)

    def leave(k):
        r = f ^ k
        d_attn = jnp.zeros((tokens, LANES), F32)
        select = jnp.zeros((tokens, LANES), F32)
        result = o_ref[r].astype(F32)
        d_mixed = mm_t(dml_ref[r], wout_ref[...])
        for e in range(5):
            part = d_mixed[:, e * LANES : (e + 1) * LANES]
            d_attn = d_attn + gates_ref[r, :, e : e + 1] * part
            column = jnp.sum(result * part, axis=1, keepdims=True) * gates_ref[r, :, 8 + e : 9 + e]
            select = jnp.where(lane == e, column, select)
        da_ref[r] = d_attn.astype(BF16)
        gsel_ref[r] = select
        to = r * groups + own_turn

        @pl.when(to != c)
        def _():
            copy_to(da_ref.at[r], do_ref.at[own_slot], da_s.at[r], da_r.at[own_slot], f, to).start()

        @pl.when(to == c)
        def _():
            do_ref[own_slot] = da_ref[r]

    line2.turn(1)
    leave(0)
    dml_gather.got(f ^ 1)
    leave(1)
    dml_gather.relay()
    line2.turn(2)
    leave(2)
    dml_gather.got(f ^ 3)
    leave(3)

    def out_tile(i, _):
        spot = pl.multiple_of(i * LANES, LANES)
        left = mixed_ref[:, :, pl.ds(spot, LANES)].reshape(all_tokens, LANES)
        right = dml_ref[...].reshape(all_tokens, width)
        gwout_ref[pl.ds(spot, LANES), :] = mm_left_t(left, right).astype(BF16)
        return 0

    lax.fori_loop(0, 5, out_tile, 0)
    second_bias = spread_vector(small_ref[:, 4, :], width // n)
    out_ref[...] = (mid_ref[...] + out_sum.total() + second_bias).astype(BF16)
    lax.fori_loop(3, n // 2 - 1, lambda k, u: (line2.turn(k), u)[1], 0)
    line2.finish()
    own = 2 * (c // 2) + lax.rem(c, 2)
    s2_ref[0] = stage2[own]
    s2_ref[1] = stage2[own + 1 - 2 * lax.rem(c, 2)]
    line2.sent()
    pair1.finish()
    for one in (attn_sum, back_sum, out_sum, n2_gather, dml_gather):
        one.sent()

    def drain(i, _):
        @pl.when(i * groups + own_turn != c)
        def _():
            copy_to(da_ref.at[i], do_ref.at[0], da_s.at[i], da_r.at[0], f, c).wait_send()

        @pl.when(block_of(lax.rem(c, groups), i, groups) != c)
        def _():
            copy_to(da_ref.at[0], do_ref.at[i], da_s.at[0], da_r.at[i], f, c).wait_recv()

        return 0

    lax.fori_loop(0, 4, drain, 0)


def feed(n, x, cot, gates, o, wout, small, w1, w2, w2e):
    t, d = x.shape
    quarter = w1.shape[1]
    line = n // 2
    return pl.pallas_call(
        functools.partial(feed_kernel, n),
        out_shape=[
            sds((t, d), BF16), sds((t, d), F32), sds((640, d), BF16), sds((line, d // n, quarter), BF16),
            sds((2, quarter // n, d), BF16), sds((4, t, LANES), BF16), sds((4, t, LANES), F32), sds((8, d), F32),
        ],
        in_specs=[VMEM] * 6 + [ANY] * 3,
        out_specs=[VMEM] * 8,
        scratch_shapes=[
            pltpu.VMEM((d, quarter), BF16), pltpu.VMEM((n, quarter // n, d), BF16), pltpu.VMEM((4, t, d), BF16),
            pltpu.VMEM((4, t, quarter), BF16), pltpu.VMEM((4, t, quarter), F32), pltpu.VMEM((4, t, quarter), BF16),
            pltpu.VMEM((4, t, 640), BF16), pltpu.VMEM((4, t, d), BF16), pltpu.VMEM((t, d), F32),
            pltpu.VMEM((d, quarter), BF16), pltpu.VMEM((quarter, d), BF16),
            pltpu.VMEM((line, d // n, quarter), BF16),
        ]
        + line_scratch(line, 2, 2 * quarter // n, d)
        + quad_sum_scratch(t, d) * 3
        + [DMA((n,))] * 8 + [DMA((line,))] * 2 + line_sems(line, 2)
        + [DMA((3,)), DMA((4,)), DMA((3,)), DMA((4,)), DMA((3,)), pltpu.VMEM((4, t, LANES), BF16), DMA((4,)), DMA((4,))],
        compiler_params=pltpu.CompilerParams(
            collective_id=1, has_side_effects=True, vmem_limit_bytes=62 << 20
        ),
        name="feed",
    )(x, cot, gates, o, wout, small, w1, w2, w2e)


class LoneShare:
    def __init__(self, total, out, send, recv):
        self.f, self.c = total.f, total.c
        self.owner = total.place // (total.size // 4)
        self.rel = total.f ^ self.owner
        start = jnp.where(self.rel == 0, (total.place - total.first) * total.subs, 0)
        self.held = total.stage.at[pl.ds(start, total.subs)]
        self.out, self.send, self.recv = out, send, recv
        self.local = pltpu.make_async_copy(self.held, out, recv)

    def copy(self, src, k, to):
        return copy_to(src, self.out, self.send.at[k], self.recv, to, self.c)

    def begin(self):
        @pl.when(self.rel == 0)
        def _():
            self.copy(self.held, 1, self.f ^ 2).start()
            self.copy(self.held, 0, self.f ^ 1).start()
            self.local.start()

    def relay(self):
        @pl.when(self.rel == 2)
        def _():
            self.copy(self.out, 0, self.f).wait_recv()
            self.copy(self.out, 0, self.f ^ 1).start()

    def finish(self):
        @pl.when(self.rel == 0)
        def _():
            self.local.wait()
            self.copy(self.held, 0, self.f).wait_send()
            self.copy(self.held, 1, self.f).wait_send()

        @pl.when(self.rel == 2)
        def _():
            self.copy(self.out, 0, self.f).wait_send()

        @pl.when(lax.rem(self.rel, 2) == 1)
        def _():
            self.copy(self.out, 0, self.f).wait_recv()


def back_kernel(
    n, far_kv,
    do_ref, gwout_ref, s1_ref, s2_ref, qcat_ref, qpos_ref, kv_ref, lse_ref, of_ref,
    tok_ref, p1_ref, ev_ref, gates_ref, gsel_ref, x_ref, small_ref, dmid_ref, vec_ref, table_ref,
    din_ref, gp_ref, gq_ref, g1_ref, g2_ref, go_ref, vq_ref, dkv_ref,
    delta_ref, grad_ref, kcat_ref, acc_ref, ring_ref, pin_ref, drel_ref, dqs_ref, dq_ref, part_ref, dp_ref,
    gpa_ref, gpb_ref, mine_ref, vin_ref,
    s0, s1, s2, s3, s4, s5, s6,
    p0, p1, p2, p3, p4, p5, p6, u1, u2, u5, u6,
    fin2, got2, two_s, two_r, w0, w1, w2, w3, w4, w5, w6, y1, y2, y5, y6, goty, swap_s, swap_r,
    kv_s, kv_r, pin_r, dq_s, dq_r, gp_s, gp_r, gq_s, gq_r, g1_s, g1_r, g2_s, g2_r, go_s, go_r,
    vc_s, vc_r, vf_s, vf_r, loc,
):
    f, c = lax.axis_index("fsdp"), lax.axis_index("ctx")
    groups = n // 4
    seq, turn = c // groups, lax.rem(c, groups)
    tokens, width = x_ref.shape
    scale = 1.0 / math.sqrt(112)
    own_turn, own_slot = holder_of(c, groups)
    rows = width // n
    greet(f, c, 4, n)

    sub_out = p0.shape[0] // max(1, groups // 2)
    cut = gwout_ref.shape[1] // sub_out
    sum_out = LineSum(
        f, c, n, lambda k, sub: gwout_ref.at[k, pl.ds(pl.multiple_of(sub * cut, cut), cut), :],
        p1, p2, p5, p6, pair=(p0, p3, p4), subs=sub_out, lone=True,
    )
    sum_one = LineSum(f, c, n, lambda o, sub: s1_ref.at[o], u1, u2, u5, u6)
    half = gpa_ref.shape[1]
    pair_to = c + 1 - 2 * lax.rem(c, 2)

    def block_rows(ref, k):
        return ref.at[pl.ds(pl.multiple_of(k * rows, rows), rows), :]

    sum_in = LineSum(
        f, c, n, lambda k, sub: block_rows(gpa_ref, k), w1, w2, w5, w6, pair=(w0, w3, w4)
    )
    sum_late = LineSum(f, c, n, lambda o, sub: block_rows(gpb_ref, 2 * o + sub), y1, y2, y5, y6, subs=2)
    swap_two = copy_to(s2_ref.at[1], got2, two_s, two_r, f, pair_to)
    swap_late = copy_to(y2.at[pair_to], goty, swap_s, swap_r, f, pair_to)

    sum_out.begin()
    swap_two.start()

    def prepare(i, _):
        delta_ref[i] = jnp.sum(do_ref[i].astype(F32).T * of_ref[i], axis=0, keepdims=True)
        grad_ref[i] = jnp.zeros((tokens, width + LANES), F32)
        return 0

    lax.fori_loop(0, 4, prepare, 0)
    row_in = lax.broadcasted_iota(jnp.int32, (tokens, tokens), 0)
    col_in = lax.broadcasted_iota(jnp.int32, (tokens, tokens), 1)
    lane = lax.broadcasted_iota(jnp.int32, (tokens, LANES), 1)
    spots = jnp.logical_or(lane == SPOT_A, lane == SPOT_B)
    last_own = block_of(turn, 3, groups)
    mine_ref[...] = vec_ref[...]

    def close_query(i, sine, cosine):
        first = grad_ref[i, :, 0 : width // 2]
        second = grad_ref[i, :, width // 2 : width]
        drel_ref[i, :, 0 : width // 2] = ((first * sine - second * cosine) * scale).astype(BF16)
        drel_ref[i, :, width // 2 : width] = ((first * cosine + second * sine) * scale).astype(BF16)
        d_place = mm(drel_ref[i], p1_ref[:, :, 896:].reshape(width, LANES))
        d_content = jnp.where(spots, 0.0, grad_ref[i, :, width:] * scale)
        dqs_ref[i] = (d_content + d_place).astype(BF16)
        mine_ref[6:7, 0:LANES] += jnp.sum(d_content, axis=0, keepdims=True)
        mine_ref[7:8, 0:LANES] += jnp.sum(d_place, axis=0, keepdims=True)
        block = block_of(turn, i, groups)

        @pl.when(block != c)
        def _():
            copy_to(dqs_ref.at[i], dq_ref.at[seq], dq_s.at[i], dq_r.at[seq], f, block).start()

        @pl.when(block == c)
        def _():
            dq_ref[seq] = dqs_ref[i]

    bit = lax.rem(c, 2)
    pair_last = block_of(turn + 1 - 2 * bit, 3, groups)

    def ring_pair(kb):
        slot = lax.rem(kb, 4)
        return copy_to(ring_ref.at[slot], pin_ref.at[kb // 2], kv_s.at[slot], pin_r.at[kb // 2], f, pair_to)

    def ring_copy(kb):
        slot = lax.rem(kb, 4)
        return copy_to(ring_ref.at[slot], dkv_ref.at[c // 2], kv_s.at[slot], kv_r.at[c // 2], f, kb)

    def ring_local(kb):
        slot = lax.rem(kb, 4)
        return pltpu.make_async_copy(ring_ref.at[slot], dkv_ref.at[c // 2], kv_s.at[slot])

    def sums(kb):
        return jnp.logical_and(lax.rem(kb, 2) == bit, kb <= jnp.maximum(last_own, pair_last))

    def gives(kb):
        return jnp.logical_and(lax.rem(kb, 2) != bit, kb <= last_own)

    def ring_free(kb):
        @pl.when(gives(kb))
        def _():
            ring_pair(kb).wait_send()

        @pl.when(jnp.logical_and(sums(kb), kb != c))
        def _():
            ring_copy(kb).wait_send()

        @pl.when(jnp.logical_and(sums(kb), kb == c))
        def _():
            ring_local(kb).wait()

    def pass_on(kb):
        @pl.when(sums(kb))
        def _():
            total = acc_ref[lax.rem(kb, 2)]
            slot = lax.rem(kb, 4)

            @pl.when(kb <= pair_last)
            def _():
                ring_pair(kb).wait_recv()
                ring_ref[slot] = (total + pin_ref[kb // 2].astype(F32)).astype(BF16)

            @pl.when(kb > pair_last)
            def _():
                ring_ref[slot] = total.astype(BF16)

            @pl.when(kb != c)
            def _():
                ring_copy(kb).start()

            @pl.when(kb == c)
            def _():
                ring_local(kb).start()

    def key_block(kb, _):
        own = [block_of(turn, i, groups) for i in range(4)]
        first = sum((b < kb).astype(jnp.int32) for b in own)
        ready = sum((b == kb).astype(jnp.int32) for b in own)
        sine, cosine = sin_cos(key_places(kv_ref[kb]), table_ref)
        kcat_ref[:, 0 : width // 2] = cosine.astype(BF16)
        kcat_ref[:, width // 2 : width] = sine.astype(BF16)
        kcat_ref[:, width:] = kv_ref[kb, :, 0:128]
        now = lax.rem(kb, 2)
        acc_ref[now] = jnp.zeros((tokens, 256), F32)

        def query_block(i, _):
            gap = (block_of(turn, i, groups) - kb) * tokens
            scores = mm_t(kcat_ref[...], qcat_ref[i])
            probs = jnp.where(row_in <= col_in + gap, jnp.exp(scores - lse_ref[i]), 0.0)
            d_probs = mm_t(kv_ref[kb, :, 128:256], do_ref[i])
            d_scores = (probs * (d_probs - delta_ref[i])).astype(BF16)
            acc_ref[now, :, 0:128] += mm(d_scores, qcat_ref[i, :, width:])
            acc_ref[now, :, 128:256] += mm(probs.astype(BF16), do_ref[i])
            grad_ref[i] += mm_left_t(d_scores, kcat_ref[...])
            return 0

        lax.fori_loop(first, 4, query_block, 0)

        @pl.when(ready == 1)
        def _():
            close_query(first, sine, cosine)

        @pl.when(kb >= 4)
        def _():
            ring_free(kb - 4)

        @pl.when(gives(kb))
        def _():
            ring_ref[lax.rem(kb, 4)] = acc_ref[now].astype(BF16)
            ring_pair(kb).start()

        @pl.when(kb >= 1)
        def _():
            pass_on(kb - 1)

        @pl.when(jnp.logical_and(now == 0, kb >= 2))
        def _():
            sum_one.turn(kb // 2 - 1)


        return 0

    lax.fori_loop(0, n, key_block, 0)
    pass_on(n - 1)
    sum_out.turn(0)
    share_out = LoneShare(sum_out, go_ref, go_s, go_r)
    gathers = []
    def hand_out(held, out, send, recv):
        local = pltpu.make_async_copy(held, out.at[f], loc.at[len(gathers)])
        local.start()
        gather = QuadGather(f, c, out, send, recv)
        gather.begin(held)
        gathers.append((gather, local))

    all_tokens = 4 * tokens
    d_rel = drel_ref[...].reshape(all_tokens, width)
    gpb_ref[:, 896 - half :] = mm_left_t(d_rel, qpos_ref[...].reshape(all_tokens, LANES)).astype(BF16)

    def collect(s, _):
        to = s * groups + own_turn

        @pl.when(to != c)
        def _():
            copy_to(dqs_ref.at[0], dq_ref.at[s], dq_s.at[0], dq_r.at[s], f, c).wait_recv()

        acc_ref[0] = jnp.zeros((tokens, 256), F32)

        def add(k, _):
            giver = 2 * k + bit
            at = (s * groups + giver) // 2
            last = jnp.maximum(block_of(giver, 3, groups), block_of(giver + 1 - 2 * bit, 3, groups))

            @pl.when(last >= c)
            def _():
                @pl.when(s * groups + giver != c)
                def _():
                    copy_to(ring_ref.at[0], dkv_ref.at[at], kv_s.at[0], kv_r.at[at], f, c).wait_recv()

                if far_kv:
                    bring = pltpu.make_async_copy(dkv_ref.at[at], part_ref, loc.at[4])
                    bring.start()
                    bring.wait()
                    acc_ref[0] += part_ref[...].astype(F32)
                else:
                    acc_ref[0] += dkv_ref[at].astype(F32)

            return 0

        lax.fori_loop(0, groups // 2, add, 0)
        dp_ref[s, :, 0:128] = dq_ref[s]
        dp_ref[s, :, 128:256] = acc_ref[0, :, 0:128].astype(BF16)
        d_values = acc_ref[0, :, 128:256]
        for e in range(5):
            values = ev_ref[s, :, e * LANES : (e + 1) * LANES].astype(F32)
            column = jnp.sum(values * d_values, axis=1, keepdims=True) * gates_ref[s, :, 24 + e : 25 + e]
            part = gates_ref[s, :, 16 + e : 17 + e] * d_values
            part = jnp.where(lane == SPOT_A, column, part)
            part = jnp.where(lane == SPOT_B, gsel_ref[s, :, e : e + 1], part)
            dp_ref[s, :, 256 + e * LANES : 384 + e * LANES] = part.astype(BF16)
        return 0

    def ring_drain(k, _):
        ring_free(n - 4 + k)
        return 0

    lax.fori_loop(0, 4, ring_drain, 0)
    lax.fori_loop(0, 4, collect, 0)
    sum_out.turn(1)
    tile = 256

    def weight_tile(i, _):
        spot = pl.multiple_of(i * tile, tile)
        left = tok_ref[:, :, pl.ds(spot, tile)].reshape(all_tokens, tile)
        right = dp_ref[...].reshape(all_tokens, 896)
        result = mm_left_t(left, right).astype(BF16)
        gpa_ref[pl.ds(spot, tile), :] = result[:, 0:half]
        gpb_ref[pl.ds(spot, tile), 0 : 896 - half] = result[:, half:]
        return 0

    lax.fori_loop(0, width // tile, weight_tile, 0)
    sum_in.begin()
    sum_late.turn(0)
    lax.fori_loop(2, n // 2 - 1, lambda k, u: (sum_out.turn(k), u)[1], 0)
    in_sum = QuadSum(f, c, s0, s1, s2, s3, s4, s5, s6)
    for k in (3, 2, 1, 0):
        weights = p1_ref[:, :, 0:896].reshape(width, 896)
        in_sum.put(k, mm_t(dp_ref[f ^ k], weights))
        if k == 2:
            in_sum.cross()
    swap_two.wait()
    fin2[...] = (s2_ref[0].astype(F32) + got2[...].astype(F32)).astype(BF16)
    sum_one.finish()
    sum_late.turn(1)
    sum_out.finish()
    hand_out(fin2, g2_ref, g2_s, g2_r)
    hand_out(u2.at[c // 2], g1_ref, g1_s, g1_r)
    share_out.begin()
    lax.fori_loop(2, n // 2 - 1, lambda k, u: (sum_late.turn(k), u)[1], 0)
    sum_in.turn(0)
    sum_late.finish()
    swap_late.start()
    lax.fori_loop(1, n // 2 - 1, lambda k, u: (sum_in.turn(k), u)[1], 0)
    for gather, _ in gathers:
        gather.relay()
    share_out.relay()
    d_norm = in_sum.total()
    xhat, spread = layer_stats(x_ref[...].astype(F32))
    gain = spread_vector(small_ref[:, 0, :], width // n)
    din_ref[...] = dmid_ref[...] + layer_back(d_norm, gain, xhat, spread)
    mine_ref[4:5, :] = jnp.sum(d_norm * xhat, axis=0, keepdims=True)
    mine_ref[5:6, :] = jnp.sum(d_norm, axis=0, keepdims=True)

    def vec_send(k, _):
        to = lax.rem(c + k, n)
        copy_to(mine_ref, vin_ref.at[c], vc_s.at[to], vc_r.at[c], f, to).start()
        return 0

    lax.fori_loop(1, n, vec_send, 0)
    vin_ref[c] = mine_ref[...]
    swap_late.wait()
    y2[c] = (y2[c].astype(F32) + goty[...].astype(F32)).astype(BF16)
    hand_out(y2.at[c], gq_ref, gq_s, gq_r)
    sum_in.finish()
    hand_out(w2.at[c // 2], gp_ref, gp_s, gp_r)

    def vec_wait(k, _):
        to = lax.rem(c + k, n)
        copy_to(mine_ref, vin_ref.at[to], vc_s.at[to], vc_r.at[to], f, to).wait()
        return 0

    lax.fori_loop(1, n, vec_wait, 0)
    vq_ref[f] = jnp.sum(vin_ref[...], axis=0)
    for k in range(1, 4):
        copy_to(vq_ref.at[f], vq_ref.at[f], vf_s.at[k], vf_r.at[f], f ^ k, c).start()
    for gather, _ in gathers[2:]:
        gather.relay()
    for k in range(1, 4):
        copy_to(vq_ref.at[f ^ k], vq_ref.at[f ^ k], vf_s.at[k], vf_r.at[f ^ k], f, c).wait_recv()
        copy_to(vq_ref.at[f], vq_ref.at[f], vf_s.at[k], vf_r.at[f], f, c).wait_send()
    for one, local in gathers:
        one.got(f ^ 1)
        one.got(f ^ 3)
        one.sent()
        local.wait()
    share_out.finish()
    for one in (sum_one, sum_out, sum_in, sum_late):
        one.sent()
    in_sum.sent()

    def drain(i, _):
        @pl.when(block_of(turn, i, groups) != c)
        def _():
            copy_to(dqs_ref.at[i], dq_ref.at[0], dq_s.at[i], dq_r.at[0], f, c).wait_send()

        return 0

    lax.fori_loop(0, 4, drain, 0)


def early_rows(count):
    return count // 2 if count % 32 == 0 else count


def cuts(count):
    parts = max(1, count // 64)
    return parts if count % (16 * parts) == 0 else 1


def pair_scratch(blocks, subs, rows, cols):
    return [pltpu.VMEM((blocks * subs, rows // subs, cols), BF16)]


def line_scratch(blocks, subs, rows, cols):
    return [
        pltpu.VMEM(((blocks + 1) * subs, rows // subs, cols), BF16),
        pltpu.VMEM((blocks * subs, rows // subs, cols), BF16),
    ]


def line_sems(blocks, subs):
    return [DMA((blocks * subs,)), DMA(((blocks + 1) * subs,))]


def back(n, da, gwout, s1, s2, qcat, qpos, kv, lse, of, tok, p1, ev, gates, gsel, x, small, dmid, vec, table):
    t, d = x.shape
    g = n // 4
    quarter = s1.shape[2]
    rows, out_rows, two_rows = d // n, gwout.shape[1], s2.shape[1]
    half = d // 2
    sub_out = cuts(out_rows)
    lone, line = n // 8, n // 2
    far_kv = g > 4
    return pl.pallas_call(
        functools.partial(back_kernel, n, far_kv),
        out_shape=[
            sds((t, d), F32), sds((4, rows, half), BF16), sds((4, rows, half), BF16), sds((4, rows, quarter), BF16),
            sds((4, two_rows, d), BF16), sds((sub_out, out_rows // sub_out, d), BF16),
            sds((4, 8, d), F32), sds((line, t, 256), BF16),
        ],
        in_specs=[VMEM] * 19,
        out_specs=[VMEM, ANY, ANY, ANY, ANY, ANY, VMEM, ANY if far_kv else VMEM],
        scratch_shapes=[
            pltpu.VMEM((4, 1, t), F32), pltpu.VMEM((4, t, d + LANES), F32),
            pltpu.VMEM((t, d + LANES), BF16), pltpu.VMEM((2, t, 256), F32), pltpu.VMEM((4, t, 256), BF16),
            pltpu.VMEM((line, t, 256), BF16),
            pltpu.VMEM((4, t, d), BF16), pltpu.VMEM((4, t, LANES), BF16), pltpu.VMEM((4, t, LANES), BF16),
            pltpu.VMEM((t, 256), BF16), pltpu.VMEM((4, t, 896), BF16), pltpu.VMEM((d, half), BF16), pltpu.VMEM((d, half), BF16),
            pltpu.VMEM((8, d), F32), pltpu.VMEM((n, 8, d), F32),
        ]
        + quad_sum_scratch(t, d)
        + pair_scratch(lone, sub_out, out_rows, d) + line_scratch(lone, sub_out, out_rows, d)
        + [DMA((lone * sub_out,))] * 2 + line_sems(lone, sub_out)
        + line_scratch(line, 1, rows, quarter) + line_sems(line, 1)
        + [pltpu.VMEM((two_rows, d), BF16), pltpu.VMEM((two_rows, d), BF16), DMA, DMA]
        + pair_scratch(line, 1, rows, half) + line_scratch(line, 1, rows, half)
        + [DMA((line,))] * 2 + line_sems(line, 1)
        + line_scratch(line, 2, 2 * rows, half) + line_sems(line, 2)
        + [pltpu.VMEM((rows, half), BF16), DMA, DMA]
        + [
            DMA((4,)), DMA((line,)), DMA((line,)), DMA((4,)), DMA((4,)), DMA((3,)), DMA((4,)),
            DMA((3,)), DMA((4,)), DMA((3,)), DMA((4,)), DMA((3,)), DMA((4,)), DMA((2,)), DMA, DMA((n,)), DMA((n,)), DMA((4,)), DMA((4,)), DMA((5,)),
        ],
        compiler_params=pltpu.CompilerParams(
            collective_id=2, has_side_effects=True, vmem_limit_bytes=63 << 20
        ),
        name="back",
    )(da, gwout, s1, s2, qcat, qpos, kv, lse, of, tok, p1, ev, gates, gsel, x, small, dmid, vec, table)


def pad_channels(v, group):
    lead = v.shape[:-1]
    v = v.reshape(lead + (112 // group, group))
    v = jnp.pad(v, [(0, 0)] * len(lead) + [(0, 0), (0, group // 7)])
    return v.reshape(lead + (LANES,))


def head_pick(w, f, heads=4):
    w = w.reshape(w.shape[0], heads, -1)
    return lax.dynamic_index_in_dim(w, f, 1, keepdims=False)


def route_lanes(routes):
    hot = routes[..., None] == jnp.arange(8, dtype=jnp.int32)
    return jnp.sum(hot.astype(F32), axis=-2)


def pack_inputs(
    n, f, positions, value_routes, output_routes, ln1_gain, ln1_bias, wq, wk, wrel, u_bias, v_bias,
    wvsel, wv, wosel, wout, ln2_gain, ln2_bias, b1, b2,
):
    t = positions.shape[0]
    rows = wq.shape[0]
    group = math.gcd(112, wout.shape[0])
    masks = jnp.concatenate([route_lanes(value_routes), route_lanes(output_routes)], axis=-1).reshape(t, 64)
    place = jnp.stack([positions // 128, positions % 128], axis=-1).astype(F32)
    aux = jnp.concatenate([masks, place, jnp.zeros((t, 62), F32)], axis=-1).astype(BF16)
    lane = jnp.arange(LANES)
    experts = pad_channels(head_pick(wv, f).reshape(rows, 5, 112), group)
    experts = jnp.where(lane == SPOT_A, head_pick(wvsel, f)[..., None], experts)
    experts = jnp.where(lane == SPOT_B, head_pick(wosel, f)[..., None], experts)
    p1 = jnp.concatenate(
        [
            pad_channels(head_pick(wq, f), group), pad_channels(head_pick(wk, f), group),
            experts.reshape(rows, 640), pad_channels(head_pick(wrel, f), group),
        ],
        axis=-1,
    )
    piece = b1.shape[0] // 4
    vectors = [ln1_gain, ln1_bias, ln2_gain, ln2_bias, b2]
    vectors = [jnp.pad(v, (0, LANES - v.shape[0])) for v in vectors]
    extra = jnp.pad(b1.reshape(-1, piece), ((0, 0), (0, LANES - piece)))
    small = jnp.concatenate([jnp.stack(vectors), extra]).astype(F32)
    small = jnp.pad(small, ((0, 16 - small.shape[0]), (0, 0)))
    pieces = wout.reshape(-1, group, wout.shape[1])
    pieces = jnp.pad(pieces, ((0, 0), (0, group // 7), (0, 0))).reshape(-1, wout.shape[1])
    pieces = jnp.pad(pieces, ((0, -pieces.shape[0] % 16), (0, 0)))
    bias = jnp.concatenate([pad_channels(u_bias, group), pad_channels(v_bias, group)]).astype(F32)
    return aux, p1, small, pieces, bias


def unpack_kernel(
    gp_ref, gq_ref, g1_ref, g2_ref, go_ref, vq_ref, y_ref, din_ref,
    query_ref, key_ref, rel_ref, value_ref, vsel_ref, osel_ref, one_ref, two_ref, out_ref,
    gain1_ref, shift1_ref, gain2_ref, shift2_ref, b2_ref, b1_ref, u_ref, v_ref, y_out, din_out,
    heads_ref,
):
    c = lax.axis_index("ctx")
    rows, half = gp_ref.shape[1], gp_ref.shape[2]
    y_out[...] = y_ref[...]
    din_out[...] = din_ref[...]

    def block(h, k):
        ref, spot = (gp_ref, k * LANES) if k * LANES < half else (gq_ref, k * LANES - half)
        return ref[h, :, spot : spot + LANES].astype(F32).T

    def place(ref, start, piece):
        ref[start : start + 56, :] = piece[0:56]
        ref[start + 56 : start + 112, :] = piece[64:120]

    for h in range(4):
        for ref, k in ((query_ref, 0), (key_ref, 1), (rel_ref, 7)):
            place(ref, 112 * h, block(h, k))
        for e in range(5):
            piece = block(h, 2 + e)
            place(value_ref, 560 * h + 112 * e, piece)
            vsel_ref[5 * h + e : 5 * h + e + 1, :] = piece[SPOT_A : SPOT_A + 1]
            osel_ref[5 * h + e : 5 * h + e + 1, :] = piece[SPOT_B : SPOT_B + 1]
    part = g2_ref.shape[1]
    for h in range(4):
        two_ref[h * part : (h + 1) * part, :] = g2_ref[h].astype(F32)
        for k in range(g1_ref.shape[2] // part):
            spot = (4 * k + h) * part
            one_ref[:, spot : spot + part] = g1_ref[h, :, k * part : (k + 1) * part].astype(F32)
    for k in range(go_ref.shape[0]):
        out_ref[56 * k : 56 * k + 56, :] = go_ref[k, 0:56, :].astype(F32)
    own = pl.ds(pl.multiple_of(c * rows, rows), rows)
    for ref, k in ((gain2_ref, 0), (shift2_ref, 1), (b2_ref, 2), (gain1_ref, 4), (shift1_ref, 5)):
        ref[...] = sum(vq_ref[h, k : k + 1, own] for h in range(4))
    for h in range(4):
        b1_ref[:, h * part : (h + 1) * part] = vq_ref[h, 3:4, own]
    lane = lax.broadcasted_iota(jnp.int32, (8, LANES), 1)
    for ref, k in ((u_ref, 6), (v_ref, 7)):
        for h in range(4):
            heads_ref[h : h + 1, :] = vq_ref[h, k : k + 1, 0:LANES]
        value = heads_ref[...]
        moved = jnp.where(lane < 56, value, pltpu.roll(value, LANES - 8, 1))
        ref[...] = moved[0:4, 0:112]


def unpack(gp, gq, g1, g2, go, vq, y, d_in):
    rows, part, d = gp.shape[1], g2.shape[1], g2.shape[2]
    shapes = [
        (448, rows), (448, rows), (448, rows), (2240, rows), (20, rows), (20, rows), (rows, 4 * g1.shape[2]),
        (4 * part, d), (go.shape[0] * 56, d), (1, rows), (1, rows), (1, rows), (1, rows), (1, rows),
        (1, 4 * part), (4, 112), (4, 112),
    ]
    return pl.pallas_call(
        unpack_kernel,
        out_shape=[sds(shape, F32) for shape in shapes] + [sds(y.shape, BF16), sds(d_in.shape, F32)],
        in_specs=[VMEM] * 8,
        out_specs=[VMEM] * (len(shapes) + 2),
        scratch_shapes=[pltpu.VMEM((8, LANES), F32)],
        compiler_params=pltpu.CompilerParams(vmem_limit_bytes=62 << 20),
        name="unpack",
    )(gp, gq, g1, g2, go, vq, y, d_in)


def drop_pads(v, group):
    lead = v.shape[:-1]
    wide = group * 8 // 7
    return v.reshape(lead + (LANES // wide, wide))[..., :group].reshape(lead + (112,))


def on_device(n, *args):
    (
        x, positions, value_routes, output_routes, ln1_gain, ln1_bias, wq, wk, wrel, u_bias, v_bias,
        wvsel, wv, wosel, wout, ln2_gain, ln2_bias, w1, b1, w2, b2, cot,
    ) = args
    f, c = lax.axis_index("fsdp"), lax.axis_index("ctx")
    d = x.shape[1]
    g = n // 4
    group = math.gcd(112, wout.shape[0])
    aux, p1, small, pieces, bias = pack_inputs(
        n, f, positions, value_routes, output_routes, ln1_gain, ln1_bias, wq, wk, wrel, u_bias, v_bias,
        wvsel, wv, wosel, wout, ln2_gain, ln2_bias, b1, b2,
    )
    table = jnp.asarray(turn_table(d))
    rows, hidden = w1.shape
    part = hidden // n // 4
    w1_own = lax.dynamic_index_in_dim(w1.reshape(rows, n, 4, part), f, 2, keepdims=False).reshape(rows, n * part)
    tok, p1g, smallg, woutg, w2e, cotg, ev, gates, o, qcat, qpos, kv, lse, of = attend(
        n, x, aux, cot, p1, small, pieces, w2, bias, table
    )
    block = 640 // g
    out, dmid, gwout, s1, s2, d_o, gsel, vec = feed(
        n, x, cotg, gates, o, woutg[:, :block].reshape(640, d), smallg, w1_own, w2, w2e
    )
    gwout = gwout.reshape(g, block, d)
    gwout = jnp.pad(gwout, ((0, 0), (0, pieces.shape[0] - block), (0, 0)))
    d_in, gp, gq, g1, g2, go, vq, _ = back(
        n, d_o, gwout, s1, s2, qcat, qpos, kv, lse, of, tok, p1g, ev, gates, gsel, x, smallg, dmid, vec, table
    )
    if group == 56 and part == LANES and rows == LANES:
        (
            g_query, g_key, g_rel, g_value, g_vsel, g_osel, g_one, g_two, g_out,
            gain1, shift1, gain2, shift2, g_b2, g_b1, g_u, g_v, out, d_in,
        ) = unpack(gp, gq, g1, g2, go.reshape(-1, 64, d), vq, out, d_in)
        return (
            out, d_in, gain1[0], shift1[0], g_query.T, g_key.T, g_rel.T, g_u, g_v, g_vsel.T, g_value.T, g_osel.T, g_out,
            gain2[0], shift2[0], g_one, g_b1[0], g_two, g_b2[0],
        )
    gp = jnp.transpose(jnp.concatenate([gp, gq], axis=-1), (1, 0, 2))
    g_query = drop_pads(gp[..., 0:128], group).reshape(rows, 448).astype(F32)
    g_key = drop_pads(gp[..., 128:256], group).reshape(rows, 448).astype(F32)
    g_rel = drop_pads(gp[..., 896:], group).reshape(rows, 448).astype(F32)
    experts = gp[..., 256:896].reshape(rows, 4, 5, LANES)
    g_value = drop_pads(experts, group).reshape(rows, 2240).astype(F32)
    g_vsel = experts[..., SPOT_A].reshape(rows, 20).astype(F32)
    g_osel = experts[..., SPOT_B].reshape(rows, 20).astype(F32)
    g_one = jnp.transpose(g1.reshape(4, rows, n, part), (1, 2, 0, 3)).reshape(rows, hidden).astype(F32)
    g_two = g2.reshape(-1, d).astype(F32)
    g_out = go.reshape(-1, d)[:block].reshape(-1, group * 8 // 7, d)[:, :group].reshape(-1, d).astype(F32)
    sums = jnp.sum(vq, axis=0)
    own = lax.dynamic_slice_in_dim(sums, c * rows, rows, 1)
    g_b1 = lax.dynamic_slice_in_dim(vq[:, 3, :], c * part, part, 1).reshape(-1)
    g_u = drop_pads(vq[:, 6, 0:LANES], group)
    g_v = drop_pads(vq[:, 7, 0:LANES], group)
    return (
        out, d_in, own[4], own[5], g_query, g_key, g_rel, g_u, g_v, g_vsel, g_value, g_osel, g_out,
        own[0], own[1], g_one, g_b1, g_two, own[2],
    )


def solution(mesh):
    both = ("fsdp", "ctx")
    row, vector, matrix = P(both, None), P("ctx"), P("ctx", None)
    in_specs = (
        row, P(both), P(both, None, None), P(both, None, None), vector, vector, matrix, matrix, matrix,
        P(), P(), matrix, matrix, matrix, matrix, vector, vector, matrix, vector, matrix, vector, row,
    )
    out_specs = (
        row, row, vector, vector, matrix, matrix, matrix, P(), P(), matrix, matrix, matrix, matrix,
        vector, vector, matrix, vector, matrix, vector,
    )
    return jax.shard_map(
        functools.partial(on_device, mesh.shape["ctx"]),
        mesh=mesh, in_specs=in_specs, out_specs=out_specs, check_vma=False,
    )
```

```python
import functools
import math

import jax
import jax.numpy as jnp
import numpy as np
from jax import lax
from jax.experimental import pallas as pl
from jax.experimental.pallas import tpu as pltpu
from jax.sharding import PartitionSpec as P

MESH = pl.DeviceIdType.MESH
F32 = jnp.float32
BF16 = jnp.bfloat16
LN_EPS = 1e-05
MASKED = -1e30
LANES = 128
SPOT_A, SPOT_B = 63, 127
VMEM = pl.BlockSpec(memory_space=pltpu.VMEM)
ANY = pl.BlockSpec(memory_space=pl.ANY)
DMA = pltpu.SemaphoreType.DMA


def turn_coefficients():
    nodes = (np.cos(np.pi * (np.arange(400) + 0.5) / 400) + 1) / 8
    root = np.sqrt(nodes)
    powers = nodes[:, None] ** np.arange(7)[None, :]
    sine = np.linalg.lstsq(powers, np.sin(2 * np.pi * root) / root, rcond=None)[0]
    cosine = np.linalg.lstsq(powers, np.cos(2 * np.pi * root), rcond=None)[0]
    return [float(v) for v in sine], [float(v) for v in cosine]


SIN_TURN, COS_TURN = turn_coefficients()


def horner(coefs, v):
    total = coefs[-1]
    for coef in coefs[-2::-1]:
        total = total * v + coef
    return total


def turn_table(model_width):
    freq = 10000.0 ** (-np.arange(0, model_width, 2, dtype=np.float64) / model_width) / (2 * np.pi)
    mantissa, exponent = np.frexp(freq)
    coarse = np.ldexp(np.floor(mantissa * 256) / 256, exponent)
    table = np.zeros((8, model_width // 2), np.float32)
    table[0] = coarse
    table[1] = freq - coarse
    return table


def sin_cos(places, table_ref):
    coarse = places * table_ref[0:1, :]
    part = (coarse - jnp.round(coarse)) + places * table_ref[1:2, :]
    part = part - jnp.round(part)
    square = part * part
    return horner(SIN_TURN, square) * part, horner(COS_TURN, square)


def mm(left, right):
    return lax.dot_general(left, right, (((1,), (0,)), ((), ())), preferred_element_type=F32)


def mm_t(left, right):
    return lax.dot_general(left, right, (((1,), (1,)), ((), ())), preferred_element_type=F32)


def mm_left_t(left, right):
    return lax.dot_general(left, right, (((0,), (0,)), ((), ())), preferred_element_type=F32)


def copy_to(src, dst, send, recv, f, c):
    return pltpu.make_async_remote_copy(
        src_ref=src, dst_ref=dst, send_sem=send, recv_sem=recv, device_id=(f, c), device_id_type=MESH
    )


def greet(f, c, fsdp, n):
    barrier = pltpu.get_barrier_semaphore()

    def one(k, _):
        pl.semaphore_signal(barrier, inc=1, device_id=(f, lax.rem(c + k, n)), device_id_type=MESH)
        return 0

    lax.fori_loop(1, n, one, 0)
    for k in range(1, fsdp):
        pl.semaphore_signal(barrier, inc=1, device_id=(f ^ k, c), device_id_type=MESH)
    pl.semaphore_wait(barrier, n - 1 + fsdp - 1)


class LineGather:
    def __init__(self, f, c, n, own, at, recv, right, left, pair, subs=1, lone=False):
        self.f, self.c, self.n, self.size = f, c, n, n // 2
        self.place, self.bit = c // 2, lax.rem(c, 2)
        self.own, self.at = own, at
        self.recv, self.right, self.left, self.pair = recv, right, left, pair
        self.subs, self.lone = subs, lone

    def valid(self, o):
        ok = jnp.logical_and(o >= 0, o < self.size)
        if self.lone:
            span = self.size // 4
            ok = jnp.logical_and(ok, jnp.logical_and(o >= self.f * span, o < (self.f + 1) * span))
        return ok

    def slot(self, block):
        return block - self.f * (self.n // 4) if self.lone else block

    def copy(self, src, block, sub, sems, c):
        slot = self.slot(block)
        i = slot * self.subs + sub
        return copy_to(src, self.at(slot, sub), sems.at[i], self.recv.at[i], self.f, c)

    def held(self, block, sub):
        return self.at(self.slot(block), sub)

    def each(self, work):
        if self.subs == 1:
            work(0)
        else:
            lax.fori_loop(0, self.subs, lambda sub, u: (work(sub), u)[1], 0)

    def spread(self, src, block, sub, go_right, go_left):
        @pl.when(go_right)
        def _():
            self.copy(src, block, sub, self.right, self.c + 2).start()

        @pl.when(go_left)
        def _():
            self.copy(src, block, sub, self.left, self.c - 2).start()

        self.copy(src, block, sub, self.pair, self.c + 1 - 2 * self.bit).start()

    def begin(self, local):
        @pl.when(self.valid(self.place))
        def _():
            self.each(
                lambda sub: self.spread(
                    self.own(sub), self.c, sub, self.place < self.size - 1, self.place > 0
                )
            )
            local()

    def arrived(self, block, sub):
        self.copy(self.held(block, sub), block, sub, self.pair, self.c).wait_recv()

    def step(self, t):
        for sign in (-1, 1):
            o = self.place + sign * t
            block = 2 * o + self.bit

            @pl.when(self.valid(o))
            def _():
                def one(sub):
                    self.arrived(block, sub)
                    self.spread(
                        self.held(block, sub), block, sub,
                        jnp.logical_and(sign < 0, self.place < self.size - 1),
                        jnp.logical_and(sign > 0, self.place > 0),
                    )

                self.each(one)

    def steps(self, first=1):
        lax.fori_loop(first, self.size, lambda t, u: (self.step(t), u)[1], 0)

    def finish(self):
        def one(o, _):
            block = 2 * o + self.bit

            def piece(sub):
                self.arrived(2 * o + 1 - self.bit, sub)
                source = self.held(block, sub)
                self.copy(source, block, sub, self.pair, self.c).wait_send()

                @pl.when(jnp.logical_and(o <= self.place, self.place < self.size - 1))
                def _():
                    self.copy(source, block, sub, self.right, self.c).wait_send()

                @pl.when(jnp.logical_and(o >= self.place, self.place > 0))
                def _():
                    self.copy(source, block, sub, self.left, self.c).wait_send()

            @pl.when(self.valid(o))
            def _():
                self.each(piece)

            return 0

        lax.fori_loop(0, self.size, one, 0)


class QuadGather:
    def __init__(self, f, c, out, send, recv, part=None):
        self.f, self.c, self.out, self.send, self.recv = f, c, out, send, recv
        self.part = part

    def at(self, slot):
        return self.out.at[slot] if self.part is None else self.out.at[slot, self.part, :]

    def copy(self, slot, k, to, src=None):
        src = self.at(slot) if src is None else src
        return copy_to(src, self.at(slot), self.send.at[k], self.recv.at[slot], to, self.c)

    def begin(self, src=None):
        self.copy(self.f, 1, self.f ^ 2, src).start()
        self.copy(self.f, 0, self.f ^ 1, src).start()

    def got(self, slot):
        self.copy(slot, 0, self.f).wait_recv()

    def relay(self):
        self.got(self.f ^ 2)
        self.copy(self.f ^ 2, 2, self.f ^ 1).start()

    def sent(self):
        for k in range(3):
            self.copy(self.f, k, self.f).wait_send()


def spread_vector(rows, width):
    count = rows.shape[0]
    total = count * width
    lane = lax.broadcasted_iota(jnp.int32, (LANES, total), 0)
    column = lax.broadcasted_iota(jnp.int32, (LANES, total), 1)
    onehot = jnp.where(lane == lax.rem(column, width), 1.0, 0.0).astype(BF16)
    wide = mm(rows.astype(BF16), onehot)
    row = lax.broadcasted_iota(jnp.int32, (count, total), 0)
    column = lax.broadcasted_iota(jnp.int32, (count, total), 1)
    return jnp.sum(jnp.where(column // width == row, wide, 0.0), axis=0, keepdims=True)


def block_of(j, i, groups):
    return i * groups + jnp.where(lax.rem(i, 2) == 0, j, groups - 1 - j)


def holder_of(block, groups):
    row, within = block // groups, lax.rem(block, groups)
    return jnp.where(lax.rem(row, 2) == 0, within, groups - 1 - within), row


def key_places(kv):
    return kv[:, SPOT_A : SPOT_A + 1].astype(F32) * 128.0 + kv[:, SPOT_B : SPOT_B + 1].astype(F32)


def attend_kernel(
    n,
    x_ref, aux_ref, cot_ref, p1_ref, small_ref, wout_ref, w2_ref, bias_ref, table_ref,
    tok_ref, p1g_ref, smallg_ref, woutg_ref, w2e_ref, cotg_ref, ev_ref, gates_ref, o_ref,
    qcat_ref, qpos_ref, kv_ref, lse_ref, of_ref,
    qs_ref, kvs_ref, qr_ref, os_ref, kcat_ref, vt_ref, m_ref, l_ref,
    sm_s, sm_r, p_r, p_a, p_b, p_c, w_r, w_a, w_b, w_c, h_r, h_a, h_b, h_c,
    t_s, t_r, c_s, c_r, q_s, q_r, kv_s, kv_r, kv_p, o_s, o_r, loc,
):
    f, c = lax.axis_index("fsdp"), lax.axis_index("ctx")
    groups = n // 4
    seq, turn = c // groups, lax.rem(c, groups)
    tokens, width = x_ref.shape
    scale = 1.0 / math.sqrt(112)
    greet(f, c, 4, n)

    def small_send(k, _):
        to = lax.rem(c + k, n)
        copy_to(small_ref, smallg_ref.at[c], sm_s.at[to], sm_r.at[c], f, to).start()
        return 0

    lax.fori_loop(1, n, small_send, 0)
    smallg_ref[c] = small_ref[...]
    gather_p = LineGather(f, c, n, lambda sub: p1_ref, lambda k, sub: p1g_ref.at[k], p_r, p_a, p_b, p_c)

    def own_p():
        p1g_ref[c] = p1_ref[...]

    gather_p.begin(own_p)
    wout_copy = pltpu.make_async_copy(wout_ref, woutg_ref.at[c - f * groups], loc.at[0])
    subs = w_r.shape[0] // groups
    piece = wout_ref.shape[0] // subs
    gather_w = LineGather(
        f, c, n,
        lambda sub: wout_ref.at[pl.ds(pl.multiple_of(sub * piece, piece), piece), :],
        lambda k, sub: woutg_ref.at[k, pl.ds(pl.multiple_of(sub * piece, piece), piece), :],
        w_r, w_a, w_b, w_c, subs=subs, lone=True,
    )
    early = w2e_ref.shape[1]
    own2 = w2_ref.at[pl.ds(pl.multiple_of(f * (w2_ref.shape[0] // 4), 16), early), :]
    w2_copy = pltpu.make_async_copy(own2, w2e_ref.at[c], loc.at[2])
    gather_h = LineGather(f, c, n, lambda sub: own2, lambda k, sub: w2e_ref.at[k], h_r, h_a, h_b, h_c)
    cot_copy = pltpu.make_async_copy(cot_ref, cotg_ref.at[f], loc.at[1])
    cot_copy.start()

    hidden = x_ref[...].astype(F32)
    offsets = hidden - jnp.mean(hidden, axis=1, keepdims=True)
    spread = jnp.mean(offsets * offsets, axis=1, keepdims=True)
    xhat = offsets * lax.rsqrt(spread + LN_EPS)

    def small_wait(k, _):
        to = lax.rem(c + k, n)
        copy_to(small_ref, smallg_ref.at[to], sm_s.at[to], sm_r.at[to], f, to).wait()
        return 0

    lax.fori_loop(1, n, small_wait, 0)
    gain = spread_vector(smallg_ref[:, 0, :], width // n)
    shift = spread_vector(smallg_ref[:, 1, :], width // n)
    tok_ref[f, :, 0:width] = (xhat * gain + shift).astype(BF16)
    tok_ref[f, :, width:] = aux_ref[...]
    tok_gather = QuadGather(f, c, tok_ref, t_s, t_r)
    tok_gather.begin()
    gather_p.steps()
    tok_gather.relay()
    gather_p.finish()
    tok_gather.got(f ^ 1)
    tok_gather.got(f ^ 3)
    tok_gather.sent()
    cot_gather = QuadGather(f, c, cotg_ref, c_s, c_r)
    cot_gather.begin(cot_ref)

    lane = lax.broadcasted_iota(jnp.int32, (tokens, LANES), 1)
    source = lax.broadcasted_iota(jnp.int32, (LANES, LANES), 0)
    target = lax.broadcasted_iota(jnp.int32, (LANES, LANES), 1)
    wanted = f * 16 + lax.rem(target, 8) + jnp.where(target < 16, 8, 0)
    pick = jnp.where(
        jnp.logical_and(source == wanted, jnp.logical_and(target < 32, lax.rem(target, 8) < 5)), 1.0, 0.0
    ).astype(BF16)
    own_turn, own_slot = holder_of(c, groups)
    bit = lax.rem(c, 2)
    spots = jnp.logical_or(lane == SPOT_A, lane == SPOT_B)

    def project(t, _):
        s = lax.rem(seq + 1 + t, 4)
        normed = tok_ref[s, :, 0:width]
        aux = tok_ref[s, :, width:]
        weights = p1g_ref[...].reshape(width, p1g_ref.shape[2])
        qk = mm(normed, weights[:, 0:256])
        experts = mm(normed, weights[:, 256:896])
        ev_ref[s] = experts.astype(BF16)
        logits = jnp.zeros((tokens, LANES), F32)
        for e in range(5):
            for spot, first in ((SPOT_B, 0), (SPOT_A, 16)):
                column = experts[:, e * LANES + spot : e * LANES + spot + 1]
                logits = jnp.where(
                    jnp.logical_or(lane == first + e, lane == first + 8 + e), column, logits
                )
        sig = jax.nn.sigmoid(logits)
        gates = mm(aux, pick) * jnp.where(lax.rem(lane, 16) >= 8, sig * (1.0 - sig), sig)
        gates_ref[s] = gates
        values = jnp.zeros((tokens, LANES), F32)
        for e in range(5):
            values = values + gates[:, 16 + e : 17 + e] * experts[:, e * LANES : (e + 1) * LANES]
        values = jnp.where(spots, 0.0, values)
        high, rest = aux[:, 64:65].astype(F32), aux[:, 65:66].astype(F32)

        def with_place(v):
            return jnp.where(lane == SPOT_A, high, jnp.where(lane == SPOT_B, rest, v)).astype(BF16)

        qs_ref[s] = with_place(qk[:, 0:128])
        kvs_ref[s, :, 0:128] = with_place(qk[:, 128:256])
        kvs_ref[s, :, 128:256] = values.astype(BF16)
        to = s * groups + own_turn

        @pl.when(to != c)
        def _():
            copy_to(qs_ref.at[s], qr_ref.at[own_slot], q_s.at[s], q_r.at[own_slot], f, to).start()

        @pl.when(to == c)
        def _():
            qr_ref[own_slot] = qs_ref[s]

        def kv_send(k, _):
            to = s * groups + 2 * k + bit

            @pl.when(to != c)
            def _():
                copy_to(kvs_ref.at[s], kv_ref.at[c], kv_s.at[to], kv_r.at[c], f, to).start()

            @pl.when(to == c)
            def _():
                kv_ref[c] = kvs_ref[s]

            return 0

        lax.fori_loop(0, groups // 2, kv_send, 0)
        return 0

    gather_h.begin(w2_copy.start)
    lax.fori_loop(0, 4, project, 0)
    gather_w.begin(wout_copy.start)

    def kv_wait(block):
        copy_to(kvs_ref.at[0], kv_ref.at[block], kv_s.at[0], kv_r.at[block], f, c).wait_recv()

    def kv_pass(block):
        return copy_to(kv_ref.at[block], kv_ref.at[block], kv_p.at[block // 2], kv_r.at[block], f, c + 1 - 2 * bit)

    def hand_on(m):
        block = 2 * m + bit

        @pl.when(block != c)
        def _():
            kv_wait(block)

        kv_pass(block).start()

    def prepare(i, _):
        block = block_of(turn, i, groups)

        @pl.when(block != c)
        def _():
            copy_to(qs_ref.at[0], qr_ref.at[i], q_s.at[0], q_r.at[i], f, c).wait_recv()

        places = key_places(qr_ref[i])
        query = jnp.where(spots, 0.0, qr_ref[i].astype(F32))
        q_position = (query + bias_ref[pl.ds(4 + f, 1), :]).astype(BF16)
        qpos_ref[i] = q_position
        qcat_ref[i, :, width:] = ((query + bias_ref[pl.ds(f, 1), :]) * scale).astype(BF16)
        rel = p1g_ref[:, :, 896:].reshape(width, LANES)
        rel_query = mm_t(q_position, rel)
        sine, cosine = sin_cos(places, table_ref)
        first, second = rel_query[:, : width // 2], rel_query[:, width // 2 :]
        qcat_ref[i, :, 0 : width // 2] = ((first * sine + second * cosine) * scale).astype(BF16)
        qcat_ref[i, :, width // 2 : width] = ((second * sine - first * cosine) * scale).astype(BF16)
        m_ref[i] = jnp.full((1, tokens), MASKED, F32)
        l_ref[i] = jnp.zeros((1, tokens), F32)
        of_ref[i] = jnp.zeros((LANES, tokens), F32)
        return 0

    lax.fori_loop(0, 4, prepare, 0)
    hand_on(0)
    row_in = lax.broadcasted_iota(jnp.int32, (tokens, tokens), 0)
    col_in = lax.broadcasted_iota(jnp.int32, (tokens, tokens), 1)

    def give(i):
        total = l_ref[i]
        result = of_ref[i] / total
        of_ref[i] = result
        lse_ref[i] = m_ref[i] + jnp.log(total)
        os_ref[i] = result.T.astype(BF16)
        block = block_of(turn, i, groups)

        @pl.when(block != c)
        def _():
            copy_to(os_ref.at[i], o_ref.at[seq], o_s.at[i], o_r.at[seq], f, block).start()

        @pl.when(block == c)
        def _():
            o_ref[seq] = os_ref[i]

    def key_block(kb, _):
        own = [block_of(turn, i, groups) for i in range(4)]
        first = sum((b < kb).astype(jnp.int32) for b in own)
        ready = sum((b == kb).astype(jnp.int32) for b in own)

        @pl.when(lax.rem(kb, 2) != bit)
        def _():
            kv_wait(kb)

        @pl.when(jnp.logical_and(lax.rem(kb, 2) == 0, kb < n - 2))
        def _():
            hand_on(kb // 2 + 1)

        sine, cosine = sin_cos(key_places(kv_ref[kb]), table_ref)
        kcat_ref[:, 0 : width // 2] = cosine.astype(BF16)
        kcat_ref[:, width // 2 : width] = sine.astype(BF16)
        kcat_ref[:, width:] = kv_ref[kb, :, 0:128]
        vt_ref[...] = kv_ref[kb, :, 128:256].astype(F32).T.astype(BF16)

        def query_block(i, _):
            gap = (block_of(turn, i, groups) - kb) * tokens
            scores = mm_t(kcat_ref[...], qcat_ref[i])
            scores = jnp.where(row_in <= col_in + gap, scores, MASKED)
            before = m_ref[i]
            best = jnp.maximum(before, jnp.max(scores, axis=0, keepdims=True))
            shrink = jnp.exp(before - best)
            probs = jnp.exp(scores - best)
            m_ref[i] = best
            l_ref[i] = l_ref[i] * shrink + jnp.sum(probs, axis=0, keepdims=True)
            of_ref[i] = of_ref[i] * shrink + mm(vt_ref[...], probs.astype(BF16))
            return 0

        lax.fori_loop(first, 4, query_block, 0)

        @pl.when(ready == 1)
        def _():
            give(first)

        @pl.when(kb == n // 2 - 1)
        def _():
            cot_gather.relay()

        @pl.when(jnp.logical_and(kb > 0, kb < n // 2))
        def _():
            gather_w.step(kb)

        @pl.when(kb < n // 2 - 1)
        def _():
            gather_h.step(kb + 1)

        return 0

    lax.fori_loop(0, n, key_block, 0)
    cot_gather.got(f ^ 1)
    cot_gather.got(f ^ 3)
    cot_gather.sent()
    gather_w.finish()
    gather_h.finish()
    w2_copy.wait()

    @pl.when(gather_w.valid(c // 2))
    def _():
        wout_copy.wait()

    cot_copy.wait()

    def drain(s, _):
        to = s * groups + own_turn

        @pl.when(to != c)
        def _():
            copy_to(qs_ref.at[s], qr_ref.at[own_slot], q_s.at[s], q_r.at[0], f, to).wait_send()
            copy_to(os_ref.at[0], o_ref.at[s], o_s.at[0], o_r.at[s], f, to).wait_recv()

        @pl.when(block_of(turn, s, groups) != c)
        def _():
            copy_to(os_ref.at[s], o_ref.at[s], o_s.at[s], o_r.at[0], f, to).wait_send()

        return 0

    lax.fori_loop(0, 4, drain, 0)

    def kv_drain(k, _):
        to = 2 * k + bit

        @pl.when(to != c)
        def _():
            copy_to(kvs_ref.at[0], kv_ref.at[0], kv_s.at[to], kv_r.at[0], f, c).wait_send()

        kv_pass(to).wait_send()
        return 0

    lax.fori_loop(0, n // 2, kv_drain, 0)


def sds(shape, dtype):
    return jax.ShapeDtypeStruct(shape, dtype)


def attend(n, x, aux, cot, p1, small, wout, w2, bias, table):
    t, d = x.shape
    rows = p1.shape[0]
    out_rows = wout.shape[0]
    g = n // 4
    subs = cuts(out_rows)
    return pl.pallas_call(
        functools.partial(attend_kernel, n),
        out_shape=[
            sds((4, t, d + LANES), BF16), sds((n, rows, d), BF16), sds((n, 16, LANES), F32),
            sds((g, out_rows, d), BF16), sds((n, early_rows(w2.shape[0] // 4), d), BF16), sds((4, t, d), BF16), sds((4, t, 640), BF16),
            sds((4, t, LANES), F32), sds((4, t, LANES), BF16), sds((4, t, d + LANES), BF16),
            sds((4, t, LANES), BF16), sds((n, t, 256), BF16), sds((4, 1, t), F32), sds((4, LANES, t), F32),
        ],
        in_specs=[VMEM, VMEM, ANY, VMEM, VMEM, ANY, ANY, VMEM, VMEM],
        out_specs=[VMEM, VMEM, VMEM, ANY, ANY, ANY] + [VMEM] * 8,
        scratch_shapes=[
            pltpu.VMEM((4, t, LANES), BF16), pltpu.VMEM((4, t, 256), BF16), pltpu.VMEM((4, t, LANES), BF16),
            pltpu.VMEM((4, t, LANES), BF16), pltpu.VMEM((t, d + LANES), BF16),
            pltpu.VMEM((LANES, t), BF16), pltpu.VMEM((4, 1, t), F32), pltpu.VMEM((4, 1, t), F32),
            DMA((n,)), DMA((n,)), DMA((n,)), DMA((n,)), DMA((n,)), DMA((n,)),
            DMA((g * subs,)), DMA((g * subs,)), DMA((g * subs,)), DMA((g * subs,)),
            DMA((n,)), DMA((n,)), DMA((n,)), DMA((n,)),
            DMA((3,)), DMA((4,)), DMA((3,)), DMA((4,)), DMA((4,)), DMA((4,)),
            DMA((n,)), DMA((n,)), DMA((n // 2,)), DMA((4,)), DMA((4,)), DMA((3,)),
        ],
        compiler_params=pltpu.CompilerParams(
            collective_id=0, has_side_effects=True, vmem_limit_bytes=56 << 20
        ),
        name="attend",
    )(x, aux, cot, p1, small, wout, w2, bias, table)


class QuadSum:
    def __init__(self, f, c, core_out, core_in, x_out, x_in, keep, send, recv):
        self.f, self.c = f, c
        self.core_out, self.core_in, self.x_out, self.x_in = core_out, core_in, x_out, x_in
        self.keep, self.send, self.recv = keep, send, recv

    def core(self, k):
        return copy_to(
            self.core_out.at[k], self.core_in.at[k], self.send.at[k], self.recv.at[k], self.f ^ 1, self.c
        )

    def across(self):
        return copy_to(self.x_out, self.x_in, self.send.at[2], self.recv.at[2], self.f ^ 2, self.c)

    def put(self, k, value):
        if k in (1, 3):
            self.core_out[k // 2] = value.astype(BF16)
            self.core(k // 2).start()
        else:
            self.keep[k // 2] = value

    def cross(self):
        self.core(1).wait_recv()
        self.x_out[...] = (self.keep[1] + self.core_in[1].astype(F32)).astype(BF16)
        self.across().start()

    def total(self):
        self.core(0).wait_recv()
        self.across().wait_recv()
        return self.keep[0] + self.core_in[0].astype(F32) + self.x_in[...].astype(F32)

    def sent(self):
        self.core(0).wait_send()
        self.core(1).wait_send()
        self.across().wait_send()


def quad_sum_scratch(t, d):
    return [
        pltpu.VMEM((2, t, d), BF16), pltpu.VMEM((2, t, d), BF16), pltpu.VMEM((t, d), BF16),
        pltpu.VMEM((t, d), BF16), pltpu.VMEM((2, t, d), F32), DMA((3,)), DMA((3,)),
    ]


def layer_stats(v):
    offsets = v - jnp.mean(v, axis=1, keepdims=True)
    scale = lax.rsqrt(jnp.mean(offsets * offsets, axis=1, keepdims=True) + LN_EPS)
    return offsets * scale, scale


def layer_back(grad, gain, xhat, scale):
    inner = grad * gain
    return scale * (
        inner - jnp.mean(inner, axis=1, keepdims=True) - xhat * jnp.mean(inner * xhat, axis=1, keepdims=True)
    )


def gelu_pair(v):
    k = math.sqrt(2.0 / math.pi)
    square = v * v
    t = jnp.tanh(k * v * (1.0 + 0.044715 * square))
    half = 0.5 * (1.0 + t)
    return v * half, half + 0.5 * v * (1.0 - t * t) * (k * (1.0 + 3 * 0.044715 * square))


class PairSum:
    def __init__(self, f, c, n, source, got, out, send, recv):
        self.f, self.c, self.size = f, c, n // 2
        self.bit = lax.rem(c, 2)
        self.source, self.got, self.out, self.send, self.recv = source, got, out, send, recv

    def copy(self, o):
        return copy_to(
            self.source(2 * o + 1 - self.bit), self.got.at[o], self.send.at[o], self.recv.at[o],
            self.f, self.c + 1 - 2 * self.bit,
        )

    def begin(self):
        lax.fori_loop(0, self.size, lambda o, u: (self.copy(o).start(), u)[1], 0)

    def finish(self):
        def one(o, _):
            self.copy(o).wait_recv()
            term = self.source(2 * o + self.bit)[...].astype(F32)
            self.out[o] = (term + self.got[o].astype(F32)).astype(BF16)
            self.copy(o).wait_send()
            return 0

        lax.fori_loop(0, self.size, one, 0)


class LineSum:
    def __init__(self, f, c, n, source, inbox, stage, line_s, line_r, pair=None, subs=1, lone=False):
        self.f, self.c, self.n, self.size = f, c, n, n // 2
        self.place, self.bit = c // 2, lax.rem(c, 2)
        self.source = source
        self.inbox, self.stage, self.line_s, self.line_r = inbox, stage, line_s, line_r
        self.pair = pair
        self.subs = subs
        self.span = self.size // 4 if lone else self.size
        self.first = f * self.span if lone else 0

    def valid(self, o):
        return jnp.logical_and(o >= self.first, o < self.first + self.span)

    def index(self, o, sub):
        return (o - self.first) * self.subs + sub

    def pair_copy(self, o, sub):
        i = self.index(o, sub)
        got, send, recv = self.pair
        return copy_to(
            self.source(2 * (o - self.first) + 1 - self.bit, sub), got.at[i], send.at[i], recv.at[i],
            self.f, self.c + 1 - 2 * self.bit,
        )

    def line_copy(self, i, slot, c):
        return copy_to(self.stage.at[i], self.inbox.at[slot], self.line_s.at[i], self.line_r.at[slot], self.f, c)

    def each(self, work):
        def one(k, _):
            work(self.first + k // self.subs, lax.rem(k, self.subs))
            return 0

        lax.fori_loop(0, self.span * self.subs, one, 0)

    def begin(self):
        self.each(lambda o, sub: self.pair_copy(o, sub).start())

    def begin_block(self, block):
        @pl.when(lax.rem(block, 2) != self.bit)
        def _():
            self.pair_copy(block // 2, 0).start()

    def term(self, o, sub):
        if self.pair is None:
            return self.source(o - self.first, sub)[...].astype(F32)
        self.pair_copy(o, sub).wait_recv()
        own = self.source(2 * (o - self.first) + self.bit, sub)[...].astype(F32)
        return own + self.pair[0][self.index(o, sub)].astype(F32)

    def extra(self, sub):
        return self.span * self.subs + sub

    def move(self, o, sub, go_right):
        i = self.index(o, sub)
        total = self.term(o, sub)
        starts = self.place == 0 if go_right else self.place == self.size - 1

        @pl.when(starts)
        def _():
            self.stage[i] = total.astype(BF16)

        @pl.when(jnp.logical_not(starts))
        def _():
            self.line_copy(i, i, self.c).wait_recv()
            self.stage[i] = (total + self.inbox[i].astype(F32)).astype(BF16)

        if go_right:
            self.line_copy(i, i, self.c + 2).start()
        else:
            slot = jnp.where(o == self.place - 1, self.extra(sub), i)
            self.line_copy(i, slot, self.c - 2).start()

    def turn(self, time):
        far = self.size - 1 - (time - self.place)
        near = time - (self.size - 1 - self.place)

        def one(sub, _):
            @pl.when(jnp.logical_and(jnp.logical_and(far < self.size, self.valid(far)), far > self.place))
            def _():
                self.move(far, sub, True)

            @pl.when(jnp.logical_and(jnp.logical_and(near >= 0, self.valid(near)), near < self.place))
            def _():
                self.move(near, sub, False)

            return 0

        lax.fori_loop(0, self.subs, one, 0)

    def settle(self, sub):
        i = self.index(self.place, sub)
        own = self.term(self.place, sub)
        left = self.place > 0
        right = self.place < self.size - 1

        @pl.when(left)
        def _():
            self.line_copy(i, i, self.c).wait_recv()

        @pl.when(right)
        def _():
            self.line_copy(i, self.extra(sub), self.c).wait_recv()

        @pl.when(jnp.logical_and(left, right))
        def _():
            self.stage[i] = (
                own + self.inbox[i].astype(F32) + self.inbox[self.extra(sub)].astype(F32)
            ).astype(BF16)

        @pl.when(jnp.logical_and(left, jnp.logical_not(right)))
        def _():
            self.stage[i] = (own + self.inbox[i].astype(F32)).astype(BF16)

        @pl.when(jnp.logical_and(right, jnp.logical_not(left)))
        def _():
            self.stage[i] = (own + self.inbox[self.extra(sub)].astype(F32)).astype(BF16)

    def finish(self):
        @pl.when(self.valid(self.place))
        def _():
            lax.fori_loop(0, self.subs, lambda sub, u: (self.settle(sub), u)[1], 0)

    def sent(self):
        def one(o, sub):
            if self.pair is not None:
                self.pair_copy(o, sub).wait_send()

            @pl.when(o != self.place)
            def _():
                self.line_copy(self.index(o, sub), 0, self.c).wait_send()

        self.each(one)


def feed_kernel(
    n,
    x_ref, cot_ref, gates_ref, o_ref, wout_ref, small_ref, w1_ref, w2_ref, w2e_ref,
    out_ref, dmid_ref, gwout_ref, s1_ref, s2_ref, do_ref, gsel_ref, vec_ref,
    w1g, w2g, n2_ref, act_ref, slope_ref, dpre_ref, mixed_ref, dml_ref, mid_ref, gw1_ref, gw2_ref, got1, in2, stage2,
    a0, a1, a2, a3, a4, a5, a6, i0, i1, i2, i3, i4, i5, i6, b0, b1, b2, b3, b4, b5, b6, j0, j1, j2, j3, j4, j5, j6,
    e0, e1, e2, e3, e4, e5, e6,
    w1_r, w1_a, w1_b, w1_c, w2_r, w2_a, w2_b, w2_c, h1_s, h1_r, h2_s, h2_r, n_s, n_r, d_s, d_r, m_s, m_r, k_s, k_r, loc, da_ref, da_s, da_r,
):
    f, c = lax.axis_index("fsdp"), lax.axis_index("ctx")
    tokens, width = x_ref.shape
    quarter = w1g.shape[1]
    groups = n // 4
    own_turn, own_slot = holder_of(c, groups)
    greet(f, c, 4, n)
    rows1, rows2 = width // n, quarter // n

    def rows_of(ref, count):
        return lambda k: ref.at[pl.ds(pl.multiple_of(k * count, count), count), :]

    early = w2e_ref.shape[1]
    at1 = rows_of(w1g, rows1)
    gather1 = LineGather(f, c, n, lambda sub: w1_ref, lambda k, sub: at1(k), w1_r, w1_a, w1_b, w1_c)
    local1 = pltpu.make_async_copy(w1_ref, at1(c), loc.at[0])
    bring2 = pltpu.make_async_copy(w2e_ref, w2g.at[:, 0:early, :], loc.at[1])
    gather1.begin(local1.start)
    bring2.start()
    gather2 = None
    if early < rows2:
        own2 = w2_ref.at[pl.ds(pl.multiple_of(f * rows2 + early, 16), rows2 - early), :]
        at2 = lambda k: w2g.at[k, early:rows2, :]
        gather2 = LineGather(f, c, n, lambda sub: own2, lambda k, sub: at2(k), w2_r, w2_a, w2_b, w2_c)
        local2 = pltpu.make_async_copy(own2, at2(c), loc.at[2])
    pair1 = PairSum(f, c, n, rows_of(gw1_ref, rows1), got1, s1_ref, h1_s, h1_r)
    line2 = LineSum(f, c, n, lambda o, sub: rows_of(gw2_ref, rows2)(2 * o + sub), in2, stage2, h2_s, h2_r, subs=2)
    attn_sum = (QuadSum(f, c, a0, a1, a2, a3, a4, a5, a6), QuadSum(f, c, i0, i1, i2, i3, i4, i5, i6))
    back_sum = (QuadSum(f, c, b0, b1, b2, b3, b4, b5, b6), QuadSum(f, c, j0, j1, j2, j3, j4, j5, j6))
    span = tokens // 2
    halves = (slice(0, span), slice(span, tokens))
    out_sum = QuadSum(f, c, e0, e1, e2, e3, e4, e5, e6)

    for half, one in zip(halves, attn_sum):
        for k in (3, 2, 1, 0):
            r = f ^ k
            for e in range(5):
                mixed_ref[r, half, e * LANES : (e + 1) * LANES] = (
                    gates_ref[r, half, e : e + 1] * o_ref[r, half, :].astype(F32)
                ).astype(BF16)
            one.put(k, mm(mixed_ref[r, half, :], wout_ref[...]))
            if k == 2:
                one.cross()
    gather1.step(1)
    gain = spread_vector(small_ref[:, 2, :], width // n)
    shift = spread_vector(small_ref[:, 3, :], width // n)
    n2_gather = (QuadGather(f, c, n2_ref, n_s, n_r, halves[0]), QuadGather(f, c, n2_ref, m_s, m_r, halves[1]))
    for half, one, gather in zip(halves, attn_sum, n2_gather):
        middle = x_ref[half, :].astype(F32) + one.total()
        mid_ref[half, :] = middle
        xhat, _ = layer_stats(middle)
        n2_ref[f, half, :] = (xhat * gain + shift).astype(BF16)
        gather.begin()
    gather1.steps(2)
    if gather2 is not None:
        gather2.begin(local2.start)
    gather1.finish()
    local1.wait()
    first_bias = spread_vector(small_ref[:, pl.ds(5 + f, 1), :].reshape(n, LANES), rows2)

    def enter(k):
        r = f ^ k
        act, slope = gelu_pair(mm(n2_ref[r], w1g[...]) + first_bias)
        act_ref[r] = act.astype(BF16)
        slope_ref[r] = slope

    def got(pair, slot):
        for gather in pair:
            gather.got(slot)

    enter(0)
    got(n2_gather, f ^ 1)
    n2_gather[0].relay()
    if gather2 is not None:
        gather2.step(1)
    enter(1)
    n2_gather[1].relay()
    if gather2 is not None:
        gather2.step(2)
    enter(2)
    if gather2 is not None:
        gather2.steps(3)
    got(n2_gather, f ^ 3)
    enter(3)
    tile = 256
    all_tokens = 4 * tokens

    def weight_tile(left_ref, right_ref, result_ref):
        def one(i, _):
            spot = pl.multiple_of(i * tile, tile)
            left = left_ref[:, :, pl.ds(spot, tile)].reshape(all_tokens, tile)
            right = right_ref[...].reshape(all_tokens, right_ref.shape[2])
            result_ref[pl.ds(spot, tile), :] = mm_left_t(left, right).astype(BF16)
            return 0

        lax.fori_loop(0, left_ref.shape[2] // tile, one, 0)

    weight_tile(act_ref, cot_ref, gw2_ref)
    line2.turn(0)
    if gather2 is not None:
        gather2.finish()
        local2.wait()
    bring2.wait()
    second = w2g[...].reshape(quarter, width)

    for k in (3, 2, 1, 0):
        r = f ^ k
        d_act = mm_t(cot_ref[r], second)
        dpre_ref[r] = (d_act * slope_ref[r]).astype(BF16)
        term = mm_t(dpre_ref[r], w1g[...])
        for half, one in zip(halves, back_sum):
            one.put(k, term[half])
        if k == 2:
            for one in back_sum:
                one.cross()
    weight_tile(n2_ref, dpre_ref, gw1_ref)
    pair1.begin()
    line2.turn(1)
    for k in (3, 2, 1, 0):
        out_sum.put(k, mm(act_ref[f ^ k], second))
    vec_ref[...] = jnp.zeros_like(vec_ref)
    dml_gather = (QuadGather(f, c, dml_ref, d_s, d_r, halves[0]), QuadGather(f, c, dml_ref, k_s, k_r, halves[1]))
    for half, one, gather in zip(halves, back_sum, dml_gather):
        d_norm = one.total()
        xhat, scale = layer_stats(mid_ref[half, :])
        d_middle = cot_ref[f, half, :].astype(F32) + layer_back(d_norm, gain, xhat, scale)
        dmid_ref[half, :] = d_middle
        dml_ref[f, half, :] = d_middle.astype(BF16)
        gather.begin()
        vec_ref[0:1, :] += jnp.sum(d_norm * xhat, axis=0, keepdims=True)
        vec_ref[1:2, :] += jnp.sum(d_norm, axis=0, keepdims=True)
    out_sum.cross()
    vec_ref[2:3, :] = jnp.sum(cot_ref[f].astype(F32), axis=0, keepdims=True)
    total = jnp.zeros((1, quarter), F32)
    for r in range(4):
        total = total + jnp.sum(dpre_ref[r].astype(F32), axis=0, keepdims=True)
    vec_ref[3:4, :] = total
    lane = lax.broadcasted_iota(jnp.int32, (tokens, LANES), 1)

    def leave(k):
        r = f ^ k
        d_attn = jnp.zeros((tokens, LANES), F32)
        select = jnp.zeros((tokens, LANES), F32)
        result = o_ref[r].astype(F32)
        d_mixed = mm_t(dml_ref[r], wout_ref[...])
        for e in range(5):
            part = d_mixed[:, e * LANES : (e + 1) * LANES]
            d_attn = d_attn + gates_ref[r, :, e : e + 1] * part
            column = jnp.sum(result * part, axis=1, keepdims=True) * gates_ref[r, :, 8 + e : 9 + e]
            select = jnp.where(lane == e, column, select)
        da_ref[r] = d_attn.astype(BF16)
        gsel_ref[r] = select
        to = r * groups + own_turn

        @pl.when(to != c)
        def _():
            copy_to(da_ref.at[r], do_ref.at[own_slot], da_s.at[r], da_r.at[own_slot], f, to).start()

        @pl.when(to == c)
        def _():
            do_ref[own_slot] = da_ref[r]

    line2.turn(2)
    leave(0)
    got(dml_gather, f ^ 1)
    leave(1)
    dml_gather[0].relay()
    dml_gather[1].relay()
    leave(2)
    got(dml_gather, f ^ 3)
    leave(3)

    def out_tile(i, _):
        spot = pl.multiple_of(i * LANES, LANES)
        left = mixed_ref[:, :, pl.ds(spot, LANES)].reshape(all_tokens, LANES)
        right = dml_ref[...].reshape(all_tokens, width)
        gwout_ref[pl.ds(spot, LANES), :] = mm_left_t(left, right).astype(BF16)
        return 0

    lax.fori_loop(0, 5, out_tile, 0)
    second_bias = spread_vector(small_ref[:, 4, :], width // n)
    out_ref[...] = (mid_ref[...] + out_sum.total() + second_bias).astype(BF16)
    lax.fori_loop(3, n // 2 - 1, lambda k, u: (line2.turn(k), u)[1], 0)
    line2.finish()
    own = 2 * (c // 2) + lax.rem(c, 2)
    s2_ref[0] = stage2[own]
    s2_ref[1] = stage2[own + 1 - 2 * lax.rem(c, 2)]
    line2.sent()
    pair1.finish()
    for one in attn_sum + back_sum + n2_gather + dml_gather + (out_sum,):
        one.sent()

    def drain(i, _):
        @pl.when(i * groups + own_turn != c)
        def _():
            copy_to(da_ref.at[i], do_ref.at[0], da_s.at[i], da_r.at[0], f, c).wait_send()

        @pl.when(block_of(lax.rem(c, groups), i, groups) != c)
        def _():
            copy_to(da_ref.at[0], do_ref.at[i], da_s.at[0], da_r.at[i], f, c).wait_recv()

        return 0

    lax.fori_loop(0, 4, drain, 0)


def feed(n, x, cot, gates, o, wout, small, w1, w2, w2e):
    t, d = x.shape
    quarter = w1.shape[1]
    line = n // 2
    return pl.pallas_call(
        functools.partial(feed_kernel, n),
        out_shape=[
            sds((t, d), BF16), sds((t, d), F32), sds((640, d), BF16), sds((line, d // n, quarter), BF16),
            sds((2, quarter // n, d), BF16), sds((4, t, LANES), BF16), sds((4, t, LANES), F32), sds((8, d), F32),
        ],
        in_specs=[VMEM] * 6 + [ANY] * 3,
        out_specs=[VMEM] * 8,
        scratch_shapes=[
            pltpu.VMEM((d, quarter), BF16), pltpu.VMEM((n, quarter // n, d), BF16), pltpu.VMEM((4, t, d), BF16),
            pltpu.VMEM((4, t, quarter), BF16), pltpu.VMEM((4, t, quarter), F32), pltpu.VMEM((4, t, quarter), BF16),
            pltpu.VMEM((4, t, 640), BF16), pltpu.VMEM((4, t, d), BF16), pltpu.VMEM((t, d), F32),
            pltpu.VMEM((d, quarter), BF16), pltpu.VMEM((quarter, d), BF16),
            pltpu.VMEM((line, d // n, quarter), BF16),
        ]
        + line_scratch(line, 2, 2 * quarter // n, d)
        + quad_sum_scratch(t // 2, d) * 4
        + quad_sum_scratch(t, d)
        + [DMA((n,))] * 8 + [DMA((line,))] * 2 + line_sems(line, 2)
        + [DMA((3,)), DMA((4,))] * 4 + [DMA((3,)), pltpu.VMEM((4, t, LANES), BF16), DMA((4,)), DMA((4,))],
        compiler_params=pltpu.CompilerParams(
            collective_id=1, has_side_effects=True, vmem_limit_bytes=62 << 20
        ),
        name="feed",
    )(x, cot, gates, o, wout, small, w1, w2, w2e)


class LoneShare:
    def __init__(self, total, out, send, recv):
        self.f, self.c = total.f, total.c
        self.owner = total.place // (total.size // 4)
        self.rel = total.f ^ self.owner
        start = jnp.where(self.rel == 0, (total.place - total.first) * total.subs, 0)
        self.held = total.stage.at[pl.ds(start, total.subs)]
        self.out, self.send, self.recv = out, send, recv
        self.local = pltpu.make_async_copy(self.held, out, recv)

    def copy(self, src, k, to):
        return copy_to(src, self.out, self.send.at[k], self.recv, to, self.c)

    def begin(self):
        @pl.when(self.rel == 0)
        def _():
            self.copy(self.held, 1, self.f ^ 2).start()
            self.copy(self.held, 0, self.f ^ 1).start()
            self.local.start()

    def relay(self):
        @pl.when(self.rel == 2)
        def _():
            self.copy(self.out, 0, self.f).wait_recv()
            self.copy(self.out, 0, self.f ^ 1).start()

    def finish(self):
        @pl.when(self.rel == 0)
        def _():
            self.local.wait()
            self.copy(self.held, 0, self.f).wait_send()
            self.copy(self.held, 1, self.f).wait_send()

        @pl.when(self.rel == 2)
        def _():
            self.copy(self.out, 0, self.f).wait_send()

        @pl.when(lax.rem(self.rel, 2) == 1)
        def _():
            self.copy(self.out, 0, self.f).wait_recv()


def back_kernel(
    n, far_kv,
    do_ref, gwout_ref, s1_ref, s2_ref, qcat_ref, qpos_ref, kv_ref, lse_ref, of_ref,
    tok_ref, p1_ref, ev_ref, gates_ref, gsel_ref, x_ref, small_ref, dmid_ref, vec_ref, table_ref,
    din_ref, gp_ref, gq_ref, g1_ref, g2_ref, go_ref, vq_ref, dkv_ref,
    delta_ref, grad_ref, kcat_ref, acc_ref, ring_ref, pin_ref, drel_ref, dqs_ref, dq_ref, part_ref, dp_ref,
    gpa_ref, gpb_ref, mine_ref, vin_ref,
    s0, s1, s2, s3, s4, s5, s6,
    p0, p1, p2, p3, p4, p5, p6, u1, u2, u5, u6,
    fin2, got2, two_s, two_r, w0, w1, w2, w3, w4, w5, w6, y1, y2, y5, y6, goty, swap_s, swap_r,
    kv_s, kv_r, pin_r, dq_s, dq_r, gp_s, gp_r, gq_s, gq_r, g1_s, g1_r, g2_s, g2_r, go_s, go_r,
    vc_s, vc_r, vf_s, vf_r, loc,
):
    f, c = lax.axis_index("fsdp"), lax.axis_index("ctx")
    groups = n // 4
    seq, turn = c // groups, lax.rem(c, groups)
    tokens, width = x_ref.shape
    scale = 1.0 / math.sqrt(112)
    own_turn, own_slot = holder_of(c, groups)
    rows = width // n
    greet(f, c, 4, n)

    sub_out = p0.shape[0] // max(1, groups // 2)
    cut = gwout_ref.shape[1] // sub_out
    sum_out = LineSum(
        f, c, n, lambda k, sub: gwout_ref.at[k, pl.ds(pl.multiple_of(sub * cut, cut), cut), :],
        p1, p2, p5, p6, pair=(p0, p3, p4), subs=sub_out, lone=True,
    )
    sum_one = LineSum(f, c, n, lambda o, sub: s1_ref.at[o], u1, u2, u5, u6)
    half = gpa_ref.shape[1]
    pair_to = c + 1 - 2 * lax.rem(c, 2)

    def block_rows(ref, k):
        return ref.at[pl.ds(pl.multiple_of(k * rows, rows), rows), :]

    sum_in = LineSum(
        f, c, n, lambda k, sub: block_rows(gpa_ref, k), w1, w2, w5, w6, pair=(w0, w3, w4)
    )
    sum_late = LineSum(f, c, n, lambda o, sub: block_rows(gpb_ref, 2 * o + sub), y1, y2, y5, y6, subs=2)
    swap_two = copy_to(s2_ref.at[1], got2, two_s, two_r, f, pair_to)
    swap_late = copy_to(y2.at[pair_to], goty, swap_s, swap_r, f, pair_to)

    sum_out.begin()
    swap_two.start()

    def prepare(i, _):
        delta_ref[i] = jnp.sum(do_ref[i].astype(F32).T * of_ref[i], axis=0, keepdims=True)
        grad_ref[i] = jnp.zeros((tokens, width + LANES), F32)
        return 0

    lax.fori_loop(0, 4, prepare, 0)
    row_in = lax.broadcasted_iota(jnp.int32, (tokens, tokens), 0)
    col_in = lax.broadcasted_iota(jnp.int32, (tokens, tokens), 1)
    lane = lax.broadcasted_iota(jnp.int32, (tokens, LANES), 1)
    spots = jnp.logical_or(lane == SPOT_A, lane == SPOT_B)
    last_own = block_of(turn, 3, groups)
    mine_ref[...] = vec_ref[...]

    def close_query(i, sine, cosine):
        first = grad_ref[i, :, 0 : width // 2]
        second = grad_ref[i, :, width // 2 : width]
        drel_ref[i, :, 0 : width // 2] = ((first * sine - second * cosine) * scale).astype(BF16)
        drel_ref[i, :, width // 2 : width] = ((first * cosine + second * sine) * scale).astype(BF16)
        d_place = mm(drel_ref[i], p1_ref[:, :, 896:].reshape(width, LANES))
        d_content = jnp.where(spots, 0.0, grad_ref[i, :, width:] * scale)
        dqs_ref[i] = (d_content + d_place).astype(BF16)
        mine_ref[6:7, 0:LANES] += jnp.sum(d_content, axis=0, keepdims=True)
        mine_ref[7:8, 0:LANES] += jnp.sum(d_place, axis=0, keepdims=True)
        block = block_of(turn, i, groups)

        @pl.when(block != c)
        def _():
            copy_to(dqs_ref.at[i], dq_ref.at[seq], dq_s.at[i], dq_r.at[seq], f, block).start()

        @pl.when(block == c)
        def _():
            dq_ref[seq] = dqs_ref[i]

    bit = lax.rem(c, 2)
    pair_last = block_of(turn + 1 - 2 * bit, 3, groups)

    def ring_pair(kb):
        slot = lax.rem(kb, 4)
        return copy_to(ring_ref.at[slot], pin_ref.at[kb // 2], kv_s.at[slot], pin_r.at[kb // 2], f, pair_to)

    def ring_copy(kb):
        slot = lax.rem(kb, 4)
        return copy_to(ring_ref.at[slot], dkv_ref.at[c // 2], kv_s.at[slot], kv_r.at[c // 2], f, kb)

    def ring_local(kb):
        slot = lax.rem(kb, 4)
        return pltpu.make_async_copy(ring_ref.at[slot], dkv_ref.at[c // 2], kv_s.at[slot])

    def sums(kb):
        return jnp.logical_and(lax.rem(kb, 2) == bit, kb <= jnp.maximum(last_own, pair_last))

    def gives(kb):
        return jnp.logical_and(lax.rem(kb, 2) != bit, kb <= last_own)

    def ring_free(kb):
        @pl.when(gives(kb))
        def _():
            ring_pair(kb).wait_send()

        @pl.when(jnp.logical_and(sums(kb), kb != c))
        def _():
            ring_copy(kb).wait_send()

        @pl.when(jnp.logical_and(sums(kb), kb == c))
        def _():
            ring_local(kb).wait()

    def pass_on(kb):
        @pl.when(sums(kb))
        def _():
            total = acc_ref[lax.rem(kb, 2)]
            slot = lax.rem(kb, 4)

            @pl.when(kb <= pair_last)
            def _():
                ring_pair(kb).wait_recv()
                ring_ref[slot] = (total + pin_ref[kb // 2].astype(F32)).astype(BF16)

            @pl.when(kb > pair_last)
            def _():
                ring_ref[slot] = total.astype(BF16)

            @pl.when(kb != c)
            def _():
                ring_copy(kb).start()

            @pl.when(kb == c)
            def _():
                ring_local(kb).start()

    def key_block(kb, _):
        own = [block_of(turn, i, groups) for i in range(4)]
        first = sum((b < kb).astype(jnp.int32) for b in own)
        ready = sum((b == kb).astype(jnp.int32) for b in own)
        sine, cosine = sin_cos(key_places(kv_ref[kb]), table_ref)
        kcat_ref[:, 0 : width // 2] = cosine.astype(BF16)
        kcat_ref[:, width // 2 : width] = sine.astype(BF16)
        kcat_ref[:, width:] = kv_ref[kb, :, 0:128]
        now = lax.rem(kb, 2)
        acc_ref[now] = jnp.zeros((tokens, 256), F32)

        def query_block(i, _):
            gap = (block_of(turn, i, groups) - kb) * tokens
            scores = mm_t(kcat_ref[...], qcat_ref[i])
            probs = jnp.where(row_in <= col_in + gap, jnp.exp(scores - lse_ref[i]), 0.0)
            d_probs = mm_t(kv_ref[kb, :, 128:256], do_ref[i])
            d_scores = (probs * (d_probs - delta_ref[i])).astype(BF16)
            acc_ref[now, :, 0:128] += mm(d_scores, qcat_ref[i, :, width:])
            acc_ref[now, :, 128:256] += mm(probs.astype(BF16), do_ref[i])
            grad_ref[i] += mm_left_t(d_scores, kcat_ref[...])
            return 0

        lax.fori_loop(first, 4, query_block, 0)

        @pl.when(ready == 1)
        def _():
            close_query(first, sine, cosine)

        @pl.when(kb >= 4)
        def _():
            ring_free(kb - 4)

        @pl.when(gives(kb))
        def _():
            ring_ref[lax.rem(kb, 4)] = acc_ref[now].astype(BF16)
            ring_pair(kb).start()

        @pl.when(kb >= 1)
        def _():
            pass_on(kb - 1)

        @pl.when(jnp.logical_and(now == 0, kb >= 2))
        def _():
            sum_one.turn(kb // 2 - 1)


        return 0

    lax.fori_loop(0, n, key_block, 0)
    pass_on(n - 1)
    sum_out.turn(0)
    share_out = LoneShare(sum_out, go_ref, go_s, go_r)
    gathers = []
    def hand_out(held, out, send, recv):
        local = pltpu.make_async_copy(held, out.at[f], loc.at[len(gathers)])
        local.start()
        gather = QuadGather(f, c, out, send, recv)
        gather.begin(held)
        gathers.append((gather, local))

    all_tokens = 4 * tokens
    d_rel = drel_ref[...].reshape(all_tokens, width)
    gpb_ref[:, 896 - half :] = mm_left_t(d_rel, qpos_ref[...].reshape(all_tokens, LANES)).astype(BF16)

    def collect(s, _):
        to = s * groups + own_turn

        @pl.when(to != c)
        def _():
            copy_to(dqs_ref.at[0], dq_ref.at[s], dq_s.at[0], dq_r.at[s], f, c).wait_recv()

        acc_ref[0] = jnp.zeros((tokens, 256), F32)

        def add(k, _):
            giver = 2 * k + bit
            at = (s * groups + giver) // 2
            last = jnp.maximum(block_of(giver, 3, groups), block_of(giver + 1 - 2 * bit, 3, groups))

            @pl.when(last >= c)
            def _():
                @pl.when(s * groups + giver != c)
                def _():
                    copy_to(ring_ref.at[0], dkv_ref.at[at], kv_s.at[0], kv_r.at[at], f, c).wait_recv()

                if far_kv:
                    bring = pltpu.make_async_copy(dkv_ref.at[at], part_ref, loc.at[4])
                    bring.start()
                    bring.wait()
                    acc_ref[0] += part_ref[...].astype(F32)
                else:
                    acc_ref[0] += dkv_ref[at].astype(F32)

            return 0

        lax.fori_loop(0, groups // 2, add, 0)
        dp_ref[s, :, 0:128] = dq_ref[s]
        dp_ref[s, :, 128:256] = acc_ref[0, :, 0:128].astype(BF16)
        d_values = acc_ref[0, :, 128:256]
        for e in range(5):
            values = ev_ref[s, :, e * LANES : (e + 1) * LANES].astype(F32)
            column = jnp.sum(values * d_values, axis=1, keepdims=True) * gates_ref[s, :, 24 + e : 25 + e]
            part = gates_ref[s, :, 16 + e : 17 + e] * d_values
            part = jnp.where(lane == SPOT_A, column, part)
            part = jnp.where(lane == SPOT_B, gsel_ref[s, :, e : e + 1], part)
            dp_ref[s, :, 256 + e * LANES : 384 + e * LANES] = part.astype(BF16)
        return 0

    def ring_drain(k, _):
        ring_free(n - 4 + k)
        return 0

    lax.fori_loop(0, 4, ring_drain, 0)
    lax.fori_loop(0, 4, collect, 0)
    sum_out.turn(1)
    tile = 256

    def weight_tile(i, _):
        spot = pl.multiple_of(i * tile, tile)
        left = tok_ref[:, :, pl.ds(spot, tile)].reshape(all_tokens, tile)
        right = dp_ref[...].reshape(all_tokens, 896)
        result = mm_left_t(left, right).astype(BF16)
        gpa_ref[pl.ds(spot, tile), :] = result[:, 0:half]
        gpb_ref[pl.ds(spot, tile), 0 : 896 - half] = result[:, half:]
        return 0

    lax.fori_loop(0, width // tile, weight_tile, 0)
    sum_in.begin()
    sum_late.turn(0)
    lax.fori_loop(2, n // 2 - 1, lambda k, u: (sum_out.turn(k), u)[1], 0)
    in_sum = QuadSum(f, c, s0, s1, s2, s3, s4, s5, s6)
    for k in (3, 2, 1, 0):
        weights = p1_ref[:, :, 0:896].reshape(width, 896)
        in_sum.put(k, mm_t(dp_ref[f ^ k], weights))
        if k == 2:
            in_sum.cross()
    swap_two.wait()
    fin2[...] = (s2_ref[0].astype(F32) + got2[...].astype(F32)).astype(BF16)
    sum_one.finish()
    sum_late.turn(1)
    sum_out.finish()
    hand_out(fin2, g2_ref, g2_s, g2_r)
    hand_out(u2.at[c // 2], g1_ref, g1_s, g1_r)
    share_out.begin()
    lax.fori_loop(2, n // 2 - 1, lambda k, u: (sum_late.turn(k), u)[1], 0)
    d_norm = in_sum.total()
    xhat, spread = layer_stats(x_ref[...].astype(F32))
    gain = spread_vector(small_ref[:, 0, :], width // n)
    din_ref[...] = dmid_ref[...] + layer_back(d_norm, gain, xhat, spread)
    mine_ref[4:5, :] = jnp.sum(d_norm * xhat, axis=0, keepdims=True)
    mine_ref[5:6, :] = jnp.sum(d_norm, axis=0, keepdims=True)

    def vec_send(k, _):
        to = lax.rem(c + k, n)
        copy_to(mine_ref, vin_ref.at[c], vc_s.at[to], vc_r.at[c], f, to).start()
        return 0

    lax.fori_loop(1, n, vec_send, 0)
    vin_ref[c] = mine_ref[...]
    sum_in.turn(0)
    sum_late.finish()
    swap_late.start()
    lax.fori_loop(1, n // 2 - 1, lambda k, u: (sum_in.turn(k), u)[1], 0)
    for gather, _ in gathers:
        gather.relay()
    share_out.relay()
    swap_late.wait()
    y2[c] = (y2[c].astype(F32) + goty[...].astype(F32)).astype(BF16)
    hand_out(y2.at[c], gq_ref, gq_s, gq_r)
    sum_in.finish()
    hand_out(w2.at[c // 2], gp_ref, gp_s, gp_r)

    def vec_wait(k, _):
        to = lax.rem(c + k, n)
        copy_to(mine_ref, vin_ref.at[to], vc_s.at[to], vc_r.at[to], f, to).wait()
        return 0

    lax.fori_loop(1, n, vec_wait, 0)
    vq_ref[f] = jnp.sum(vin_ref[...], axis=0)
    for k in range(1, 4):
        copy_to(vq_ref.at[f], vq_ref.at[f], vf_s.at[k], vf_r.at[f], f ^ k, c).start()
    for gather, _ in gathers[2:]:
        gather.relay()
    for k in range(1, 4):
        copy_to(vq_ref.at[f ^ k], vq_ref.at[f ^ k], vf_s.at[k], vf_r.at[f ^ k], f, c).wait_recv()
        copy_to(vq_ref.at[f], vq_ref.at[f], vf_s.at[k], vf_r.at[f], f, c).wait_send()
    for one, local in gathers:
        one.got(f ^ 1)
        one.got(f ^ 3)
        one.sent()
        local.wait()
    share_out.finish()
    for one in (sum_one, sum_out, sum_in, sum_late):
        one.sent()
    in_sum.sent()

    def drain(i, _):
        @pl.when(block_of(turn, i, groups) != c)
        def _():
            copy_to(dqs_ref.at[i], dq_ref.at[0], dq_s.at[i], dq_r.at[0], f, c).wait_send()

        return 0

    lax.fori_loop(0, 4, drain, 0)


def early_rows(count):
    return count // 2 if count % 32 == 0 else count


def cuts(count):
    parts = max(1, count // 64)
    return parts if count % (16 * parts) == 0 else 1


def pair_scratch(blocks, subs, rows, cols):
    return [pltpu.VMEM((blocks * subs, rows // subs, cols), BF16)]


def line_scratch(blocks, subs, rows, cols):
    return [
        pltpu.VMEM(((blocks + 1) * subs, rows // subs, cols), BF16),
        pltpu.VMEM((blocks * subs, rows // subs, cols), BF16),
    ]


def line_sems(blocks, subs):
    return [DMA((blocks * subs,)), DMA(((blocks + 1) * subs,))]


def back(n, da, gwout, s1, s2, qcat, qpos, kv, lse, of, tok, p1, ev, gates, gsel, x, small, dmid, vec, table):
    t, d = x.shape
    g = n // 4
    quarter = s1.shape[2]
    rows, out_rows, two_rows = d // n, gwout.shape[1], s2.shape[1]
    half = d // 2
    sub_out = cuts(out_rows)
    lone, line = n // 8, n // 2
    far_kv = g > 4
    return pl.pallas_call(
        functools.partial(back_kernel, n, far_kv),
        out_shape=[
            sds((t, d), F32), sds((4, rows, half), BF16), sds((4, rows, half), BF16), sds((4, rows, quarter), BF16),
            sds((4, two_rows, d), BF16), sds((sub_out, out_rows // sub_out, d), BF16),
            sds((4, 8, d), F32), sds((line, t, 256), BF16),
        ],
        in_specs=[VMEM] * 19,
        out_specs=[VMEM, ANY, ANY, ANY, ANY, ANY, VMEM, ANY if far_kv else VMEM],
        scratch_shapes=[
            pltpu.VMEM((4, 1, t), F32), pltpu.VMEM((4, t, d + LANES), F32),
            pltpu.VMEM((t, d + LANES), BF16), pltpu.VMEM((2, t, 256), F32), pltpu.VMEM((4, t, 256), BF16),
            pltpu.VMEM((line, t, 256), BF16),
            pltpu.VMEM((4, t, d), BF16), pltpu.VMEM((4, t, LANES), BF16), pltpu.VMEM((4, t, LANES), BF16),
            pltpu.VMEM((t, 256), BF16), pltpu.VMEM((4, t, 896), BF16), pltpu.VMEM((d, half), BF16), pltpu.VMEM((d, half), BF16),
            pltpu.VMEM((8, d), F32), pltpu.VMEM((n, 8, d), F32),
        ]
        + quad_sum_scratch(t, d)
        + pair_scratch(lone, sub_out, out_rows, d) + line_scratch(lone, sub_out, out_rows, d)
        + [DMA((lone * sub_out,))] * 2 + line_sems(lone, sub_out)
        + line_scratch(line, 1, rows, quarter) + line_sems(line, 1)
        + [pltpu.VMEM((two_rows, d), BF16), pltpu.VMEM((two_rows, d), BF16), DMA, DMA]
        + pair_scratch(line, 1, rows, half) + line_scratch(line, 1, rows, half)
        + [DMA((line,))] * 2 + line_sems(line, 1)
        + line_scratch(line, 2, 2 * rows, half) + line_sems(line, 2)
        + [pltpu.VMEM((rows, half), BF16), DMA, DMA]
        + [
            DMA((4,)), DMA((line,)), DMA((line,)), DMA((4,)), DMA((4,)), DMA((3,)), DMA((4,)),
            DMA((3,)), DMA((4,)), DMA((3,)), DMA((4,)), DMA((3,)), DMA((4,)), DMA((2,)), DMA, DMA((n,)), DMA((n,)), DMA((4,)), DMA((4,)), DMA((5,)),
        ],
        compiler_params=pltpu.CompilerParams(
            collective_id=2, has_side_effects=True, vmem_limit_bytes=63 << 20
        ),
        name="back",
    )(da, gwout, s1, s2, qcat, qpos, kv, lse, of, tok, p1, ev, gates, gsel, x, small, dmid, vec, table)


def pad_channels(v, group):
    lead = v.shape[:-1]
    v = v.reshape(lead + (112 // group, group))
    v = jnp.pad(v, [(0, 0)] * len(lead) + [(0, 0), (0, group // 7)])
    return v.reshape(lead + (LANES,))


def head_pick(w, f, heads=4):
    w = w.reshape(w.shape[0], heads, -1)
    return lax.dynamic_index_in_dim(w, f, 1, keepdims=False)


def route_lanes(routes):
    hot = routes[..., None] == jnp.arange(8, dtype=jnp.int32)
    return jnp.sum(hot.astype(F32), axis=-2)


def pack_inputs(
    n, f, positions, value_routes, output_routes, ln1_gain, ln1_bias, wq, wk, wrel, u_bias, v_bias,
    wvsel, wv, wosel, wout, ln2_gain, ln2_bias, b1, b2,
):
    t = positions.shape[0]
    rows = wq.shape[0]
    group = math.gcd(112, wout.shape[0])
    masks = jnp.concatenate([route_lanes(value_routes), route_lanes(output_routes)], axis=-1).reshape(t, 64)
    place = jnp.stack([positions // 128, positions % 128], axis=-1).astype(F32)
    aux = jnp.concatenate([masks, place, jnp.zeros((t, 62), F32)], axis=-1).astype(BF16)
    lane = jnp.arange(LANES)
    experts = pad_channels(head_pick(wv, f).reshape(rows, 5, 112), group)
    experts = jnp.where(lane == SPOT_A, head_pick(wvsel, f)[..., None], experts)
    experts = jnp.where(lane == SPOT_B, head_pick(wosel, f)[..., None], experts)
    p1 = jnp.concatenate(
        [
            pad_channels(head_pick(wq, f), group), pad_channels(head_pick(wk, f), group),
            experts.reshape(rows, 640), pad_channels(head_pick(wrel, f), group),
        ],
        axis=-1,
    )
    piece = b1.shape[0] // 4
    vectors = [ln1_gain, ln1_bias, ln2_gain, ln2_bias, b2]
    vectors = [jnp.pad(v, (0, LANES - v.shape[0])) for v in vectors]
    extra = jnp.pad(b1.reshape(-1, piece), ((0, 0), (0, LANES - piece)))
    small = jnp.concatenate([jnp.stack(vectors), extra]).astype(F32)
    small = jnp.pad(small, ((0, 16 - small.shape[0]), (0, 0)))
    pieces = wout.reshape(-1, group, wout.shape[1])
    pieces = jnp.pad(pieces, ((0, 0), (0, group // 7), (0, 0))).reshape(-1, wout.shape[1])
    pieces = jnp.pad(pieces, ((0, -pieces.shape[0] % 16), (0, 0)))
    bias = jnp.concatenate([pad_channels(u_bias, group), pad_channels(v_bias, group)]).astype(F32)
    return aux, p1, small, pieces, bias


def unpack_kernel(
    gp_ref, gq_ref, g1_ref, g2_ref, go_ref, vq_ref, y_ref, din_ref,
    query_ref, key_ref, rel_ref, value_ref, vsel_ref, osel_ref, one_ref, two_ref, out_ref,
    gain1_ref, shift1_ref, gain2_ref, shift2_ref, b2_ref, b1_ref, u_ref, v_ref, y_out, din_out,
    heads_ref,
):
    c = lax.axis_index("ctx")
    rows, half = gp_ref.shape[1], gp_ref.shape[2]
    y_out[...] = y_ref[...]
    din_out[...] = din_ref[...]

    def block(h, k):
        ref, spot = (gp_ref, k * LANES) if k * LANES < half else (gq_ref, k * LANES - half)
        return ref[h, :, spot : spot + LANES].astype(F32).T

    def place(ref, start, piece):
        ref[start : start + 56, :] = piece[0:56]
        ref[start + 56 : start + 112, :] = piece[64:120]

    for h in range(4):
        for ref, k in ((query_ref, 0), (key_ref, 1), (rel_ref, 7)):
            place(ref, 112 * h, block(h, k))
        for e in range(5):
            piece = block(h, 2 + e)
            place(value_ref, 560 * h + 112 * e, piece)
            vsel_ref[5 * h + e : 5 * h + e + 1, :] = piece[SPOT_A : SPOT_A + 1]
            osel_ref[5 * h + e : 5 * h + e + 1, :] = piece[SPOT_B : SPOT_B + 1]
    part = g2_ref.shape[1]
    for h in range(4):
        two_ref[h * part : (h + 1) * part, :] = g2_ref[h].astype(F32)
        for k in range(g1_ref.shape[2] // part):
            spot = (4 * k + h) * part
            one_ref[:, spot : spot + part] = g1_ref[h, :, k * part : (k + 1) * part].astype(F32)
    for k in range(go_ref.shape[0]):
        out_ref[56 * k : 56 * k + 56, :] = go_ref[k, 0:56, :].astype(F32)
    own = pl.ds(pl.multiple_of(c * rows, rows), rows)
    for ref, k in ((gain2_ref, 0), (shift2_ref, 1), (b2_ref, 2), (gain1_ref, 4), (shift1_ref, 5)):
        ref[...] = sum(vq_ref[h, k : k + 1, own] for h in range(4))
    for h in range(4):
        b1_ref[:, h * part : (h + 1) * part] = vq_ref[h, 3:4, own]
    lane = lax.broadcasted_iota(jnp.int32, (8, LANES), 1)
    for ref, k in ((u_ref, 6), (v_ref, 7)):
        for h in range(4):
            heads_ref[h : h + 1, :] = vq_ref[h, k : k + 1, 0:LANES]
        value = heads_ref[...]
        moved = jnp.where(lane < 56, value, pltpu.roll(value, LANES - 8, 1))
        ref[...] = moved[0:4, 0:112]


def unpack(gp, gq, g1, g2, go, vq, y, d_in):
    rows, part, d = gp.shape[1], g2.shape[1], g2.shape[2]
    shapes = [
        (448, rows), (448, rows), (448, rows), (2240, rows), (20, rows), (20, rows), (rows, 4 * g1.shape[2]),
        (4 * part, d), (go.shape[0] * 56, d), (1, rows), (1, rows), (1, rows), (1, rows), (1, rows),
        (1, 4 * part), (4, 112), (4, 112),
    ]
    return pl.pallas_call(
        unpack_kernel,
        out_shape=[sds(shape, F32) for shape in shapes] + [sds(y.shape, BF16), sds(d_in.shape, F32)],
        in_specs=[VMEM] * 8,
        out_specs=[VMEM] * (len(shapes) + 2),
        scratch_shapes=[pltpu.VMEM((8, LANES), F32)],
        compiler_params=pltpu.CompilerParams(vmem_limit_bytes=62 << 20),
        name="unpack",
    )(gp, gq, g1, g2, go, vq, y, d_in)


def drop_pads(v, group):
    lead = v.shape[:-1]
    wide = group * 8 // 7
    return v.reshape(lead + (LANES // wide, wide))[..., :group].reshape(lead + (112,))


def on_device(n, *args):
    (
        x, positions, value_routes, output_routes, ln1_gain, ln1_bias, wq, wk, wrel, u_bias, v_bias,
        wvsel, wv, wosel, wout, ln2_gain, ln2_bias, w1, b1, w2, b2, cot,
    ) = args
    f, c = lax.axis_index("fsdp"), lax.axis_index("ctx")
    d = x.shape[1]
    g = n // 4
    group = math.gcd(112, wout.shape[0])
    aux, p1, small, pieces, bias = pack_inputs(
        n, f, positions, value_routes, output_routes, ln1_gain, ln1_bias, wq, wk, wrel, u_bias, v_bias,
        wvsel, wv, wosel, wout, ln2_gain, ln2_bias, b1, b2,
    )
    table = jnp.asarray(turn_table(d))
    rows, hidden = w1.shape
    part = hidden // n // 4
    w1_own = lax.dynamic_index_in_dim(w1.reshape(rows, n, 4, part), f, 2, keepdims=False).reshape(rows, n * part)
    tok, p1g, smallg, woutg, w2e, cotg, ev, gates, o, qcat, qpos, kv, lse, of = attend(
        n, x, aux, cot, p1, small, pieces, w2, bias, table
    )
    block = 640 // g
    out, dmid, gwout, s1, s2, d_o, gsel, vec = feed(
        n, x, cotg, gates, o, woutg[:, :block].reshape(640, d), smallg, w1_own, w2, w2e
    )
    gwout = gwout.reshape(g, block, d)
    gwout = jnp.pad(gwout, ((0, 0), (0, pieces.shape[0] - block), (0, 0)))
    d_in, gp, gq, g1, g2, go, vq, _ = back(
        n, d_o, gwout, s1, s2, qcat, qpos, kv, lse, of, tok, p1g, ev, gates, gsel, x, smallg, dmid, vec, table
    )
    if group == 56 and part == LANES and rows == LANES:
        (
            g_query, g_key, g_rel, g_value, g_vsel, g_osel, g_one, g_two, g_out,
            gain1, shift1, gain2, shift2, g_b2, g_b1, g_u, g_v, out, d_in,
        ) = unpack(gp, gq, g1, g2, go.reshape(-1, 64, d), vq, out, d_in)
        return (
            out, d_in, gain1[0], shift1[0], g_query.T, g_key.T, g_rel.T, g_u, g_v, g_vsel.T, g_value.T, g_osel.T, g_out,
            gain2[0], shift2[0], g_one, g_b1[0], g_two, g_b2[0],
        )
    gp = jnp.transpose(jnp.concatenate([gp, gq], axis=-1), (1, 0, 2))
    g_query = drop_pads(gp[..., 0:128], group).reshape(rows, 448).astype(F32)
    g_key = drop_pads(gp[..., 128:256], group).reshape(rows, 448).astype(F32)
    g_rel = drop_pads(gp[..., 896:], group).reshape(rows, 448).astype(F32)
    experts = gp[..., 256:896].reshape(rows, 4, 5, LANES)
    g_value = drop_pads(experts, group).reshape(rows, 2240).astype(F32)
    g_vsel = experts[..., SPOT_A].reshape(rows, 20).astype(F32)
    g_osel = experts[..., SPOT_B].reshape(rows, 20).astype(F32)
    g_one = jnp.transpose(g1.reshape(4, rows, n, part), (1, 2, 0, 3)).reshape(rows, hidden).astype(F32)
    g_two = g2.reshape(-1, d).astype(F32)
    g_out = go.reshape(-1, d)[:block].reshape(-1, group * 8 // 7, d)[:, :group].reshape(-1, d).astype(F32)
    sums = jnp.sum(vq, axis=0)
    own = lax.dynamic_slice_in_dim(sums, c * rows, rows, 1)
    g_b1 = lax.dynamic_slice_in_dim(vq[:, 3, :], c * part, part, 1).reshape(-1)
    g_u = drop_pads(vq[:, 6, 0:LANES], group)
    g_v = drop_pads(vq[:, 7, 0:LANES], group)
    return (
        out, d_in, own[4], own[5], g_query, g_key, g_rel, g_u, g_v, g_vsel, g_value, g_osel, g_out,
        own[0], own[1], g_one, g_b1, g_two, own[2],
    )


def solution(mesh):
    both = ("fsdp", "ctx")
    row, vector, matrix = P(both, None), P("ctx"), P("ctx", None)
    in_specs = (
        row, P(both), P(both, None, None), P(both, None, None), vector, vector, matrix, matrix, matrix,
        P(), P(), matrix, matrix, matrix, matrix, vector, vector, matrix, vector, matrix, vector, row,
    )
    out_specs = (
        row, row, vector, vector, matrix, matrix, matrix, P(), P(), matrix, matrix, matrix, matrix,
        vector, vector, matrix, vector, matrix, vector,
    )
    return jax.shard_map(
        functools.partial(on_device, mesh.shape["ctx"]),
        mesh=mesh, in_specs=in_specs, out_specs=out_specs, check_vma=False,
    )
```

```python
import functools
import math

import jax
import jax.numpy as jnp
import numpy as np
from jax import lax
from jax.experimental import pallas as pl
from jax.experimental.pallas import tpu as pltpu
from jax.sharding import PartitionSpec as P

MESH = pl.DeviceIdType.MESH
F32 = jnp.float32
BF16 = jnp.bfloat16
LN_EPS = 1e-05
MASKED = -1e30
LANES = 128
SPOT_A, SPOT_B = 63, 127
VMEM = pl.BlockSpec(memory_space=pltpu.VMEM)
ANY = pl.BlockSpec(memory_space=pl.ANY)
DMA = pltpu.SemaphoreType.DMA


def turn_coefficients():
    nodes = (np.cos(np.pi * (np.arange(400) + 0.5) / 400) + 1) / 8
    root = np.sqrt(nodes)
    powers = nodes[:, None] ** np.arange(7)[None, :]
    sine = np.linalg.lstsq(powers, np.sin(2 * np.pi * root) / root, rcond=None)[0]
    cosine = np.linalg.lstsq(powers, np.cos(2 * np.pi * root), rcond=None)[0]
    return [float(v) for v in sine], [float(v) for v in cosine]


SIN_TURN, COS_TURN = turn_coefficients()


def horner(coefs, v):
    total = coefs[-1]
    for coef in coefs[-2::-1]:
        total = total * v + coef
    return total


def turn_table(model_width):
    freq = 10000.0 ** (-np.arange(0, model_width, 2, dtype=np.float64) / model_width) / (2 * np.pi)
    mantissa, exponent = np.frexp(freq)
    coarse = np.ldexp(np.floor(mantissa * 256) / 256, exponent)
    table = np.zeros((8, model_width // 2), np.float32)
    table[0] = coarse
    table[1] = freq - coarse
    return table


def sin_cos(places, table_ref):
    coarse = places * table_ref[0:1, :]
    part = (coarse - jnp.round(coarse)) + places * table_ref[1:2, :]
    part = part - jnp.round(part)
    square = part * part
    return horner(SIN_TURN, square) * part, horner(COS_TURN, square)


def mm(left, right):
    return lax.dot_general(left, right, (((1,), (0,)), ((), ())), preferred_element_type=F32)


def mm_t(left, right):
    return lax.dot_general(left, right, (((1,), (1,)), ((), ())), preferred_element_type=F32)


def mm_left_t(left, right):
    return lax.dot_general(left, right, (((0,), (0,)), ((), ())), preferred_element_type=F32)


def copy_to(src, dst, send, recv, f, c):
    return pltpu.make_async_remote_copy(
        src_ref=src, dst_ref=dst, send_sem=send, recv_sem=recv, device_id=(f, c), device_id_type=MESH
    )


def greet(f, c, fsdp, n):
    barrier = pltpu.get_barrier_semaphore()

    def one(k, _):
        pl.semaphore_signal(barrier, inc=1, device_id=(f, lax.rem(c + k, n)), device_id_type=MESH)
        return 0

    lax.fori_loop(1, n, one, 0)
    for k in range(1, fsdp):
        pl.semaphore_signal(barrier, inc=1, device_id=(f ^ k, c), device_id_type=MESH)
    pl.semaphore_wait(barrier, n - 1 + fsdp - 1)


class LineGather:
    def __init__(self, f, c, n, own, at, recv, right, left, pair, subs=1, lone=False):
        self.f, self.c, self.n, self.size = f, c, n, n // 2
        self.place, self.bit = c // 2, lax.rem(c, 2)
        self.own, self.at = own, at
        self.recv, self.right, self.left, self.pair = recv, right, left, pair
        self.subs, self.lone = subs, lone

    def valid(self, o):
        ok = jnp.logical_and(o >= 0, o < self.size)
        if self.lone:
            span = self.size // 4
            ok = jnp.logical_and(ok, jnp.logical_and(o >= self.f * span, o < (self.f + 1) * span))
        return ok

    def slot(self, block):
        return block - self.f * (self.n // 4) if self.lone else block

    def copy(self, src, block, sub, sems, c):
        slot = self.slot(block)
        i = slot * self.subs + sub
        return copy_to(src, self.at(slot, sub), sems.at[i], self.recv.at[i], self.f, c)

    def held(self, block, sub):
        return self.at(self.slot(block), sub)

    def each(self, work):
        if self.subs == 1:
            work(0)
        else:
            lax.fori_loop(0, self.subs, lambda sub, u: (work(sub), u)[1], 0)

    def spread(self, src, block, sub, go_right, go_left):
        @pl.when(go_right)
        def _():
            self.copy(src, block, sub, self.right, self.c + 2).start()

        @pl.when(go_left)
        def _():
            self.copy(src, block, sub, self.left, self.c - 2).start()

        self.copy(src, block, sub, self.pair, self.c + 1 - 2 * self.bit).start()

    def begin(self, local):
        @pl.when(self.valid(self.place))
        def _():
            self.each(
                lambda sub: self.spread(
                    self.own(sub), self.c, sub, self.place < self.size - 1, self.place > 0
                )
            )
            local()

    def arrived(self, block, sub):
        self.copy(self.held(block, sub), block, sub, self.pair, self.c).wait_recv()

    def step(self, t):
        for sign in (-1, 1):
            o = self.place + sign * t
            block = 2 * o + self.bit

            @pl.when(self.valid(o))
            def _():
                def one(sub):
                    self.arrived(block, sub)
                    self.spread(
                        self.held(block, sub), block, sub,
                        jnp.logical_and(sign < 0, self.place < self.size - 1),
                        jnp.logical_and(sign > 0, self.place > 0),
                    )

                self.each(one)

    def steps(self, first=1):
        lax.fori_loop(first, self.size, lambda t, u: (self.step(t), u)[1], 0)

    def finish(self):
        def one(o, _):
            block = 2 * o + self.bit

            def piece(sub):
                self.arrived(2 * o + 1 - self.bit, sub)
                source = self.held(block, sub)
                self.copy(source, block, sub, self.pair, self.c).wait_send()

                @pl.when(jnp.logical_and(o <= self.place, self.place < self.size - 1))
                def _():
                    self.copy(source, block, sub, self.right, self.c).wait_send()

                @pl.when(jnp.logical_and(o >= self.place, self.place > 0))
                def _():
                    self.copy(source, block, sub, self.left, self.c).wait_send()

            @pl.when(self.valid(o))
            def _():
                self.each(piece)

            return 0

        lax.fori_loop(0, self.size, one, 0)


class QuadGather:
    def __init__(self, f, c, out, send, recv, part=None):
        self.f, self.c, self.out, self.send, self.recv = f, c, out, send, recv
        self.part = part

    def at(self, slot):
        return self.out.at[slot] if self.part is None else self.out.at[slot, self.part, :]

    def copy(self, slot, k, to, src=None):
        src = self.at(slot) if src is None else src
        return copy_to(src, self.at(slot), self.send.at[k], self.recv.at[slot], to, self.c)

    def begin(self, src=None):
        self.copy(self.f, 1, self.f ^ 2, src).start()
        self.copy(self.f, 0, self.f ^ 1, src).start()

    def got(self, slot):
        self.copy(slot, 0, self.f).wait_recv()

    def relay(self):
        self.got(self.f ^ 2)
        self.copy(self.f ^ 2, 2, self.f ^ 1).start()

    def sent(self):
        for k in range(3):
            self.copy(self.f, k, self.f).wait_send()


def spread_vector(rows, width):
    count = rows.shape[0]
    total = count * width
    lane = lax.broadcasted_iota(jnp.int32, (LANES, total), 0)
    column = lax.broadcasted_iota(jnp.int32, (LANES, total), 1)
    onehot = jnp.where(lane == lax.rem(column, width), 1.0, 0.0).astype(BF16)
    wide = mm(rows.astype(BF16), onehot)
    row = lax.broadcasted_iota(jnp.int32, (count, total), 0)
    column = lax.broadcasted_iota(jnp.int32, (count, total), 1)
    return jnp.sum(jnp.where(column // width == row, wide, 0.0), axis=0, keepdims=True)


def block_of(j, i, groups):
    return i * groups + jnp.where(lax.rem(i, 2) == 0, j, groups - 1 - j)


def holder_of(block, groups):
    row, within = block // groups, lax.rem(block, groups)
    return jnp.where(lax.rem(row, 2) == 0, within, groups - 1 - within), row


def key_places(kv):
    return kv[:, SPOT_A : SPOT_A + 1].astype(F32) * 128.0 + kv[:, SPOT_B : SPOT_B + 1].astype(F32)


def attend_kernel(
    n,
    x_ref, aux_ref, cot_ref, p1_ref, small_ref, wout_ref, w2_ref, bias_ref, table_ref,
    tok_ref, p1g_ref, smallg_ref, woutg_ref, w2e_ref, cotg_ref, ev_ref, gates_ref, o_ref,
    qcat_ref, qpos_ref, kv_ref, lse_ref, of_ref,
    qs_ref, kvs_ref, qr_ref, os_ref, kcat_ref, vt_ref, m_ref, l_ref,
    sm_s, sm_r, p_r, p_a, p_b, p_c, w_r, w_a, w_b, w_c, h_r, h_a, h_b, h_c,
    t_s, t_r, c_s, c_r, q_s, q_r, kv_s, kv_r, kv_p, o_s, o_r, loc,
):
    f, c = lax.axis_index("fsdp"), lax.axis_index("ctx")
    groups = n // 4
    seq, turn = c // groups, lax.rem(c, groups)
    tokens, width = x_ref.shape
    scale = 1.0 / math.sqrt(112)
    greet(f, c, 4, n)

    def small_send(k, _):
        to = lax.rem(c + k, n)
        copy_to(small_ref, smallg_ref.at[c], sm_s.at[to], sm_r.at[c], f, to).start()
        return 0

    lax.fori_loop(1, n, small_send, 0)
    smallg_ref[c] = small_ref[...]
    gather_p = LineGather(f, c, n, lambda sub: p1_ref, lambda k, sub: p1g_ref.at[k], p_r, p_a, p_b, p_c)

    def own_p():
        p1g_ref[c] = p1_ref[...]

    gather_p.begin(own_p)
    wout_copy = pltpu.make_async_copy(wout_ref, woutg_ref.at[c - f * groups], loc.at[0])
    subs = w_r.shape[0] // groups
    piece = wout_ref.shape[0] // subs
    gather_w = LineGather(
        f, c, n,
        lambda sub: wout_ref.at[pl.ds(pl.multiple_of(sub * piece, piece), piece), :],
        lambda k, sub: woutg_ref.at[k, pl.ds(pl.multiple_of(sub * piece, piece), piece), :],
        w_r, w_a, w_b, w_c, subs=subs, lone=True,
    )
    early = w2e_ref.shape[1]
    own2 = w2_ref.at[pl.ds(pl.multiple_of(f * (w2_ref.shape[0] // 4), 16), early), :]
    w2_copy = pltpu.make_async_copy(own2, w2e_ref.at[c], loc.at[2])
    gather_h = LineGather(f, c, n, lambda sub: own2, lambda k, sub: w2e_ref.at[k], h_r, h_a, h_b, h_c)
    cot_copy = pltpu.make_async_copy(cot_ref, cotg_ref.at[f], loc.at[1])
    cot_copy.start()

    hidden = x_ref[...].astype(F32)
    offsets = hidden - jnp.mean(hidden, axis=1, keepdims=True)
    spread = jnp.mean(offsets * offsets, axis=1, keepdims=True)
    xhat = offsets * lax.rsqrt(spread + LN_EPS)

    def small_wait(k, _):
        to = lax.rem(c + k, n)
        copy_to(small_ref, smallg_ref.at[to], sm_s.at[to], sm_r.at[to], f, to).wait()
        return 0

    lax.fori_loop(1, n, small_wait, 0)
    gain = spread_vector(smallg_ref[:, 0, :], width // n)
    shift = spread_vector(smallg_ref[:, 1, :], width // n)
    tok_ref[f, :, 0:width] = (xhat * gain + shift).astype(BF16)
    tok_ref[f, :, width:] = aux_ref[...]
    tok_gather = QuadGather(f, c, tok_ref, t_s, t_r)
    tok_gather.begin()
    gather_p.steps()
    tok_gather.relay()
    gather_p.finish()
    tok_gather.got(f ^ 1)
    tok_gather.got(f ^ 3)
    tok_gather.sent()
    cot_gather = QuadGather(f, c, cotg_ref, c_s, c_r)
    cot_gather.begin(cot_ref)

    lane = lax.broadcasted_iota(jnp.int32, (tokens, LANES), 1)
    source = lax.broadcasted_iota(jnp.int32, (LANES, LANES), 0)
    target = lax.broadcasted_iota(jnp.int32, (LANES, LANES), 1)
    wanted = f * 16 + lax.rem(target, 8) + jnp.where(target < 16, 8, 0)
    pick = jnp.where(
        jnp.logical_and(source == wanted, jnp.logical_and(target < 32, lax.rem(target, 8) < 5)), 1.0, 0.0
    ).astype(BF16)
    own_turn, own_slot = holder_of(c, groups)
    bit = lax.rem(c, 2)
    spots = jnp.logical_or(lane == SPOT_A, lane == SPOT_B)

    def project(t, _):
        s = lax.rem(seq + 1 + t, 4)
        normed = tok_ref[s, :, 0:width]
        aux = tok_ref[s, :, width:]
        weights = p1g_ref[...].reshape(width, p1g_ref.shape[2])
        qk = mm(normed, weights[:, 0:256])
        experts = mm(normed, weights[:, 256:896])
        ev_ref[s] = experts.astype(BF16)
        logits = jnp.zeros((tokens, LANES), F32)
        for e in range(5):
            for spot, first in ((SPOT_B, 0), (SPOT_A, 16)):
                column = experts[:, e * LANES + spot : e * LANES + spot + 1]
                logits = jnp.where(
                    jnp.logical_or(lane == first + e, lane == first + 8 + e), column, logits
                )
        sig = jax.nn.sigmoid(logits)
        gates = mm(aux, pick) * jnp.where(lax.rem(lane, 16) >= 8, sig * (1.0 - sig), sig)
        gates_ref[s] = gates
        values = jnp.zeros((tokens, LANES), F32)
        for e in range(5):
            values = values + gates[:, 16 + e : 17 + e] * experts[:, e * LANES : (e + 1) * LANES]
        values = jnp.where(spots, 0.0, values)
        high, rest = aux[:, 64:65].astype(F32), aux[:, 65:66].astype(F32)

        def with_place(v):
            return jnp.where(lane == SPOT_A, high, jnp.where(lane == SPOT_B, rest, v)).astype(BF16)

        qs_ref[s] = with_place(qk[:, 0:128])
        kvs_ref[s, :, 0:128] = with_place(qk[:, 128:256])
        kvs_ref[s, :, 128:256] = values.astype(BF16)
        to = s * groups + own_turn

        @pl.when(to != c)
        def _():
            copy_to(qs_ref.at[s], qr_ref.at[own_slot], q_s.at[s], q_r.at[own_slot], f, to).start()

        @pl.when(to == c)
        def _():
            qr_ref[own_slot] = qs_ref[s]

        def kv_send(k, _):
            to = s * groups + 2 * k + bit

            @pl.when(to != c)
            def _():
                copy_to(kvs_ref.at[s], kv_ref.at[c], kv_s.at[to], kv_r.at[c], f, to).start()

            @pl.when(to == c)
            def _():
                kv_ref[c] = kvs_ref[s]

            return 0

        lax.fori_loop(0, groups // 2, kv_send, 0)
        return 0

    gather_h.begin(w2_copy.start)
    lax.fori_loop(0, 4, project, 0)
    gather_w.begin(wout_copy.start)

    def kv_wait(block):
        copy_to(kvs_ref.at[0], kv_ref.at[block], kv_s.at[0], kv_r.at[block], f, c).wait_recv()

    def kv_pass(block):
        return copy_to(kv_ref.at[block], kv_ref.at[block], kv_p.at[block // 2], kv_r.at[block], f, c + 1 - 2 * bit)

    def hand_on(m):
        block = 2 * m + bit

        @pl.when(block != c)
        def _():
            kv_wait(block)

        kv_pass(block).start()

    def prepare(i, _):
        block = block_of(turn, i, groups)

        @pl.when(block != c)
        def _():
            copy_to(qs_ref.at[0], qr_ref.at[i], q_s.at[0], q_r.at[i], f, c).wait_recv()

        places = key_places(qr_ref[i])
        query = jnp.where(spots, 0.0, qr_ref[i].astype(F32))
        q_position = (query + bias_ref[pl.ds(4 + f, 1), :]).astype(BF16)
        qpos_ref[i] = q_position
        qcat_ref[i, :, width:] = ((query + bias_ref[pl.ds(f, 1), :]) * scale).astype(BF16)
        rel = p1g_ref[:, :, 896:].reshape(width, LANES)
        rel_query = mm_t(q_position, rel)
        sine, cosine = sin_cos(places, table_ref)
        first, second = rel_query[:, : width // 2], rel_query[:, width // 2 :]
        qcat_ref[i, :, 0 : width // 2] = ((first * sine + second * cosine) * scale).astype(BF16)
        qcat_ref[i, :, width // 2 : width] = ((second * sine - first * cosine) * scale).astype(BF16)
        m_ref[i] = jnp.full((1, tokens), MASKED, F32)
        l_ref[i] = jnp.zeros((1, tokens), F32)
        of_ref[i] = jnp.zeros((LANES, tokens), F32)
        return 0

    lax.fori_loop(0, 4, prepare, 0)
    hand_on(0)
    row_in = lax.broadcasted_iota(jnp.int32, (tokens, tokens), 0)
    col_in = lax.broadcasted_iota(jnp.int32, (tokens, tokens), 1)

    def give(i):
        total = l_ref[i]
        result = of_ref[i] / total
        of_ref[i] = result
        lse_ref[i] = m_ref[i] + jnp.log(total)
        os_ref[i] = result.T.astype(BF16)
        block = block_of(turn, i, groups)

        @pl.when(block != c)
        def _():
            copy_to(os_ref.at[i], o_ref.at[seq], o_s.at[i], o_r.at[seq], f, block).start()

        @pl.when(block == c)
        def _():
            o_ref[seq] = os_ref[i]

    def key_block(kb, _):
        own = [block_of(turn, i, groups) for i in range(4)]
        first = sum((b < kb).astype(jnp.int32) for b in own)
        ready = sum((b == kb).astype(jnp.int32) for b in own)

        @pl.when(lax.rem(kb, 2) != bit)
        def _():
            kv_wait(kb)

        @pl.when(jnp.logical_and(lax.rem(kb, 2) == 0, kb < n - 2))
        def _():
            hand_on(kb // 2 + 1)

        sine, cosine = sin_cos(key_places(kv_ref[kb]), table_ref)
        kcat_ref[:, 0 : width // 2] = cosine.astype(BF16)
        kcat_ref[:, width // 2 : width] = sine.astype(BF16)
        kcat_ref[:, width:] = kv_ref[kb, :, 0:128]
        vt_ref[...] = kv_ref[kb, :, 128:256].astype(F32).T.astype(BF16)

        def query_block(i, _):
            gap = (block_of(turn, i, groups) - kb) * tokens
            scores = mm_t(kcat_ref[...], qcat_ref[i])
            scores = jnp.where(row_in <= col_in + gap, scores, MASKED)
            before = m_ref[i]
            best = jnp.maximum(before, jnp.max(scores, axis=0, keepdims=True))
            shrink = jnp.exp(before - best)
            probs = jnp.exp(scores - best)
            m_ref[i] = best
            l_ref[i] = l_ref[i] * shrink + jnp.sum(probs, axis=0, keepdims=True)
            of_ref[i] = of_ref[i] * shrink + mm(vt_ref[...], probs.astype(BF16))
            return 0

        lax.fori_loop(first, 4, query_block, 0)

        @pl.when(ready == 1)
        def _():
            give(first)

        @pl.when(kb == n // 2 - 1)
        def _():
            cot_gather.relay()

        @pl.when(jnp.logical_and(kb > 0, kb < n // 2))
        def _():
            gather_w.step(kb)

        @pl.when(kb < n // 2 - 1)
        def _():
            gather_h.step(kb + 1)

        return 0

    lax.fori_loop(0, n, key_block, 0)
    cot_gather.got(f ^ 1)
    cot_gather.got(f ^ 3)
    cot_gather.sent()
    gather_w.finish()
    gather_h.finish()
    w2_copy.wait()

    @pl.when(gather_w.valid(c // 2))
    def _():
        wout_copy.wait()

    cot_copy.wait()

    def drain(s, _):
        to = s * groups + own_turn

        @pl.when(to != c)
        def _():
            copy_to(qs_ref.at[s], qr_ref.at[own_slot], q_s.at[s], q_r.at[0], f, to).wait_send()
            copy_to(os_ref.at[0], o_ref.at[s], o_s.at[0], o_r.at[s], f, to).wait_recv()

        @pl.when(block_of(turn, s, groups) != c)
        def _():
            copy_to(os_ref.at[s], o_ref.at[s], o_s.at[s], o_r.at[0], f, to).wait_send()

        return 0

    lax.fori_loop(0, 4, drain, 0)

    def kv_drain(k, _):
        to = 2 * k + bit

        @pl.when(to != c)
        def _():
            copy_to(kvs_ref.at[0], kv_ref.at[0], kv_s.at[to], kv_r.at[0], f, c).wait_send()

        kv_pass(to).wait_send()
        return 0

    lax.fori_loop(0, n // 2, kv_drain, 0)


def sds(shape, dtype):
    return jax.ShapeDtypeStruct(shape, dtype)


def attend(n, x, aux, cot, p1, small, wout, w2, bias, table):
    t, d = x.shape
    rows = p1.shape[0]
    out_rows = wout.shape[0]
    g = n // 4
    subs = cuts(out_rows)
    return pl.pallas_call(
        functools.partial(attend_kernel, n),
        out_shape=[
            sds((4, t, d + LANES), BF16), sds((n, rows, d), BF16), sds((n, 16, LANES), F32),
            sds((g, out_rows, d), BF16), sds((n, early_rows(w2.shape[0] // 4), d), BF16), sds((4, t, d), BF16), sds((4, t, 640), BF16),
            sds((4, t, LANES), F32), sds((4, t, LANES), BF16), sds((4, t, d + LANES), BF16),
            sds((4, t, LANES), BF16), sds((n, t, 256), BF16), sds((4, 1, t), F32), sds((4, LANES, t), F32),
        ],
        in_specs=[VMEM, VMEM, ANY, VMEM, VMEM, ANY, ANY, VMEM, VMEM],
        out_specs=[VMEM, VMEM, VMEM, ANY, ANY, ANY] + [VMEM] * 8,
        scratch_shapes=[
            pltpu.VMEM((4, t, LANES), BF16), pltpu.VMEM((4, t, 256), BF16), pltpu.VMEM((4, t, LANES), BF16),
            pltpu.VMEM((4, t, LANES), BF16), pltpu.VMEM((t, d + LANES), BF16),
            pltpu.VMEM((LANES, t), BF16), pltpu.VMEM((4, 1, t), F32), pltpu.VMEM((4, 1, t), F32),
            DMA((n,)), DMA((n,)), DMA((n,)), DMA((n,)), DMA((n,)), DMA((n,)),
            DMA((g * subs,)), DMA((g * subs,)), DMA((g * subs,)), DMA((g * subs,)),
            DMA((n,)), DMA((n,)), DMA((n,)), DMA((n,)),
            DMA((3,)), DMA((4,)), DMA((3,)), DMA((4,)), DMA((4,)), DMA((4,)),
            DMA((n,)), DMA((n,)), DMA((n // 2,)), DMA((4,)), DMA((4,)), DMA((3,)),
        ],
        compiler_params=pltpu.CompilerParams(
            collective_id=0, has_side_effects=True, vmem_limit_bytes=56 << 20
        ),
        name="attend",
    )(x, aux, cot, p1, small, wout, w2, bias, table)


class QuadSum:
    def __init__(self, f, c, core_out, core_in, x_out, x_in, keep, send, recv):
        self.f, self.c = f, c
        self.core_out, self.core_in, self.x_out, self.x_in = core_out, core_in, x_out, x_in
        self.keep, self.send, self.recv = keep, send, recv

    def core(self, k):
        return copy_to(
            self.core_out.at[k], self.core_in.at[k], self.send.at[k], self.recv.at[k], self.f ^ 1, self.c
        )

    def across(self):
        return copy_to(self.x_out, self.x_in, self.send.at[2], self.recv.at[2], self.f ^ 2, self.c)

    def put(self, k, value):
        if k in (1, 3):
            self.core_out[k // 2] = value.astype(BF16)
            self.core(k // 2).start()
        else:
            self.keep[k // 2] = value

    def cross(self):
        self.core(1).wait_recv()
        self.x_out[...] = (self.keep[1] + self.core_in[1].astype(F32)).astype(BF16)
        self.across().start()

    def total(self):
        self.core(0).wait_recv()
        self.across().wait_recv()
        return self.keep[0] + self.core_in[0].astype(F32) + self.x_in[...].astype(F32)

    def sent(self):
        self.core(0).wait_send()
        self.core(1).wait_send()
        self.across().wait_send()


def quad_sum_scratch(t, d):
    return [
        pltpu.VMEM((2, t, d), BF16), pltpu.VMEM((2, t, d), BF16), pltpu.VMEM((t, d), BF16),
        pltpu.VMEM((t, d), BF16), pltpu.VMEM((2, t, d), F32), DMA((3,)), DMA((3,)),
    ]


def layer_stats(v):
    offsets = v - jnp.mean(v, axis=1, keepdims=True)
    scale = lax.rsqrt(jnp.mean(offsets * offsets, axis=1, keepdims=True) + LN_EPS)
    return offsets * scale, scale


def layer_back(grad, gain, xhat, scale):
    inner = grad * gain
    return scale * (
        inner - jnp.mean(inner, axis=1, keepdims=True) - xhat * jnp.mean(inner * xhat, axis=1, keepdims=True)
    )


def gelu_pair(v):
    k = math.sqrt(2.0 / math.pi)
    square = v * v
    t = jnp.tanh(k * v * (1.0 + 0.044715 * square))
    half = 0.5 * (1.0 + t)
    return v * half, half + 0.5 * v * (1.0 - t * t) * (k * (1.0 + 3 * 0.044715 * square))


class PairSum:
    def __init__(self, f, c, n, source, got, out, send, recv):
        self.f, self.c, self.size = f, c, n // 2
        self.bit = lax.rem(c, 2)
        self.source, self.got, self.out, self.send, self.recv = source, got, out, send, recv

    def copy(self, o):
        return copy_to(
            self.source(2 * o + 1 - self.bit), self.got.at[o], self.send.at[o], self.recv.at[o],
            self.f, self.c + 1 - 2 * self.bit,
        )

    def begin(self):
        lax.fori_loop(0, self.size, lambda o, u: (self.copy(o).start(), u)[1], 0)

    def finish(self):
        def one(o, _):
            self.copy(o).wait_recv()
            term = self.source(2 * o + self.bit)[...].astype(F32)
            self.out[o] = (term + self.got[o].astype(F32)).astype(BF16)
            self.copy(o).wait_send()
            return 0

        lax.fori_loop(0, self.size, one, 0)


class LineSum:
    def __init__(self, f, c, n, source, inbox, stage, line_s, line_r, pair=None, subs=1, lone=False):
        self.f, self.c, self.n, self.size = f, c, n, n // 2
        self.place, self.bit = c // 2, lax.rem(c, 2)
        self.source = source
        self.inbox, self.stage, self.line_s, self.line_r = inbox, stage, line_s, line_r
        self.pair = pair
        self.subs = subs
        self.span = self.size // 4 if lone else self.size
        self.first = f * self.span if lone else 0

    def valid(self, o):
        return jnp.logical_and(o >= self.first, o < self.first + self.span)

    def index(self, o, sub):
        return (o - self.first) * self.subs + sub

    def pair_copy(self, o, sub):
        i = self.index(o, sub)
        got, send, recv = self.pair
        return copy_to(
            self.source(2 * (o - self.first) + 1 - self.bit, sub), got.at[i], send.at[i], recv.at[i],
            self.f, self.c + 1 - 2 * self.bit,
        )

    def line_copy(self, i, slot, c):
        return copy_to(self.stage.at[i], self.inbox.at[slot], self.line_s.at[i], self.line_r.at[slot], self.f, c)

    def each(self, work):
        def one(k, _):
            work(self.first + k // self.subs, lax.rem(k, self.subs))
            return 0

        lax.fori_loop(0, self.span * self.subs, one, 0)

    def begin(self):
        self.each(lambda o, sub: self.pair_copy(o, sub).start())

    def begin_block(self, block):
        @pl.when(lax.rem(block, 2) != self.bit)
        def _():
            self.pair_copy(block // 2, 0).start()

    def term(self, o, sub):
        if self.pair is None:
            return self.source(o - self.first, sub)[...].astype(F32)
        self.pair_copy(o, sub).wait_recv()
        own = self.source(2 * (o - self.first) + self.bit, sub)[...].astype(F32)
        return own + self.pair[0][self.index(o, sub)].astype(F32)

    def extra(self, sub):
        return self.span * self.subs + sub

    def move(self, o, sub, go_right):
        i = self.index(o, sub)
        total = self.term(o, sub)
        starts = self.place == 0 if go_right else self.place == self.size - 1

        @pl.when(starts)
        def _():
            self.stage[i] = total.astype(BF16)

        @pl.when(jnp.logical_not(starts))
        def _():
            self.line_copy(i, i, self.c).wait_recv()
            self.stage[i] = (total + self.inbox[i].astype(F32)).astype(BF16)

        if go_right:
            self.line_copy(i, i, self.c + 2).start()
        else:
            slot = jnp.where(o == self.place - 1, self.extra(sub), i)
            self.line_copy(i, slot, self.c - 2).start()

    def turn(self, time):
        far = self.size - 1 - (time - self.place)
        near = time - (self.size - 1 - self.place)

        def one(sub, _):
            @pl.when(jnp.logical_and(jnp.logical_and(far < self.size, self.valid(far)), far > self.place))
            def _():
                self.move(far, sub, True)

            @pl.when(jnp.logical_and(jnp.logical_and(near >= 0, self.valid(near)), near < self.place))
            def _():
                self.move(near, sub, False)

            return 0

        lax.fori_loop(0, self.subs, one, 0)

    def settle(self, sub):
        i = self.index(self.place, sub)
        own = self.term(self.place, sub)
        left = self.place > 0
        right = self.place < self.size - 1

        @pl.when(left)
        def _():
            self.line_copy(i, i, self.c).wait_recv()

        @pl.when(right)
        def _():
            self.line_copy(i, self.extra(sub), self.c).wait_recv()

        @pl.when(jnp.logical_and(left, right))
        def _():
            self.stage[i] = (
                own + self.inbox[i].astype(F32) + self.inbox[self.extra(sub)].astype(F32)
            ).astype(BF16)

        @pl.when(jnp.logical_and(left, jnp.logical_not(right)))
        def _():
            self.stage[i] = (own + self.inbox[i].astype(F32)).astype(BF16)

        @pl.when(jnp.logical_and(right, jnp.logical_not(left)))
        def _():
            self.stage[i] = (own + self.inbox[self.extra(sub)].astype(F32)).astype(BF16)

    def finish(self):
        @pl.when(self.valid(self.place))
        def _():
            lax.fori_loop(0, self.subs, lambda sub, u: (self.settle(sub), u)[1], 0)

    def sent(self):
        def one(o, sub):
            if self.pair is not None:
                self.pair_copy(o, sub).wait_send()

            @pl.when(o != self.place)
            def _():
                self.line_copy(self.index(o, sub), 0, self.c).wait_send()

        self.each(one)


def feed_kernel(
    n,
    x_ref, cot_ref, gates_ref, o_ref, wout_ref, small_ref, w1_ref, w2_ref, w2e_ref,
    out_ref, dmid_ref, gwout_ref, s1_ref, s2_ref, do_ref, gsel_ref, vec_ref,
    w1g, w2g, n2_ref, act_ref, slope_ref, dpre_ref, mixed_ref, dml_ref, mid_ref, gw1_ref, gw2_ref, got1, in2, stage2,
    a0, a1, a2, a3, a4, a5, a6, i0, i1, i2, i3, i4, i5, i6, b0, b1, b2, b3, b4, b5, b6, j0, j1, j2, j3, j4, j5, j6,
    e0, e1, e2, e3, e4, e5, e6,
    w1_r, w1_a, w1_b, w1_c, w2_r, w2_a, w2_b, w2_c, h1_s, h1_r, h2_s, h2_r, n_s, n_r, d_s, d_r, m_s, m_r, k_s, k_r, loc, da_ref, da_s, da_r,
):
    f, c = lax.axis_index("fsdp"), lax.axis_index("ctx")
    tokens, width = x_ref.shape
    quarter = w1g.shape[1]
    groups = n // 4
    own_turn, own_slot = holder_of(c, groups)
    greet(f, c, 4, n)
    rows1, rows2 = width // n, quarter // n

    def rows_of(ref, count):
        return lambda k: ref.at[pl.ds(pl.multiple_of(k * count, count), count), :]

    early = w2e_ref.shape[1]
    at1 = rows_of(w1g, rows1)
    gather1 = LineGather(f, c, n, lambda sub: w1_ref, lambda k, sub: at1(k), w1_r, w1_a, w1_b, w1_c)
    local1 = pltpu.make_async_copy(w1_ref, at1(c), loc.at[0])
    bring2 = pltpu.make_async_copy(w2e_ref, w2g.at[:, 0:early, :], loc.at[1])
    gather1.begin(local1.start)
    bring2.start()
    gather2 = None
    if early < rows2:
        own2 = w2_ref.at[pl.ds(pl.multiple_of(f * rows2 + early, 16), rows2 - early), :]
        at2 = lambda k: w2g.at[k, early:rows2, :]
        gather2 = LineGather(f, c, n, lambda sub: own2, lambda k, sub: at2(k), w2_r, w2_a, w2_b, w2_c)
        local2 = pltpu.make_async_copy(own2, at2(c), loc.at[2])
    pair1 = PairSum(f, c, n, rows_of(gw1_ref, rows1), got1, s1_ref, h1_s, h1_r)
    line2 = LineSum(f, c, n, lambda o, sub: rows_of(gw2_ref, rows2)(2 * o + sub), in2, stage2, h2_s, h2_r, subs=2)
    attn_sum = (QuadSum(f, c, a0, a1, a2, a3, a4, a5, a6), QuadSum(f, c, i0, i1, i2, i3, i4, i5, i6))
    back_sum = (QuadSum(f, c, b0, b1, b2, b3, b4, b5, b6), QuadSum(f, c, j0, j1, j2, j3, j4, j5, j6))
    span = tokens // 2
    halves = (slice(0, span), slice(span, tokens))
    out_sum = QuadSum(f, c, e0, e1, e2, e3, e4, e5, e6)

    for half, one in zip(halves, attn_sum):
        for k in (3, 2, 1, 0):
            r = f ^ k
            for e in range(5):
                mixed_ref[r, half, e * LANES : (e + 1) * LANES] = (
                    gates_ref[r, half, e : e + 1] * o_ref[r, half, :].astype(F32)
                ).astype(BF16)
            one.put(k, mm(mixed_ref[r, half, :], wout_ref[...]))
            if k == 2:
                one.cross()
    gather1.step(1)
    if gather2 is not None:
        gather2.begin(local2.start)
    gain = spread_vector(small_ref[:, 2, :], width // n)
    shift = spread_vector(small_ref[:, 3, :], width // n)
    n2_gather = (QuadGather(f, c, n2_ref, n_s, n_r, halves[0]), QuadGather(f, c, n2_ref, m_s, m_r, halves[1]))
    for half, one, gather in zip(halves, attn_sum, n2_gather):
        middle = x_ref[half, :].astype(F32) + one.total()
        mid_ref[half, :] = middle
        xhat, _ = layer_stats(middle)
        n2_ref[f, half, :] = (xhat * gain + shift).astype(BF16)
        gather.begin()
    gather1.steps(2)
    gather1.finish()
    local1.wait()
    first_bias = spread_vector(small_ref[:, pl.ds(5 + f, 1), :].reshape(n, LANES), rows2)

    def enter(k):
        r = f ^ k
        act, slope = gelu_pair(mm(n2_ref[r], w1g[...]) + first_bias)
        act_ref[r] = act.astype(BF16)
        slope_ref[r] = slope

    def got(pair, slot):
        for gather in pair:
            gather.got(slot)

    enter(0)
    got(n2_gather, f ^ 1)
    n2_gather[0].relay()
    if gather2 is not None:
        gather2.step(1)
    enter(1)
    n2_gather[1].relay()
    if gather2 is not None:
        gather2.step(2)
    enter(2)
    if gather2 is not None:
        gather2.steps(3)
    got(n2_gather, f ^ 3)
    enter(3)
    tile = 256
    all_tokens = 4 * tokens

    def weight_tile(left_ref, right_ref, result_ref):
        def one(i, _):
            spot = pl.multiple_of(i * tile, tile)
            left = left_ref[:, :, pl.ds(spot, tile)].reshape(all_tokens, tile)
            right = right_ref[...].reshape(all_tokens, right_ref.shape[2])
            result_ref[pl.ds(spot, tile), :] = mm_left_t(left, right).astype(BF16)
            return 0

        lax.fori_loop(0, left_ref.shape[2] // tile, one, 0)

    weight_tile(act_ref, cot_ref, gw2_ref)
    line2.turn(0)
    if gather2 is not None:
        gather2.finish()
        local2.wait()
    bring2.wait()
    second = w2g[...].reshape(quarter, width)

    for k in (3, 2, 1, 0):
        r = f ^ k
        d_act = mm_t(cot_ref[r], second)
        dpre_ref[r] = (d_act * slope_ref[r]).astype(BF16)
        term = mm_t(dpre_ref[r], w1g[...])
        for half, one in zip(halves, back_sum):
            one.put(k, term[half])
        if k == 2:
            for one in back_sum:
                one.cross()
    weight_tile(n2_ref, dpre_ref, gw1_ref)
    pair1.begin()
    line2.turn(1)
    for k in (3, 2, 1, 0):
        out_sum.put(k, mm(act_ref[f ^ k], second))
    vec_ref[...] = jnp.zeros_like(vec_ref)
    dml_gather = (QuadGather(f, c, dml_ref, d_s, d_r, halves[0]), QuadGather(f, c, dml_ref, k_s, k_r, halves[1]))
    for half, one, gather in zip(halves, back_sum, dml_gather):
        d_norm = one.total()
        xhat, scale = layer_stats(mid_ref[half, :])
        d_middle = cot_ref[f, half, :].astype(F32) + layer_back(d_norm, gain, xhat, scale)
        dmid_ref[half, :] = d_middle
        dml_ref[f, half, :] = d_middle.astype(BF16)
        gather.begin()
        vec_ref[0:1, :] += jnp.sum(d_norm * xhat, axis=0, keepdims=True)
        vec_ref[1:2, :] += jnp.sum(d_norm, axis=0, keepdims=True)
    out_sum.cross()
    vec_ref[2:3, :] = jnp.sum(cot_ref[f].astype(F32), axis=0, keepdims=True)
    total = jnp.zeros((1, quarter), F32)
    for r in range(4):
        total = total + jnp.sum(dpre_ref[r].astype(F32), axis=0, keepdims=True)
    vec_ref[3:4, :] = total
    lane = lax.broadcasted_iota(jnp.int32, (tokens, LANES), 1)

    def leave(k):
        r = f ^ k
        d_attn = jnp.zeros((tokens, LANES), F32)
        select = jnp.zeros((tokens, LANES), F32)
        result = o_ref[r].astype(F32)
        d_mixed = mm_t(dml_ref[r], wout_ref[...])
        for e in range(5):
            part = d_mixed[:, e * LANES : (e + 1) * LANES]
            d_attn = d_attn + gates_ref[r, :, e : e + 1] * part
            column = jnp.sum(result * part, axis=1, keepdims=True) * gates_ref[r, :, 8 + e : 9 + e]
            select = jnp.where(lane == e, column, select)
        da_ref[r] = d_attn.astype(BF16)
        gsel_ref[r] = select
        to = r * groups + own_turn

        @pl.when(to != c)
        def _():
            copy_to(da_ref.at[r], do_ref.at[own_slot], da_s.at[r], da_r.at[own_slot], f, to).start()

        @pl.when(to == c)
        def _():
            do_ref[own_slot] = da_ref[r]

    line2.turn(2)
    leave(0)
    got(dml_gather, f ^ 1)
    leave(1)
    dml_gather[0].relay()
    dml_gather[1].relay()
    leave(2)
    got(dml_gather, f ^ 3)
    leave(3)

    def out_tile(i, _):
        spot = pl.multiple_of(i * LANES, LANES)
        left = mixed_ref[:, :, pl.ds(spot, LANES)].reshape(all_tokens, LANES)
        right = dml_ref[...].reshape(all_tokens, width)
        gwout_ref[pl.ds(spot, LANES), :] = mm_left_t(left, right).astype(BF16)
        return 0

    lax.fori_loop(0, 5, out_tile, 0)
    second_bias = spread_vector(small_ref[:, 4, :], width // n)
    out_ref[...] = (mid_ref[...] + out_sum.total() + second_bias).astype(BF16)
    lax.fori_loop(3, n // 2 - 1, lambda k, u: (line2.turn(k), u)[1], 0)
    line2.finish()
    own = 2 * (c // 2) + lax.rem(c, 2)
    s2_ref[0] = stage2[own]
    s2_ref[1] = stage2[own + 1 - 2 * lax.rem(c, 2)]
    line2.sent()
    pair1.finish()
    for one in attn_sum + back_sum + n2_gather + dml_gather + (out_sum,):
        one.sent()

    def drain(i, _):
        @pl.when(i * groups + own_turn != c)
        def _():
            copy_to(da_ref.at[i], do_ref.at[0], da_s.at[i], da_r.at[0], f, c).wait_send()

        @pl.when(block_of(lax.rem(c, groups), i, groups) != c)
        def _():
            copy_to(da_ref.at[0], do_ref.at[i], da_s.at[0], da_r.at[i], f, c).wait_recv()

        return 0

    lax.fori_loop(0, 4, drain, 0)


def feed(n, x, cot, gates, o, wout, small, w1, w2, w2e):
    t, d = x.shape
    quarter = w1.shape[1]
    line = n // 2
    return pl.pallas_call(
        functools.partial(feed_kernel, n),
        out_shape=[
            sds((t, d), BF16), sds((t, d), F32), sds((640, d), BF16), sds((line, d // n, quarter), BF16),
            sds((2, quarter // n, d), BF16), sds((4, t, LANES), BF16), sds((4, t, LANES), F32), sds((8, d), F32),
        ],
        in_specs=[VMEM] * 6 + [ANY] * 3,
        out_specs=[VMEM] * 8,
        scratch_shapes=[
            pltpu.VMEM((d, quarter), BF16), pltpu.VMEM((n, quarter // n, d), BF16), pltpu.VMEM((4, t, d), BF16),
            pltpu.VMEM((4, t, quarter), BF16), pltpu.VMEM((4, t, quarter), F32), pltpu.VMEM((4, t, quarter), BF16),
            pltpu.VMEM((4, t, 640), BF16), pltpu.VMEM((4, t, d), BF16), pltpu.VMEM((t, d), F32),
            pltpu.VMEM((d, quarter), BF16), pltpu.VMEM((quarter, d), BF16),
            pltpu.VMEM((line, d // n, quarter), BF16),
        ]
        + line_scratch(line, 2, 2 * quarter // n, d)
        + quad_sum_scratch(t // 2, d) * 4
        + quad_sum_scratch(t, d)
        + [DMA((n,))] * 8 + [DMA((line,))] * 2 + line_sems(line, 2)
        + [DMA((3,)), DMA((4,))] * 4 + [DMA((3,)), pltpu.VMEM((4, t, LANES), BF16), DMA((4,)), DMA((4,))],
        compiler_params=pltpu.CompilerParams(
            collective_id=1, has_side_effects=True, vmem_limit_bytes=62 << 20
        ),
        name="feed",
    )(x, cot, gates, o, wout, small, w1, w2, w2e)


class LoneShare:
    def __init__(self, total, out, send, recv):
        self.f, self.c = total.f, total.c
        self.owner = total.place // (total.size // 4)
        self.rel = total.f ^ self.owner
        start = jnp.where(self.rel == 0, (total.place - total.first) * total.subs, 0)
        self.held = total.stage.at[pl.ds(start, total.subs)]
        self.out, self.send, self.recv = out, send, recv
        self.local = pltpu.make_async_copy(self.held, out, recv)

    def copy(self, src, k, to):
        return copy_to(src, self.out, self.send.at[k], self.recv, to, self.c)

    def begin(self):
        @pl.when(self.rel == 0)
        def _():
            self.copy(self.held, 1, self.f ^ 2).start()
            self.copy(self.held, 0, self.f ^ 1).start()
            self.local.start()

    def relay(self):
        @pl.when(self.rel == 2)
        def _():
            self.copy(self.out, 0, self.f).wait_recv()
            self.copy(self.out, 0, self.f ^ 1).start()

    def finish(self):
        @pl.when(self.rel == 0)
        def _():
            self.local.wait()
            self.copy(self.held, 0, self.f).wait_send()
            self.copy(self.held, 1, self.f).wait_send()

        @pl.when(self.rel == 2)
        def _():
            self.copy(self.out, 0, self.f).wait_send()

        @pl.when(lax.rem(self.rel, 2) == 1)
        def _():
            self.copy(self.out, 0, self.f).wait_recv()


def back_kernel(
    n, far_kv,
    do_ref, gwout_ref, s1_ref, s2_ref, qcat_ref, qpos_ref, kv_ref, lse_ref, of_ref,
    tok_ref, p1_ref, ev_ref, gates_ref, gsel_ref, x_ref, small_ref, dmid_ref, vec_ref, table_ref,
    din_ref, gp_ref, gq_ref, g1_ref, g2_ref, go_ref, vq_ref, dkv_ref,
    delta_ref, grad_ref, kcat_ref, acc_ref, ring_ref, pin_ref, drel_ref, dqs_ref, dq_ref, part_ref, dp_ref,
    gpa_ref, gpb_ref, mine_ref, vin_ref,
    s0, s1, s2, s3, s4, s5, s6,
    p0, p1, p2, p3, p4, p5, p6, u1, u2, u5, u6,
    fin2, got2, two_s, two_r, w0, w1, w2, w3, w4, w5, w6, y1, y2, y5, y6, goty, swap_s, swap_r,
    kv_s, kv_r, pin_r, dq_s, dq_r, gp_s, gp_r, gq_s, gq_r, g1_s, g1_r, g2_s, g2_r, go_s, go_r,
    vc_s, vc_r, vf_s, vf_r, loc,
):
    f, c = lax.axis_index("fsdp"), lax.axis_index("ctx")
    groups = n // 4
    seq, turn = c // groups, lax.rem(c, groups)
    tokens, width = x_ref.shape
    scale = 1.0 / math.sqrt(112)
    own_turn, own_slot = holder_of(c, groups)
    rows = width // n
    greet(f, c, 4, n)

    sub_out = p0.shape[0] // max(1, groups // 2)
    cut = gwout_ref.shape[1] // sub_out
    sum_out = LineSum(
        f, c, n, lambda k, sub: gwout_ref.at[k, pl.ds(pl.multiple_of(sub * cut, cut), cut), :],
        p1, p2, p5, p6, pair=(p0, p3, p4), subs=sub_out, lone=True,
    )
    sum_one = LineSum(f, c, n, lambda o, sub: s1_ref.at[o], u1, u2, u5, u6)
    half = gpa_ref.shape[1]
    pair_to = c + 1 - 2 * lax.rem(c, 2)

    def block_rows(ref, k):
        return ref.at[pl.ds(pl.multiple_of(k * rows, rows), rows), :]

    sum_in = LineSum(
        f, c, n, lambda k, sub: block_rows(gpa_ref, k), w1, w2, w5, w6, pair=(w0, w3, w4)
    )
    sum_late = LineSum(f, c, n, lambda o, sub: block_rows(gpb_ref, 2 * o + sub), y1, y2, y5, y6, subs=2)
    swap_two = copy_to(s2_ref.at[1], got2, two_s, two_r, f, pair_to)
    swap_late = copy_to(y2.at[pair_to], goty, swap_s, swap_r, f, pair_to)

    sum_out.begin()
    swap_two.start()

    def prepare(i, _):
        delta_ref[i] = jnp.sum(do_ref[i].astype(F32).T * of_ref[i], axis=0, keepdims=True)
        grad_ref[i] = jnp.zeros((tokens, width + LANES), F32)
        return 0

    lax.fori_loop(0, 4, prepare, 0)
    row_in = lax.broadcasted_iota(jnp.int32, (tokens, tokens), 0)
    col_in = lax.broadcasted_iota(jnp.int32, (tokens, tokens), 1)
    lane = lax.broadcasted_iota(jnp.int32, (tokens, LANES), 1)
    spots = jnp.logical_or(lane == SPOT_A, lane == SPOT_B)
    last_own = block_of(turn, 3, groups)
    mine_ref[...] = vec_ref[...]

    def close_query(i, sine, cosine):
        first = grad_ref[i, :, 0 : width // 2]
        second = grad_ref[i, :, width // 2 : width]
        drel_ref[i, :, 0 : width // 2] = ((first * sine - second * cosine) * scale).astype(BF16)
        drel_ref[i, :, width // 2 : width] = ((first * cosine + second * sine) * scale).astype(BF16)
        d_place = mm(drel_ref[i], p1_ref[:, :, 896:].reshape(width, LANES))
        d_content = jnp.where(spots, 0.0, grad_ref[i, :, width:] * scale)
        dqs_ref[i] = (d_content + d_place).astype(BF16)
        mine_ref[6:7, 0:LANES] += jnp.sum(d_content, axis=0, keepdims=True)
        mine_ref[7:8, 0:LANES] += jnp.sum(d_place, axis=0, keepdims=True)
        block = block_of(turn, i, groups)

        @pl.when(block != c)
        def _():
            copy_to(dqs_ref.at[i], dq_ref.at[seq], dq_s.at[i], dq_r.at[seq], f, block).start()

        @pl.when(block == c)
        def _():
            dq_ref[seq] = dqs_ref[i]

    bit = lax.rem(c, 2)
    pair_last = block_of(turn + 1 - 2 * bit, 3, groups)

    def ring_pair(kb):
        slot = lax.rem(kb, 4)
        return copy_to(ring_ref.at[slot], pin_ref.at[kb // 2], kv_s.at[slot], pin_r.at[kb // 2], f, pair_to)

    def ring_copy(kb):
        slot = lax.rem(kb, 4)
        return copy_to(ring_ref.at[slot], dkv_ref.at[c // 2], kv_s.at[slot], kv_r.at[c // 2], f, kb)

    def ring_local(kb):
        slot = lax.rem(kb, 4)
        return pltpu.make_async_copy(ring_ref.at[slot], dkv_ref.at[c // 2], kv_s.at[slot])

    def sums(kb):
        return jnp.logical_and(lax.rem(kb, 2) == bit, kb <= jnp.maximum(last_own, pair_last))

    def gives(kb):
        return jnp.logical_and(lax.rem(kb, 2) != bit, kb <= last_own)

    def ring_free(kb):
        @pl.when(gives(kb))
        def _():
            ring_pair(kb).wait_send()

        @pl.when(jnp.logical_and(sums(kb), kb != c))
        def _():
            ring_copy(kb).wait_send()

        @pl.when(jnp.logical_and(sums(kb), kb == c))
        def _():
            ring_local(kb).wait()

    def pass_on(kb):
        @pl.when(sums(kb))
        def _():
            total = acc_ref[lax.rem(kb, 2)]
            slot = lax.rem(kb, 4)

            @pl.when(kb <= pair_last)
            def _():
                ring_pair(kb).wait_recv()
                ring_ref[slot] = (total + pin_ref[kb // 2].astype(F32)).astype(BF16)

            @pl.when(kb > pair_last)
            def _():
                ring_ref[slot] = total.astype(BF16)

            @pl.when(kb != c)
            def _():
                ring_copy(kb).start()

            @pl.when(kb == c)
            def _():
                ring_local(kb).start()

    def key_block(kb, _):
        own = [block_of(turn, i, groups) for i in range(4)]
        first = sum((b < kb).astype(jnp.int32) for b in own)
        ready = sum((b == kb).astype(jnp.int32) for b in own)
        sine, cosine = sin_cos(key_places(kv_ref[kb]), table_ref)
        kcat_ref[:, 0 : width // 2] = cosine.astype(BF16)
        kcat_ref[:, width // 2 : width] = sine.astype(BF16)
        kcat_ref[:, width:] = kv_ref[kb, :, 0:128]
        now = lax.rem(kb, 2)
        acc_ref[now] = jnp.zeros((tokens, 256), F32)

        def query_block(i, _):
            gap = (block_of(turn, i, groups) - kb) * tokens
            scores = mm_t(kcat_ref[...], qcat_ref[i])
            probs = jnp.where(row_in <= col_in + gap, jnp.exp(scores - lse_ref[i]), 0.0)
            d_probs = mm_t(kv_ref[kb, :, 128:256], do_ref[i])
            d_scores = (probs * (d_probs - delta_ref[i])).astype(BF16)
            acc_ref[now, :, 0:128] += mm(d_scores, qcat_ref[i, :, width:])
            acc_ref[now, :, 128:256] += mm(probs.astype(BF16), do_ref[i])
            grad_ref[i] += mm_left_t(d_scores, kcat_ref[...])
            return 0

        lax.fori_loop(first, 4, query_block, 0)

        @pl.when(ready == 1)
        def _():
            close_query(first, sine, cosine)

        @pl.when(kb >= 4)
        def _():
            ring_free(kb - 4)

        @pl.when(gives(kb))
        def _():
            ring_ref[lax.rem(kb, 4)] = acc_ref[now].astype(BF16)
            ring_pair(kb).start()

        @pl.when(kb >= 1)
        def _():
            pass_on(kb - 1)

        @pl.when(jnp.logical_and(now == 1, kb < n - 1))
        def _():
            sum_one.turn(kb // 2)


        return 0

    lax.fori_loop(0, n, key_block, 0)
    pass_on(n - 1)
    sum_out.turn(0)
    share_out = LoneShare(sum_out, go_ref, go_s, go_r)
    gathers = []
    def hand_out(held, out, send, recv):
        local = pltpu.make_async_copy(held, out.at[f], loc.at[len(gathers)])
        local.start()
        gather = QuadGather(f, c, out, send, recv)
        gather.begin(held)
        gathers.append((gather, local))

    all_tokens = 4 * tokens
    d_rel = drel_ref[...].reshape(all_tokens, width)
    gpb_ref[:, 896 - half :] = mm_left_t(d_rel, qpos_ref[...].reshape(all_tokens, LANES)).astype(BF16)

    def collect(s, _):
        to = s * groups + own_turn

        @pl.when(to != c)
        def _():
            copy_to(dqs_ref.at[0], dq_ref.at[s], dq_s.at[0], dq_r.at[s], f, c).wait_recv()

        acc_ref[0] = jnp.zeros((tokens, 256), F32)

        def add(k, _):
            giver = 2 * k + bit
            at = (s * groups + giver) // 2
            last = jnp.maximum(block_of(giver, 3, groups), block_of(giver + 1 - 2 * bit, 3, groups))

            @pl.when(last >= c)
            def _():
                @pl.when(s * groups + giver != c)
                def _():
                    copy_to(ring_ref.at[0], dkv_ref.at[at], kv_s.at[0], kv_r.at[at], f, c).wait_recv()

                if far_kv:
                    bring = pltpu.make_async_copy(dkv_ref.at[at], part_ref, loc.at[4])
                    bring.start()
                    bring.wait()
                    acc_ref[0] += part_ref[...].astype(F32)
                else:
                    acc_ref[0] += dkv_ref[at].astype(F32)

            return 0

        lax.fori_loop(0, groups // 2, add, 0)
        dp_ref[s, :, 0:128] = dq_ref[s]
        dp_ref[s, :, 128:256] = acc_ref[0, :, 0:128].astype(BF16)
        d_values = acc_ref[0, :, 128:256]
        for e in range(5):
            values = ev_ref[s, :, e * LANES : (e + 1) * LANES].astype(F32)
            column = jnp.sum(values * d_values, axis=1, keepdims=True) * gates_ref[s, :, 24 + e : 25 + e]
            part = gates_ref[s, :, 16 + e : 17 + e] * d_values
            part = jnp.where(lane == SPOT_A, column, part)
            part = jnp.where(lane == SPOT_B, gsel_ref[s, :, e : e + 1], part)
            dp_ref[s, :, 256 + e * LANES : 384 + e * LANES] = part.astype(BF16)
        return 0

    def ring_drain(k, _):
        ring_free(n - 4 + k)
        return 0

    lax.fori_loop(0, 4, ring_drain, 0)
    lax.fori_loop(0, 4, collect, 0)
    sum_out.turn(1)
    tile = 256

    def weight_tile(i, _):
        spot = pl.multiple_of(i * tile, tile)
        left = tok_ref[:, :, pl.ds(spot, tile)].reshape(all_tokens, tile)
        right = dp_ref[...].reshape(all_tokens, 896)
        result = mm_left_t(left, right).astype(BF16)
        gpa_ref[pl.ds(spot, tile), :] = result[:, 0:half]
        gpb_ref[pl.ds(spot, tile), 0 : 896 - half] = result[:, half:]
        return 0

    lax.fori_loop(0, width // tile, weight_tile, 0)
    sum_in.begin()
    sum_late.turn(0)
    lax.fori_loop(2, n // 2 - 1, lambda k, u: (sum_out.turn(k), u)[1], 0)
    in_sum = QuadSum(f, c, s0, s1, s2, s3, s4, s5, s6)
    for k in (3, 2, 1, 0):
        weights = p1_ref[:, :, 0:896].reshape(width, 896)
        in_sum.put(k, mm_t(dp_ref[f ^ k], weights))
        if k == 2:
            in_sum.cross()
    swap_two.wait()
    fin2[...] = (s2_ref[0].astype(F32) + got2[...].astype(F32)).astype(BF16)
    sum_one.finish()
    sum_late.turn(1)
    sum_out.finish()
    hand_out(fin2, g2_ref, g2_s, g2_r)
    hand_out(u2.at[c // 2], g1_ref, g1_s, g1_r)
    share_out.begin()
    lax.fori_loop(2, n // 2 - 1, lambda k, u: (sum_late.turn(k), u)[1], 0)
    d_norm = in_sum.total()
    xhat, spread = layer_stats(x_ref[...].astype(F32))
    gain = spread_vector(small_ref[:, 0, :], width // n)
    din_ref[...] = dmid_ref[...] + layer_back(d_norm, gain, xhat, spread)
    mine_ref[4:5, :] = jnp.sum(d_norm * xhat, axis=0, keepdims=True)
    mine_ref[5:6, :] = jnp.sum(d_norm, axis=0, keepdims=True)

    def vec_send(k, _):
        to = lax.rem(c + k, n)
        copy_to(mine_ref, vin_ref.at[c], vc_s.at[to], vc_r.at[c], f, to).start()
        return 0

    lax.fori_loop(1, n, vec_send, 0)
    vin_ref[c] = mine_ref[...]
    sum_in.turn(0)
    sum_late.finish()
    swap_late.start()
    lax.fori_loop(1, n // 2 - 1, lambda k, u: (sum_in.turn(k), u)[1], 0)
    for gather, _ in gathers:
        gather.relay()
    share_out.relay()
    swap_late.wait()
    y2[c] = (y2[c].astype(F32) + goty[...].astype(F32)).astype(BF16)
    hand_out(y2.at[c], gq_ref, gq_s, gq_r)
    sum_in.finish()
    hand_out(w2.at[c // 2], gp_ref, gp_s, gp_r)

    def vec_wait(k, _):
        to = lax.rem(c + k, n)
        copy_to(mine_ref, vin_ref.at[to], vc_s.at[to], vc_r.at[to], f, to).wait()
        return 0

    lax.fori_loop(1, n, vec_wait, 0)
    vq_ref[f] = jnp.sum(vin_ref[...], axis=0)
    for k in range(1, 4):
        copy_to(vq_ref.at[f], vq_ref.at[f], vf_s.at[k], vf_r.at[f], f ^ k, c).start()
    for gather, _ in gathers[2:]:
        gather.relay()
    for k in range(1, 4):
        copy_to(vq_ref.at[f ^ k], vq_ref.at[f ^ k], vf_s.at[k], vf_r.at[f ^ k], f, c).wait_recv()
        copy_to(vq_ref.at[f], vq_ref.at[f], vf_s.at[k], vf_r.at[f], f, c).wait_send()
    for one, local in gathers:
        one.got(f ^ 1)
        one.got(f ^ 3)
        one.sent()
        local.wait()
    share_out.finish()
    for one in (sum_one, sum_out, sum_in, sum_late):
        one.sent()
    in_sum.sent()

    def drain(i, _):
        @pl.when(block_of(turn, i, groups) != c)
        def _():
            copy_to(dqs_ref.at[i], dq_ref.at[0], dq_s.at[i], dq_r.at[0], f, c).wait_send()

        return 0

    lax.fori_loop(0, 4, drain, 0)


def early_rows(count):
    return count // 2 if count % 32 == 0 else count


def cuts(count):
    parts = max(1, count // 64)
    return parts if count % (16 * parts) == 0 else 1


def pair_scratch(blocks, subs, rows, cols):
    return [pltpu.VMEM((blocks * subs, rows // subs, cols), BF16)]


def line_scratch(blocks, subs, rows, cols):
    return [
        pltpu.VMEM(((blocks + 1) * subs, rows // subs, cols), BF16),
        pltpu.VMEM((blocks * subs, rows // subs, cols), BF16),
    ]


def line_sems(blocks, subs):
    return [DMA((blocks * subs,)), DMA(((blocks + 1) * subs,))]


def back(n, da, gwout, s1, s2, qcat, qpos, kv, lse, of, tok, p1, ev, gates, gsel, x, small, dmid, vec, table):
    t, d = x.shape
    g = n // 4
    quarter = s1.shape[2]
    rows, out_rows, two_rows = d // n, gwout.shape[1], s2.shape[1]
    half = d // 2
    sub_out = cuts(out_rows)
    lone, line = n // 8, n // 2
    far_kv = g > 4
    return pl.pallas_call(
        functools.partial(back_kernel, n, far_kv),
        out_shape=[
            sds((t, d), F32), sds((4, rows, half), BF16), sds((4, rows, half), BF16), sds((4, rows, quarter), BF16),
            sds((4, two_rows, d), BF16), sds((sub_out, out_rows // sub_out, d), BF16),
            sds((4, 8, d), F32), sds((line, t, 256), BF16),
        ],
        in_specs=[VMEM] * 19,
        out_specs=[VMEM, ANY, ANY, ANY, ANY, ANY, VMEM, ANY if far_kv else VMEM],
        scratch_shapes=[
            pltpu.VMEM((4, 1, t), F32), pltpu.VMEM((4, t, d + LANES), F32),
            pltpu.VMEM((t, d + LANES), BF16), pltpu.VMEM((2, t, 256), F32), pltpu.VMEM((4, t, 256), BF16),
            pltpu.VMEM((line, t, 256), BF16),
            pltpu.VMEM((4, t, d), BF16), pltpu.VMEM((4, t, LANES), BF16), pltpu.VMEM((4, t, LANES), BF16),
            pltpu.VMEM((t, 256), BF16), pltpu.VMEM((4, t, 896), BF16), pltpu.VMEM((d, half), BF16), pltpu.VMEM((d, half), BF16),
            pltpu.VMEM((8, d), F32), pltpu.VMEM((n, 8, d), F32),
        ]
        + quad_sum_scratch(t, d)
        + pair_scratch(lone, sub_out, out_rows, d) + line_scratch(lone, sub_out, out_rows, d)
        + [DMA((lone * sub_out,))] * 2 + line_sems(lone, sub_out)
        + line_scratch(line, 1, rows, quarter) + line_sems(line, 1)
        + [pltpu.VMEM((two_rows, d), BF16), pltpu.VMEM((two_rows, d), BF16), DMA, DMA]
        + pair_scratch(line, 1, rows, half) + line_scratch(line, 1, rows, half)
        + [DMA((line,))] * 2 + line_sems(line, 1)
        + line_scratch(line, 2, 2 * rows, half) + line_sems(line, 2)
        + [pltpu.VMEM((rows, half), BF16), DMA, DMA]
        + [
            DMA((4,)), DMA((line,)), DMA((line,)), DMA((4,)), DMA((4,)), DMA((3,)), DMA((4,)),
            DMA((3,)), DMA((4,)), DMA((3,)), DMA((4,)), DMA((3,)), DMA((4,)), DMA((2,)), DMA, DMA((n,)), DMA((n,)), DMA((4,)), DMA((4,)), DMA((5,)),
        ],
        compiler_params=pltpu.CompilerParams(
            collective_id=2, has_side_effects=True, vmem_limit_bytes=63 << 20
        ),
        name="back",
    )(da, gwout, s1, s2, qcat, qpos, kv, lse, of, tok, p1, ev, gates, gsel, x, small, dmid, vec, table)


def pad_channels(v, group):
    lead = v.shape[:-1]
    v = v.reshape(lead + (112 // group, group))
    v = jnp.pad(v, [(0, 0)] * len(lead) + [(0, 0), (0, group // 7)])
    return v.reshape(lead + (LANES,))


def head_pick(w, f, heads=4):
    w = w.reshape(w.shape[0], heads, -1)
    return lax.dynamic_index_in_dim(w, f, 1, keepdims=False)


def route_lanes(routes):
    hot = routes[..., None] == jnp.arange(8, dtype=jnp.int32)
    return jnp.sum(hot.astype(F32), axis=-2)


def pack_inputs(
    n, f, positions, value_routes, output_routes, ln1_gain, ln1_bias, wq, wk, wrel, u_bias, v_bias,
    wvsel, wv, wosel, wout, ln2_gain, ln2_bias, b1, b2,
):
    t = positions.shape[0]
    rows = wq.shape[0]
    group = math.gcd(112, wout.shape[0])
    masks = jnp.concatenate([route_lanes(value_routes), route_lanes(output_routes)], axis=-1).reshape(t, 64)
    place = jnp.stack([positions // 128, positions % 128], axis=-1).astype(F32)
    aux = jnp.concatenate([masks, place, jnp.zeros((t, 62), F32)], axis=-1).astype(BF16)
    lane = jnp.arange(LANES)
    experts = pad_channels(head_pick(wv, f).reshape(rows, 5, 112), group)
    experts = jnp.where(lane == SPOT_A, head_pick(wvsel, f)[..., None], experts)
    experts = jnp.where(lane == SPOT_B, head_pick(wosel, f)[..., None], experts)
    p1 = jnp.concatenate(
        [
            pad_channels(head_pick(wq, f), group), pad_channels(head_pick(wk, f), group),
            experts.reshape(rows, 640), pad_channels(head_pick(wrel, f), group),
        ],
        axis=-1,
    )
    piece = b1.shape[0] // 4
    vectors = [ln1_gain, ln1_bias, ln2_gain, ln2_bias, b2]
    vectors = [jnp.pad(v, (0, LANES - v.shape[0])) for v in vectors]
    extra = jnp.pad(b1.reshape(-1, piece), ((0, 0), (0, LANES - piece)))
    small = jnp.concatenate([jnp.stack(vectors), extra]).astype(F32)
    small = jnp.pad(small, ((0, 16 - small.shape[0]), (0, 0)))
    pieces = wout.reshape(-1, group, wout.shape[1])
    pieces = jnp.pad(pieces, ((0, 0), (0, group // 7), (0, 0))).reshape(-1, wout.shape[1])
    pieces = jnp.pad(pieces, ((0, -pieces.shape[0] % 16), (0, 0)))
    bias = jnp.concatenate([pad_channels(u_bias, group), pad_channels(v_bias, group)]).astype(F32)
    return aux, p1, small, pieces, bias


def unpack_kernel(
    gp_ref, gq_ref, g1_ref, g2_ref, go_ref, vq_ref, y_ref, din_ref,
    query_ref, key_ref, rel_ref, value_ref, vsel_ref, osel_ref, one_ref, two_ref, out_ref,
    gain1_ref, shift1_ref, gain2_ref, shift2_ref, b2_ref, b1_ref, u_ref, v_ref, y_out, din_out,
    heads_ref,
):
    c = lax.axis_index("ctx")
    rows, half = gp_ref.shape[1], gp_ref.shape[2]
    y_out[...] = y_ref[...]
    din_out[...] = din_ref[...]

    def block(h, k):
        ref, spot = (gp_ref, k * LANES) if k * LANES < half else (gq_ref, k * LANES - half)
        return ref[h, :, spot : spot + LANES].astype(F32).T

    def place(ref, start, piece):
        ref[start : start + 56, :] = piece[0:56]
        ref[start + 56 : start + 112, :] = piece[64:120]

    for h in range(4):
        for ref, k in ((query_ref, 0), (key_ref, 1), (rel_ref, 7)):
            place(ref, 112 * h, block(h, k))
        for e in range(5):
            piece = block(h, 2 + e)
            place(value_ref, 560 * h + 112 * e, piece)
            vsel_ref[5 * h + e : 5 * h + e + 1, :] = piece[SPOT_A : SPOT_A + 1]
            osel_ref[5 * h + e : 5 * h + e + 1, :] = piece[SPOT_B : SPOT_B + 1]
    part = g2_ref.shape[1]
    for h in range(4):
        two_ref[h * part : (h + 1) * part, :] = g2_ref[h].astype(F32)
        for k in range(g1_ref.shape[2] // part):
            spot = (4 * k + h) * part
            one_ref[:, spot : spot + part] = g1_ref[h, :, k * part : (k + 1) * part].astype(F32)
    for k in range(go_ref.shape[0]):
        out_ref[56 * k : 56 * k + 56, :] = go_ref[k, 0:56, :].astype(F32)
    own = pl.ds(pl.multiple_of(c * rows, rows), rows)
    for ref, k in ((gain2_ref, 0), (shift2_ref, 1), (b2_ref, 2), (gain1_ref, 4), (shift1_ref, 5)):
        ref[...] = sum(vq_ref[h, k : k + 1, own] for h in range(4))
    for h in range(4):
        b1_ref[:, h * part : (h + 1) * part] = vq_ref[h, 3:4, own]
    lane = lax.broadcasted_iota(jnp.int32, (8, LANES), 1)
    for ref, k in ((u_ref, 6), (v_ref, 7)):
        for h in range(4):
            heads_ref[h : h + 1, :] = vq_ref[h, k : k + 1, 0:LANES]
        value = heads_ref[...]
        moved = jnp.where(lane < 56, value, pltpu.roll(value, LANES - 8, 1))
        ref[...] = moved[0:4, 0:112]


def unpack(gp, gq, g1, g2, go, vq, y, d_in):
    rows, part, d = gp.shape[1], g2.shape[1], g2.shape[2]
    shapes = [
        (448, rows), (448, rows), (448, rows), (2240, rows), (20, rows), (20, rows), (rows, 4 * g1.shape[2]),
        (4 * part, d), (go.shape[0] * 56, d), (1, rows), (1, rows), (1, rows), (1, rows), (1, rows),
        (1, 4 * part), (4, 112), (4, 112),
    ]
    return pl.pallas_call(
        unpack_kernel,
        out_shape=[sds(shape, F32) for shape in shapes] + [sds(y.shape, BF16), sds(d_in.shape, F32)],
        in_specs=[VMEM] * 8,
        out_specs=[VMEM] * (len(shapes) + 2),
        scratch_shapes=[pltpu.VMEM((8, LANES), F32)],
        compiler_params=pltpu.CompilerParams(vmem_limit_bytes=62 << 20),
        name="unpack",
    )(gp, gq, g1, g2, go, vq, y, d_in)


def drop_pads(v, group):
    lead = v.shape[:-1]
    wide = group * 8 // 7
    return v.reshape(lead + (LANES // wide, wide))[..., :group].reshape(lead + (112,))


def on_device(n, *args):
    (
        x, positions, value_routes, output_routes, ln1_gain, ln1_bias, wq, wk, wrel, u_bias, v_bias,
        wvsel, wv, wosel, wout, ln2_gain, ln2_bias, w1, b1, w2, b2, cot,
    ) = args
    f, c = lax.axis_index("fsdp"), lax.axis_index("ctx")
    d = x.shape[1]
    g = n // 4
    group = math.gcd(112, wout.shape[0])
    aux, p1, small, pieces, bias = pack_inputs(
        n, f, positions, value_routes, output_routes, ln1_gain, ln1_bias, wq, wk, wrel, u_bias, v_bias,
        wvsel, wv, wosel, wout, ln2_gain, ln2_bias, b1, b2,
    )
    table = jnp.asarray(turn_table(d))
    rows, hidden = w1.shape
    part = hidden // n // 4
    w1_own = lax.dynamic_index_in_dim(w1.reshape(rows, n, 4, part), f, 2, keepdims=False).reshape(rows, n * part)
    tok, p1g, smallg, woutg, w2e, cotg, ev, gates, o, qcat, qpos, kv, lse, of = attend(
        n, x, aux, cot, p1, small, pieces, w2, bias, table
    )
    block = 640 // g
    out, dmid, gwout, s1, s2, d_o, gsel, vec = feed(
        n, x, cotg, gates, o, woutg[:, :block].reshape(640, d), smallg, w1_own, w2, w2e
    )
    gwout = gwout.reshape(g, block, d)
    gwout = jnp.pad(gwout, ((0, 0), (0, pieces.shape[0] - block), (0, 0)))
    d_in, gp, gq, g1, g2, go, vq, _ = back(
        n, d_o, gwout, s1, s2, qcat, qpos, kv, lse, of, tok, p1g, ev, gates, gsel, x, smallg, dmid, vec, table
    )
    if group == 56 and part == LANES and rows == LANES:
        (
            g_query, g_key, g_rel, g_value, g_vsel, g_osel, g_one, g_two, g_out,
            gain1, shift1, gain2, shift2, g_b2, g_b1, g_u, g_v, out, d_in,
        ) = unpack(gp, gq, g1, g2, go.reshape(-1, 64, d), vq, out, d_in)
        return (
            out, d_in, gain1[0], shift1[0], g_query.T, g_key.T, g_rel.T, g_u, g_v, g_vsel.T, g_value.T, g_osel.T, g_out,
            gain2[0], shift2[0], g_one, g_b1[0], g_two, g_b2[0],
        )
    gp = jnp.transpose(jnp.concatenate([gp, gq], axis=-1), (1, 0, 2))
    g_query = drop_pads(gp[..., 0:128], group).reshape(rows, 448).astype(F32)
    g_key = drop_pads(gp[..., 128:256], group).reshape(rows, 448).astype(F32)
    g_rel = drop_pads(gp[..., 896:], group).reshape(rows, 448).astype(F32)
    experts = gp[..., 256:896].reshape(rows, 4, 5, LANES)
    g_value = drop_pads(experts, group).reshape(rows, 2240).astype(F32)
    g_vsel = experts[..., SPOT_A].reshape(rows, 20).astype(F32)
    g_osel = experts[..., SPOT_B].reshape(rows, 20).astype(F32)
    g_one = jnp.transpose(g1.reshape(4, rows, n, part), (1, 2, 0, 3)).reshape(rows, hidden).astype(F32)
    g_two = g2.reshape(-1, d).astype(F32)
    g_out = go.reshape(-1, d)[:block].reshape(-1, group * 8 // 7, d)[:, :group].reshape(-1, d).astype(F32)
    sums = jnp.sum(vq, axis=0)
    own = lax.dynamic_slice_in_dim(sums, c * rows, rows, 1)
    g_b1 = lax.dynamic_slice_in_dim(vq[:, 3, :], c * part, part, 1).reshape(-1)
    g_u = drop_pads(vq[:, 6, 0:LANES], group)
    g_v = drop_pads(vq[:, 7, 0:LANES], group)
    return (
        out, d_in, own[4], own[5], g_query, g_key, g_rel, g_u, g_v, g_vsel, g_value, g_osel, g_out,
        own[0], own[1], g_one, g_b1, g_two, own[2],
    )


def solution(mesh):
    both = ("fsdp", "ctx")
    row, vector, matrix = P(both, None), P("ctx"), P("ctx", None)
    in_specs = (
        row, P(both), P(both, None, None), P(both, None, None), vector, vector, matrix, matrix, matrix,
        P(), P(), matrix, matrix, matrix, matrix, vector, vector, matrix, vector, matrix, vector, row,
    )
    out_specs = (
        row, row, vector, vector, matrix, matrix, matrix, P(), P(), matrix, matrix, matrix, matrix,
        vector, vector, matrix, vector, matrix, vector,
    )
    return jax.shard_map(
        functools.partial(on_device, mesh.shape["ctx"]),
        mesh=mesh, in_specs=in_specs, out_specs=out_specs, check_vma=False,
    )
```

```python
import functools
import math

import jax
import jax.numpy as jnp
import numpy as np
from jax import lax
from jax.experimental import pallas as pl
from jax.experimental.pallas import tpu as pltpu
from jax.sharding import PartitionSpec as P

MESH = pl.DeviceIdType.MESH
F32 = jnp.float32
BF16 = jnp.bfloat16
LN_EPS = 1e-05
MASKED = -1e30
LANES = 128
SPOT_A, SPOT_B = 63, 127
VMEM = pl.BlockSpec(memory_space=pltpu.VMEM)
ANY = pl.BlockSpec(memory_space=pl.ANY)
DMA = pltpu.SemaphoreType.DMA


def turn_coefficients():
    nodes = (np.cos(np.pi * (np.arange(400) + 0.5) / 400) + 1) / 8
    root = np.sqrt(nodes)
    powers = nodes[:, None] ** np.arange(7)[None, :]
    sine = np.linalg.lstsq(powers, np.sin(2 * np.pi * root) / root, rcond=None)[0]
    cosine = np.linalg.lstsq(powers, np.cos(2 * np.pi * root), rcond=None)[0]
    return [float(v) for v in sine], [float(v) for v in cosine]


SIN_TURN, COS_TURN = turn_coefficients()


def horner(coefs, v):
    total = coefs[-1]
    for coef in coefs[-2::-1]:
        total = total * v + coef
    return total


def turn_table(model_width):
    freq = 10000.0 ** (-np.arange(0, model_width, 2, dtype=np.float64) / model_width) / (2 * np.pi)
    mantissa, exponent = np.frexp(freq)
    coarse = np.ldexp(np.floor(mantissa * 256) / 256, exponent)
    table = np.zeros((8, model_width // 2), np.float32)
    table[0] = coarse
    table[1] = freq - coarse
    return table


def sin_cos(places, table_ref):
    coarse = places * table_ref[0:1, :]
    part = (coarse - jnp.round(coarse)) + places * table_ref[1:2, :]
    part = part - jnp.round(part)
    square = part * part
    return horner(SIN_TURN, square) * part, horner(COS_TURN, square)


def mm(left, right):
    return lax.dot_general(left, right, (((1,), (0,)), ((), ())), preferred_element_type=F32)


def mm_t(left, right):
    return lax.dot_general(left, right, (((1,), (1,)), ((), ())), preferred_element_type=F32)


def mm_left_t(left, right):
    return lax.dot_general(left, right, (((0,), (0,)), ((), ())), preferred_element_type=F32)


def copy_to(src, dst, send, recv, f, c):
    return pltpu.make_async_remote_copy(
        src_ref=src, dst_ref=dst, send_sem=send, recv_sem=recv, device_id=(f, c), device_id_type=MESH
    )


def greet(f, c, fsdp, n):
    barrier = pltpu.get_barrier_semaphore()

    def one(k, _):
        pl.semaphore_signal(barrier, inc=1, device_id=(f, lax.rem(c + k, n)), device_id_type=MESH)
        return 0

    lax.fori_loop(1, n, one, 0)
    for k in range(1, fsdp):
        pl.semaphore_signal(barrier, inc=1, device_id=(f ^ k, c), device_id_type=MESH)
    pl.semaphore_wait(barrier, n - 1 + fsdp - 1)


class LineGather:
    def __init__(self, f, c, n, own, at, recv, right, left, pair, subs=1, lone=False):
        self.f, self.c, self.n, self.size = f, c, n, n // 2
        self.place, self.bit = c // 2, lax.rem(c, 2)
        self.own, self.at = own, at
        self.recv, self.right, self.left, self.pair = recv, right, left, pair
        self.subs, self.lone = subs, lone

    def valid(self, o):
        ok = jnp.logical_and(o >= 0, o < self.size)
        if self.lone:
            span = self.size // 4
            ok = jnp.logical_and(ok, jnp.logical_and(o >= self.f * span, o < (self.f + 1) * span))
        return ok

    def slot(self, block):
        return block - self.f * (self.n // 4) if self.lone else block

    def copy(self, src, block, sub, sems, c):
        slot = self.slot(block)
        i = slot * self.subs + sub
        return copy_to(src, self.at(slot, sub), sems.at[i], self.recv.at[i], self.f, c)

    def held(self, block, sub):
        return self.at(self.slot(block), sub)

    def each(self, work):
        if self.subs == 1:
            work(0)
        else:
            lax.fori_loop(0, self.subs, lambda sub, u: (work(sub), u)[1], 0)

    def spread(self, src, block, sub, go_right, go_left):
        @pl.when(go_right)
        def _():
            self.copy(src, block, sub, self.right, self.c + 2).start()

        @pl.when(go_left)
        def _():
            self.copy(src, block, sub, self.left, self.c - 2).start()

        self.copy(src, block, sub, self.pair, self.c + 1 - 2 * self.bit).start()

    def begin(self, local):
        @pl.when(self.valid(self.place))
        def _():
            self.each(
                lambda sub: self.spread(
                    self.own(sub), self.c, sub, self.place < self.size - 1, self.place > 0
                )
            )
            local()

    def arrived(self, block, sub):
        self.copy(self.held(block, sub), block, sub, self.pair, self.c).wait_recv()

    def step(self, t):
        for sign in (-1, 1):
            o = self.place + sign * t
            block = 2 * o + self.bit

            @pl.when(self.valid(o))
            def _():
                def one(sub):
                    self.arrived(block, sub)
                    self.spread(
                        self.held(block, sub), block, sub,
                        jnp.logical_and(sign < 0, self.place < self.size - 1),
                        jnp.logical_and(sign > 0, self.place > 0),
                    )

                self.each(one)

    def steps(self, first=1):
        lax.fori_loop(first, self.size, lambda t, u: (self.step(t), u)[1], 0)

    def finish(self):
        def one(o, _):
            block = 2 * o + self.bit

            def piece(sub):
                self.arrived(2 * o + 1 - self.bit, sub)
                source = self.held(block, sub)
                self.copy(source, block, sub, self.pair, self.c).wait_send()

                @pl.when(jnp.logical_and(o <= self.place, self.place < self.size - 1))
                def _():
                    self.copy(source, block, sub, self.right, self.c).wait_send()

                @pl.when(jnp.logical_and(o >= self.place, self.place > 0))
                def _():
                    self.copy(source, block, sub, self.left, self.c).wait_send()

            @pl.when(self.valid(o))
            def _():
                self.each(piece)

            return 0

        lax.fori_loop(0, self.size, one, 0)


class QuadGather:
    def __init__(self, f, c, out, send, recv, part=None):
        self.f, self.c, self.out, self.send, self.recv = f, c, out, send, recv
        self.part = part

    def at(self, slot):
        return self.out.at[slot] if self.part is None else self.out.at[slot, self.part, :]

    def copy(self, slot, k, to, src=None):
        src = self.at(slot) if src is None else src
        return copy_to(src, self.at(slot), self.send.at[k], self.recv.at[slot], to, self.c)

    def begin(self, src=None):
        self.copy(self.f, 1, self.f ^ 2, src).start()
        self.copy(self.f, 0, self.f ^ 1, src).start()

    def got(self, slot):
        self.copy(slot, 0, self.f).wait_recv()

    def relay(self):
        self.got(self.f ^ 2)
        self.copy(self.f ^ 2, 2, self.f ^ 1).start()

    def sent(self):
        for k in range(3):
            self.copy(self.f, k, self.f).wait_send()


def spread_vector(rows, width):
    count = rows.shape[0]
    total = count * width
    lane = lax.broadcasted_iota(jnp.int32, (LANES, total), 0)
    column = lax.broadcasted_iota(jnp.int32, (LANES, total), 1)
    onehot = jnp.where(lane == lax.rem(column, width), 1.0, 0.0).astype(BF16)
    wide = mm(rows.astype(BF16), onehot)
    row = lax.broadcasted_iota(jnp.int32, (count, total), 0)
    column = lax.broadcasted_iota(jnp.int32, (count, total), 1)
    return jnp.sum(jnp.where(column // width == row, wide, 0.0), axis=0, keepdims=True)


def block_of(j, i, groups):
    return i * groups + jnp.where(lax.rem(i, 2) == 0, j, groups - 1 - j)


def holder_of(block, groups):
    row, within = block // groups, lax.rem(block, groups)
    return jnp.where(lax.rem(row, 2) == 0, within, groups - 1 - within), row


def key_places(kv):
    return kv[:, SPOT_A : SPOT_A + 1].astype(F32) * 128.0 + kv[:, SPOT_B : SPOT_B + 1].astype(F32)


def attend_kernel(
    n,
    x_ref, aux_ref, cot_ref, p1_ref, small_ref, wout_ref, w2_ref, bias_ref, table_ref,
    tok_ref, p1g_ref, smallg_ref, woutg_ref, w2e_ref, cotg_ref, ev_ref, gates_ref, o_ref,
    qcat_ref, qpos_ref, kv_ref, lse_ref, of_ref,
    qs_ref, kvs_ref, qr_ref, os_ref, kcat_ref, vt_ref, m_ref, l_ref,
    sm_s, sm_r, p_r, p_a, p_b, p_c, w_r, w_a, w_b, w_c, h_r, h_a, h_b, h_c,
    t_s, t_r, c_s, c_r, q_s, q_r, kv_s, kv_r, kv_p, o_s, o_r, loc,
):
    f, c = lax.axis_index("fsdp"), lax.axis_index("ctx")
    groups = n // 4
    seq, turn = c // groups, lax.rem(c, groups)
    tokens, width = x_ref.shape
    scale = 1.0 / math.sqrt(112)
    greet(f, c, 4, n)

    def small_send(k, _):
        to = lax.rem(c + k, n)
        copy_to(small_ref, smallg_ref.at[c], sm_s.at[to], sm_r.at[c], f, to).start()
        return 0

    lax.fori_loop(1, n, small_send, 0)
    smallg_ref[c] = small_ref[...]
    gather_p = LineGather(f, c, n, lambda sub: p1_ref, lambda k, sub: p1g_ref.at[k], p_r, p_a, p_b, p_c)

    def own_p():
        p1g_ref[c] = p1_ref[...]

    gather_p.begin(own_p)
    wout_copy = pltpu.make_async_copy(wout_ref, woutg_ref.at[c - f * groups], loc.at[0])
    subs = w_r.shape[0] // groups
    piece = wout_ref.shape[0] // subs
    gather_w = LineGather(
        f, c, n,
        lambda sub: wout_ref.at[pl.ds(pl.multiple_of(sub * piece, piece), piece), :],
        lambda k, sub: woutg_ref.at[k, pl.ds(pl.multiple_of(sub * piece, piece), piece), :],
        w_r, w_a, w_b, w_c, subs=subs, lone=True,
    )
    early = w2e_ref.shape[1]
    own2 = w2_ref.at[pl.ds(pl.multiple_of(f * (w2_ref.shape[0] // 4), 16), early), :]
    w2_copy = pltpu.make_async_copy(own2, w2e_ref.at[c], loc.at[2])
    gather_h = LineGather(f, c, n, lambda sub: own2, lambda k, sub: w2e_ref.at[k], h_r, h_a, h_b, h_c)
    cot_copy = pltpu.make_async_copy(cot_ref, cotg_ref.at[f], loc.at[1])
    cot_copy.start()

    hidden = x_ref[...].astype(F32)
    offsets = hidden - jnp.mean(hidden, axis=1, keepdims=True)
    spread = jnp.mean(offsets * offsets, axis=1, keepdims=True)
    xhat = offsets * lax.rsqrt(spread + LN_EPS)

    def small_wait(k, _):
        to = lax.rem(c + k, n)
        copy_to(small_ref, smallg_ref.at[to], sm_s.at[to], sm_r.at[to], f, to).wait()
        return 0

    lax.fori_loop(1, n, small_wait, 0)
    gain = spread_vector(smallg_ref[:, 0, :], width // n)
    shift = spread_vector(smallg_ref[:, 1, :], width // n)
    tok_ref[f, :, 0:width] = (xhat * gain + shift).astype(BF16)
    tok_ref[f, :, width:] = aux_ref[...]
    tok_gather = QuadGather(f, c, tok_ref, t_s, t_r)
    tok_gather.begin()
    gather_p.steps()
    tok_gather.relay()
    gather_p.finish()
    tok_gather.got(f ^ 1)
    tok_gather.got(f ^ 3)
    tok_gather.sent()
    cot_gather = QuadGather(f, c, cotg_ref, c_s, c_r)
    cot_gather.begin(cot_ref)

    lane = lax.broadcasted_iota(jnp.int32, (tokens, LANES), 1)
    source = lax.broadcasted_iota(jnp.int32, (LANES, LANES), 0)
    target = lax.broadcasted_iota(jnp.int32, (LANES, LANES), 1)
    wanted = f * 16 + lax.rem(target, 8) + jnp.where(target < 16, 8, 0)
    pick = jnp.where(
        jnp.logical_and(source == wanted, jnp.logical_and(target < 32, lax.rem(target, 8) < 5)), 1.0, 0.0
    ).astype(BF16)
    own_turn, own_slot = holder_of(c, groups)
    bit = lax.rem(c, 2)
    spots = jnp.logical_or(lane == SPOT_A, lane == SPOT_B)

    def project(t, _):
        s = lax.rem(seq + 1 + t, 4)
        normed = tok_ref[s, :, 0:width]
        aux = tok_ref[s, :, width:]
        weights = p1g_ref[...].reshape(width, p1g_ref.shape[2])
        qk = mm(normed, weights[:, 0:256])
        experts = mm(normed, weights[:, 256:896])
        ev_ref[s] = experts.astype(BF16)
        logits = jnp.zeros((tokens, LANES), F32)
        for e in range(5):
            for spot, first in ((SPOT_B, 0), (SPOT_A, 16)):
                column = experts[:, e * LANES + spot : e * LANES + spot + 1]
                logits = jnp.where(
                    jnp.logical_or(lane == first + e, lane == first + 8 + e), column, logits
                )
        sig = jax.nn.sigmoid(logits)
        gates = mm(aux, pick) * jnp.where(lax.rem(lane, 16) >= 8, sig * (1.0 - sig), sig)
        gates_ref[s] = gates
        values = jnp.zeros((tokens, LANES), F32)
        for e in range(5):
            values = values + gates[:, 16 + e : 17 + e] * experts[:, e * LANES : (e + 1) * LANES]
        values = jnp.where(spots, 0.0, values)
        high, rest = aux[:, 64:65].astype(F32), aux[:, 65:66].astype(F32)

        def with_place(v):
            return jnp.where(lane == SPOT_A, high, jnp.where(lane == SPOT_B, rest, v)).astype(BF16)

        qs_ref[s] = with_place(qk[:, 0:128])
        kvs_ref[s, :, 0:128] = with_place(qk[:, 128:256])
        kvs_ref[s, :, 128:256] = values.astype(BF16)
        to = s * groups + own_turn

        @pl.when(to != c)
        def _():
            copy_to(qs_ref.at[s], qr_ref.at[own_slot], q_s.at[s], q_r.at[own_slot], f, to).start()

        @pl.when(to == c)
        def _():
            qr_ref[own_slot] = qs_ref[s]

        def kv_send(k, _):
            to = s * groups + 2 * k + bit

            @pl.when(to != c)
            def _():
                copy_to(kvs_ref.at[s], kv_ref.at[c], kv_s.at[to], kv_r.at[c], f, to).start()

            @pl.when(to == c)
            def _():
                kv_ref[c] = kvs_ref[s]

            return 0

        lax.fori_loop(0, groups // 2, kv_send, 0)
        return 0

    gather_h.begin(w2_copy.start)
    lax.fori_loop(0, 4, project, 0)
    gather_w.begin(wout_copy.start)

    def kv_wait(block):
        copy_to(kvs_ref.at[0], kv_ref.at[block], kv_s.at[0], kv_r.at[block], f, c).wait_recv()

    def kv_pass(block):
        return copy_to(kv_ref.at[block], kv_ref.at[block], kv_p.at[block // 2], kv_r.at[block], f, c + 1 - 2 * bit)

    def hand_on(m):
        block = 2 * m + bit

        @pl.when(block != c)
        def _():
            kv_wait(block)

        kv_pass(block).start()

    def prepare(i, _):
        block = block_of(turn, i, groups)

        @pl.when(block != c)
        def _():
            copy_to(qs_ref.at[0], qr_ref.at[i], q_s.at[0], q_r.at[i], f, c).wait_recv()

        places = key_places(qr_ref[i])
        query = jnp.where(spots, 0.0, qr_ref[i].astype(F32))
        q_position = (query + bias_ref[pl.ds(4 + f, 1), :]).astype(BF16)
        qpos_ref[i] = q_position
        qcat_ref[i, :, width:] = ((query + bias_ref[pl.ds(f, 1), :]) * scale).astype(BF16)
        rel = p1g_ref[:, :, 896:].reshape(width, LANES)
        rel_query = mm_t(q_position, rel)
        sine, cosine = sin_cos(places, table_ref)
        first, second = rel_query[:, : width // 2], rel_query[:, width // 2 :]
        qcat_ref[i, :, 0 : width // 2] = ((first * sine + second * cosine) * scale).astype(BF16)
        qcat_ref[i, :, width // 2 : width] = ((second * sine - first * cosine) * scale).astype(BF16)
        m_ref[i] = jnp.full((1, tokens), MASKED, F32)
        l_ref[i] = jnp.zeros((1, tokens), F32)
        of_ref[i] = jnp.zeros((LANES, tokens), F32)
        return 0

    lax.fori_loop(0, 4, prepare, 0)
    hand_on(0)
    row_in = lax.broadcasted_iota(jnp.int32, (tokens, tokens), 0)
    col_in = lax.broadcasted_iota(jnp.int32, (tokens, tokens), 1)

    def give(i):
        total = l_ref[i]
        result = of_ref[i] / total
        of_ref[i] = result
        lse_ref[i] = m_ref[i] + jnp.log(total)
        os_ref[i] = result.T.astype(BF16)
        block = block_of(turn, i, groups)

        @pl.when(block != c)
        def _():
            copy_to(os_ref.at[i], o_ref.at[seq], o_s.at[i], o_r.at[seq], f, block).start()

        @pl.when(block == c)
        def _():
            o_ref[seq] = os_ref[i]

    def key_block(kb, _):
        own = [block_of(turn, i, groups) for i in range(4)]
        first = sum((b < kb).astype(jnp.int32) for b in own)
        ready = sum((b == kb).astype(jnp.int32) for b in own)

        @pl.when(lax.rem(kb, 2) != bit)
        def _():
            kv_wait(kb)

        @pl.when(jnp.logical_and(lax.rem(kb, 2) == 0, kb < n - 2))
        def _():
            hand_on(kb // 2 + 1)

        sine, cosine = sin_cos(key_places(kv_ref[kb]), table_ref)
        kcat_ref[:, 0 : width // 2] = cosine.astype(BF16)
        kcat_ref[:, width // 2 : width] = sine.astype(BF16)
        kcat_ref[:, width:] = kv_ref[kb, :, 0:128]
        vt_ref[...] = kv_ref[kb, :, 128:256].astype(F32).T.astype(BF16)

        def query_block(i, _):
            gap = (block_of(turn, i, groups) - kb) * tokens
            scores = mm_t(kcat_ref[...], qcat_ref[i])
            scores = jnp.where(row_in <= col_in + gap, scores, MASKED)
            before = m_ref[i]
            best = jnp.maximum(before, jnp.max(scores, axis=0, keepdims=True))
            shrink = jnp.exp(before - best)
            probs = jnp.exp(scores - best)
            m_ref[i] = best
            l_ref[i] = l_ref[i] * shrink + jnp.sum(probs, axis=0, keepdims=True)
            of_ref[i] = of_ref[i] * shrink + mm(vt_ref[...], probs.astype(BF16))
            return 0

        lax.fori_loop(first, 4, query_block, 0)

        @pl.when(ready == 1)
        def _():
            give(first)

        @pl.when(kb == n // 2 - 1)
        def _():
            cot_gather.relay()

        @pl.when(jnp.logical_and(kb > 0, kb < n // 2))
        def _():
            gather_w.step(kb)

        @pl.when(kb < n // 2 - 1)
        def _():
            gather_h.step(kb + 1)

        return 0

    lax.fori_loop(0, n, key_block, 0)
    cot_gather.got(f ^ 1)
    cot_gather.got(f ^ 3)
    cot_gather.sent()
    gather_w.finish()
    gather_h.finish()
    w2_copy.wait()

    @pl.when(gather_w.valid(c // 2))
    def _():
        wout_copy.wait()

    cot_copy.wait()

    def drain(s, _):
        to = s * groups + own_turn

        @pl.when(to != c)
        def _():
            copy_to(qs_ref.at[s], qr_ref.at[own_slot], q_s.at[s], q_r.at[0], f, to).wait_send()
            copy_to(os_ref.at[0], o_ref.at[s], o_s.at[0], o_r.at[s], f, to).wait_recv()

        @pl.when(block_of(turn, s, groups) != c)
        def _():
            copy_to(os_ref.at[s], o_ref.at[s], o_s.at[s], o_r.at[0], f, to).wait_send()

        return 0

    lax.fori_loop(0, 4, drain, 0)

    def kv_drain(k, _):
        to = 2 * k + bit

        @pl.when(to != c)
        def _():
            copy_to(kvs_ref.at[0], kv_ref.at[0], kv_s.at[to], kv_r.at[0], f, c).wait_send()

        kv_pass(to).wait_send()
        return 0

    lax.fori_loop(0, n // 2, kv_drain, 0)


def sds(shape, dtype):
    return jax.ShapeDtypeStruct(shape, dtype)


def attend(n, x, aux, cot, p1, small, wout, w2, bias, table):
    t, d = x.shape
    rows = p1.shape[0]
    out_rows = wout.shape[0]
    g = n // 4
    subs = cuts(out_rows)
    return pl.pallas_call(
        functools.partial(attend_kernel, n),
        out_shape=[
            sds((4, t, d + LANES), BF16), sds((n, rows, d), BF16), sds((n, 16, LANES), F32),
            sds((g, out_rows, d), BF16), sds((n, early_rows(w2.shape[0] // 4), d), BF16), sds((4, t, d), BF16), sds((4, t, 640), BF16),
            sds((4, t, LANES), F32), sds((4, t, LANES), BF16), sds((4, t, d + LANES), BF16),
            sds((4, t, LANES), BF16), sds((n, t, 256), BF16), sds((4, 1, t), F32), sds((4, LANES, t), F32),
        ],
        in_specs=[VMEM, VMEM, ANY, VMEM, VMEM, ANY, ANY, VMEM, VMEM],
        out_specs=[VMEM, VMEM, VMEM, ANY, ANY, ANY] + [VMEM] * 8,
        scratch_shapes=[
            pltpu.VMEM((4, t, LANES), BF16), pltpu.VMEM((4, t, 256), BF16), pltpu.VMEM((4, t, LANES), BF16),
            pltpu.VMEM((4, t, LANES), BF16), pltpu.VMEM((t, d + LANES), BF16),
            pltpu.VMEM((LANES, t), BF16), pltpu.VMEM((4, 1, t), F32), pltpu.VMEM((4, 1, t), F32),
            DMA((n,)), DMA((n,)), DMA((n,)), DMA((n,)), DMA((n,)), DMA((n,)),
            DMA((g * subs,)), DMA((g * subs,)), DMA((g * subs,)), DMA((g * subs,)),
            DMA((n,)), DMA((n,)), DMA((n,)), DMA((n,)),
            DMA((3,)), DMA((4,)), DMA((3,)), DMA((4,)), DMA((4,)), DMA((4,)),
            DMA((n,)), DMA((n,)), DMA((n // 2,)), DMA((4,)), DMA((4,)), DMA((3,)),
        ],
        compiler_params=pltpu.CompilerParams(
            collective_id=0, has_side_effects=True, vmem_limit_bytes=56 << 20
        ),
        name="attend",
    )(x, aux, cot, p1, small, wout, w2, bias, table)


class QuadSum:
    def __init__(self, f, c, core_out, core_in, x_out, x_in, keep, send, recv):
        self.f, self.c = f, c
        self.core_out, self.core_in, self.x_out, self.x_in = core_out, core_in, x_out, x_in
        self.keep, self.send, self.recv = keep, send, recv

    def core(self, k):
        return copy_to(
            self.core_out.at[k], self.core_in.at[k], self.send.at[k], self.recv.at[k], self.f ^ 1, self.c
        )

    def across(self):
        return copy_to(self.x_out, self.x_in, self.send.at[2], self.recv.at[2], self.f ^ 2, self.c)

    def put(self, k, value):
        if k in (1, 3):
            self.core_out[k // 2] = value.astype(BF16)
            self.core(k // 2).start()
        else:
            self.keep[k // 2] = value

    def cross(self):
        self.core(1).wait_recv()
        self.x_out[...] = (self.keep[1] + self.core_in[1].astype(F32)).astype(BF16)
        self.across().start()

    def total(self):
        self.core(0).wait_recv()
        self.across().wait_recv()
        return self.keep[0] + self.core_in[0].astype(F32) + self.x_in[...].astype(F32)

    def sent(self):
        self.core(0).wait_send()
        self.core(1).wait_send()
        self.across().wait_send()


def quad_sum_scratch(t, d):
    return [
        pltpu.VMEM((2, t, d), BF16), pltpu.VMEM((2, t, d), BF16), pltpu.VMEM((t, d), BF16),
        pltpu.VMEM((t, d), BF16), pltpu.VMEM((2, t, d), F32), DMA((3,)), DMA((3,)),
    ]


def layer_stats(v):
    offsets = v - jnp.mean(v, axis=1, keepdims=True)
    scale = lax.rsqrt(jnp.mean(offsets * offsets, axis=1, keepdims=True) + LN_EPS)
    return offsets * scale, scale


def layer_back(grad, gain, xhat, scale):
    inner = grad * gain
    return scale * (
        inner - jnp.mean(inner, axis=1, keepdims=True) - xhat * jnp.mean(inner * xhat, axis=1, keepdims=True)
    )


def gelu_pair(v):
    k = math.sqrt(2.0 / math.pi)
    square = v * v
    t = jnp.tanh(k * v * (1.0 + 0.044715 * square))
    half = 0.5 * (1.0 + t)
    return v * half, half + 0.5 * v * (1.0 - t * t) * (k * (1.0 + 3 * 0.044715 * square))


class PairSum:
    def __init__(self, f, c, n, source, got, out, send, recv):
        self.f, self.c, self.size = f, c, n // 2
        self.bit = lax.rem(c, 2)
        self.source, self.got, self.out, self.send, self.recv = source, got, out, send, recv

    def copy(self, o):
        return copy_to(
            self.source(2 * o + 1 - self.bit), self.got.at[o], self.send.at[o], self.recv.at[o],
            self.f, self.c + 1 - 2 * self.bit,
        )

    def begin(self):
        lax.fori_loop(0, self.size, lambda o, u: (self.copy(o).start(), u)[1], 0)

    def finish(self):
        def one(o, _):
            self.copy(o).wait_recv()
            term = self.source(2 * o + self.bit)[...].astype(F32)
            self.out[o] = (term + self.got[o].astype(F32)).astype(BF16)
            self.copy(o).wait_send()
            return 0

        lax.fori_loop(0, self.size, one, 0)


class LineSum:
    def __init__(self, f, c, n, source, inbox, stage, line_s, line_r, pair=None, subs=1, lone=False):
        self.f, self.c, self.n, self.size = f, c, n, n // 2
        self.place, self.bit = c // 2, lax.rem(c, 2)
        self.source = source
        self.inbox, self.stage, self.line_s, self.line_r = inbox, stage, line_s, line_r
        self.pair = pair
        self.subs = subs
        self.span = self.size // 4 if lone else self.size
        self.first = f * self.span if lone else 0

    def valid(self, o):
        return jnp.logical_and(o >= self.first, o < self.first + self.span)

    def index(self, o, sub):
        return (o - self.first) * self.subs + sub

    def pair_copy(self, o, sub):
        i = self.index(o, sub)
        got, send, recv = self.pair
        return copy_to(
            self.source(2 * (o - self.first) + 1 - self.bit, sub), got.at[i], send.at[i], recv.at[i],
            self.f, self.c + 1 - 2 * self.bit,
        )

    def line_copy(self, i, slot, c):
        return copy_to(self.stage.at[i], self.inbox.at[slot], self.line_s.at[i], self.line_r.at[slot], self.f, c)

    def each(self, work):
        def one(k, _):
            work(self.first + k // self.subs, lax.rem(k, self.subs))
            return 0

        lax.fori_loop(0, self.span * self.subs, one, 0)

    def begin(self):
        self.each(lambda o, sub: self.pair_copy(o, sub).start())

    def begin_block(self, block):
        @pl.when(lax.rem(block, 2) != self.bit)
        def _():
            self.pair_copy(block // 2, 0).start()

    def term(self, o, sub):
        if self.pair is None:
            return self.source(o - self.first, sub)[...].astype(F32)
        self.pair_copy(o, sub).wait_recv()
        own = self.source(2 * (o - self.first) + self.bit, sub)[...].astype(F32)
        return own + self.pair[0][self.index(o, sub)].astype(F32)

    def extra(self, sub):
        return self.span * self.subs + sub

    def move(self, o, sub, go_right):
        i = self.index(o, sub)
        total = self.term(o, sub)
        starts = self.place == 0 if go_right else self.place == self.size - 1

        @pl.when(starts)
        def _():
            self.stage[i] = total.astype(BF16)

        @pl.when(jnp.logical_not(starts))
        def _():
            self.line_copy(i, i, self.c).wait_recv()
            self.stage[i] = (total + self.inbox[i].astype(F32)).astype(BF16)

        if go_right:
            self.line_copy(i, i, self.c + 2).start()
        else:
            slot = jnp.where(o == self.place - 1, self.extra(sub), i)
            self.line_copy(i, slot, self.c - 2).start()

    def turn(self, time):
        far = self.size - 1 - (time - self.place)
        near = time - (self.size - 1 - self.place)

        def one(sub, _):
            @pl.when(jnp.logical_and(jnp.logical_and(far < self.size, self.valid(far)), far > self.place))
            def _():
                self.move(far, sub, True)

            @pl.when(jnp.logical_and(jnp.logical_and(near >= 0, self.valid(near)), near < self.place))
            def _():
                self.move(near, sub, False)

            return 0

        lax.fori_loop(0, self.subs, one, 0)

    def settle(self, sub):
        i = self.index(self.place, sub)
        own = self.term(self.place, sub)
        left = self.place > 0
        right = self.place < self.size - 1

        @pl.when(left)
        def _():
            self.line_copy(i, i, self.c).wait_recv()

        @pl.when(right)
        def _():
            self.line_copy(i, self.extra(sub), self.c).wait_recv()

        @pl.when(jnp.logical_and(left, right))
        def _():
            self.stage[i] = (
                own + self.inbox[i].astype(F32) + self.inbox[self.extra(sub)].astype(F32)
            ).astype(BF16)

        @pl.when(jnp.logical_and(left, jnp.logical_not(right)))
        def _():
            self.stage[i] = (own + self.inbox[i].astype(F32)).astype(BF16)

        @pl.when(jnp.logical_and(right, jnp.logical_not(left)))
        def _():
            self.stage[i] = (own + self.inbox[self.extra(sub)].astype(F32)).astype(BF16)

    def finish(self):
        @pl.when(self.valid(self.place))
        def _():
            lax.fori_loop(0, self.subs, lambda sub, u: (self.settle(sub), u)[1], 0)

    def sent(self):
        def one(o, sub):
            if self.pair is not None:
                self.pair_copy(o, sub).wait_send()

            @pl.when(o != self.place)
            def _():
                self.line_copy(self.index(o, sub), 0, self.c).wait_send()

        self.each(one)


def feed_kernel(
    n,
    x_ref, cot_ref, gates_ref, o_ref, wout_ref, small_ref, w1_ref, w2_ref, w2e_ref,
    out_ref, dmid_ref, gwout_ref, s1_ref, s2_ref, do_ref, gsel_ref, vec_ref,
    w1g, w2g, n2_ref, act_ref, slope_ref, dpre_ref, mixed_ref, dml_ref, mid_ref, gw1_ref, gw2_ref, got1, in2, stage2,
    a0, a1, a2, a3, a4, a5, a6, i0, i1, i2, i3, i4, i5, i6, b0, b1, b2, b3, b4, b5, b6, j0, j1, j2, j3, j4, j5, j6,
    e0, e1, e2, e3, e4, e5, e6,
    w1_r, w1_a, w1_b, w1_c, w2_r, w2_a, w2_b, w2_c, h1_s, h1_r, h2_s, h2_r, n_s, n_r, d_s, d_r, m_s, m_r, k_s, k_r, loc, da_ref, da_s, da_r,
):
    f, c = lax.axis_index("fsdp"), lax.axis_index("ctx")
    tokens, width = x_ref.shape
    quarter = w1g.shape[1]
    groups = n // 4
    own_turn, own_slot = holder_of(c, groups)
    greet(f, c, 4, n)
    rows1, rows2 = width // n, quarter // n

    def rows_of(ref, count):
        return lambda k: ref.at[pl.ds(pl.multiple_of(k * count, count), count), :]

    early = w2e_ref.shape[1]
    at1 = rows_of(w1g, rows1)
    gather1 = LineGather(f, c, n, lambda sub: w1_ref, lambda k, sub: at1(k), w1_r, w1_a, w1_b, w1_c)
    local1 = pltpu.make_async_copy(w1_ref, at1(c), loc.at[0])
    bring2 = pltpu.make_async_copy(w2e_ref, w2g.at[:, 0:early, :], loc.at[1])
    gather1.begin(local1.start)
    bring2.start()
    gather2 = None
    if early < rows2:
        own2 = w2_ref.at[pl.ds(pl.multiple_of(f * rows2 + early, 16), rows2 - early), :]
        at2 = lambda k: w2g.at[k, early:rows2, :]
        gather2 = LineGather(f, c, n, lambda sub: own2, lambda k, sub: at2(k), w2_r, w2_a, w2_b, w2_c)
        local2 = pltpu.make_async_copy(own2, at2(c), loc.at[2])
    pair1 = PairSum(f, c, n, rows_of(gw1_ref, rows1), got1, s1_ref, h1_s, h1_r)
    line2 = LineSum(f, c, n, lambda o, sub: rows_of(gw2_ref, rows2)(2 * o + sub), in2, stage2, h2_s, h2_r, subs=2)
    attn_sum = (QuadSum(f, c, a0, a1, a2, a3, a4, a5, a6), QuadSum(f, c, i0, i1, i2, i3, i4, i5, i6))
    back_sum = (QuadSum(f, c, b0, b1, b2, b3, b4, b5, b6), QuadSum(f, c, j0, j1, j2, j3, j4, j5, j6))
    span = tokens // 2
    halves = (slice(0, span), slice(span, tokens))
    out_sum = QuadSum(f, c, e0, e1, e2, e3, e4, e5, e6)

    for half, one in zip(halves, attn_sum):
        for k in (3, 2, 1, 0):
            r = f ^ k
            for e in range(5):
                mixed_ref[r, half, e * LANES : (e + 1) * LANES] = (
                    gates_ref[r, half, e : e + 1] * o_ref[r, half, :].astype(F32)
                ).astype(BF16)
            one.put(k, mm(mixed_ref[r, half, :], wout_ref[...]))
            if k == 2:
                one.cross()
    gather1.step(1)
    if gather2 is not None:
        gather2.begin(local2.start)
    gain = spread_vector(small_ref[:, 2, :], width // n)
    shift = spread_vector(small_ref[:, 3, :], width // n)
    n2_gather = (QuadGather(f, c, n2_ref, n_s, n_r, halves[0]), QuadGather(f, c, n2_ref, m_s, m_r, halves[1]))
    for half, one, gather in zip(halves, attn_sum, n2_gather):
        middle = x_ref[half, :].astype(F32) + one.total()
        mid_ref[half, :] = middle
        xhat, _ = layer_stats(middle)
        n2_ref[f, half, :] = (xhat * gain + shift).astype(BF16)
        gather.begin()
        if gather is n2_gather[0]:
            gather1.step(2)
    gather1.steps(3)
    gather1.finish()
    local1.wait()
    first_bias = spread_vector(small_ref[:, pl.ds(5 + f, 1), :].reshape(n, LANES), rows2)

    def enter(k):
        r = f ^ k
        act, slope = gelu_pair(mm(n2_ref[r], w1g[...]) + first_bias)
        act_ref[r] = act.astype(BF16)
        slope_ref[r] = slope

    def got(pair, slot):
        for gather in pair:
            gather.got(slot)

    enter(0)
    got(n2_gather, f ^ 1)
    n2_gather[0].relay()
    if gather2 is not None:
        gather2.step(1)
    enter(1)
    n2_gather[1].relay()
    if gather2 is not None:
        gather2.step(2)
    enter(2)
    if gather2 is not None:
        gather2.steps(3)
    got(n2_gather, f ^ 3)
    enter(3)
    tile = 256
    all_tokens = 4 * tokens

    def weight_tile(left_ref, right_ref, result_ref):
        def one(i, _):
            spot = pl.multiple_of(i * tile, tile)
            left = left_ref[:, :, pl.ds(spot, tile)].reshape(all_tokens, tile)
            right = right_ref[...].reshape(all_tokens, right_ref.shape[2])
            result_ref[pl.ds(spot, tile), :] = mm_left_t(left, right).astype(BF16)
            return 0

        lax.fori_loop(0, left_ref.shape[2] // tile, one, 0)

    weight_tile(act_ref, cot_ref, gw2_ref)
    line2.turn(0)
    if gather2 is not None:
        gather2.finish()
        local2.wait()
    bring2.wait()
    second = w2g[...].reshape(quarter, width)

    for k in (3, 2, 1, 0):
        r = f ^ k
        d_act = mm_t(cot_ref[r], second)
        dpre_ref[r] = (d_act * slope_ref[r]).astype(BF16)
        term = mm_t(dpre_ref[r], w1g[...])
        for half, one in zip(halves, back_sum):
            one.put(k, term[half])
        if k == 2:
            for one in back_sum:
                one.cross()
    weight_tile(n2_ref, dpre_ref, gw1_ref)
    pair1.begin()
    line2.turn(1)
    for k in (3, 2, 1, 0):
        out_sum.put(k, mm(act_ref[f ^ k], second))
    vec_ref[...] = jnp.zeros_like(vec_ref)
    dml_gather = (QuadGather(f, c, dml_ref, d_s, d_r, halves[0]), QuadGather(f, c, dml_ref, k_s, k_r, halves[1]))
    for half, one, gather in zip(halves, back_sum, dml_gather):
        d_norm = one.total()
        xhat, scale = layer_stats(mid_ref[half, :])
        d_middle = cot_ref[f, half, :].astype(F32) + layer_back(d_norm, gain, xhat, scale)
        dmid_ref[half, :] = d_middle
        dml_ref[f, half, :] = d_middle.astype(BF16)
        gather.begin()
        vec_ref[0:1, :] += jnp.sum(d_norm * xhat, axis=0, keepdims=True)
        vec_ref[1:2, :] += jnp.sum(d_norm, axis=0, keepdims=True)
    out_sum.cross()
    vec_ref[2:3, :] = jnp.sum(cot_ref[f].astype(F32), axis=0, keepdims=True)
    total = jnp.zeros((1, quarter), F32)
    for r in range(4):
        total = total + jnp.sum(dpre_ref[r].astype(F32), axis=0, keepdims=True)
    vec_ref[3:4, :] = total
    lane = lax.broadcasted_iota(jnp.int32, (tokens, LANES), 1)

    def leave(k):
        r = f ^ k
        d_attn = jnp.zeros((tokens, LANES), F32)
        select = jnp.zeros((tokens, LANES), F32)
        result = o_ref[r].astype(F32)
        d_mixed = mm_t(dml_ref[r], wout_ref[...])
        for e in range(5):
            part = d_mixed[:, e * LANES : (e + 1) * LANES]
            d_attn = d_attn + gates_ref[r, :, e : e + 1] * part
            column = jnp.sum(result * part, axis=1, keepdims=True) * gates_ref[r, :, 8 + e : 9 + e]
            select = jnp.where(lane == e, column, select)
        da_ref[r] = d_attn.astype(BF16)
        gsel_ref[r] = select
        to = r * groups + own_turn

        @pl.when(to != c)
        def _():
            copy_to(da_ref.at[r], do_ref.at[own_slot], da_s.at[r], da_r.at[own_slot], f, to).start()

        @pl.when(to == c)
        def _():
            do_ref[own_slot] = da_ref[r]

    line2.turn(2)
    leave(0)
    got(dml_gather, f ^ 1)
    leave(1)
    dml_gather[0].relay()
    dml_gather[1].relay()
    leave(2)
    got(dml_gather, f ^ 3)
    leave(3)

    def out_tile(i, _):
        spot = pl.multiple_of(i * LANES, LANES)
        left = mixed_ref[:, :, pl.ds(spot, LANES)].reshape(all_tokens, LANES)
        right = dml_ref[...].reshape(all_tokens, width)
        gwout_ref[pl.ds(spot, LANES), :] = mm_left_t(left, right).astype(BF16)
        return 0

    lax.fori_loop(0, 5, out_tile, 0)
    second_bias = spread_vector(small_ref[:, 4, :], width // n)
    out_ref[...] = (mid_ref[...] + out_sum.total() + second_bias).astype(BF16)
    lax.fori_loop(3, n // 2 - 1, lambda k, u: (line2.turn(k), u)[1], 0)
    line2.finish()
    own = 2 * (c // 2) + lax.rem(c, 2)
    s2_ref[0] = stage2[own]
    s2_ref[1] = stage2[own + 1 - 2 * lax.rem(c, 2)]
    line2.sent()
    pair1.finish()
    for one in attn_sum + back_sum + n2_gather + dml_gather + (out_sum,):
        one.sent()

    def drain(i, _):
        @pl.when(i * groups + own_turn != c)
        def _():
            copy_to(da_ref.at[i], do_ref.at[0], da_s.at[i], da_r.at[0], f, c).wait_send()

        @pl.when(block_of(lax.rem(c, groups), i, groups) != c)
        def _():
            copy_to(da_ref.at[0], do_ref.at[i], da_s.at[0], da_r.at[i], f, c).wait_recv()

        return 0

    lax.fori_loop(0, 4, drain, 0)


def feed(n, x, cot, gates, o, wout, small, w1, w2, w2e):
    t, d = x.shape
    quarter = w1.shape[1]
    line = n // 2
    return pl.pallas_call(
        functools.partial(feed_kernel, n),
        out_shape=[
            sds((t, d), BF16), sds((t, d), F32), sds((640, d), BF16), sds((line, d // n, quarter), BF16),
            sds((2, quarter // n, d), BF16), sds((4, t, LANES), BF16), sds((4, t, LANES), F32), sds((8, d), F32),
        ],
        in_specs=[VMEM] * 6 + [ANY] * 3,
        out_specs=[VMEM] * 8,
        scratch_shapes=[
            pltpu.VMEM((d, quarter), BF16), pltpu.VMEM((n, quarter // n, d), BF16), pltpu.VMEM((4, t, d), BF16),
            pltpu.VMEM((4, t, quarter), BF16), pltpu.VMEM((4, t, quarter), F32), pltpu.VMEM((4, t, quarter), BF16),
            pltpu.VMEM((4, t, 640), BF16), pltpu.VMEM((4, t, d), BF16), pltpu.VMEM((t, d), F32),
            pltpu.VMEM((d, quarter), BF16), pltpu.VMEM((quarter, d), BF16),
            pltpu.VMEM((line, d // n, quarter), BF16),
        ]
        + line_scratch(line, 2, 2 * quarter // n, d)
        + quad_sum_scratch(t // 2, d) * 4
        + quad_sum_scratch(t, d)
        + [DMA((n,))] * 8 + [DMA((line,))] * 2 + line_sems(line, 2)
        + [DMA((3,)), DMA((4,))] * 4 + [DMA((3,)), pltpu.VMEM((4, t, LANES), BF16), DMA((4,)), DMA((4,))],
        compiler_params=pltpu.CompilerParams(
            collective_id=1, has_side_effects=True, vmem_limit_bytes=62 << 20
        ),
        name="feed",
    )(x, cot, gates, o, wout, small, w1, w2, w2e)


class LoneShare:
    def __init__(self, total, out, send, recv):
        self.f, self.c = total.f, total.c
        self.owner = total.place // (total.size // 4)
        self.rel = total.f ^ self.owner
        start = jnp.where(self.rel == 0, (total.place - total.first) * total.subs, 0)
        self.held = total.stage.at[pl.ds(start, total.subs)]
        self.out, self.send, self.recv = out, send, recv
        self.local = pltpu.make_async_copy(self.held, out, recv)

    def copy(self, src, k, to):
        return copy_to(src, self.out, self.send.at[k], self.recv, to, self.c)

    def begin(self):
        @pl.when(self.rel == 0)
        def _():
            self.copy(self.held, 1, self.f ^ 2).start()
            self.copy(self.held, 0, self.f ^ 1).start()
            self.local.start()

    def relay(self):
        @pl.when(self.rel == 2)
        def _():
            self.copy(self.out, 0, self.f).wait_recv()
            self.copy(self.out, 0, self.f ^ 1).start()

    def finish(self):
        @pl.when(self.rel == 0)
        def _():
            self.local.wait()
            self.copy(self.held, 0, self.f).wait_send()
            self.copy(self.held, 1, self.f).wait_send()

        @pl.when(self.rel == 2)
        def _():
            self.copy(self.out, 0, self.f).wait_send()

        @pl.when(lax.rem(self.rel, 2) == 1)
        def _():
            self.copy(self.out, 0, self.f).wait_recv()


def back_kernel(
    n, far_kv,
    do_ref, gwout_ref, s1_ref, s2_ref, qcat_ref, qpos_ref, kv_ref, lse_ref, of_ref,
    tok_ref, p1_ref, ev_ref, gates_ref, gsel_ref, x_ref, small_ref, dmid_ref, vec_ref, table_ref,
    din_ref, gp_ref, gq_ref, g1_ref, g2_ref, go_ref, vq_ref, dkv_ref,
    delta_ref, grad_ref, kcat_ref, acc_ref, ring_ref, pin_ref, drel_ref, dqs_ref, dq_ref, part_ref, dp_ref,
    gpa_ref, gpb_ref, mine_ref, vin_ref,
    s0, s1, s2, s3, s4, s5, s6,
    p0, p1, p2, p3, p4, p5, p6, u1, u2, u5, u6,
    fin2, got2, two_s, two_r, w0, w1, w2, w3, w4, w5, w6, y1, y2, y5, y6, goty, swap_s, swap_r,
    kv_s, kv_r, pin_r, dq_s, dq_r, gp_s, gp_r, gq_s, gq_r, g1_s, g1_r, g2_s, g2_r, go_s, go_r,
    vc_s, vc_r, vf_s, vf_r, loc,
):
    f, c = lax.axis_index("fsdp"), lax.axis_index("ctx")
    groups = n // 4
    seq, turn = c // groups, lax.rem(c, groups)
    tokens, width = x_ref.shape
    scale = 1.0 / math.sqrt(112)
    own_turn, own_slot = holder_of(c, groups)
    rows = width // n
    greet(f, c, 4, n)

    sub_out = p0.shape[0] // max(1, groups // 2)
    cut = gwout_ref.shape[1] // sub_out
    sum_out = LineSum(
        f, c, n, lambda k, sub: gwout_ref.at[k, pl.ds(pl.multiple_of(sub * cut, cut), cut), :],
        p1, p2, p5, p6, pair=(p0, p3, p4), subs=sub_out, lone=True,
    )
    sum_one = LineSum(f, c, n, lambda o, sub: s1_ref.at[o], u1, u2, u5, u6)
    half = gpa_ref.shape[1]
    pair_to = c + 1 - 2 * lax.rem(c, 2)

    def block_rows(ref, k):
        return ref.at[pl.ds(pl.multiple_of(k * rows, rows), rows), :]

    sum_in = LineSum(
        f, c, n, lambda k, sub: block_rows(gpa_ref, k), w1, w2, w5, w6, pair=(w0, w3, w4)
    )
    sum_late = LineSum(f, c, n, lambda o, sub: block_rows(gpb_ref, 2 * o + sub), y1, y2, y5, y6, subs=2)
    swap_two = copy_to(s2_ref.at[1], got2, two_s, two_r, f, pair_to)
    swap_late = copy_to(y2.at[pair_to], goty, swap_s, swap_r, f, pair_to)

    sum_out.begin()
    swap_two.start()

    def prepare(i, _):
        delta_ref[i] = jnp.sum(do_ref[i].astype(F32).T * of_ref[i], axis=0, keepdims=True)
        grad_ref[i] = jnp.zeros((tokens, width + LANES), F32)
        return 0

    lax.fori_loop(0, 4, prepare, 0)
    row_in = lax.broadcasted_iota(jnp.int32, (tokens, tokens), 0)
    col_in = lax.broadcasted_iota(jnp.int32, (tokens, tokens), 1)
    lane = lax.broadcasted_iota(jnp.int32, (tokens, LANES), 1)
    spots = jnp.logical_or(lane == SPOT_A, lane == SPOT_B)
    last_own = block_of(turn, 3, groups)
    mine_ref[...] = vec_ref[...]

    def close_query(i, sine, cosine):
        first = grad_ref[i, :, 0 : width // 2]
        second = grad_ref[i, :, width // 2 : width]
        drel_ref[i, :, 0 : width // 2] = ((first * sine - second * cosine) * scale).astype(BF16)
        drel_ref[i, :, width // 2 : width] = ((first * cosine + second * sine) * scale).astype(BF16)
        d_place = mm(drel_ref[i], p1_ref[:, :, 896:].reshape(width, LANES))
        d_content = jnp.where(spots, 0.0, grad_ref[i, :, width:] * scale)
        dqs_ref[i] = (d_content + d_place).astype(BF16)
        mine_ref[6:7, 0:LANES] += jnp.sum(d_content, axis=0, keepdims=True)
        mine_ref[7:8, 0:LANES] += jnp.sum(d_place, axis=0, keepdims=True)
        block = block_of(turn, i, groups)

        @pl.when(block != c)
        def _():
            copy_to(dqs_ref.at[i], dq_ref.at[seq], dq_s.at[i], dq_r.at[seq], f, block).start()

        @pl.when(block == c)
        def _():
            dq_ref[seq] = dqs_ref[i]

    bit = lax.rem(c, 2)
    pair_last = block_of(turn + 1 - 2 * bit, 3, groups)

    def ring_pair(kb):
        slot = lax.rem(kb, 4)
        return copy_to(ring_ref.at[slot], pin_ref.at[kb // 2], kv_s.at[slot], pin_r.at[kb // 2], f, pair_to)

    def ring_copy(kb):
        slot = lax.rem(kb, 4)
        return copy_to(ring_ref.at[slot], dkv_ref.at[c // 2], kv_s.at[slot], kv_r.at[c // 2], f, kb)

    def ring_local(kb):
        slot = lax.rem(kb, 4)
        return pltpu.make_async_copy(ring_ref.at[slot], dkv_ref.at[c // 2], kv_s.at[slot])

    def sums(kb):
        return jnp.logical_and(lax.rem(kb, 2) == bit, kb <= jnp.maximum(last_own, pair_last))

    def gives(kb):
        return jnp.logical_and(lax.rem(kb, 2) != bit, kb <= last_own)

    def ring_free(kb):
        @pl.when(gives(kb))
        def _():
            ring_pair(kb).wait_send()

        @pl.when(jnp.logical_and(sums(kb), kb != c))
        def _():
            ring_copy(kb).wait_send()

        @pl.when(jnp.logical_and(sums(kb), kb == c))
        def _():
            ring_local(kb).wait()

    def pass_on(kb):
        @pl.when(sums(kb))
        def _():
            total = acc_ref[lax.rem(kb, 2)]
            slot = lax.rem(kb, 4)

            @pl.when(kb <= pair_last)
            def _():
                ring_pair(kb).wait_recv()
                ring_ref[slot] = (total + pin_ref[kb // 2].astype(F32)).astype(BF16)

            @pl.when(kb > pair_last)
            def _():
                ring_ref[slot] = total.astype(BF16)

            @pl.when(kb != c)
            def _():
                ring_copy(kb).start()

            @pl.when(kb == c)
            def _():
                ring_local(kb).start()

    def key_block(kb, _):
        own = [block_of(turn, i, groups) for i in range(4)]
        first = sum((b < kb).astype(jnp.int32) for b in own)
        ready = sum((b == kb).astype(jnp.int32) for b in own)
        sine, cosine = sin_cos(key_places(kv_ref[kb]), table_ref)
        kcat_ref[:, 0 : width // 2] = cosine.astype(BF16)
        kcat_ref[:, width // 2 : width] = sine.astype(BF16)
        kcat_ref[:, width:] = kv_ref[kb, :, 0:128]
        now = lax.rem(kb, 2)
        acc_ref[now] = jnp.zeros((tokens, 256), F32)

        def query_block(i, _):
            gap = (block_of(turn, i, groups) - kb) * tokens
            scores = mm_t(kcat_ref[...], qcat_ref[i])
            probs = jnp.where(row_in <= col_in + gap, jnp.exp(scores - lse_ref[i]), 0.0)
            d_probs = mm_t(kv_ref[kb, :, 128:256], do_ref[i])
            d_scores = (probs * (d_probs - delta_ref[i])).astype(BF16)
            acc_ref[now, :, 0:128] += mm(d_scores, qcat_ref[i, :, width:])
            acc_ref[now, :, 128:256] += mm(probs.astype(BF16), do_ref[i])
            grad_ref[i] += mm_left_t(d_scores, kcat_ref[...])
            return 0

        lax.fori_loop(first, 4, query_block, 0)

        @pl.when(ready == 1)
        def _():
            close_query(first, sine, cosine)

        @pl.when(kb >= 4)
        def _():
            ring_free(kb - 4)

        @pl.when(gives(kb))
        def _():
            ring_ref[lax.rem(kb, 4)] = acc_ref[now].astype(BF16)
            ring_pair(kb).start()

        @pl.when(kb >= 1)
        def _():
            pass_on(kb - 1)

        @pl.when(jnp.logical_and(now == 1, kb < n - 1))
        def _():
            sum_one.turn(kb // 2)


        return 0

    lax.fori_loop(0, n, key_block, 0)
    pass_on(n - 1)
    sum_out.turn(0)
    share_out = LoneShare(sum_out, go_ref, go_s, go_r)
    gathers = []
    def hand_out(held, out, send, recv):
        local = pltpu.make_async_copy(held, out.at[f], loc.at[len(gathers)])
        local.start()
        gather = QuadGather(f, c, out, send, recv)
        gather.begin(held)
        gathers.append((gather, local))

    all_tokens = 4 * tokens
    d_rel = drel_ref[...].reshape(all_tokens, width)
    gpb_ref[:, 896 - half :] = mm_left_t(d_rel, qpos_ref[...].reshape(all_tokens, LANES)).astype(BF16)

    def collect(s, _):
        to = s * groups + own_turn

        @pl.when(to != c)
        def _():
            copy_to(dqs_ref.at[0], dq_ref.at[s], dq_s.at[0], dq_r.at[s], f, c).wait_recv()

        acc_ref[0] = jnp.zeros((tokens, 256), F32)

        def add(k, _):
            giver = 2 * k + bit
            at = (s * groups + giver) // 2
            last = jnp.maximum(block_of(giver, 3, groups), block_of(giver + 1 - 2 * bit, 3, groups))

            @pl.when(last >= c)
            def _():
                @pl.when(s * groups + giver != c)
                def _():
                    copy_to(ring_ref.at[0], dkv_ref.at[at], kv_s.at[0], kv_r.at[at], f, c).wait_recv()

                if far_kv:
                    bring = pltpu.make_async_copy(dkv_ref.at[at], part_ref, loc.at[4])
                    bring.start()
                    bring.wait()
                    acc_ref[0] += part_ref[...].astype(F32)
                else:
                    acc_ref[0] += dkv_ref[at].astype(F32)

            return 0

        lax.fori_loop(0, groups // 2, add, 0)
        dp_ref[s, :, 0:128] = dq_ref[s]
        dp_ref[s, :, 128:256] = acc_ref[0, :, 0:128].astype(BF16)
        d_values = acc_ref[0, :, 128:256]
        for e in range(5):
            values = ev_ref[s, :, e * LANES : (e + 1) * LANES].astype(F32)
            column = jnp.sum(values * d_values, axis=1, keepdims=True) * gates_ref[s, :, 24 + e : 25 + e]
            part = gates_ref[s, :, 16 + e : 17 + e] * d_values
            part = jnp.where(lane == SPOT_A, column, part)
            part = jnp.where(lane == SPOT_B, gsel_ref[s, :, e : e + 1], part)
            dp_ref[s, :, 256 + e * LANES : 384 + e * LANES] = part.astype(BF16)
        return 0

    def ring_drain(k, _):
        ring_free(n - 4 + k)
        return 0

    lax.fori_loop(0, 4, ring_drain, 0)
    lax.fori_loop(0, 4, collect, 0)
    sum_out.turn(1)
    tile = 256

    def weight_tile(i, _):
        spot = pl.multiple_of(i * tile, tile)
        left = tok_ref[:, :, pl.ds(spot, tile)].reshape(all_tokens, tile)
        right = dp_ref[...].reshape(all_tokens, 896)
        result = mm_left_t(left, right).astype(BF16)
        gpa_ref[pl.ds(spot, tile), :] = result[:, 0:half]
        gpb_ref[pl.ds(spot, tile), 0 : 896 - half] = result[:, half:]
        return 0

    lax.fori_loop(0, width // tile, weight_tile, 0)
    sum_in.begin()
    sum_late.turn(0)
    lax.fori_loop(2, n // 2 - 1, lambda k, u: (sum_out.turn(k), u)[1], 0)
    in_sum = QuadSum(f, c, s0, s1, s2, s3, s4, s5, s6)
    for k in (3, 2, 1, 0):
        weights = p1_ref[:, :, 0:896].reshape(width, 896)
        in_sum.put(k, mm_t(dp_ref[f ^ k], weights))
        if k == 2:
            in_sum.cross()
    swap_two.wait()
    fin2[...] = (s2_ref[0].astype(F32) + got2[...].astype(F32)).astype(BF16)
    sum_one.finish()
    sum_late.turn(1)
    sum_out.finish()
    hand_out(fin2, g2_ref, g2_s, g2_r)
    hand_out(u2.at[c // 2], g1_ref, g1_s, g1_r)
    share_out.begin()
    lax.fori_loop(2, n // 2 - 1, lambda k, u: (sum_late.turn(k), u)[1], 0)
    d_norm = in_sum.total()
    xhat, spread = layer_stats(x_ref[...].astype(F32))
    gain = spread_vector(small_ref[:, 0, :], width // n)
    din_ref[...] = dmid_ref[...] + layer_back(d_norm, gain, xhat, spread)
    mine_ref[4:5, :] = jnp.sum(d_norm * xhat, axis=0, keepdims=True)
    mine_ref[5:6, :] = jnp.sum(d_norm, axis=0, keepdims=True)

    def vec_send(k, _):
        to = lax.rem(c + k, n)
        copy_to(mine_ref, vin_ref.at[c], vc_s.at[to], vc_r.at[c], f, to).start()
        return 0

    lax.fori_loop(1, n, vec_send, 0)
    vin_ref[c] = mine_ref[...]
    sum_in.turn(0)
    sum_late.finish()
    swap_late.start()
    lax.fori_loop(1, n // 2 - 1, lambda k, u: (sum_in.turn(k), u)[1], 0)
    for gather, _ in gathers:
        gather.relay()
    share_out.relay()
    swap_late.wait()
    y2[c] = (y2[c].astype(F32) + goty[...].astype(F32)).astype(BF16)
    hand_out(y2.at[c], gq_ref, gq_s, gq_r)
    sum_in.finish()
    hand_out(w2.at[c // 2], gp_ref, gp_s, gp_r)

    def vec_wait(k, _):
        to = lax.rem(c + k, n)
        copy_to(mine_ref, vin_ref.at[to], vc_s.at[to], vc_r.at[to], f, to).wait()
        return 0

    lax.fori_loop(1, n, vec_wait, 0)
    vq_ref[f] = jnp.sum(vin_ref[...], axis=0)
    for k in range(1, 4):
        copy_to(vq_ref.at[f], vq_ref.at[f], vf_s.at[k], vf_r.at[f], f ^ k, c).start()
    for gather, _ in gathers[2:]:
        gather.relay()
    for k in range(1, 4):
        copy_to(vq_ref.at[f ^ k], vq_ref.at[f ^ k], vf_s.at[k], vf_r.at[f ^ k], f, c).wait_recv()
        copy_to(vq_ref.at[f], vq_ref.at[f], vf_s.at[k], vf_r.at[f], f, c).wait_send()
    for one, local in gathers:
        one.got(f ^ 1)
        one.got(f ^ 3)
        one.sent()
        local.wait()
    share_out.finish()
    for one in (sum_one, sum_out, sum_in, sum_late):
        one.sent()
    in_sum.sent()

    def drain(i, _):
        @pl.when(block_of(turn, i, groups) != c)
        def _():
            copy_to(dqs_ref.at[i], dq_ref.at[0], dq_s.at[i], dq_r.at[0], f, c).wait_send()

        return 0

    lax.fori_loop(0, 4, drain, 0)


def early_rows(count):
    return count // 2 if count % 32 == 0 else count


def cuts(count):
    parts = max(1, count // 64)
    return parts if count % (16 * parts) == 0 else 1


def pair_scratch(blocks, subs, rows, cols):
    return [pltpu.VMEM((blocks * subs, rows // subs, cols), BF16)]


def line_scratch(blocks, subs, rows, cols):
    return [
        pltpu.VMEM(((blocks + 1) * subs, rows // subs, cols), BF16),
        pltpu.VMEM((blocks * subs, rows // subs, cols), BF16),
    ]


def line_sems(blocks, subs):
    return [DMA((blocks * subs,)), DMA(((blocks + 1) * subs,))]


def back(n, da, gwout, s1, s2, qcat, qpos, kv, lse, of, tok, p1, ev, gates, gsel, x, small, dmid, vec, table):
    t, d = x.shape
    g = n // 4
    quarter = s1.shape[2]
    rows, out_rows, two_rows = d // n, gwout.shape[1], s2.shape[1]
    half = d // 2
    sub_out = cuts(out_rows)
    lone, line = n // 8, n // 2
    far_kv = g > 4
    return pl.pallas_call(
        functools.partial(back_kernel, n, far_kv),
        out_shape=[
            sds((t, d), F32), sds((4, rows, half), BF16), sds((4, rows, half), BF16), sds((4, rows, quarter), BF16),
            sds((4, two_rows, d), BF16), sds((sub_out, out_rows // sub_out, d), BF16),
            sds((4, 8, d), F32), sds((line, t, 256), BF16),
        ],
        in_specs=[VMEM] * 19,
        out_specs=[VMEM, ANY, ANY, ANY, ANY, ANY, VMEM, ANY if far_kv else VMEM],
        scratch_shapes=[
            pltpu.VMEM((4, 1, t), F32), pltpu.VMEM((4, t, d + LANES), F32),
            pltpu.VMEM((t, d + LANES), BF16), pltpu.VMEM((2, t, 256), F32), pltpu.VMEM((4, t, 256), BF16),
            pltpu.VMEM((line, t, 256), BF16),
            pltpu.VMEM((4, t, d), BF16), pltpu.VMEM((4, t, LANES), BF16), pltpu.VMEM((4, t, LANES), BF16),
            pltpu.VMEM((t, 256), BF16), pltpu.VMEM((4, t, 896), BF16), pltpu.VMEM((d, half), BF16), pltpu.VMEM((d, half), BF16),
            pltpu.VMEM((8, d), F32), pltpu.VMEM((n, 8, d), F32),
        ]
        + quad_sum_scratch(t, d)
        + pair_scratch(lone, sub_out, out_rows, d) + line_scratch(lone, sub_out, out_rows, d)
        + [DMA((lone * sub_out,))] * 2 + line_sems(lone, sub_out)
        + line_scratch(line, 1, rows, quarter) + line_sems(line, 1)
        + [pltpu.VMEM((two_rows, d), BF16), pltpu.VMEM((two_rows, d), BF16), DMA, DMA]
        + pair_scratch(line, 1, rows, half) + line_scratch(line, 1, rows, half)
        + [DMA((line,))] * 2 + line_sems(line, 1)
        + line_scratch(line, 2, 2 * rows, half) + line_sems(line, 2)
        + [pltpu.VMEM((rows, half), BF16), DMA, DMA]
        + [
            DMA((4,)), DMA((line,)), DMA((line,)), DMA((4,)), DMA((4,)), DMA((3,)), DMA((4,)),
            DMA((3,)), DMA((4,)), DMA((3,)), DMA((4,)), DMA((3,)), DMA((4,)), DMA((2,)), DMA, DMA((n,)), DMA((n,)), DMA((4,)), DMA((4,)), DMA((5,)),
        ],
        compiler_params=pltpu.CompilerParams(
            collective_id=2, has_side_effects=True, vmem_limit_bytes=63 << 20
        ),
        name="back",
    )(da, gwout, s1, s2, qcat, qpos, kv, lse, of, tok, p1, ev, gates, gsel, x, small, dmid, vec, table)


def pad_channels(v, group):
    lead = v.shape[:-1]
    v = v.reshape(lead + (112 // group, group))
    v = jnp.pad(v, [(0, 0)] * len(lead) + [(0, 0), (0, group // 7)])
    return v.reshape(lead + (LANES,))


def head_pick(w, f, heads=4):
    w = w.reshape(w.shape[0], heads, -1)
    return lax.dynamic_index_in_dim(w, f, 1, keepdims=False)


def route_lanes(routes):
    hot = routes[..., None] == jnp.arange(8, dtype=jnp.int32)
    return jnp.sum(hot.astype(F32), axis=-2)


def pack_inputs(
    n, f, positions, value_routes, output_routes, ln1_gain, ln1_bias, wq, wk, wrel, u_bias, v_bias,
    wvsel, wv, wosel, wout, ln2_gain, ln2_bias, b1, b2,
):
    t = positions.shape[0]
    rows = wq.shape[0]
    group = math.gcd(112, wout.shape[0])
    masks = jnp.concatenate([route_lanes(value_routes), route_lanes(output_routes)], axis=-1).reshape(t, 64)
    place = jnp.stack([positions // 128, positions % 128], axis=-1).astype(F32)
    aux = jnp.concatenate([masks, place, jnp.zeros((t, 62), F32)], axis=-1).astype(BF16)
    lane = jnp.arange(LANES)
    experts = pad_channels(head_pick(wv, f).reshape(rows, 5, 112), group)
    experts = jnp.where(lane == SPOT_A, head_pick(wvsel, f)[..., None], experts)
    experts = jnp.where(lane == SPOT_B, head_pick(wosel, f)[..., None], experts)
    p1 = jnp.concatenate(
        [
            pad_channels(head_pick(wq, f), group), pad_channels(head_pick(wk, f), group),
            experts.reshape(rows, 640), pad_channels(head_pick(wrel, f), group),
        ],
        axis=-1,
    )
    piece = b1.shape[0] // 4
    vectors = [ln1_gain, ln1_bias, ln2_gain, ln2_bias, b2]
    vectors = [jnp.pad(v, (0, LANES - v.shape[0])) for v in vectors]
    extra = jnp.pad(b1.reshape(-1, piece), ((0, 0), (0, LANES - piece)))
    small = jnp.concatenate([jnp.stack(vectors), extra]).astype(F32)
    small = jnp.pad(small, ((0, 16 - small.shape[0]), (0, 0)))
    pieces = wout.reshape(-1, group, wout.shape[1])
    pieces = jnp.pad(pieces, ((0, 0), (0, group // 7), (0, 0))).reshape(-1, wout.shape[1])
    pieces = jnp.pad(pieces, ((0, -pieces.shape[0] % 16), (0, 0)))
    bias = jnp.concatenate([pad_channels(u_bias, group), pad_channels(v_bias, group)]).astype(F32)
    return aux, p1, small, pieces, bias


def unpack_kernel(
    gp_ref, gq_ref, g1_ref, g2_ref, go_ref, vq_ref, y_ref, din_ref,
    query_ref, key_ref, rel_ref, value_ref, vsel_ref, osel_ref, one_ref, two_ref, out_ref,
    gain1_ref, shift1_ref, gain2_ref, shift2_ref, b2_ref, b1_ref, u_ref, v_ref, y_out, din_out,
    heads_ref,
):
    c = lax.axis_index("ctx")
    rows, half = gp_ref.shape[1], gp_ref.shape[2]
    y_out[...] = y_ref[...]
    din_out[...] = din_ref[...]

    def block(h, k):
        ref, spot = (gp_ref, k * LANES) if k * LANES < half else (gq_ref, k * LANES - half)
        return ref[h, :, spot : spot + LANES].astype(F32).T

    def place(ref, start, piece):
        ref[start : start + 56, :] = piece[0:56]
        ref[start + 56 : start + 112, :] = piece[64:120]

    for h in range(4):
        for ref, k in ((query_ref, 0), (key_ref, 1), (rel_ref, 7)):
            place(ref, 112 * h, block(h, k))
        for e in range(5):
            piece = block(h, 2 + e)
            place(value_ref, 560 * h + 112 * e, piece)
            vsel_ref[5 * h + e : 5 * h + e + 1, :] = piece[SPOT_A : SPOT_A + 1]
            osel_ref[5 * h + e : 5 * h + e + 1, :] = piece[SPOT_B : SPOT_B + 1]
    part = g2_ref.shape[1]
    for h in range(4):
        two_ref[h * part : (h + 1) * part, :] = g2_ref[h].astype(F32)
        for k in range(g1_ref.shape[2] // part):
            spot = (4 * k + h) * part
            one_ref[:, spot : spot + part] = g1_ref[h, :, k * part : (k + 1) * part].astype(F32)
    for k in range(go_ref.shape[0]):
        out_ref[56 * k : 56 * k + 56, :] = go_ref[k, 0:56, :].astype(F32)
    own = pl.ds(pl.multiple_of(c * rows, rows), rows)
    for ref, k in ((gain2_ref, 0), (shift2_ref, 1), (b2_ref, 2), (gain1_ref, 4), (shift1_ref, 5)):
        ref[...] = sum(vq_ref[h, k : k + 1, own] for h in range(4))
    for h in range(4):
        b1_ref[:, h * part : (h + 1) * part] = vq_ref[h, 3:4, own]
    lane = lax.broadcasted_iota(jnp.int32, (8, LANES), 1)
    for ref, k in ((u_ref, 6), (v_ref, 7)):
        for h in range(4):
            heads_ref[h : h + 1, :] = vq_ref[h, k : k + 1, 0:LANES]
        value = heads_ref[...]
        moved = jnp.where(lane < 56, value, pltpu.roll(value, LANES - 8, 1))
        ref[...] = moved[0:4, 0:112]


def unpack(gp, gq, g1, g2, go, vq, y, d_in):
    rows, part, d = gp.shape[1], g2.shape[1], g2.shape[2]
    shapes = [
        (448, rows), (448, rows), (448, rows), (2240, rows), (20, rows), (20, rows), (rows, 4 * g1.shape[2]),
        (4 * part, d), (go.shape[0] * 56, d), (1, rows), (1, rows), (1, rows), (1, rows), (1, rows),
        (1, 4 * part), (4, 112), (4, 112),
    ]
    return pl.pallas_call(
        unpack_kernel,
        out_shape=[sds(shape, F32) for shape in shapes] + [sds(y.shape, BF16), sds(d_in.shape, F32)],
        in_specs=[VMEM] * 8,
        out_specs=[VMEM] * (len(shapes) + 2),
        scratch_shapes=[pltpu.VMEM((8, LANES), F32)],
        compiler_params=pltpu.CompilerParams(vmem_limit_bytes=62 << 20),
        name="unpack",
    )(gp, gq, g1, g2, go, vq, y, d_in)


def drop_pads(v, group):
    lead = v.shape[:-1]
    wide = group * 8 // 7
    return v.reshape(lead + (LANES // wide, wide))[..., :group].reshape(lead + (112,))


def on_device(n, *args):
    (
        x, positions, value_routes, output_routes, ln1_gain, ln1_bias, wq, wk, wrel, u_bias, v_bias,
        wvsel, wv, wosel, wout, ln2_gain, ln2_bias, w1, b1, w2, b2, cot,
    ) = args
    f, c = lax.axis_index("fsdp"), lax.axis_index("ctx")
    d = x.shape[1]
    g = n // 4
    group = math.gcd(112, wout.shape[0])
    aux, p1, small, pieces, bias = pack_inputs(
        n, f, positions, value_routes, output_routes, ln1_gain, ln1_bias, wq, wk, wrel, u_bias, v_bias,
        wvsel, wv, wosel, wout, ln2_gain, ln2_bias, b1, b2,
    )
    table = jnp.asarray(turn_table(d))
    rows, hidden = w1.shape
    part = hidden // n // 4
    w1_own = lax.dynamic_index_in_dim(w1.reshape(rows, n, 4, part), f, 2, keepdims=False).reshape(rows, n * part)
    tok, p1g, smallg, woutg, w2e, cotg, ev, gates, o, qcat, qpos, kv, lse, of = attend(
        n, x, aux, cot, p1, small, pieces, w2, bias, table
    )
    block = 640 // g
    out, dmid, gwout, s1, s2, d_o, gsel, vec = feed(
        n, x, cotg, gates, o, woutg[:, :block].reshape(640, d), smallg, w1_own, w2, w2e
    )
    gwout = gwout.reshape(g, block, d)
    gwout = jnp.pad(gwout, ((0, 0), (0, pieces.shape[0] - block), (0, 0)))
    d_in, gp, gq, g1, g2, go, vq, _ = back(
        n, d_o, gwout, s1, s2, qcat, qpos, kv, lse, of, tok, p1g, ev, gates, gsel, x, smallg, dmid, vec, table
    )
    if group == 56 and part == LANES and rows == LANES:
        (
            g_query, g_key, g_rel, g_value, g_vsel, g_osel, g_one, g_two, g_out,
            gain1, shift1, gain2, shift2, g_b2, g_b1, g_u, g_v, out, d_in,
        ) = unpack(gp, gq, g1, g2, go.reshape(-1, 64, d), vq, out, d_in)
        return (
            out, d_in, gain1[0], shift1[0], g_query.T, g_key.T, g_rel.T, g_u, g_v, g_vsel.T, g_value.T, g_osel.T, g_out,
            gain2[0], shift2[0], g_one, g_b1[0], g_two, g_b2[0],
        )
    gp = jnp.transpose(jnp.concatenate([gp, gq], axis=-1), (1, 0, 2))
    g_query = drop_pads(gp[..., 0:128], group).reshape(rows, 448).astype(F32)
    g_key = drop_pads(gp[..., 128:256], group).reshape(rows, 448).astype(F32)
    g_rel = drop_pads(gp[..., 896:], group).reshape(rows, 448).astype(F32)
    experts = gp[..., 256:896].reshape(rows, 4, 5, LANES)
    g_value = drop_pads(experts, group).reshape(rows, 2240).astype(F32)
    g_vsel = experts[..., SPOT_A].reshape(rows, 20).astype(F32)
    g_osel = experts[..., SPOT_B].reshape(rows, 20).astype(F32)
    g_one = jnp.transpose(g1.reshape(4, rows, n, part), (1, 2, 0, 3)).reshape(rows, hidden).astype(F32)
    g_two = g2.reshape(-1, d).astype(F32)
    g_out = go.reshape(-1, d)[:block].reshape(-1, group * 8 // 7, d)[:, :group].reshape(-1, d).astype(F32)
    sums = jnp.sum(vq, axis=0)
    own = lax.dynamic_slice_in_dim(sums, c * rows, rows, 1)
    g_b1 = lax.dynamic_slice_in_dim(vq[:, 3, :], c * part, part, 1).reshape(-1)
    g_u = drop_pads(vq[:, 6, 0:LANES], group)
    g_v = drop_pads(vq[:, 7, 0:LANES], group)
    return (
        out, d_in, own[4], own[5], g_query, g_key, g_rel, g_u, g_v, g_vsel, g_value, g_osel, g_out,
        own[0], own[1], g_one, g_b1, g_two, own[2],
    )


def solution(mesh):
    both = ("fsdp", "ctx")
    row, vector, matrix = P(both, None), P("ctx"), P("ctx", None)
    in_specs = (
        row, P(both), P(both, None, None), P(both, None, None), vector, vector, matrix, matrix, matrix,
        P(), P(), matrix, matrix, matrix, matrix, vector, vector, matrix, vector, matrix, vector, row,
    )
    out_specs = (
        row, row, vector, vector, matrix, matrix, matrix, P(), P(), matrix, matrix, matrix, matrix,
        vector, vector, matrix, vector, matrix, vector,
    )
    return jax.shard_map(
        functools.partial(on_device, mesh.shape["ctx"]),
        mesh=mesh, in_specs=in_specs, out_specs=out_specs, check_vma=False,
    )
```
